32 devices in a mesh: seq: 16 (over z, y, x), dp: 2 (over core).
Axes of the slice: x: 2, y: 2, z: 4, core: 2. Of those that a mesh axis runs over, the one named last changes fastest.
Arguments:
- tokens: bfloat16 [4096, 4096], P(('dp', 'seq')), parts along dimension 0, may hold values from -6 to 6
- sign_in: int32 [4096, 256], P(('dp', 'seq')), parts along dimension 0, may hold values from 0 to 65535
- sign_out: int32 [4096, 32], P(('dp', 'seq')), parts along dimension 0, may hold values from 0 to 65535
- w_value: bfloat16 [4096, 512], P('seq'), may hold values from -0.09375 to 0.09375
- w_noise: bfloat16 [4096, 512], P('seq'), may hold values from -0.046875 to 0.046875
- w_gate: bfloat16 [4096, 512], replicated, may hold values from -0.09375 to 0.09375
- conv_taps: float32 [3, 1024], replicated, may hold values from -3.5 to 3.5
- long_filter: float32 [2048, 512], P('seq'), may hold values from -1.5 to 1.5, as said below
- w_out: bfloat16 [512, 4096], replicated, may hold values from -0.25 to 0.25
Outputs:
- mixed: bfloat16 [4096, 4096], P(('dp', 'seq')), parts along dimension 0
The draws below stay inside these ranges and needn't reach their ends.
There are 2 independent parts, one for each index of `dp`. The reference program is written for one: setup_inputs(seed, part) draws one part's arguments, and reference() takes and returns one part's arrays. A program takes and returns all parts, laid end to end along the dimension named above; an argument that names none is the same for every part. Nothing has to cross between parts.
Inputs may be any that keep to these rules, and one draw needn't show every extreme that they name: `long_filter`: filter taps are real and finite.
All inputs are finite; a program needn't handle non-finite values.
Results may differ from the reference program's by a relative error of at most 0.0064.
Values may be sent and summed in bfloat16 or wider, within the bound.
No kernel may reach another device: no remote copies, remote signals or barrier semaphores. Data moves between devices by JAX's collectives and lax.ppermute only.
A program may use at most 64 MiB of HBM per device.

```python
import jax
import jax.numpy as jnp
from jax import lax

D = 4096
CH = 512
TAPS = 3
SEQ = 2048


def draw_long_filter(key, part):
    rough_part = jnp.clip(jax.random.normal(key, (SEQ, CH), jnp.float32), -5.0, 5.0)
    lag_index = jnp.arange(SEQ, dtype=jnp.float32)[:, None]
    return 0.3 * rough_part * lax.rsqrt(1.0 + lag_index)


def plant(values, rng, smallest, largest):
    place = [jax.random.randint(jax.random.fold_in(rng, axis), (), 0, length) for axis, length in enumerate(values.shape)]
    main_axis = values.shape.index(max(values.shape))
    beside = place[:main_axis] + [(place[main_axis] + 1) % values.shape[main_axis]] + place[main_axis + 1:]
    return values.at[tuple(place)].set(smallest).at[tuple(beside)].set(largest)


def block_levels(own_key, dims, split, smallest, largest):
    gain, own = 1.0, jax.random.fold_in(own_key, 6)
    for axis_at, blocks in split:
        heights = jnp.exp(jax.random.uniform(jax.random.fold_in(own, axis_at), (blocks,), jnp.float32, smallest / len(split), largest / len(split)))
        gain = gain * jnp.repeat(heights, dims[axis_at] // blocks).reshape([-1 if axis == axis_at else 1 for axis in range(len(dims))])
    return gain


def noise(stream_key, shape, width, reach, pieces=(), kind=jnp.bfloat16):
    result = jax.random.normal(stream_key, shape, jnp.float32) * width
    if len(pieces) > 0:
        result = block_levels(stream_key, shape, pieces, -0.22, 0.18) * result
    return jnp.clip(result, min=-reach, max=reach).astype(kind)


def setup_inputs(seed: int = 0, part: int = 0) -> dict:
    key_of = jax.random.split(jax.random.key(seed), 10)
    part_splits = jax.random.split(jax.random.fold_in(key_of[9], part), 10)
    return {
        "tokens": noise(part_splits[0], (SEQ, D), 1.0, 6.0, ((0, 16),)),
        "sign_in": plant(jax.random.randint(part_splits[1], (SEQ, D // 16), 0, 65536), jax.random.fold_in(part_splits[1], 1), 0, 65535).astype(jnp.int32),
        "sign_out": plant(jax.random.randint(part_splits[2], (SEQ, CH // 16), 0, 65536), jax.random.fold_in(part_splits[2], 1), 0, 65535).astype(jnp.int32),
        "w_value": noise(key_of[3], (D, CH), D ** -0.5, 0.09375, ((0, 16),)),
        "w_noise": noise(key_of[4], (D, CH), (4 * D) ** -0.5, 0.046875, ((0, 16),)),
        "w_gate": noise(key_of[5], (D, CH), D ** -0.5, 0.09375),
        "conv_taps": noise(key_of[6], (TAPS, 2 * CH), TAPS ** -0.5, 3.5, (), jnp.float32),
        "long_filter": draw_long_filter(jax.random.fold_in(key_of[9], 71), part),
        "w_out": noise(key_of[8], (CH, D), CH ** -0.5, 0.25),
    }


HIGHEST = lax.Precision.HIGHEST


def unpack_signs(packed):
    shifts = jnp.arange(16, dtype=jnp.int32)
    bit_table = jnp.bitwise_and(jnp.right_shift(packed[:, :, None], shifts[None, None, :]), 1)
    return (2 * bit_table - 1).reshape(packed.shape[0], packed.shape[1] * 16)


def reference(tokens, sign_in, sign_out, w_value, w_noise, w_gate, conv_taps, long_filter, w_out):
    flip_in = unpack_signs(sign_in).astype(jnp.bfloat16)
    flip_out = unpack_signs(sign_out).astype(jnp.float32)
    mean_part = jnp.dot(tokens, w_value, preferred_element_type=jnp.float32)
    noise_part = jnp.dot(tokens * flip_in, w_noise, preferred_element_type=jnp.float32)
    value_rows = (mean_part + flip_out * noise_part).astype(jnp.bfloat16)
    gate_rows = jnp.dot(tokens, w_gate, preferred_element_type=jnp.float32).astype(jnp.bfloat16)
    streams = jnp.concatenate([value_rows, gate_rows], axis=1).astype(jnp.float32)
    padded = jnp.concatenate([jnp.zeros((TAPS - 1, streams.shape[1]), jnp.float32), streams], axis=0)
    kernel = conv_taps[::-1][:, None, :]
    filtered = lax.conv_general_dilated(padded[None], kernel, (1,), "VALID", dimension_numbers=("NWC", "WIO", "NWC"), feature_group_count=streams.shape[1], precision=HIGHEST)[0]
    signal = filtered[:, :CH]
    gate_short = filtered[:, CH:]
    spec_signal = jnp.fft.fft(jnp.concatenate([signal, jnp.zeros_like(signal)], axis=0), axis=0)
    spec_filter = jnp.fft.fft(jnp.concatenate([long_filter, jnp.zeros_like(long_filter)], axis=0), axis=0)
    long_mixed = jnp.real(jnp.fft.ifft(spec_signal * spec_filter, axis=0))[:SEQ].astype(jnp.float32)
    gated_mix = (gate_short * long_mixed).astype(jnp.bfloat16)
    return jnp.dot(gated_mix, w_out, preferred_element_type=jnp.float32).astype(jnp.bfloat16)
```

```python
import functools

import jax
import jax.numpy as jnp
from jax import lax
from jax.experimental import pallas as pl
from jax.experimental.pallas import tpu as pltpu
from jax.sharding import Mesh, PartitionSpec as P

F32 = jnp.float32
BF16 = jnp.bfloat16
LANES = 128
GROUP = 8
MIB = 1 << 20


def whole(shape):
    return pl.BlockSpec(shape, lambda *_: (0,) * len(shape))


def sign_bytes(packed):
    return jnp.concatenate([packed & 255, packed >> 8], axis=-1).astype(BF16)


def expand_signs(pair, columns):
    words = columns // 16
    byte_at = lax.broadcasted_iota(jnp.int32, (2 * words, columns), 0)
    column = lax.broadcasted_iota(jnp.int32, (2 * words, columns), 1)
    picked = (column >> 4) + words * ((column >> 3) & 1) == byte_at
    spread = jnp.dot(pair, picked.astype(F32).astype(BF16), preferred_element_type=F32)
    bit_at = lax.broadcasted_iota(jnp.int32, spread.shape, 1) & 7
    return (((spread.astype(jnp.int32) >> bit_at) & 1) * 2 - 1).astype(F32)


def project_kernel(depth, channels, got_ref, *refs):
    weights, out_ref = refs[:-1], refs[-1]
    got = got_ref[...]
    words = depth // 16
    flip_in = expand_signs(got[:, depth : depth + 2 * words], depth).astype(BF16)
    start = depth + 2 * words
    flip_out = expand_signs(got[:, start : start + channels // 8], channels)
    tokens = got[:, :depth]
    flipped = tokens * flip_in
    step = depth // len(weights)
    mean_part, noise_part = 0.0, 0.0
    for at, piece in enumerate(weights):
        held = slice(at * step, (at + 1) * step)
        mean_part += jnp.dot(tokens[:, held], piece[:, :channels], preferred_element_type=F32)
        noise_part += jnp.dot(flipped[:, held], piece[:, channels:], preferred_element_type=F32)
    out_ref[...] = (mean_part + flip_out * noise_part).T.astype(BF16)


def toeplitz_kernel(taps_ref, out_ref):
    row = taps_ref[pl.ds(pl.program_id(0), 1), :]
    spread = jnp.broadcast_to(row, (LANES, row.shape[1]))
    turned = pltpu.roll(spread, 0, 1, stride=1, stride_axis=0)
    at = lax.broadcasted_iota(jnp.int32, spread.shape, 1)
    lag = lax.broadcasted_iota(jnp.int32, spread.shape, 0)
    out_ref[...] = jnp.where(at >= lag, turned, 0.0).astype(BF16)


def shifted(values, steps):
    moved = pltpu.roll(values, steps, 1)
    at = lax.broadcasted_iota(jnp.int32, values.shape, 1)
    return jnp.where(at >= steps, moved, 0.0)


def mix_kernel(near, far, held, parts_ref, taps_ref, table_ref, out_ref, left_ref, sums_ref):
    group, chunk = pl.program_id(0), pl.program_id(1)
    per_group = min(held, GROUP)
    blocks = out_ref.shape[0]
    rows = blocks * GROUP
    chunk_blocks = table_ref.shape[1] // LANES

    @pl.when((group == 0) & (chunk == 0))
    def _():
        planes = []
        for plane in range(far):
            total = 0.0
            for part in range(near):
                start = (plane * near + part) * held
                total += parts_ref[start : start + held, :].astype(F32)
            planes.append(total.astype(BF16).astype(F32))
        value = jnp.concatenate(planes, axis=1)
        signal = taps_ref[:, 0:1] * value
        for lag in range(1, 3):
            signal += taps_ref[:, lag : lag + 1] * shifted(value, lag)
        if held < GROUP:
            signal = jnp.concatenate(
                [signal, jnp.zeros((GROUP - held, signal.shape[1]), F32)], axis=0
            )
        for at in range(held // per_group):
            lines = signal[at * per_group : at * per_group + GROUP, :]
            stacked = jnp.concatenate(
                [lines[:, a * LANES : (a + 1) * LANES] for a in range(blocks)], axis=0
            )
            mine = lax.broadcasted_iota(jnp.int32, stacked.shape, 0) & (GROUP - 1)
            left_ref[at] = jnp.concatenate(
                [jnp.where(mine == c, stacked, 0.0).astype(BF16) for c in range(per_group)], axis=1
            )

    @pl.when(chunk == 0)
    def _():
        sums_ref[...] = jnp.zeros_like(sums_ref)

    partial = jnp.dot(left_ref[group], table_ref[...], preferred_element_type=F32)
    for at in range(chunk_blocks):
        start = pl.multiple_of((chunk * chunk_blocks + at) * GROUP, GROUP)
        sums_ref[pl.ds(start, rows), :] += partial[:, at * LANES : (at + 1) * LANES]

    @pl.when(chunk == pl.num_programs(1) - 1)
    def _():
        out_ref[...] = sums_ref[:rows, :].reshape(blocks, GROUP, LANES)[:, :per_group]


def out_kernel(gate_ref, mixed_ref, weight_ref, out_ref, gated_ref):
    @pl.when(pl.program_id(0) == 0)
    def _():
        gated = gate_ref[...] * mixed_ref[...].astype(F32)
        gated_ref[...] = gated.T.astype(BF16)

    out_ref[...] = jnp.dot(gated_ref[...], weight_ref[...], preferred_element_type=F32).astype(BF16)


def on_device(near, far, tokens, sign_in, sign_out, w_value, w_noise, w_gate, conv_taps, long_filter, w_out):
    rows, width = tokens.shape
    channels = w_gate.shape[1]
    count = near * far
    held = channels // count
    share = w_value.shape[0]
    depth = share * far
    far_at, near_at = lax.axis_index("far"), lax.axis_index("near")
    position = far_at * near + near_at
    everyone = ("far", "near")

    weights = jnp.concatenate([w_value, w_noise], axis=1)
    pieces = [weights] + [
        lax.ppermute(weights, "far", [(i, (i + step) % far) for i in range(far)])
        for step in range(1, far)
    ]

    def columns_of(array, per_row):
        turns = [
            lax.dynamic_slice_in_dim(
                array, (far_at - step) % far * near * per_row, near * per_row, axis=1
            ).reshape(rows, near, per_row)
            for step in range(far)
        ]
        return jnp.stack(turns, axis=2).transpose(1, 0, 2, 3).reshape(near, rows, far * per_row)

    out_bytes = jnp.broadcast_to(sign_bytes(sign_out)[None], (near, rows, channels // 8))
    packed = [
        columns_of(tokens, share),
        sign_bytes(columns_of(sign_in, share // 16)),
        out_bytes,
    ]
    used = sum(part.shape[2] for part in packed)
    spare = -used % LANES
    packed = jnp.concatenate(packed + [jnp.zeros((near, rows, spare), BF16)], axis=2)
    got = lax.all_to_all(packed, "near", 0, 0, tiled=True).reshape(near * rows, used + spare)

    lags = lax.all_to_all(long_filter.T.astype(BF16), everyone, 0, 0, tiled=True)
    lags = lags.reshape(count, held, rows).transpose(1, 0, 2).reshape(held, count * rows)
    length = count * rows
    table = pl.pallas_call(
        toeplitz_kernel,
        grid=(held,),
        in_specs=[whole((held, length))],
        out_specs=pl.BlockSpec((LANES, length), lambda c: (c, 0)),
        out_shape=jax.ShapeDtypeStruct((held * LANES, length), BF16),
        compiler_params=pltpu.CompilerParams(vmem_limit_bytes=48 * MIB),
        cost_estimate=pl.CostEstimate(
            flops=held * LANES * length * 4, bytes_accessed=held * LANES * length * 2, transcendentals=0
        ),
        name="toeplitz",
    )(lags.astype(F32))

    before = lax.ppermute(
        tokens[rows - 2 :], everyone, [(i, i + 1) for i in range(count - 1)]
    )
    gate_rows = jnp.dot(tokens, w_gate, preferred_element_type=F32).astype(BF16).astype(F32)
    gate_before = jnp.dot(before, w_gate, preferred_element_type=F32).astype(BF16).astype(F32)
    extended = jnp.concatenate([gate_before, gate_rows], axis=0)
    gate_short = sum(
        conv_taps[lag, channels:] * extended[2 - lag : 2 - lag + rows] for lag in range(3)
    ).T

    partial = pl.pallas_call(
        functools.partial(project_kernel, depth, channels),
        out_shape=jax.ShapeDtypeStruct((channels, near * rows), BF16),
        compiler_params=pltpu.CompilerParams(vmem_limit_bytes=48 * MIB),
        cost_estimate=pl.CostEstimate(
            flops=4 * near * rows * depth * channels, bytes_accessed=6 * MIB, transcendentals=0
        ),
        name="project",
    )(got, *pieces)
    parts = lax.all_to_all(partial, everyone, 0, 0, tiled=True)

    taps = lax.dynamic_slice_in_dim(conv_taps, position * held, held, axis=1).T
    blocks = length // LANES
    per_group = min(held, GROUP)
    chunk = min(length, 512)
    mixed = pl.pallas_call(
        functools.partial(mix_kernel, near, far, held),
        grid=(held // per_group, length // chunk),
        in_specs=[
            whole(parts.shape),
            whole(taps.shape),
            pl.BlockSpec((per_group * LANES, chunk), lambda g, n: (g, n)),
        ],
        out_specs=pl.BlockSpec((blocks, per_group, LANES), lambda g, n: (0, g, 0)),
        out_shape=jax.ShapeDtypeStruct((blocks, held, LANES), F32),
        scratch_shapes=[
            pltpu.VMEM((held // per_group, blocks * GROUP, per_group * LANES), BF16),
            pltpu.VMEM((2 * blocks * GROUP, LANES), F32),
        ],
        compiler_params=pltpu.CompilerParams(vmem_limit_bytes=48 * MIB),
        cost_estimate=pl.CostEstimate(
            flops=2 * held * LANES * length * LANES, bytes_accessed=held * LANES * length * 2, transcendentals=0
        ),
        name="mix",
    )(parts, taps, table)

    landed = lax.all_to_all(mixed.astype(BF16), everyone, 0, 0, tiled=True).reshape(channels, rows)
    step = min(width, 512)
    return pl.pallas_call(
        out_kernel,
        grid=(width // step,),
        in_specs=[
            whole((channels, rows)),
            whole((channels, rows)),
            pl.BlockSpec((channels, step), lambda i: (0, i)),
        ],
        out_specs=pl.BlockSpec((rows, step), lambda i: (0, i)),
        out_shape=jax.ShapeDtypeStruct((rows, width), BF16),
        scratch_shapes=[pltpu.VMEM((rows, channels), BF16)],
        compiler_params=pltpu.CompilerParams(vmem_limit_bytes=48 * MIB),
        cost_estimate=pl.CostEstimate(
            flops=2 * rows * width * channels, bytes_accessed=5 * MIB, transcendentals=0
        ),
        name="project_out",
    )(gate_short, landed, w_out)


def solution(mesh):
    count = mesh.shape["seq"]
    near = 4 if count % 4 == 0 else 1
    far = count // near
    seq_at = mesh.axis_names.index("seq")
    shape = list(mesh.devices.shape)
    shape[seq_at : seq_at + 1] = [far, near]
    names = list(mesh.axis_names)
    names[seq_at : seq_at + 1] = ["far", "near"]
    inner = Mesh(mesh.devices.reshape(shape), tuple(names))
    by_token = P(("dp", "far", "near"), None)
    by_row = P(("far", "near"), None)
    placed = (by_token, by_token, by_token, by_row, by_row, P(), P(), by_row, P())
    return jax.shard_map(
        functools.partial(on_device, near, far),
        mesh=inner,
        in_specs=placed,
        out_specs=by_token,
        check_vma=False,
    )
```

```python
import functools

import jax
import jax.numpy as jnp
from jax import lax
from jax.experimental import pallas as pl
from jax.experimental.pallas import tpu as pltpu
from jax.sharding import Mesh, PartitionSpec as P

F32 = jnp.float32
BF16 = jnp.bfloat16
LANES = 128
GROUP = 8
BLOCK = 32
SLOTS = LANES // BLOCK
MIB = 1 << 20
VMEM = pl.BlockSpec(memory_space=pltpu.VMEM)
SMEM = pl.BlockSpec(memory_space=pltpu.SMEM)


def params(mib):
    return pltpu.CompilerParams(vmem_limit_bytes=mib * MIB)


def cost(flops, accessed):
    return pl.CostEstimate(flops=flops, bytes_accessed=accessed, transcendentals=0)


def whole(shape):
    return pl.BlockSpec(shape, lambda *_: (0,) * len(shape))


def sign_bytes(packed):
    parts = jnp.concatenate([packed & 255, packed >> 8], axis=1)
    return parts.astype(F32).astype(BF16)


def one_hot(rows, columns, source_of):
    at = lax.broadcasted_iota(jnp.int32, (rows, columns), 0)
    column = lax.broadcasted_iota(jnp.int32, (1, columns), 1)
    return (at == source_of(column)).astype(F32).astype(BF16)


def pack_kernel(near, far, turns, tokens_ref, in_ref, sent_ref, lags_ref, out_ref):
    width = tokens_ref.shape[1]
    depth = width // near
    share = depth // turns
    words = in_ref.shape[1]
    channels = lags_ref.shape[1]
    own_words = words // near
    per_part = own_words // far
    own_channels = channels // near
    per_owner = own_channels // far

    def word_of(column):
        owner, rest = column // (2 * own_words), column % (2 * own_words)
        half, word = rest // own_words, rest % own_words
        return half * words + (word // per_part * near + owner) * per_part + word % per_part

    def channel_of(column):
        owner, rest = column // own_channels, column % own_channels
        return (rest // per_owner * near + owner) * per_owner + rest % per_owner

    moved = jnp.dot(
        sign_bytes(in_ref[...]), one_hot(2 * words, 2 * words, word_of), preferred_element_type=F32
    ).astype(BF16)
    lags = jnp.dot(
        lags_ref[...].astype(BF16), one_hot(channels, channels, channel_of), preferred_element_type=F32
    ).astype(BF16)
    outs = sign_bytes(sent_ref[...])
    spare = -outs.shape[1] % LANES
    outs = jnp.concatenate([outs, jnp.zeros((outs.shape[0], spare), BF16)], axis=1)
    for owner in range(near):
        for turn in range(turns):
            start = (turn * near + owner) * share
            out_ref[owner, :, turn * share : (turn + 1) * share] = tokens_ref[:, start : start + share]
        start = depth
        for part, step in ((moved, 2 * own_words), (lags, own_channels)):
            out_ref[owner, :, start : start + step] = part[:, owner * step : (owner + 1) * step]
            start += step
        out_ref[owner, :, start:] = outs


def expand_signs(pair, columns):
    words = columns // 16
    picked = one_hot(2 * words, columns, lambda c: (c >> 4) + words * ((c >> 3) & 1))
    spread = jnp.dot(pair, picked, preferred_element_type=F32)
    bit_at = lax.broadcasted_iota(jnp.int32, (1, columns), 1) & 7
    return (((spread.astype(jnp.int32) >> bit_at) & 1) * 2 - 1).astype(F32)


def project_kernel(depth, out_start, turns, got_ref, weight_ref, out_ref):
    channels = weight_ref.shape[1]
    flip_in = expand_signs(got_ref[:, depth : depth + depth // 8], depth).astype(BF16)
    flip_out = expand_signs(got_ref[:, out_start : out_start + channels // 8], channels)
    step = depth // turns
    mean_part, noise_part = 0.0, 0.0
    for at in range(turns):
        held = slice(at * step, (at + 1) * step)
        tokens = got_ref[:, held]
        mean_part += jnp.dot(
            tokens, weight_ref[2 * at * step : (2 * at + 1) * step], preferred_element_type=F32
        )
        noise_part += jnp.dot(
            tokens * flip_in[:, held],
            weight_ref[(2 * at + 1) * step : (2 * at + 2) * step],
            preferred_element_type=F32,
        )
    out_ref[...] = (mean_part + flip_out * noise_part).T.astype(BF16)


def toeplitz_kernel(held, owner_ref, lags_ref, out_ref, line_ref):
    group = pl.program_id(0)
    per_group = min(held, GROUP)

    @pl.when(group == 0)
    def _():
        line_ref[...] = lags_ref[...].astype(F32).T

    for at in range(per_group):
        row = line_ref[pl.ds(owner_ref[0] * held + group * per_group + at, 1), :]
        spread = jnp.broadcast_to(row, (BLOCK, row.shape[1]))
        turned = pltpu.roll(spread, 0, 1, stride=1, stride_axis=0)
        column = lax.broadcasted_iota(jnp.int32, spread.shape, 1)
        lag = lax.broadcasted_iota(jnp.int32, spread.shape, 0)
        out_ref[at * BLOCK : (at + 1) * BLOCK, :] = jnp.where(column >= lag, turned, 0.0).astype(BF16)


def shifted(values, steps):
    moved = pltpu.roll(values, steps, 1)
    at = lax.broadcasted_iota(jnp.int32, values.shape, 1)
    return jnp.where(at >= steps, moved, 0.0)


def lane_roll(values, steps):
    return pltpu.roll(values, steps % LANES, values.ndim - 1) if steps % LANES else values


def mix_kernel(near, far, held, parts_ref, taps_ref, table_ref, out_ref, left_ref, sums_ref, done_ref):
    group = pl.program_id(0)
    per_group = min(held, GROUP)
    tiles = out_ref.shape[0]
    rows = tiles * SLOTS * GROUP
    lane = lax.broadcasted_iota(jnp.int32, (1, LANES), 1)

    @pl.when(group == 0)
    def _():
        planes = []
        for plane in range(far):
            total = 0.0
            for part in range(near):
                start = (plane * near + part) * held
                total += parts_ref[start : start + held, :].astype(F32)
            planes.append(total)
        value = jnp.concatenate(planes, axis=1)
        signal = taps_ref[:, 0:1] * value
        for lag in range(1, 3):
            signal += taps_ref[:, lag : lag + 1] * shifted(value, lag)
        if held < GROUP:
            spare = jnp.zeros((GROUP - held, signal.shape[1]), F32)
            signal = jnp.concatenate([signal, spare], axis=0)
        for at in range(held // per_group):
            lines = signal[at * per_group : at * per_group + GROUP, :]
            stacked = jnp.concatenate(
                [lines[:, a * LANES : (a + 1) * LANES] for a in range(tiles)], axis=0
            )
            slot_of = lax.broadcasted_iota(jnp.int32, stacked.shape, 0) % SLOTS
            turned = stacked
            for slot in range(1, SLOTS):
                turned = jnp.where(slot_of == slot, lane_roll(stacked, BLOCK * slot), turned)
            spread = jnp.stack(
                [
                    lane_roll(turned, -BLOCK * slot).reshape(tiles, GROUP, LANES)
                    for slot in range(SLOTS)
                ],
                axis=1,
            ).reshape(rows, LANES)
            owner = lax.broadcasted_iota(jnp.int32, (rows, LANES), 0) & (GROUP - 1)
            for half in range(per_group // SLOTS):
                kept = jnp.where(owner == lane // BLOCK + half * SLOTS, spread, 0.0)
                left_ref[at, :, half * LANES : (half + 1) * LANES] = kept.astype(BF16)

    sums_ref[...] = jnp.zeros_like(sums_ref)
    tile_rows = SLOTS * GROUP
    pair = 2 * LANES
    if tiles <= 16:
        for at in range(tiles // 2):
            start = 2 * at * tile_rows
            partial = jnp.dot(
                left_ref[group, : rows - start, :],
                table_ref[:, at * pair : (at + 1) * pair],
                preferred_element_type=F32,
            )
            sums_ref[start:rows, :] += partial[:, :LANES]
            sums_ref[start + tile_rows : rows, :] += partial[: rows - start - tile_rows, LANES:]
    else:

        def add(at, _):
            partial = jnp.dot(
                left_ref[group],
                table_ref[:, pl.ds(pl.multiple_of(at * pair, pair), pair)],
                preferred_element_type=F32,
            )
            start = pl.multiple_of(2 * at * tile_rows, tile_rows)
            sums_ref[pl.ds(start, rows), :] += partial[:, :LANES]
            sums_ref[pl.ds(start + tile_rows, rows), :] += partial[:, LANES:]
            return 0

        lax.fori_loop(0, tiles // 2, add, 0)

    sums = sums_ref[:rows, :]
    landed = [0.0] * SLOTS
    for part in range(SLOTS):
        late = sums
        if part:
            late = jnp.concatenate([jnp.zeros((part * GROUP, LANES), F32), sums[: rows - part * GROUP]], axis=0)
        late = late.reshape(tiles, SLOTS, GROUP, LANES)
        for slot in range(SLOTS):
            moved = lane_roll(late[:, slot].reshape(tiles * GROUP, LANES), BLOCK * (slot - part))
            landed[slot] += moved
    result = 0.0
    for slot in range(SLOTS):
        result += jnp.where(lane // BLOCK == slot, landed[slot], 0.0)
    start = pl.multiple_of(group * GROUP, GROUP)
    done_ref[:, pl.ds(start, GROUP), :] = result.reshape(tiles, GROUP, LANES)

    @pl.when(group == pl.num_programs(0) - 1)
    def _():
        out_ref[...] = done_ref[:, :held, :].astype(BF16)


def out_kernel(gate_ref, mixed_ref, weight_ref, out_ref, gated_ref):
    @pl.when(pl.program_id(0) == 0)
    def _():
        gated = gate_ref[...] * mixed_ref[...].astype(F32)
        gated_ref[...] = gated.T.astype(BF16)

    out_ref[...] = jnp.dot(gated_ref[...], weight_ref[...], preferred_element_type=F32).astype(BF16)


def on_device(near, far, tokens, sign_in, sign_out, w_value, w_noise, w_gate, conv_taps, long_filter, w_out):
    rows, width = tokens.shape
    channels = w_gate.shape[1]
    count = near * far
    held = channels // count
    share = w_value.shape[0]
    depth = share * far
    length = count * rows
    far_at, near_at, core = lax.axis_index("far"), lax.axis_index("near"), lax.axis_index("dp")
    position = far_at * near + near_at
    everyone = ("far", "near")

    weights = lax.all_gather(
        jnp.where(core == 0, w_value, w_noise), ("far", "dp"), axis=0, tiled=True
    )
    turns = far
    by_owner = tokens
    if share % LANES:
        turns = 1
        by_owner = tokens.reshape(rows, far, near, share).transpose(0, 2, 1, 3).reshape(rows, width)
        weights = weights.reshape(far, 2, share, channels).transpose(1, 0, 2, 3).reshape(-1, channels)

    lags_start = depth + depth // 8
    out_start = lags_start + channels // near
    packed_width = out_start + channels // 8 + -(channels // 8) % LANES
    packed = pl.pallas_call(
        functools.partial(pack_kernel, near, far, turns),
        in_specs=[VMEM] * 4,
        out_specs=VMEM,
        out_shape=jax.ShapeDtypeStruct((near, rows, packed_width), BF16),
        compiler_params=params(16),
        cost_estimate=cost(2 * rows * 512 * 1024, 3 * MIB),
        name="pack",
    )(by_owner, sign_in, sign_out, long_filter)
    got = lax.all_to_all(packed, "near", 0, 0, tiled=True).reshape(near * rows, packed_width)
    lags = lax.all_gather(
        got[:, lags_start:out_start], "far", axis=0, tiled=True
    )

    gate_rows = jnp.dot(tokens, w_gate, preferred_element_type=F32).astype(BF16)
    got, gate_rows = lax.optimization_barrier((got, gate_rows))

    partial = pl.pallas_call(
        functools.partial(project_kernel, depth, out_start, turns),
        in_specs=[VMEM] * 2,
        out_specs=VMEM,
        out_shape=jax.ShapeDtypeStruct((channels, near * rows), BF16),
        compiler_params=params(24),
        cost_estimate=cost(4 * near * rows * depth * channels, 6 * MIB),
        name="project",
    )(got, weights)
    parts = lax.all_to_all(partial, everyone, 0, 0, tiled=True)

    per_group = min(held, GROUP)
    groups = held // per_group
    table = pl.pallas_call(
        functools.partial(toeplitz_kernel, held),
        grid=(groups,),
        in_specs=[SMEM, whole(lags.shape)],
        out_specs=pl.BlockSpec((per_group * BLOCK, length), lambda g: (g, 0)),
        out_shape=jax.ShapeDtypeStruct((held * BLOCK, length), BF16),
        scratch_shapes=[pltpu.VMEM((lags.shape[1], length), F32)],
        compiler_params=params(32),
        cost_estimate=cost(held * BLOCK * length * 4, held * BLOCK * length * 2),
        name="toeplitz",
    )(far_at.reshape(1), lags)

    before = lax.ppermute(gate_rows[rows - 2 :], everyone, [(i, i + 1) for i in range(count - 1)])
    extended = jnp.concatenate([before, gate_rows], axis=0).astype(F32)
    gate_short = sum(
        conv_taps[lag, channels:] * extended[2 - lag : 2 - lag + rows] for lag in range(3)
    ).T

    taps = lax.dynamic_slice_in_dim(conv_taps, position * held, held, axis=1).T
    tiles = length // LANES
    all_rows = tiles * SLOTS * GROUP
    mixed = pl.pallas_call(
        functools.partial(mix_kernel, near, far, held),
        grid=(groups,),
        in_specs=[
            whole(parts.shape),
            whole(taps.shape),
            pl.BlockSpec((per_group * BLOCK, length), lambda g: (g, 0)),
        ],
        out_specs=whole((tiles, held, LANES)),
        out_shape=jax.ShapeDtypeStruct((tiles, held, LANES), BF16),
        scratch_shapes=[
            pltpu.VMEM((groups, all_rows, per_group * BLOCK), BF16),
            pltpu.VMEM((all_rows * (1 if tiles <= 16 else 2), LANES), F32),
            pltpu.VMEM((tiles, groups * GROUP, LANES), F32),
        ],
        compiler_params=params(32),
        cost_estimate=cost(held * BLOCK * length * 256, held * BLOCK * length * 2),
        name="mix",
    )(parts, taps, table)

    landed = lax.all_to_all(mixed, everyone, 0, 0, tiled=True).reshape(channels, rows)
    step = min(width, 512)
    return pl.pallas_call(
        out_kernel,
        grid=(width // step,),
        in_specs=[
            whole((channels, rows)),
            whole((channels, rows)),
            pl.BlockSpec((channels, step), lambda i: (0, i)),
        ],
        out_specs=pl.BlockSpec((rows, step), lambda i: (0, i)),
        out_shape=jax.ShapeDtypeStruct((rows, width), BF16),
        scratch_shapes=[pltpu.VMEM((rows, channels), BF16)],
        compiler_params=params(16),
        cost_estimate=cost(2 * rows * width * channels, 5 * MIB),
        name="project_out",
    )(gate_short, landed, w_out)


def solution(mesh):
    count = mesh.shape["seq"]
    near = 4 if count % 4 == 0 else 1
    far = count // near
    seq_at = mesh.axis_names.index("seq")
    shape = list(mesh.devices.shape)
    shape[seq_at : seq_at + 1] = [far, near]
    names = list(mesh.axis_names)
    names[seq_at : seq_at + 1] = ["far", "near"]
    inner = Mesh(mesh.devices.reshape(shape), tuple(names))
    by_token = P(("dp", "far", "near"), None)
    by_row = P(("far", "near"), None)
    placed = (by_token, by_token, by_token, by_row, by_row, P(), P(), by_row, P())
    return jax.shard_map(
        functools.partial(on_device, near, far),
        mesh=inner,
        in_specs=placed,
        out_specs=by_token,
        check_vma=False,
    )
```

```python
import functools

import jax
import jax.numpy as jnp
from jax import lax
from jax.experimental import pallas as pl
from jax.experimental.pallas import tpu as pltpu
from jax.sharding import Mesh, PartitionSpec as P

F32 = jnp.float32
BF16 = jnp.bfloat16
LANES = 128
GROUP = 8
BLOCK = 32
SLOTS = LANES // BLOCK
MIB = 1 << 20
VMEM = pl.BlockSpec(memory_space=pltpu.VMEM)
SMEM = pl.BlockSpec(memory_space=pltpu.SMEM)
HBM = pl.BlockSpec(memory_space=pltpu.HBM)


def params(mib):
    return pltpu.CompilerParams(vmem_limit_bytes=mib * MIB)


def cost(flops, accessed):
    return pl.CostEstimate(flops=flops, bytes_accessed=accessed, transcendentals=0)


def sign_bytes(packed):
    parts = jnp.concatenate([packed & 255, packed >> 8], axis=1)
    return parts.astype(F32).astype(BF16)


def one_hot(rows, columns, source_of):
    at = lax.broadcasted_iota(jnp.int32, (rows, columns), 0)
    column = lax.broadcasted_iota(jnp.int32, (1, columns), 1)
    return (at == source_of(column)).astype(F32).astype(BF16)


def pack_kernel(
    near, far, turns, core_ref, tokens_ref, in_ref, sent_ref, lags_ref, value_ref, noise_ref,
    out_ref, weight_ref, in_held, sent_held, lags_held, rest_held, read_sems, token_sems, rest_sems, weight_sem,
):
    width = tokens_ref.shape[1]
    depth = width // near
    share = depth // turns
    words = in_ref.shape[1]
    channels = lags_ref.shape[1]
    own_words = words // near
    per_part = own_words // far
    own_channels = channels // near
    per_owner = own_channels // far

    reads = [
        pltpu.make_async_copy(source, target, read_sems.at[at])
        for at, (source, target) in enumerate(
            ((in_ref, in_held), (lags_ref, lags_held), (sent_ref, sent_held))
        )
    ]
    for read in reads:
        read.start()
    moves = [
        pltpu.make_async_copy(
            tokens_ref.at[:, pl.ds((turn * near + owner) * share, share)],
            out_ref.at[owner, :, pl.ds(turn * share, share)],
            token_sems.at[owner * turns + turn],
        )
        for owner in range(near)
        for turn in range(turns)
    ]
    for move in moves:
        move.start()

    @pl.when(core_ref[0] == 0)
    def _():
        pltpu.make_async_copy(value_ref, weight_ref, weight_sem).start()

    @pl.when(core_ref[0] != 0)
    def _():
        pltpu.make_async_copy(noise_ref, weight_ref, weight_sem).start()

    def word_of(column):
        owner, rest = column // (2 * own_words), column % (2 * own_words)
        half, word = rest // own_words, rest % own_words
        return half * words + (word // per_part * near + owner) * per_part + word % per_part

    def channel_of(column):
        owner, rest = column // own_channels, column % own_channels
        return (rest // per_owner * near + owner) * per_owner + rest % per_owner

    by_word = one_hot(2 * words, 2 * words, word_of)
    by_channel = one_hot(channels, channels, channel_of)
    reads[0].wait()
    moved = jnp.dot(sign_bytes(in_held[...]), by_word, preferred_element_type=F32).astype(BF16)
    reads[1].wait()
    lags = jnp.dot(lags_held[...].astype(BF16), by_channel, preferred_element_type=F32).astype(BF16)
    reads[2].wait()
    outs = sign_bytes(sent_held[...].astype(F32).T.astype(jnp.int32))
    spare = -outs.shape[1] % LANES
    outs = jnp.concatenate([outs, jnp.zeros((outs.shape[0], spare), BF16)], axis=1)
    writes = []
    for owner in range(near):
        start = 0
        for part, step in ((moved, 2 * own_words), (lags, own_channels)):
            rest_held[owner, :, start : start + step] = part[:, owner * step : (owner + 1) * step]
            start += step
        rest_held[owner, :, start:] = outs
        write = pltpu.make_async_copy(
            rest_held.at[owner],
            out_ref.at[owner, :, pl.ds(depth, rest_held.shape[2])],
            rest_sems.at[owner],
        )
        write.start()
        writes.append(write)
    pltpu.make_async_copy(value_ref, weight_ref, weight_sem).wait()
    for copy in moves + writes:
        copy.wait()


def expand_signs(pair, columns):
    words = columns // 16
    picked = one_hot(2 * words, columns, lambda c: (c >> 4) + words * ((c >> 3) & 1))
    spread = jnp.dot(pair, picked, preferred_element_type=F32)
    bit_at = lax.broadcasted_iota(jnp.int32, (1, columns), 1) & 7
    return (((spread.astype(jnp.int32) >> bit_at) & 1) * 2 - 1).astype(F32)


def project_kernel(
    depth, lags_start, out_start, turns, where_ref, got_ref, own_ref, other_ref, out_ref, lags_ref, held_ref
):
    channels = own_ref.shape[1]
    second = jnp.full((1, 1), where_ref[0], jnp.int32) != 0
    flip_in = expand_signs(got_ref[:, depth : depth + depth // 8], depth).astype(BF16)
    flip_out = expand_signs(got_ref[:, out_start : out_start + channels // 8], channels)
    tokens = got_ref[:, :depth]
    flipped = tokens * flip_in
    by_own = jnp.where(second, flipped, tokens)
    by_other = jnp.where(second, tokens, flipped)
    own_part = jnp.dot(by_own, own_ref[...], preferred_element_type=F32)
    other_part = jnp.dot(by_other, other_ref[...], preferred_element_type=F32)
    mean_part = jnp.where(second, other_part, own_part)
    noise_part = jnp.where(second, own_part, other_part)
    out_ref[...] = (mean_part + flip_out * noise_part).T.astype(BF16)
    held_ref[...] = got_ref[:, lags_start:out_start].astype(F32).T
    step = held_ref.shape[0] // turns
    for turn in range(turns):
        at = lax.rem(where_ref[1] + turn, turns) * step
        lags_ref[turn * step : (turn + 1) * step, :] = held_ref[pl.ds(at, step), :].astype(BF16)


def toeplitz_kernel(turns, where_ref, *refs):
    pieces, out_ref, line_ref = refs[:turns], refs[turns], refs[turns + 1]
    held = out_ref.shape[0] // BLOCK
    if turns == 1:
        line_ref[...] = pieces[0][...].astype(F32)
    else:
        step = pieces[0].shape[1]
        for turn, piece in enumerate(pieces):
            at = lax.rem(where_ref[1] + turns - turn, turns) * step
            line_ref[:, pl.ds(pl.multiple_of(at, step), step)] = piece[...].astype(F32)
    for at in range(held):
        row = line_ref[at : at + 1, :]
        spread = jnp.broadcast_to(row, (BLOCK, row.shape[1]))
        turned = pltpu.roll(spread, 0, 1, stride=1, stride_axis=0)
        column = lax.broadcasted_iota(jnp.int32, spread.shape, 1)
        lag = lax.broadcasted_iota(jnp.int32, spread.shape, 0)
        out_ref[at * BLOCK : (at + 1) * BLOCK, :] = jnp.where(column >= lag, turned, 0.0).astype(BF16)


def shifted(values, steps):
    moved = pltpu.roll(values, steps, 1)
    at = lax.broadcasted_iota(jnp.int32, values.shape, 1)
    return jnp.where(at >= steps, moved, 0.0)


def lane_roll(values, steps):
    return pltpu.roll(values, steps % LANES, values.ndim - 1) if steps % LANES else values


def mix_kernel(near, far, held, parts_ref, taps_ref, table_ref, out_ref, left_ref, sums_ref, done_ref):
    per_group = min(held, GROUP)
    tiles = out_ref.shape[0]
    rows = tiles * SLOTS * GROUP
    lane = lax.broadcasted_iota(jnp.int32, (1, LANES), 1)
    tile_rows = SLOTS * GROUP
    pair = 2 * LANES

    planes = []
    for plane in range(far):
        total = 0.0
        for part in range(near):
            start = (plane * near + part) * held
            total += parts_ref[start : start + held, :].astype(F32)
        planes.append(total)
    value = jnp.concatenate(planes, axis=1)
    signal = taps_ref[:, 0:1] * value
    for lag in range(1, 3):
        signal += taps_ref[:, lag : lag + 1] * shifted(value, lag)
    if held < GROUP:
        spare = jnp.zeros((GROUP - held, signal.shape[1]), F32)
        signal = jnp.concatenate([signal, spare], axis=0)

    for group in range(held // per_group):
        lines = signal[group * per_group : group * per_group + GROUP, :]
        stacked = jnp.concatenate(
            [lines[:, a * LANES : (a + 1) * LANES] for a in range(tiles)], axis=0
        )
        slot_of = lax.broadcasted_iota(jnp.int32, stacked.shape, 0) % SLOTS
        turned = stacked
        for slot in range(1, SLOTS):
            turned = jnp.where(slot_of == slot, lane_roll(stacked, BLOCK * slot), turned)
        spread = jnp.stack(
            [
                lane_roll(turned, -BLOCK * slot).reshape(tiles, GROUP, LANES)
                for slot in range(SLOTS)
            ],
            axis=1,
        ).reshape(rows, LANES)
        owner = lax.broadcasted_iota(jnp.int32, (rows, LANES), 0) & (GROUP - 1)
        for half in range(per_group // SLOTS):
            kept = jnp.where(owner == lane // BLOCK + half * SLOTS, spread, 0.0)
            left_ref[:, half * LANES : (half + 1) * LANES] = kept.astype(BF16)

        table = table_ref.at[group * per_group * BLOCK : (group + 1) * per_group * BLOCK]
        sums_ref[...] = jnp.zeros_like(sums_ref)
        if tiles <= 16:
            for at in range(tiles // 2):
                start = 2 * at * tile_rows
                partial = jnp.dot(
                    left_ref[: rows - start, :],
                    table[:, at * pair : (at + 1) * pair],
                    preferred_element_type=F32,
                )
                sums_ref[start:rows, :] += partial[:, :LANES]
                sums_ref[start + tile_rows : rows, :] += partial[: rows - start - tile_rows, LANES:]
        else:

            def add(at, _):
                partial = jnp.dot(
                    left_ref[...],
                    table[:, pl.ds(pl.multiple_of(at * pair, pair), pair)],
                    preferred_element_type=F32,
                )
                start = pl.multiple_of(2 * at * tile_rows, tile_rows)
                sums_ref[pl.ds(start, rows), :] += partial[:, :LANES]
                sums_ref[pl.ds(start + tile_rows, rows), :] += partial[:, LANES:]
                return 0

            lax.fori_loop(0, tiles // 2, add, 0)

        sums = sums_ref[:rows, :]
        landed = [0.0] * SLOTS
        for part in range(SLOTS):
            late = sums
            if part:
                ahead = jnp.zeros((part * GROUP, LANES), F32)
                late = jnp.concatenate([ahead, sums[: rows - part * GROUP]], axis=0)
            late = late.reshape(tiles, SLOTS, GROUP, LANES)
            for slot in range(SLOTS):
                moved = late[:, slot].reshape(tiles * GROUP, LANES)
                landed[slot] += lane_roll(moved, BLOCK * (slot - part))
        result = 0.0
        for slot in range(SLOTS):
            result += jnp.where(lane // BLOCK == slot, landed[slot], 0.0)
        done_ref[:, group * GROUP : (group + 1) * GROUP, :] = result.reshape(tiles, GROUP, LANES)

    out_ref[...] = done_ref[:, :held, :].astype(BF16)


def fetch_kernel(source_ref, out_ref, sem):
    copy = pltpu.make_async_copy(source_ref, out_ref, sem)
    copy.start()
    copy.wait()


def out_kernel(gate_ref, mixed_ref, weight_ref, out_ref, gated_ref):
    at = pl.program_id(0)
    step = out_ref.shape[1]

    @pl.when(at == 0)
    def _():
        gated = gate_ref[...] * mixed_ref[...].astype(F32)
        gated_ref[...] = gated.T.astype(BF16)

    weight = weight_ref[:, pl.ds(pl.multiple_of(at * step, step), step)]
    out_ref[...] = jnp.dot(gated_ref[...], weight, preferred_element_type=F32).astype(BF16)


def on_device(near, far, tokens, sign_in, sign_out, w_value, w_noise, w_gate, conv_taps, long_filter, w_out):
    rows, width = tokens.shape
    channels = w_gate.shape[1]
    count = near * far
    held = channels // count
    share = w_value.shape[0]
    depth = share * far
    length = count * rows
    far_at, near_at, core = lax.axis_index("far"), lax.axis_index("near"), lax.axis_index("dp")
    position = far_at * near + near_at
    everyone = ("far", "near")

    where = jnp.stack([core, far_at]).astype(jnp.int32)

    turns = far
    by_owner = tokens
    if share % LANES:
        turns = 1
        by_owner = tokens.reshape(rows, far, near, share).transpose(0, 2, 1, 3).reshape(rows, width)
    lags_start = depth + depth // 8
    out_start = lags_start + channels // near
    packed_width = out_start + channels // 8 + -(channels // 8) % LANES
    packed, weights = pl.pallas_call(
        functools.partial(pack_kernel, near, far, turns),
        in_specs=[SMEM] + [HBM] * 6,
        out_specs=[HBM] * 2,
        out_shape=[
            jax.ShapeDtypeStruct((near, rows, packed_width), BF16),
            jax.ShapeDtypeStruct(w_value.shape, BF16),
        ],
        scratch_shapes=[
            pltpu.VMEM(sign_in.shape, jnp.int32),
            pltpu.VMEM(sign_out.shape[::-1], jnp.int32),
            pltpu.VMEM(long_filter.shape, F32),
            pltpu.VMEM((near, rows, packed_width - depth), BF16),
            pltpu.SemaphoreType.DMA((3,)),
            pltpu.SemaphoreType.DMA((near * turns,)),
            pltpu.SemaphoreType.DMA((near,)),
            pltpu.SemaphoreType.DMA,
        ],
        compiler_params=params(12),
        cost_estimate=cost(2 * rows * 512 * 1024, 3 * MIB),
        name="pack",
    )(where, by_owner, sign_in, sign_out.T, long_filter, w_value, w_noise)
    got = lax.all_to_all(packed, "near", 0, 0, tiled=True).reshape(near * rows, packed_width)

    own = lax.all_gather(weights, "far", axis=0, tiled=True)
    other = lax.ppermute(own, "dp", [(0, 1), (1, 0)])

    gate_rows = jnp.dot(tokens, w_gate, preferred_element_type=F32).astype(BF16)
    before = lax.ppermute(gate_rows[rows - 2 :], everyone, [(i, i + 1) for i in range(count - 1)])
    extended = jnp.concatenate([before, gate_rows], axis=0).astype(F32)
    gate_short = sum(
        conv_taps[lag, channels:] * extended[2 - lag : 2 - lag + rows] for lag in range(3)
    ).T
    taps = lax.dynamic_slice_in_dim(conv_taps, position * held, held, axis=1).T
    got, gate_short, taps = lax.optimization_barrier((got, gate_short, taps))

    turns = far if far <= 8 else 1
    partial, lags = pl.pallas_call(
        functools.partial(project_kernel, depth, lags_start, out_start, turns),
        in_specs=[SMEM] + [VMEM] * 3,
        out_specs=[VMEM] * 2,
        out_shape=[
            jax.ShapeDtypeStruct((channels, near * rows), BF16),
            jax.ShapeDtypeStruct((far * held, near * rows), BF16),
        ],
        scratch_shapes=[pltpu.VMEM((far * held, near * rows), F32)],
        compiler_params=params(24),
        cost_estimate=cost(4 * near * rows * depth * channels, 6 * MIB),
        name="project",
    )(where, got, own, other)
    parts = lax.all_to_all(partial, everyone, 0, 0, tiled=True)

    if turns == 1:
        lags = lax.all_to_all(lags, "far", 0, 0, tiled=True)
        pieces = [lags.reshape(far, held, near * rows).transpose(1, 0, 2).reshape(held, length)]
    else:
        pieces = [lags[:held]] + [
            lax.ppermute(
                lags[turn * held : (turn + 1) * held], "far", [(i, (i + turn) % far) for i in range(far)]
            )
            for turn in range(1, far)
        ]
    table = pl.pallas_call(
        functools.partial(toeplitz_kernel, turns),
        in_specs=[SMEM] + [VMEM] * turns,
        out_specs=VMEM,
        out_shape=jax.ShapeDtypeStruct((held * BLOCK, length), BF16),
        scratch_shapes=[pltpu.VMEM((held, length), F32)],
        compiler_params=params(16),
        cost_estimate=cost(held * BLOCK * length * 4, held * BLOCK * length * 2),
        name="toeplitz",
    )(where, *pieces)

    tiles = length // LANES
    per_group = min(held, GROUP)
    all_rows = tiles * SLOTS * GROUP
    mixed = pl.pallas_call(
        functools.partial(mix_kernel, near, far, held),
        in_specs=[VMEM] * 3,
        out_specs=VMEM,
        out_shape=jax.ShapeDtypeStruct((tiles, held, LANES), BF16),
        scratch_shapes=[
            pltpu.VMEM((all_rows, per_group * BLOCK), BF16),
            pltpu.VMEM((all_rows * (1 if tiles <= 16 else 2), LANES), F32),
            pltpu.VMEM((tiles, max(held, GROUP), LANES), F32),
        ],
        compiler_params=params(24),
        cost_estimate=cost(held * BLOCK * length * 256, held * BLOCK * length * 2),
        name="mix",
    )(parts, taps, table)

    landed = lax.all_to_all(mixed, everyone, 0, 0, tiled=True).reshape(channels, rows)
    late_w_out, _ = lax.optimization_barrier((w_out, mixed))
    near_w_out = pl.pallas_call(
        fetch_kernel,
        in_specs=[HBM],
        out_specs=VMEM,
        out_shape=pltpu.VMEM(w_out.shape, BF16),
        scratch_shapes=[pltpu.SemaphoreType.DMA],
        compiler_params=params(1),
        cost_estimate=cost(0, 8 * MIB),
        name="fetch",
    )(late_w_out)
    step = min(width, 512)
    return pl.pallas_call(
        out_kernel,
        grid=(width // step,),
        in_specs=[VMEM] * 3,
        out_specs=pl.BlockSpec((rows, step), lambda i: (0, i)),
        out_shape=jax.ShapeDtypeStruct((rows, width), BF16),
        scratch_shapes=[pltpu.VMEM((rows, channels), BF16)],
        compiler_params=params(8),
        cost_estimate=cost(2 * rows * width * channels, 5 * MIB),
        name="project_out",
    )(gate_short, landed, near_w_out)


def solution(mesh):
    count = mesh.shape["seq"]
    near = 4 if count % 4 == 0 else 1
    far = count // near
    seq_at = mesh.axis_names.index("seq")
    shape = list(mesh.devices.shape)
    shape[seq_at : seq_at + 1] = [far, near]
    names = list(mesh.axis_names)
    names[seq_at : seq_at + 1] = ["far", "near"]
    inner = Mesh(mesh.devices.reshape(shape), tuple(names))
    by_token = P(("dp", "far", "near"), None)
    by_row = P(("far", "near"), None)
    placed = (by_token, by_token, by_token, by_row, by_row, P(), P(), by_row, P())
    return jax.shard_map(
        functools.partial(on_device, near, far),
        mesh=inner,
        in_specs=placed,
        out_specs=by_token,
        check_vma=False,
    )
```

```python
import functools

import jax
import jax.numpy as jnp
from jax import lax
from jax.experimental import pallas as pl
from jax.experimental.pallas import tpu as pltpu
from jax.sharding import Mesh, PartitionSpec as P

F32 = jnp.float32
BF16 = jnp.bfloat16
LANES = 128
GROUP = 8
BLOCK = 32
SLOTS = LANES // BLOCK
MIB = 1 << 20
VMEM_BYTES = 60 * MIB
VMEM = pl.BlockSpec(memory_space=pltpu.VMEM)
SMEM = pl.BlockSpec(memory_space=pltpu.SMEM)
HBM = pl.BlockSpec(memory_space=pltpu.HBM)


def params(spare_kib):
    return pltpu.CompilerParams(vmem_limit_bytes=VMEM_BYTES - spare_kib * 1024)


def cost(flops, accessed):
    return pl.CostEstimate(flops=flops, bytes_accessed=accessed, transcendentals=0)


def sign_bytes(packed):
    parts = jnp.concatenate([packed & 255, packed >> 8], axis=1)
    return parts.astype(F32).astype(BF16)


def one_hot(rows, columns, source_of):
    at = lax.broadcasted_iota(jnp.int32, (rows, columns), 0)
    column = lax.broadcasted_iota(jnp.int32, (1, columns), 1)
    return (at == source_of(column)).astype(F32).astype(BF16)


def pack_kernel(
    near, far, turns, lag_turns, where_ref, tokens_ref, in_ref, sent_ref, lags_ref, value_ref, noise_ref, *refs
):
    out_ref, weight_ref, *lag_outs = refs[: 2 + lag_turns]
    (in_held, sent_held, lags_held, lines_held, rest_held) = refs[2 + lag_turns : 7 + lag_turns]
    (read_sems, token_sems, rest_sems, weight_sem) = refs[7 + lag_turns :]
    width = tokens_ref.shape[1]
    depth = width // near
    share = depth // turns
    words = in_ref.shape[1]
    own_words = words // near
    per_part = own_words // far

    reads = [
        pltpu.make_async_copy(source, target, read_sems.at[at])
        for at, (source, target) in enumerate(
            ((in_ref, in_held), (lags_ref, lags_held), (sent_ref, sent_held))
        )
    ]
    for read in reads:
        read.start()

    @pl.when(where_ref[0] == 0)
    def _():
        pltpu.make_async_copy(value_ref, weight_ref, weight_sem).start()

    @pl.when(where_ref[0] != 0)
    def _():
        pltpu.make_async_copy(noise_ref, weight_ref, weight_sem).start()

    moves = [
        pltpu.make_async_copy(
            tokens_ref.at[:, pl.ds((turn * near + owner) * share, share)],
            out_ref.at[owner, :, pl.ds(turn * share, share)],
            token_sems.at[owner * turns + turn],
        )
        for owner in range(near)
        for turn in range(turns)
    ]
    for move in moves:
        move.start()

    def word_of(column):
        owner, rest = column // (2 * own_words), column % (2 * own_words)
        half, word = rest // own_words, rest % own_words
        return half * words + (word // per_part * near + owner) * per_part + word % per_part

    by_word = one_hot(2 * words, 2 * words, word_of)
    reads[0].wait()
    moved = jnp.dot(sign_bytes(in_held[...]), by_word, preferred_element_type=F32).astype(BF16)
    reads[2].wait()
    outs = sign_bytes(sent_held[...].astype(F32).T.astype(jnp.int32))
    spare = -outs.shape[1] % LANES
    outs = jnp.concatenate([outs, jnp.zeros((outs.shape[0], spare), BF16)], axis=1)
    writes = []
    step = 2 * own_words
    for owner in range(near):
        rest_held[owner, :, :step] = moved[:, owner * step : (owner + 1) * step]
        rest_held[owner, :, step:] = outs
        write = pltpu.make_async_copy(
            rest_held.at[owner],
            out_ref.at[owner, :, pl.ds(depth, rest_held.shape[2])],
            rest_sems.at[owner],
        )
        write.start()
        writes.append(write)
    reads[1].wait()
    lines_held[...] = lags_held[...].T
    step = lines_held.shape[0] // lag_turns
    for turn, lag_out in enumerate(lag_outs):
        at = lax.rem(where_ref[1] + turn, lag_turns) * step
        lag_out[...] = lines_held[pl.ds(pl.multiple_of(at, step), step), :].astype(BF16)
    pltpu.make_async_copy(value_ref, weight_ref, weight_sem).wait()
    for copy in moves + writes:
        copy.wait()


def expand_signs(pair, columns):
    words = columns // 16
    picked = one_hot(2 * words, columns, lambda c: (c >> 4) + words * ((c >> 3) & 1))
    spread = jnp.dot(pair, picked, preferred_element_type=F32)
    bit_at = lax.broadcasted_iota(jnp.int32, (1, columns), 1) & 7
    return (((spread.astype(jnp.int32) >> bit_at) & 1) * 2 - 1).astype(F32)


def project_kernel(depth, out_start, turns, got_ref, weight_ref, out_ref, held_ref, sems):
    channels = weight_ref.shape[1]
    share = depth // turns
    reads = []
    for at in range(2 * turns):
        rows = pl.ds(at * share, share)
        reads.append(pltpu.make_async_copy(weight_ref.at[rows], held_ref.at[rows], sems.at[at]))
        reads[-1].start()
    flip_in = expand_signs(got_ref[:, depth : depth + depth // 8], depth).astype(BF16)
    flip_out = expand_signs(got_ref[:, out_start : out_start + channels // 8], channels)
    mean_part, noise_part = 0.0, 0.0
    for at in range(turns):
        columns = slice(at * share, (at + 1) * share)
        tokens = got_ref[:, columns]
        reads[2 * at].wait()
        rows = slice(2 * at * share, (2 * at + 1) * share)
        mean_part += jnp.dot(tokens, held_ref[rows], preferred_element_type=F32)
        reads[2 * at + 1].wait()
        rows = slice((2 * at + 1) * share, (2 * at + 2) * share)
        noise_part += jnp.dot(tokens * flip_in[:, columns], held_ref[rows], preferred_element_type=F32)
    out_ref[...] = (mean_part + flip_out * noise_part).T.astype(BF16)


def turn_kernel(near, far, where_ref, *refs):
    pieces, outs = refs[:far], refs[far:]
    rows = pieces[0].shape[1]
    step = outs[0].shape[0]
    for turn, out in enumerate(outs):
        at = pl.multiple_of(lax.rem(where_ref[2] + turn, near) * step, step)
        for plane, piece in enumerate(pieces):
            out[:, plane * rows : (plane + 1) * rows] = piece[pl.ds(at, step), :]


def toeplitz_kernel(near, far, where_ref, *refs):
    pieces, (out_ref, line_ref) = refs[:-2], refs[-2:]
    held = out_ref.shape[0] // BLOCK
    if len(pieces) == 1:
        line_ref[...] = pieces[0][...].astype(F32)
    else:
        rows = pieces[0].shape[1] // far
        for turn, piece in enumerate(pieces):
            part = lax.rem(where_ref[2] + near - turn, near)
            for plane in range(far):
                at = lax.rem(where_ref[1] + far - plane, far) * near + part
                target = pl.ds(pl.multiple_of(at * rows, rows), rows)
                line_ref[:, target] = piece[:, plane * rows : (plane + 1) * rows].astype(F32)
    for at in range(held):
        row = line_ref[at : at + 1, :]
        spread = jnp.broadcast_to(row, (BLOCK, row.shape[1]))
        turned = pltpu.roll(spread, 0, 1, stride=1, stride_axis=0)
        column = lax.broadcasted_iota(jnp.int32, spread.shape, 1)
        lag = lax.broadcasted_iota(jnp.int32, spread.shape, 0)
        out_ref[at * BLOCK : (at + 1) * BLOCK, :] = jnp.where(column >= lag, turned, 0.0).astype(BF16)


def shifted(values, steps):
    moved = pltpu.roll(values, steps, 1)
    at = lax.broadcasted_iota(jnp.int32, values.shape, 1)
    return jnp.where(at >= steps, moved, 0.0)


def lane_roll(values, steps):
    return pltpu.roll(values, steps % LANES, values.ndim - 1) if steps % LANES else values


def mix_kernel(
    near, far, held, parts_ref, taps_ref, source_ref, out_ref, left_ref, sums_ref, done_ref, table_ref, sems
):
    per_group = min(held, GROUP)
    reads = []
    for group in range(held // per_group):
        own = pl.ds(group * per_group * BLOCK, per_group * BLOCK)
        reads.append(pltpu.make_async_copy(source_ref.at[own], table_ref.at[own], sems.at[group]))
        reads[-1].start()
    tiles = out_ref.shape[0]
    rows = tiles * SLOTS * GROUP
    lane = lax.broadcasted_iota(jnp.int32, (1, LANES), 1)
    tile_rows = SLOTS * GROUP
    pair = 2 * LANES

    planes = []
    for plane in range(far):
        total = 0.0
        for part in range(near):
            start = (plane * near + part) * held
            total += parts_ref[start : start + held, :].astype(F32)
        planes.append(total)
    value = jnp.concatenate(planes, axis=1)
    signal = taps_ref[:, 0:1] * value
    for lag in range(1, 3):
        signal += taps_ref[:, lag : lag + 1] * shifted(value, lag)
    if held < GROUP:
        spare = jnp.zeros((GROUP - held, signal.shape[1]), F32)
        signal = jnp.concatenate([signal, spare], axis=0)

    for group in range(held // per_group):
        lines = signal[group * per_group : group * per_group + GROUP, :]
        stacked = jnp.concatenate(
            [lines[:, a * LANES : (a + 1) * LANES] for a in range(tiles)], axis=0
        )
        slot_of = lax.broadcasted_iota(jnp.int32, stacked.shape, 0) % SLOTS
        turned = stacked
        for slot in range(1, SLOTS):
            turned = jnp.where(slot_of == slot, lane_roll(stacked, BLOCK * slot), turned)
        spread = jnp.stack(
            [
                lane_roll(turned, -BLOCK * slot).reshape(tiles, GROUP, LANES)
                for slot in range(SLOTS)
            ],
            axis=1,
        ).reshape(rows, LANES)
        owner = lax.broadcasted_iota(jnp.int32, (rows, LANES), 0) & (GROUP - 1)
        for half in range(per_group // SLOTS):
            kept = jnp.where(owner == lane // BLOCK + half * SLOTS, spread, 0.0)
            left_ref[:, half * LANES : (half + 1) * LANES] = kept.astype(BF16)

        table = table_ref.at[group * per_group * BLOCK : (group + 1) * per_group * BLOCK]
        reads[group].wait()
        sums_ref[...] = jnp.zeros_like(sums_ref)
        if tiles <= 16:
            for at in range(tiles // 2):
                start = 2 * at * tile_rows
                partial = jnp.dot(
                    left_ref[: rows - start, :],
                    table[:, at * pair : (at + 1) * pair],
                    preferred_element_type=F32,
                )
                sums_ref[start:rows, :] += partial[:, :LANES]
                sums_ref[start + tile_rows : rows, :] += partial[: rows - start - tile_rows, LANES:]
        else:

            def add(at, _):
                partial = jnp.dot(
                    left_ref[...],
                    table[:, pl.ds(pl.multiple_of(at * pair, pair), pair)],
                    preferred_element_type=F32,
                )
                start = pl.multiple_of(2 * at * tile_rows, tile_rows)
                sums_ref[pl.ds(start, rows), :] += partial[:, :LANES]
                sums_ref[pl.ds(start + tile_rows, rows), :] += partial[:, LANES:]
                return 0

            lax.fori_loop(0, tiles // 2, add, 0)

        sums = sums_ref[:rows, :]
        landed = [0.0] * SLOTS
        for part in range(SLOTS):
            late = sums
            if part:
                ahead = jnp.zeros((part * GROUP, LANES), F32)
                late = jnp.concatenate([ahead, sums[: rows - part * GROUP]], axis=0)
            late = late.reshape(tiles, SLOTS, GROUP, LANES)
            for slot in range(SLOTS):
                moved = late[:, slot].reshape(tiles * GROUP, LANES)
                landed[slot] += lane_roll(moved, BLOCK * (slot - part))
        result = 0.0
        for slot in range(SLOTS):
            result += jnp.where(lane // BLOCK == slot, landed[slot], 0.0)
        done_ref[:, group * GROUP : (group + 1) * GROUP, :] = result.reshape(tiles, GROUP, LANES)

    out_ref[...] = done_ref[:, :held, :].astype(BF16)


def out_kernel(gate_ref, mixed_ref, source_ref, target_ref, weight_ref, held_ref, read_sems, write_sems):
    chunks, _, step = weight_ref.shape
    reads = []
    for at in range(chunks):
        columns = source_ref.at[:, pl.ds(at * step, step)]
        reads.append(pltpu.make_async_copy(columns, weight_ref.at[at], read_sems.at[at]))
        reads[-1].start()
    gated = (gate_ref[...] * mixed_ref[...].astype(F32)).T.astype(BF16)
    writes = []
    for at in range(chunks):
        reads[at].wait()
        held_ref[at] = jnp.dot(gated, weight_ref[at], preferred_element_type=F32).astype(BF16)
        columns = target_ref.at[:, pl.ds(at * step, step)]
        writes.append(pltpu.make_async_copy(held_ref.at[at], columns, write_sems.at[at]))
        writes[-1].start()
    for write in writes:
        write.wait()


def on_device(near, far, tokens, sign_in, sign_out, w_value, w_noise, w_gate, conv_taps, long_filter, w_out):
    rows, width = tokens.shape
    channels = w_gate.shape[1]
    count = near * far
    held = channels // count
    share = w_value.shape[0]
    depth = share * far
    length = count * rows
    far_at, near_at, core = lax.axis_index("far"), lax.axis_index("near"), lax.axis_index("dp")
    position = far_at * near + near_at
    everyone = ("far", "near")

    where = jnp.stack([core, far_at, near_at]).astype(jnp.int32)

    turns = far
    by_owner = tokens
    if share % LANES:
        turns = 1
        by_owner = tokens.reshape(rows, far, near, share).transpose(0, 2, 1, 3).reshape(rows, width)
    lag_turns = far if far <= 8 else 1
    out_start = depth + depth // 8
    packed_width = out_start + channels // 8 + -(channels // 8) % LANES
    packed, weights, *lags = pl.pallas_call(
        functools.partial(pack_kernel, near, far, turns, lag_turns),
        in_specs=[SMEM] + [HBM] * 6,
        out_specs=[HBM] * 2 + [VMEM] * lag_turns,
        out_shape=[
            jax.ShapeDtypeStruct((near, rows, packed_width), BF16),
            jax.ShapeDtypeStruct(w_value.shape, BF16),
        ]
        + [jax.ShapeDtypeStruct((channels // lag_turns, rows), BF16)] * lag_turns,
        scratch_shapes=[
            pltpu.VMEM(sign_in.shape, jnp.int32),
            pltpu.VMEM(sign_out.shape[::-1], jnp.int32),
            pltpu.VMEM(long_filter.shape, F32),
            pltpu.VMEM(long_filter.shape[::-1], F32),
            pltpu.VMEM((near, rows, packed_width - depth), BF16),
            pltpu.SemaphoreType.DMA((3,)),
            pltpu.SemaphoreType.DMA((near * turns,)),
            pltpu.SemaphoreType.DMA((near,)),
            pltpu.SemaphoreType.DMA,
        ],
        compiler_params=params(0),
        cost_estimate=cost(2 * rows * 512 * 512, 3 * MIB),
        name="pack",
    )(where, by_owner, sign_in, sign_out.T, long_filter, w_value, w_noise)
    got = lax.all_to_all(packed, "near", 0, 0, tiled=True).reshape(near * rows, packed_width)

    weights = lax.all_gather(weights, ("far", "dp"), axis=0, tiled=True)
    if turns == 1:
        weights = weights.reshape(far, 2, share, channels).transpose(1, 0, 2, 3).reshape(-1, channels)

    gate_rows = jnp.dot(tokens, w_gate, preferred_element_type=F32).astype(BF16)
    before = lax.ppermute(gate_rows[rows - 2 :], everyone, [(i, i + 1) for i in range(count - 1)])
    extended = jnp.concatenate([before, gate_rows], axis=0).astype(F32)
    gate_short = sum(
        conv_taps[lag, channels:] * extended[2 - lag : 2 - lag + rows] for lag in range(3)
    ).T
    taps = lax.dynamic_slice_in_dim(conv_taps, position * held, held, axis=1).T

    if lag_turns == 1:
        lags = lax.all_to_all(lags[0], everyone, 0, 0, tiled=True)
        lags = [lags.reshape(count, held, rows).transpose(1, 0, 2).reshape(held, length)]
    else:
        lags = [lags[0]] + [
            lax.ppermute(lags[turn], "far", [(i, (i + turn) % far) for i in range(far)])
            for turn in range(1, far)
        ]
        lags = pl.pallas_call(
            functools.partial(turn_kernel, near, far),
            in_specs=[SMEM] + [VMEM] * far,
            out_specs=[VMEM] * near,
            out_shape=[jax.ShapeDtypeStruct((held, far * rows), BF16)] * near,
            compiler_params=params(1024),
            cost_estimate=cost(0, MIB),
            name="turn",
        )(where, *lags)
        lags = [lags[0]] + [
            lax.ppermute(lags[turn], "near", [(i, (i + turn) % near) for i in range(near)])
            for turn in range(1, near)
        ]
    table = pl.pallas_call(
        functools.partial(toeplitz_kernel, near, far),
        in_specs=[SMEM] + [VMEM] * len(lags),
        out_specs=VMEM,
        out_shape=jax.ShapeDtypeStruct((held * BLOCK, length), BF16),
        scratch_shapes=[pltpu.VMEM((held, length), F32)],
        compiler_params=params(1024),
        cost_estimate=cost(held * BLOCK * length * 4, held * BLOCK * length * 2),
        name="toeplitz",
    )(where, *lags)
    got, gate_short, taps, table = lax.optimization_barrier((got, gate_short, taps, table))

    partial = pl.pallas_call(
        functools.partial(project_kernel, depth, out_start, turns),
        in_specs=[VMEM, HBM],
        out_specs=VMEM,
        out_shape=jax.ShapeDtypeStruct((channels, near * rows), BF16),
        scratch_shapes=[
            pltpu.VMEM((2 * depth, channels), BF16),
            pltpu.SemaphoreType.DMA((2 * turns,)),
        ],
        compiler_params=params(1792),
        cost_estimate=cost(4 * near * rows * depth * channels, 6 * MIB),
        name="project",
    )(got, weights)
    parts = lax.all_to_all(partial, everyone, 0, 0, tiled=True)

    tiles = length // LANES
    per_group = min(held, GROUP)
    all_rows = tiles * SLOTS * GROUP
    mixed = pl.pallas_call(
        functools.partial(mix_kernel, near, far, held),
        in_specs=[VMEM, VMEM, HBM],
        out_specs=VMEM,
        out_shape=jax.ShapeDtypeStruct((tiles, held, LANES), BF16),
        scratch_shapes=[
            pltpu.VMEM((all_rows, per_group * BLOCK), BF16),
            pltpu.VMEM((all_rows * (1 if tiles <= 16 else 2), LANES), F32),
            pltpu.VMEM((tiles, max(held, GROUP), LANES), F32),
            pltpu.VMEM(table.shape, BF16),
            pltpu.SemaphoreType.DMA((held // per_group,)),
        ],
        compiler_params=params(1024),
        cost_estimate=cost(held * BLOCK * length * 256, held * BLOCK * length * 2),
        name="mix",
    )(parts, taps, table)

    landed = lax.all_to_all(mixed, everyone, 0, 0, tiled=True).reshape(channels, rows)
    chunks = 8
    return pl.pallas_call(
        out_kernel,
        in_specs=[VMEM, VMEM, HBM],
        out_specs=HBM,
        out_shape=jax.ShapeDtypeStruct((rows, width), BF16),
        scratch_shapes=[
            pltpu.VMEM((chunks, channels, width // chunks), BF16),
            pltpu.VMEM((chunks, rows, width // chunks), BF16),
            pltpu.SemaphoreType.DMA((chunks,)),
            pltpu.SemaphoreType.DMA((chunks,)),
        ],
        compiler_params=params(1024),
        cost_estimate=cost(2 * rows * width * channels, 5 * MIB),
        name="project_out",
    )(gate_short, landed, w_out)


def solution(mesh):
    count = mesh.shape["seq"]
    near = 4 if count % 4 == 0 else 1
    far = count // near
    seq_at = mesh.axis_names.index("seq")
    shape = list(mesh.devices.shape)
    shape[seq_at : seq_at + 1] = [far, near]
    names = list(mesh.axis_names)
    names[seq_at : seq_at + 1] = ["far", "near"]
    inner = Mesh(mesh.devices.reshape(shape), tuple(names))
    by_token = P(("dp", "far", "near"), None)
    by_row = P(("far", "near"), None)
    placed = (by_token, by_token, by_token, by_row, by_row, P(), P(), by_row, P())
    return jax.shard_map(
        functools.partial(on_device, near, far),
        mesh=inner,
        in_specs=placed,
        out_specs=by_token,
        check_vma=False,
    )
```

```python
import functools

import jax
import jax.numpy as jnp
from jax import lax
from jax.experimental import pallas as pl
from jax.experimental.pallas import tpu as pltpu
from jax.sharding import Mesh, PartitionSpec as P

F32 = jnp.float32
BF16 = jnp.bfloat16
LANES = 128
GROUP = 8
BLOCK = 32
SLOTS = LANES // BLOCK
MIB = 1 << 20
VMEM = pl.BlockSpec(memory_space=pltpu.VMEM)
SMEM = pl.BlockSpec(memory_space=pltpu.SMEM)
HBM = pl.BlockSpec(memory_space=pltpu.HBM)


def params(mib):
    return pltpu.CompilerParams(vmem_limit_bytes=mib * MIB)


def cost(flops, accessed):
    return pl.CostEstimate(flops=flops, bytes_accessed=accessed, transcendentals=0)


def in_hbm(*arrays):
    return [pltpu.with_memory_space_constraint(array, pltpu.HBM) for array in arrays]


def sign_bytes(packed):
    parts = jnp.concatenate([packed & 255, packed >> 8], axis=1)
    return parts.astype(F32).astype(BF16)


def one_hot(rows, columns, source_of):
    at = lax.broadcasted_iota(jnp.int32, (rows, columns), 0)
    column = lax.broadcasted_iota(jnp.int32, (1, columns), 1)
    return (at == source_of(column)).astype(F32).astype(BF16)


def pack_kernel(
    near, far, where_ref, tokens_ref, in_ref, sent_ref, value_ref, noise_ref, weight_ref, *refs
):
    outs, (in_held, sent_held, read_sems, weight_sems, token_sems) = refs[:near], refs[near:]
    core, far_at, near_at = where_ref[0], where_ref[1], where_ref[2]
    half = weight_ref.shape[1] // 2
    share = weight_ref.shape[0]
    depth = share * far
    words = in_ref.shape[1]
    per_part = words // (near * far)
    own_words = per_part * far

    copies = []
    for at, source in enumerate((value_ref, noise_ref)):
        columns = pl.ds(pl.multiple_of(core * half, half), half)
        target = weight_ref.at[:, at * half : (at + 1) * half]
        copies.append(pltpu.make_async_copy(source.at[:, columns], target, weight_sems.at[at]))
    reads = [
        pltpu.make_async_copy(in_ref, in_held, read_sems.at[0]),
        pltpu.make_async_copy(sent_ref, sent_held, read_sems.at[1]),
    ]
    for step, out in enumerate(outs):
        for turn in range(far):
            start = ((far_at ^ turn) * near + (near_at ^ step)) * share
            columns = pl.ds(pl.multiple_of(start, share), share)
            target = out.at[:, turn * share : (turn + 1) * share]
            copies.append(
                pltpu.make_async_copy(tokens_ref.at[:, columns], target, token_sems.at[step * far + turn])
            )
    for copy in reads + copies:
        copy.start()

    def word_of(column):
        step, rest = column // (2 * own_words), column % (2 * own_words)
        part, word = rest // own_words, rest % own_words
        plane = (word // per_part) ^ far_at
        return part * words + (plane * near + (step ^ near_at)) * per_part + word % per_part

    by_word = one_hot(2 * words, 2 * words, word_of)
    reads[0].wait()
    moved = jnp.dot(sign_bytes(in_held[...]), by_word, preferred_element_type=F32).astype(BF16)
    reads[1].wait()
    sent = sign_bytes(sent_held[...].astype(F32).T.astype(jnp.int32))
    spare = -sent.shape[1] % LANES
    sent = jnp.concatenate([sent, jnp.zeros((sent.shape[0], spare), BF16)], axis=1)
    width = 2 * own_words
    for step, out in enumerate(outs):
        out[:, depth : depth + width] = moved[:, step * width : (step + 1) * width]
        out[:, depth + width :] = sent
    for copy in copies:
        copy.wait()


def spread_signs(pair, byte_of, columns):
    spread = jnp.dot(pair, one_hot(pair.shape[1], columns, byte_of), preferred_element_type=F32)
    mask = 1 << (lax.broadcasted_iota(jnp.int32, (1, columns), 1) & 7)
    return jnp.where((spread.astype(jnp.int32) & mask) != 0, 1.0, -1.0)


def project_kernel(near, cores, planes, depth, where_ref, lags_ref, *refs):
    chunks, pieces, out_ref = refs[: near * cores], refs[near * cores : -1], refs[-1]
    core, near_at = where_ref[0], where_ref[2]
    rows = chunks[0].shape[0]
    half = pieces[0].shape[1] // 2
    words = depth // 16
    sent_words = cores * half // 16
    sent_start = depth + 2 * words

    def in_byte(column):
        return (column >> 4) + words * ((column >> 3) & 1)

    def out_byte(column):
        return core * (half // 16) + (column >> 4) + sent_words * ((column >> 3) & 1)

    def joined(start, stop):
        return jnp.concatenate([chunk[:, start:stop] for chunk in chunks], axis=0)

    flip_in = spread_signs(joined(depth, sent_start), in_byte, depth).astype(BF16)
    flip_out = spread_signs(joined(sent_start, sent_start + 2 * sent_words), out_byte, half)
    mean_part, noise_part = 0.0, 0.0
    step = depth // len(pieces)
    for at, piece in enumerate(pieces):
        tokens = joined(at * step, (at + 1) * step)
        flipped = tokens * flip_in[:, at * step : (at + 1) * step]
        mean_part += jnp.dot(tokens, piece[:, :half], preferred_element_type=F32)
        noise_part += jnp.dot(flipped, piece[:, half:], preferred_element_type=F32)
    value = (mean_part + flip_out * noise_part).T.astype(BF16)
    for part in range(cores):
        for turn in range(near):
            at = part * near + turn
            target = ((core ^ part) * near + (near_at ^ turn)) * rows
            out_ref[:, pl.ds(pl.multiple_of(target, rows), rows)] = value[:, at * rows : (at + 1) * rows]
    lags = lags_ref[:, pl.ds(pl.multiple_of(core * half, half), half)]
    out_ref[:, cores * near * rows :] = lags.T.astype(BF16)


def shifted(values, steps):
    moved = pltpu.roll(values, steps, 1)
    at = lax.broadcasted_iota(jnp.int32, values.shape, 1)
    return jnp.where(at >= steps, moved, 0.0)


def lane_roll(values, steps):
    return pltpu.roll(values, steps % LANES, values.ndim - 1) if steps % LANES else values


def mix_kernel(near, far, cores, held, parts_ref, taps_ref, out_ref, left_ref, sums_ref, done_ref, table_ref):
    tiles = out_ref.shape[0] // cores
    block_rows = cores * GROUP
    tile_rows = SLOTS * block_rows
    rows = tiles * tile_rows
    lane = lax.broadcasted_iota(jnp.int32, (1, LANES), 1)
    pair = 2 * LANES
    span = near * LANES

    def padded(lines):
        if held >= GROUP:
            return lines
        return jnp.concatenate([lines, jnp.zeros((GROUP - held, lines.shape[1]), F32)], axis=0)

    signals = []
    for part in range(cores):
        planes = []
        for plane in range(far):
            total = 0.0
            for turn in range(near):
                start = (plane * near + turn) * held
                piece = parts_ref[start : start + held, part * span : (part + 1) * span]
                total += piece.astype(F32)
            planes.append(total)
        value = jnp.concatenate(planes, axis=1)
        signal = taps_ref[:, 0:1] * value
        for lag in range(1, 3):
            signal += taps_ref[:, lag : lag + 1] * shifted(value, lag)
        signals.append(padded(signal))
    lags = padded(
        jnp.concatenate(
            [
                parts_ref[at * held : (at + 1) * held, cores * span :].astype(F32)
                for at in range(near * far)
            ],
            axis=1,
        )
    )

    for group in range(max(held, GROUP) // GROUP):
        own = slice(group * GROUP, (group + 1) * GROUP)
        for at in range(GROUP):
            row = lags[group * GROUP + at : group * GROUP + at + 1, :]
            repeated = jnp.broadcast_to(row, (BLOCK, row.shape[1]))
            turned = pltpu.roll(repeated, 0, 1, stride=1, stride_axis=0)
            column = lax.broadcasted_iota(jnp.int32, repeated.shape, 1)
            lag = lax.broadcasted_iota(jnp.int32, repeated.shape, 0)
            kept = jnp.where(column >= lag, turned, 0.0).astype(BF16)
            table_ref[at * BLOCK : (at + 1) * BLOCK, :] = kept

        stacked = jnp.concatenate(
            [
                signal[own, a * LANES : (a + 1) * LANES]
                for a in range(tiles)
                for signal in signals
            ],
            axis=0,
        )
        slot_of = lax.broadcasted_iota(jnp.int32, stacked.shape, 0) % SLOTS
        turned = stacked
        for slot in range(1, SLOTS):
            turned = jnp.where(slot_of == slot, lane_roll(stacked, BLOCK * slot), turned)
        spread = jnp.stack(
            [
                lane_roll(turned, -BLOCK * slot).reshape(tiles, block_rows, LANES)
                for slot in range(SLOTS)
            ],
            axis=1,
        ).reshape(rows, LANES)
        owner = lax.broadcasted_iota(jnp.int32, (rows, LANES), 0) % GROUP
        for half in range(GROUP // SLOTS):
            kept = jnp.where(owner == lane // BLOCK + half * SLOTS, spread, 0.0)
            left_ref[:, half * LANES : (half + 1) * LANES] = kept.astype(BF16)

        sums_ref[...] = jnp.zeros_like(sums_ref)
        if tiles <= 16:
            for at in range(tiles // 2):
                start = 2 * at * tile_rows
                partial = jnp.dot(
                    left_ref[: rows - start, :],
                    table_ref[:, at * pair : (at + 1) * pair],
                    preferred_element_type=F32,
                )
                sums_ref[start:rows, :] += partial[:, :LANES]
                sums_ref[start + tile_rows : rows, :] += partial[: rows - start - tile_rows, LANES:]
        else:

            def add(at, _):
                partial = jnp.dot(
                    left_ref[...],
                    table_ref[:, pl.ds(pl.multiple_of(at * pair, pair), pair)],
                    preferred_element_type=F32,
                )
                start = pl.multiple_of(2 * at * tile_rows, tile_rows)
                sums_ref[pl.ds(start, rows), :] += partial[:, :LANES]
                sums_ref[pl.ds(start + tile_rows, rows), :] += partial[:, LANES:]
                return 0

            lax.fori_loop(0, tiles // 2, add, 0)

        sums = sums_ref[:rows, :]
        landed = [0.0] * SLOTS
        for part in range(SLOTS):
            late = sums
            if part:
                ahead = jnp.zeros((part * block_rows, LANES), F32)
                late = jnp.concatenate([ahead, sums[: rows - part * block_rows]], axis=0)
            late = late.reshape(tiles, SLOTS, block_rows, LANES)
            for slot in range(SLOTS):
                moved = late[:, slot].reshape(tiles * block_rows, LANES)
                landed[slot] += lane_roll(moved, BLOCK * (slot - part))
        result = 0.0
        for slot in range(SLOTS):
            result += jnp.where(lane // BLOCK == slot, landed[slot], 0.0)
        result = result.reshape(tiles, cores, GROUP, LANES)
        for part in range(cores):
            done_ref[part * tiles : (part + 1) * tiles, own, :] = result[:, part]

    out_ref[...] = done_ref[:, :held, :].astype(BF16)


def out_kernel(gate_ref, mixed_ref, source_ref, target_ref, weight_ref, held_ref, read_sems, write_sems):
    chunks, _, step = weight_ref.shape
    reads = []
    for at in range(chunks):
        columns = source_ref.at[:, pl.ds(at * step, step)]
        reads.append(pltpu.make_async_copy(columns, weight_ref.at[at], read_sems.at[at]))
        reads[-1].start()
    gated = (gate_ref[...] * mixed_ref[...].astype(F32)).T.astype(BF16)
    writes = []
    for at in range(chunks):
        reads[at].wait()
        held_ref[at] = jnp.dot(gated, weight_ref[at], preferred_element_type=F32).astype(BF16)
        columns = target_ref.at[:, pl.ds(at * step, step)]
        writes.append(pltpu.make_async_copy(held_ref.at[at], columns, write_sems.at[at]))
        writes[-1].start()
    for write in writes:
        write.wait()


def exchanged(value, axis, step):
    return lax.ppermute(value, axis, [(i, i ^ step) for i in range(lax.axis_size(axis))])


def on_device(near, far, tokens, sign_in, sign_out, w_value, w_noise, w_gate, conv_taps, long_filter, w_out):
    rows, width = tokens.shape
    channels = w_gate.shape[1]
    cores = lax.axis_size("dp")
    count = near * far
    half = channels // cores
    held = half // count
    share = w_value.shape[0]
    depth = share * far
    length = count * rows
    far_at, near_at, core = lax.axis_index("far"), lax.axis_index("near"), lax.axis_index("dp")
    where = jnp.stack([core, far_at, near_at]).astype(jnp.int32)

    packed_width = depth + depth // 8 + channels // 8 + -(channels // 8) % LANES
    if share % LANES == 0 and far <= 8:
        weights, *chunks = pl.pallas_call(
            functools.partial(pack_kernel, near, far),
            in_specs=[SMEM] + [HBM] * 5,
            out_specs=[VMEM] * (1 + near),
            out_shape=[jax.ShapeDtypeStruct((share, 2 * half), BF16)]
            + [jax.ShapeDtypeStruct((rows, packed_width), BF16)] * near,
            scratch_shapes=[
                pltpu.VMEM(sign_in.shape, jnp.int32),
                pltpu.VMEM(sign_out.shape[::-1], jnp.int32),
                pltpu.SemaphoreType.DMA((2,)),
                pltpu.SemaphoreType.DMA((2,)),
                pltpu.SemaphoreType.DMA((near * far,)),
            ],
            compiler_params=params(16),
            cost_estimate=cost(2 * rows * 512 * 512, 3 * MIB),
            name="pack",
        )(where, *in_hbm(tokens, sign_in, sign_out.T, w_value, w_noise))
        pieces = [weights] + [exchanged(weights, "far", turn) for turn in range(1, far)]
    else:
        own = lax.dynamic_slice_in_dim(jnp.stack([w_value, w_noise]), core * half, half, axis=2)
        own = own.transpose(1, 0, 2).reshape(share, 2 * half)
        pieces = [lax.all_gather(own, "far", axis=0, tiled=True)]
        order = jnp.arange(near) ^ near_at

        def by_owner(array):
            parts = array.reshape(rows, far, near, -1).transpose(2, 0, 1, 3).reshape(near, rows, -1)
            return jnp.take(parts, order, axis=0)

        words = by_owner(sign_in)
        sent = jnp.broadcast_to(sign_out[None], (near, *sign_out.shape))
        spare = jnp.zeros((near, rows, -(channels // 8) % LANES), jnp.int32)
        signs = [words & 255, words >> 8, sent & 255, sent >> 8, spare]
        packed = [by_owner(tokens)] + [part.astype(BF16) for part in signs]
        chunks = list(jnp.concatenate(packed, axis=2))
    chunks = [chunks[0]] + [exchanged(chunks[step], "near", step) for step in range(1, near)]
    chunks += [exchanged(chunk, "dp", 1) for chunk in chunks]

    late_tokens, _ = lax.optimization_barrier((tokens, pieces[0]))
    gate_rows = jnp.dot(late_tokens, w_gate, preferred_element_type=F32).astype(BF16)
    before = lax.ppermute(
        gate_rows[rows - 2 :], ("far", "near"), [(i, i + 1) for i in range(count - 1)]
    )
    extended = jnp.concatenate([before, gate_rows], axis=0).astype(F32)
    gate_short = sum(
        conv_taps[lag, channels:] * extended[2 - lag : 2 - lag + rows] for lag in range(3)
    ).T
    first = core * half + (far_at * near + near_at) * held
    taps = lax.dynamic_slice_in_dim(conv_taps, first, held, axis=1).T
    pieces[0], gate_short, taps = lax.optimization_barrier((pieces[0], gate_short, taps))

    partial = pl.pallas_call(
        functools.partial(project_kernel, near, cores, far, depth),
        in_specs=[SMEM] + [VMEM] * (1 + len(chunks) + len(pieces)),
        out_specs=VMEM,
        out_shape=jax.ShapeDtypeStruct((half, (cores * near + 1) * rows), BF16),
        compiler_params=params(40),
        cost_estimate=cost(4 * cores * near * rows * depth * half, 6 * MIB),
        name="project",
    )(where, long_filter, *chunks, *pieces)
    parts = lax.all_to_all(partial, ("far", "near"), 0, 0, tiled=True)

    tiles = length // LANES
    all_rows = tiles * SLOTS * cores * GROUP
    held_rows = max(held, GROUP)
    mixed = pl.pallas_call(
        functools.partial(mix_kernel, near, far, cores, held),
        in_specs=[VMEM] * 2,
        out_specs=VMEM,
        out_shape=jax.ShapeDtypeStruct((cores * tiles, held, LANES), BF16),
        scratch_shapes=[
            pltpu.VMEM((all_rows, GROUP * BLOCK), BF16),
            pltpu.VMEM((all_rows * (1 if tiles <= 16 else 2), LANES), F32),
            pltpu.VMEM((cores * tiles, held_rows, LANES), F32),
            pltpu.VMEM((GROUP * BLOCK, length), BF16),
        ],
        compiler_params=params(48),
        cost_estimate=cost(cores * held_rows * BLOCK * length * 256, 2 * MIB),
        name="mix",
    )(parts, taps)

    landed = lax.all_to_all(mixed, ("dp", "far", "near"), 0, 0, tiled=True).reshape(channels, rows)
    chunks = 8
    return pl.pallas_call(
        out_kernel,
        in_specs=[VMEM, VMEM, HBM],
        out_specs=HBM,
        out_shape=jax.ShapeDtypeStruct((rows, width), BF16),
        scratch_shapes=[
            pltpu.VMEM((chunks, channels, width // chunks), BF16),
            pltpu.VMEM((chunks, rows, width // chunks), BF16),
            pltpu.SemaphoreType.DMA((chunks,)),
            pltpu.SemaphoreType.DMA((chunks,)),
        ],
        compiler_params=params(16),
        cost_estimate=cost(2 * rows * width * channels, 5 * MIB),
        name="project_out",
    )(gate_short, landed, *in_hbm(w_out))


def solution(mesh):
    count = mesh.shape["seq"]
    near = 4 if count % 4 == 0 else 1
    far = count // near
    seq_at = mesh.axis_names.index("seq")
    shape = list(mesh.devices.shape)
    shape[seq_at : seq_at + 1] = [far, near]
    names = list(mesh.axis_names)
    names[seq_at : seq_at + 1] = ["far", "near"]
    inner = Mesh(mesh.devices.reshape(shape), tuple(names))
    by_token = P(("dp", "far", "near"), None)
    by_row = P(("far", "near"), None)
    placed = (by_token, by_token, by_token, by_row, by_row, P(), P(), by_row, P())
    return jax.shard_map(
        functools.partial(on_device, near, far),
        mesh=inner,
        in_specs=placed,
        out_specs=by_token,
        check_vma=False,
    )
```

```python
import functools

import jax
import jax.numpy as jnp
from jax import lax
from jax.experimental import pallas as pl
from jax.experimental.pallas import tpu as pltpu
from jax.sharding import Mesh, PartitionSpec as P

F32 = jnp.float32
BF16 = jnp.bfloat16
LANES = 128
GROUP = 8
BLOCK = 32
SLOTS = LANES // BLOCK
MIB = 1 << 20
VMEM = pl.BlockSpec(memory_space=pltpu.VMEM)
SMEM = pl.BlockSpec(memory_space=pltpu.SMEM)
HBM = pl.BlockSpec(memory_space=pltpu.HBM)


def params(mib):
    return pltpu.CompilerParams(vmem_limit_bytes=mib * MIB)


def cost(flops, accessed):
    return pl.CostEstimate(flops=flops, bytes_accessed=accessed, transcendentals=0)


def in_hbm(*arrays):
    return [pltpu.with_memory_space_constraint(array, pltpu.HBM) for array in arrays]


def sign_bytes(packed):
    parts = jnp.concatenate([packed & 255, packed >> 8], axis=1)
    return parts.astype(F32).astype(BF16)


def one_hot(rows, columns, source_of):
    at = lax.broadcasted_iota(jnp.int32, (rows, columns), 0)
    column = lax.broadcasted_iota(jnp.int32, (1, columns), 1)
    return (at == source_of(column)).astype(F32).astype(BF16)


def pack_kernel(
    near, far, where_ref, tokens_ref, in_ref, sent_ref, value_ref, noise_ref, weight_ref, *refs
):
    outs, (in_held, sent_held, read_sems, weight_sems, token_sems) = refs[:near], refs[near:]
    core, far_at, near_at = where_ref[0], where_ref[1], where_ref[2]
    half = weight_ref.shape[1] // 2
    share = weight_ref.shape[0]
    depth = share * far
    words = in_ref.shape[1]
    per_part = words // (near * far)
    own_words = per_part * far

    copies = []
    for at, source in enumerate((value_ref, noise_ref)):
        columns = pl.ds(pl.multiple_of(core * half, half), half)
        target = weight_ref.at[:, at * half : (at + 1) * half]
        copies.append(pltpu.make_async_copy(source.at[:, columns], target, weight_sems.at[at]))
    reads = [
        pltpu.make_async_copy(in_ref, in_held, read_sems.at[0]),
        pltpu.make_async_copy(sent_ref, sent_held, read_sems.at[1]),
    ]
    for step, out in enumerate(outs):
        for turn in range(far):
            start = ((far_at ^ turn) * near + (near_at ^ step)) * share
            columns = pl.ds(pl.multiple_of(start, share), share)
            target = out.at[:, turn * share : (turn + 1) * share]
            copies.append(
                pltpu.make_async_copy(tokens_ref.at[:, columns], target, token_sems.at[step * far + turn])
            )
    for copy in reads + copies:
        copy.start()

    def word_of(column):
        step, rest = column // (2 * own_words), column % (2 * own_words)
        part, word = rest // own_words, rest % own_words
        plane = (word // per_part) ^ far_at
        return part * words + (plane * near + (step ^ near_at)) * per_part + word % per_part

    by_word = one_hot(2 * words, 2 * words, word_of)
    reads[0].wait()
    moved = jnp.dot(sign_bytes(in_held[...]), by_word, preferred_element_type=F32).astype(BF16)
    reads[1].wait()
    sent = sign_bytes(sent_held[...].astype(F32).T.astype(jnp.int32))
    spare = -sent.shape[1] % LANES
    sent = jnp.concatenate([sent, jnp.zeros((sent.shape[0], spare), BF16)], axis=1)
    width = 2 * own_words
    for step, out in enumerate(outs):
        out[:, depth : depth + width] = moved[:, step * width : (step + 1) * width]
        out[:, depth + width :] = sent
    for copy in copies:
        copy.wait()


def spread_signs(pair, byte_of, columns):
    spread = jnp.dot(pair, one_hot(pair.shape[1], columns, byte_of), preferred_element_type=F32)
    mask = 1 << (lax.broadcasted_iota(jnp.int32, (1, columns), 1) & 7)
    return jnp.where((spread.astype(jnp.int32) & mask) != 0, 1.0, -1.0)


def project_kernel(near, cores, planes, depth, where_ref, lags_ref, *refs):
    chunks, pieces, out_ref = refs[: near * cores], refs[near * cores : -1], refs[-1]
    core, near_at = where_ref[0], where_ref[2]
    rows = chunks[0].shape[0]
    half = pieces[0].shape[1] // 2
    words = depth // 16
    sent_words = cores * half // 16
    sent_start = depth + 2 * words

    def in_byte(column):
        return (column >> 4) + words * ((column >> 3) & 1)

    def out_byte(column):
        return core * (half // 16) + (column >> 4) + sent_words * ((column >> 3) & 1)

    def joined(start, stop):
        return jnp.concatenate([chunk[:, start:stop] for chunk in chunks], axis=0)

    flip_in = spread_signs(joined(depth, sent_start), in_byte, depth).astype(BF16)
    flip_out = spread_signs(joined(sent_start, sent_start + 2 * sent_words), out_byte, half)
    mean_part, noise_part = 0.0, 0.0
    step = depth // len(pieces)
    for at, piece in enumerate(pieces):
        tokens = joined(at * step, (at + 1) * step)
        flipped = tokens * flip_in[:, at * step : (at + 1) * step]
        mean_part += jnp.dot(tokens, piece[:, :half], preferred_element_type=F32)
        noise_part += jnp.dot(flipped, piece[:, half:], preferred_element_type=F32)
    value = (mean_part + flip_out * noise_part).T.astype(BF16)
    for part in range(cores):
        for turn in range(near):
            at = part * near + turn
            target = ((core ^ part) * near + (near_at ^ turn)) * rows
            out_ref[:, pl.ds(pl.multiple_of(target, rows), rows)] = value[:, at * rows : (at + 1) * rows]
    lags = lags_ref[:, pl.ds(pl.multiple_of(core * half, half), half)]
    out_ref[:, cores * near * rows :] = lags.T.astype(BF16)


def shifted(values, steps):
    moved = pltpu.roll(values, steps, 1)
    at = lax.broadcasted_iota(jnp.int32, values.shape, 1)
    return jnp.where(at >= steps, moved, 0.0)


def lane_roll(values, steps):
    return pltpu.roll(values, steps % LANES, values.ndim - 1) if steps % LANES else values


def mix_kernel(near, far, cores, held, parts_ref, taps_ref, out_ref, left_ref, sums_ref, done_ref, table_ref):
    tiles = out_ref.shape[0] // cores
    block_rows = cores * GROUP
    tile_rows = SLOTS * block_rows
    rows = tiles * tile_rows
    lane = lax.broadcasted_iota(jnp.int32, (1, LANES), 1)
    pair = 2 * LANES
    span = near * LANES

    def padded(lines):
        if held >= GROUP:
            return lines
        return jnp.concatenate([lines, jnp.zeros((GROUP - held, lines.shape[1]), F32)], axis=0)

    signals = []
    for part in range(cores):
        planes = []
        for plane in range(far):
            total = 0.0
            for turn in range(near):
                start = (plane * near + turn) * held
                piece = parts_ref[start : start + held, part * span : (part + 1) * span]
                total += piece.astype(F32)
            planes.append(total)
        value = jnp.concatenate(planes, axis=1)
        signal = taps_ref[:, 0:1] * value
        for lag in range(1, 3):
            signal += taps_ref[:, lag : lag + 1] * shifted(value, lag)
        signals.append(padded(signal))
    lags = padded(
        jnp.concatenate(
            [
                parts_ref[at * held : (at + 1) * held, cores * span :].astype(F32)
                for at in range(near * far)
            ],
            axis=1,
        )
    )

    for group in range(max(held, GROUP) // GROUP):
        own = slice(group * GROUP, (group + 1) * GROUP)
        for at in range(GROUP):
            row = lags[group * GROUP + at : group * GROUP + at + 1, :]
            repeated = jnp.broadcast_to(row, (BLOCK, row.shape[1]))
            turned = pltpu.roll(repeated, 0, 1, stride=1, stride_axis=0)
            column = lax.broadcasted_iota(jnp.int32, repeated.shape, 1)
            lag = lax.broadcasted_iota(jnp.int32, repeated.shape, 0)
            kept = jnp.where(column >= lag, turned, 0.0).astype(BF16)
            table_ref[at * BLOCK : (at + 1) * BLOCK, :] = kept

        stacked = jnp.concatenate(
            [
                signal[own, a * LANES : (a + 1) * LANES]
                for a in range(tiles)
                for signal in signals
            ],
            axis=0,
        )
        slot_of = lax.broadcasted_iota(jnp.int32, stacked.shape, 0) % SLOTS
        turned = stacked
        for slot in range(1, SLOTS):
            turned = jnp.where(slot_of == slot, lane_roll(stacked, BLOCK * slot), turned)
        spread = jnp.stack(
            [
                lane_roll(turned, -BLOCK * slot).reshape(tiles, block_rows, LANES)
                for slot in range(SLOTS)
            ],
            axis=1,
        ).reshape(rows, LANES)
        owner = lax.broadcasted_iota(jnp.int32, (rows, LANES), 0) % GROUP
        for half in range(GROUP // SLOTS):
            kept = jnp.where(owner == lane // BLOCK + half * SLOTS, spread, 0.0)
            left_ref[:, half * LANES : (half + 1) * LANES] = kept.astype(BF16)

        sums_ref[...] = jnp.zeros_like(sums_ref)
        if tiles <= 16:
            for at in range(tiles // 2):
                start = 2 * at * tile_rows
                partial = jnp.dot(
                    left_ref[: rows - start, :],
                    table_ref[:, at * pair : (at + 1) * pair],
                    preferred_element_type=F32,
                )
                sums_ref[start:rows, :] += partial[:, :LANES]
                sums_ref[start + tile_rows : rows, :] += partial[: rows - start - tile_rows, LANES:]
        else:

            def add(at, _):
                partial = jnp.dot(
                    left_ref[...],
                    table_ref[:, pl.ds(pl.multiple_of(at * pair, pair), pair)],
                    preferred_element_type=F32,
                )
                start = pl.multiple_of(2 * at * tile_rows, tile_rows)
                sums_ref[pl.ds(start, rows), :] += partial[:, :LANES]
                sums_ref[pl.ds(start + tile_rows, rows), :] += partial[:, LANES:]
                return 0

            lax.fori_loop(0, tiles // 2, add, 0)

        sums = sums_ref[:rows, :]
        landed = [0.0] * SLOTS
        for part in range(SLOTS):
            late = sums
            if part:
                ahead = jnp.zeros((part * block_rows, LANES), F32)
                late = jnp.concatenate([ahead, sums[: rows - part * block_rows]], axis=0)
            late = late.reshape(tiles, SLOTS, block_rows, LANES)
            for slot in range(SLOTS):
                moved = late[:, slot].reshape(tiles * block_rows, LANES)
                landed[slot] += lane_roll(moved, BLOCK * (slot - part))
        result = 0.0
        for slot in range(SLOTS):
            result += jnp.where(lane // BLOCK == slot, landed[slot], 0.0)
        result = result.reshape(tiles, cores, GROUP, LANES)
        for part in range(cores):
            done_ref[part * tiles : (part + 1) * tiles, own, :] = result[:, part]

    out_ref[...] = done_ref[:, :held, :].astype(BF16)


def out_kernel(gate_ref, mixed_ref, source_ref, target_ref, weight_ref, held_ref, read_sems, write_sems):
    chunks, _, step = weight_ref.shape
    reads = []
    for at in range(chunks):
        columns = source_ref.at[:, pl.ds(at * step, step)]
        reads.append(pltpu.make_async_copy(columns, weight_ref.at[at], read_sems.at[at]))
        reads[-1].start()
    gated = (gate_ref[...] * mixed_ref[...].astype(F32)).T.astype(BF16)
    writes = []
    for at in range(chunks):
        reads[at].wait()
        held_ref[at] = jnp.dot(gated, weight_ref[at], preferred_element_type=F32).astype(BF16)
        columns = target_ref.at[:, pl.ds(at * step, step)]
        writes.append(pltpu.make_async_copy(held_ref.at[at], columns, write_sems.at[at]))
        writes[-1].start()
    for write in writes:
        write.wait()


def exchanged(value, axis, step):
    return lax.ppermute(value, axis, [(i, i ^ step) for i in range(lax.axis_size(axis))])


def on_device(near, far, tokens, sign_in, sign_out, w_value, w_noise, w_gate, conv_taps, long_filter, w_out):
    rows, width = tokens.shape
    channels = w_gate.shape[1]
    cores = lax.axis_size("dp")
    count = near * far
    half = channels // cores
    held = half // count
    share = w_value.shape[0]
    depth = share * far
    length = count * rows
    far_at, near_at, core = lax.axis_index("far"), lax.axis_index("near"), lax.axis_index("dp")
    where = jnp.stack([core, far_at, near_at]).astype(jnp.int32)

    packed_width = depth + depth // 8 + channels // 8 + -(channels // 8) % LANES
    if share % LANES == 0 and far <= 8:
        weights, *chunks = pl.pallas_call(
            functools.partial(pack_kernel, near, far),
            in_specs=[SMEM] + [HBM] * 5,
            out_specs=[VMEM] * (1 + near),
            out_shape=[jax.ShapeDtypeStruct((share, 2 * half), BF16)]
            + [jax.ShapeDtypeStruct((rows, packed_width), BF16)] * near,
            scratch_shapes=[
                pltpu.VMEM(sign_in.shape, jnp.int32),
                pltpu.VMEM(sign_out.shape[::-1], jnp.int32),
                pltpu.SemaphoreType.DMA((2,)),
                pltpu.SemaphoreType.DMA((2,)),
                pltpu.SemaphoreType.DMA((near * far,)),
            ],
            compiler_params=params(16),
            cost_estimate=cost(2 * rows * 512 * 512, 3 * MIB),
            name="pack",
        )(where, *in_hbm(tokens, sign_in, sign_out.T, w_value, w_noise))
        pieces = [weights] * far
        for turn in sorted(range(1, far), key=lambda v: (v.bit_count(), -v)):
            top = 1 << (turn.bit_length() - 1)
            pieces[turn] = exchanged(pieces[top] if turn > top else weights, "far", turn - top or top)
    else:
        own = lax.dynamic_slice_in_dim(jnp.stack([w_value, w_noise]), core * half, half, axis=2)
        own = own.transpose(1, 0, 2).reshape(share, 2 * half)
        pieces = [lax.all_gather(own, "far", axis=0, tiled=True)]
        order = jnp.arange(near) ^ near_at

        def by_owner(array):
            parts = array.reshape(rows, far, near, -1).transpose(2, 0, 1, 3).reshape(near, rows, -1)
            return jnp.take(parts, order, axis=0)

        words = by_owner(sign_in)
        sent = jnp.broadcast_to(sign_out[None], (near, *sign_out.shape))
        spare = jnp.zeros((near, rows, -(channels // 8) % LANES), jnp.int32)
        signs = [words & 255, words >> 8, sent & 255, sent >> 8, spare]
        packed = [by_owner(tokens)] + [part.astype(BF16) for part in signs]
        chunks = list(jnp.concatenate(packed, axis=2))
    chunks = [chunks[0]] + [exchanged(chunks[step], "near", step) for step in range(1, near)]
    late = 1 % len(pieces)
    late_tokens, chunks[0], pieces[late] = lax.optimization_barrier((tokens, chunks[0], pieces[late]))
    chunks += [exchanged(chunk, "dp", 1) for chunk in chunks]

    gate_rows = jnp.dot(late_tokens, w_gate, preferred_element_type=F32).astype(BF16)
    before = lax.ppermute(
        gate_rows[rows - 2 :], ("far", "near"), [(i, i + 1) for i in range(count - 1)]
    )
    extended = jnp.concatenate([before, gate_rows], axis=0).astype(F32)
    gate_short = sum(
        conv_taps[lag, channels:] * extended[2 - lag : 2 - lag + rows] for lag in range(3)
    ).T
    first = core * half + (far_at * near + near_at) * held
    taps = lax.dynamic_slice_in_dim(conv_taps, first, held, axis=1).T
    pieces[0], gate_short, taps = lax.optimization_barrier((pieces[0], gate_short, taps))

    partial = pl.pallas_call(
        functools.partial(project_kernel, near, cores, far, depth),
        in_specs=[SMEM] + [VMEM] * (1 + len(chunks) + len(pieces)),
        out_specs=VMEM,
        out_shape=jax.ShapeDtypeStruct((half, (cores * near + 1) * rows), BF16),
        compiler_params=params(40),
        cost_estimate=cost(4 * cores * near * rows * depth * half, 6 * MIB),
        name="project",
    )(where, long_filter, *chunks, *pieces)
    parts = lax.all_to_all(partial, ("far", "near"), 0, 0, tiled=True)

    tiles = length // LANES
    all_rows = tiles * SLOTS * cores * GROUP
    held_rows = max(held, GROUP)
    mixed = pl.pallas_call(
        functools.partial(mix_kernel, near, far, cores, held),
        in_specs=[VMEM] * 2,
        out_specs=VMEM,
        out_shape=jax.ShapeDtypeStruct((cores * tiles, held, LANES), BF16),
        scratch_shapes=[
            pltpu.VMEM((all_rows, GROUP * BLOCK), BF16),
            pltpu.VMEM((all_rows * (1 if tiles <= 16 else 2), LANES), F32),
            pltpu.VMEM((cores * tiles, held_rows, LANES), F32),
            pltpu.VMEM((GROUP * BLOCK, length), BF16),
        ],
        compiler_params=params(48),
        cost_estimate=cost(cores * held_rows * BLOCK * length * 256, 2 * MIB),
        name="mix",
    )(parts, taps)

    landed = lax.all_to_all(mixed, ("dp", "far", "near"), 0, 0, tiled=True).reshape(channels, rows)
    chunks = 8
    return pl.pallas_call(
        out_kernel,
        in_specs=[VMEM, VMEM, HBM],
        out_specs=HBM,
        out_shape=jax.ShapeDtypeStruct((rows, width), BF16),
        scratch_shapes=[
            pltpu.VMEM((chunks, channels, width // chunks), BF16),
            pltpu.VMEM((chunks, rows, width // chunks), BF16),
            pltpu.SemaphoreType.DMA((chunks,)),
            pltpu.SemaphoreType.DMA((chunks,)),
        ],
        compiler_params=params(16),
        cost_estimate=cost(2 * rows * width * channels, 5 * MIB),
        name="project_out",
    )(gate_short, landed, *in_hbm(w_out))


def solution(mesh):
    count = mesh.shape["seq"]
    near = 4 if count % 4 == 0 else 1
    far = count // near
    seq_at = mesh.axis_names.index("seq")
    shape = list(mesh.devices.shape)
    shape[seq_at : seq_at + 1] = [far, near]
    names = list(mesh.axis_names)
    names[seq_at : seq_at + 1] = ["far", "near"]
    inner = Mesh(mesh.devices.reshape(shape), tuple(names))
    by_token = P(("dp", "far", "near"), None)
    by_row = P(("far", "near"), None)
    placed = (by_token, by_token, by_token, by_row, by_row, P(), P(), by_row, P())
    return jax.shard_map(
        functools.partial(on_device, near, far),
        mesh=inner,
        in_specs=placed,
        out_specs=by_token,
        check_vma=False,
    )
```

```python
import functools

import jax
import jax.numpy as jnp
from jax import lax
from jax.experimental import pallas as pl
from jax.experimental.pallas import tpu as pltpu
from jax.sharding import Mesh, PartitionSpec as P

F32 = jnp.float32
BF16 = jnp.bfloat16
LANES = 128
GROUP = 8
BLOCK = 32
SLOTS = LANES // BLOCK
MIB = 1 << 20
VMEM = pl.BlockSpec(memory_space=pltpu.VMEM)
SMEM = pl.BlockSpec(memory_space=pltpu.SMEM)
HBM = pl.BlockSpec(memory_space=pltpu.HBM)


def params(mib):
    return pltpu.CompilerParams(vmem_limit_bytes=mib * MIB)


def cost(flops, accessed):
    return pl.CostEstimate(flops=flops, bytes_accessed=accessed, transcendentals=0)


def in_hbm(*arrays):
    return [pltpu.with_memory_space_constraint(array, pltpu.HBM) for array in arrays]


def sign_bytes(packed):
    parts = jnp.concatenate([packed & 255, packed >> 8], axis=1)
    return parts.astype(F32).astype(BF16)


def one_hot(rows, columns, source_of):
    at = lax.broadcasted_iota(jnp.int32, (rows, columns), 0)
    column = lax.broadcasted_iota(jnp.int32, (1, columns), 1)
    return (at == source_of(column)).astype(F32).astype(BF16)


def pack_kernel(
    near, far, where_ref, tokens_ref, in_ref, sent_ref, value_ref, noise_ref, weight_ref, *refs
):
    outs, (in_held, sent_held, read_sems, weight_sems, token_sems) = refs[:near], refs[near:]
    core, far_at, near_at = where_ref[0], where_ref[1], where_ref[2]
    half = weight_ref.shape[1] // 2
    share = weight_ref.shape[0]
    depth = share * far
    words = in_ref.shape[1]
    per_part = words // (near * far)
    own_words = per_part * far

    copies = []
    for at, source in enumerate((value_ref, noise_ref)):
        columns = pl.ds(pl.multiple_of(core * half, half), half)
        target = weight_ref.at[:, at * half : (at + 1) * half]
        copies.append(pltpu.make_async_copy(source.at[:, columns], target, weight_sems.at[at]))
    reads = [
        pltpu.make_async_copy(in_ref, in_held, read_sems.at[0]),
        pltpu.make_async_copy(sent_ref, sent_held, read_sems.at[1]),
    ]
    for step, out in enumerate(outs):
        for turn in range(far):
            start = ((far_at ^ turn) * near + (near_at ^ step)) * share
            columns = pl.ds(pl.multiple_of(start, share), share)
            target = out.at[:, turn * share : (turn + 1) * share]
            copies.append(
                pltpu.make_async_copy(tokens_ref.at[:, columns], target, token_sems.at[step * far + turn])
            )
    for copy in reads + copies:
        copy.start()

    def word_of(column):
        step, rest = column // (2 * own_words), column % (2 * own_words)
        part, word = rest // own_words, rest % own_words
        plane = (word // per_part) ^ far_at
        return part * words + (plane * near + (step ^ near_at)) * per_part + word % per_part

    by_word = one_hot(2 * words, 2 * words, word_of)
    reads[0].wait()
    moved = jnp.dot(sign_bytes(in_held[...]), by_word, preferred_element_type=F32).astype(BF16)
    reads[1].wait()
    sent = sign_bytes(sent_held[...].astype(F32).T.astype(jnp.int32))
    spare = -sent.shape[1] % LANES
    sent = jnp.concatenate([sent, jnp.zeros((sent.shape[0], spare), BF16)], axis=1)
    width = 2 * own_words
    for step, out in enumerate(outs):
        out[:, depth : depth + width] = moved[:, step * width : (step + 1) * width]
        out[:, depth + width :] = sent
    for copy in copies:
        copy.wait()


def spread_signs(pair, byte_of, columns):
    spread = jnp.dot(pair, one_hot(pair.shape[1], columns, byte_of), preferred_element_type=F32)
    mask = 1 << (lax.broadcasted_iota(jnp.int32, (1, columns), 1) & 7)
    return jnp.where((spread.astype(jnp.int32) & mask) != 0, 1.0, -1.0)


def project_kernel(near, cores, planes, depth, where_ref, lags_ref, *refs):
    chunks, pieces, out_ref = refs[: near * cores], refs[near * cores : -1], refs[-1]
    core, near_at = where_ref[0], where_ref[2]
    rows = chunks[0].shape[0]
    half = pieces[0].shape[1] // 2
    words = depth // 16
    sent_words = cores * half // 16
    sent_start = depth + 2 * words

    def in_byte(column):
        return (column >> 4) + words * ((column >> 3) & 1)

    def out_byte(column):
        return core * (half // 16) + (column >> 4) + sent_words * ((column >> 3) & 1)

    def joined(start, stop):
        return jnp.concatenate([chunk[:, start:stop] for chunk in chunks], axis=0)

    flip_in = spread_signs(joined(depth, sent_start), in_byte, depth).astype(BF16)
    flip_out = spread_signs(joined(sent_start, sent_start + 2 * sent_words), out_byte, half)
    mean_part, noise_part = 0.0, 0.0
    step = depth // len(pieces)
    for at, piece in enumerate(pieces):
        tokens = joined(at * step, (at + 1) * step)
        flipped = tokens * flip_in[:, at * step : (at + 1) * step]
        mean_part += jnp.dot(tokens, piece[:, :half], preferred_element_type=F32)
        noise_part += jnp.dot(flipped, piece[:, half:], preferred_element_type=F32)
    value = (mean_part + flip_out * noise_part).T.astype(BF16)
    for part in range(cores):
        for turn in range(near):
            at = part * near + turn
            target = ((core ^ part) * near + (near_at ^ turn)) * rows
            out_ref[:, pl.ds(pl.multiple_of(target, rows), rows)] = value[:, at * rows : (at + 1) * rows]
    lags = lags_ref[:, pl.ds(pl.multiple_of(core * half, half), half)]
    out_ref[:, cores * near * rows :] = lags.T.astype(BF16)


def shifted(values, steps):
    moved = pltpu.roll(values, steps, 1)
    at = lax.broadcasted_iota(jnp.int32, values.shape, 1)
    return jnp.where(at >= steps, moved, 0.0)


def lane_roll(values, steps):
    return pltpu.roll(values, steps % LANES, values.ndim - 1) if steps % LANES else values


def mix_kernel(near, far, cores, held, parts_ref, taps_ref, out_ref, left_ref, sums_ref, done_ref, table_ref):
    tiles = out_ref.shape[0] // cores
    block_rows = cores * GROUP
    tile_rows = SLOTS * block_rows
    rows = tiles * tile_rows
    lane = lax.broadcasted_iota(jnp.int32, (1, LANES), 1)
    pair = 2 * LANES
    span = near * LANES

    def padded(lines):
        if held >= GROUP:
            return lines
        return jnp.concatenate([lines, jnp.zeros((GROUP - held, lines.shape[1]), F32)], axis=0)

    signals = []
    for part in range(cores):
        planes = []
        for plane in range(far):
            total = 0.0
            for turn in range(near):
                start = (plane * near + turn) * held
                piece = parts_ref[start : start + held, part * span : (part + 1) * span]
                total += piece.astype(F32)
            planes.append(total)
        value = jnp.concatenate(planes, axis=1)
        signal = taps_ref[:, 0:1] * value
        for lag in range(1, 3):
            signal += taps_ref[:, lag : lag + 1] * shifted(value, lag)
        signals.append(padded(signal))
    lags = padded(
        jnp.concatenate(
            [
                parts_ref[at * held : (at + 1) * held, cores * span :].astype(F32)
                for at in range(near * far)
            ],
            axis=1,
        )
    )

    for group in range(max(held, GROUP) // GROUP):
        own = slice(group * GROUP, (group + 1) * GROUP)
        for at in range(GROUP):
            row = lags[group * GROUP + at : group * GROUP + at + 1, :]
            repeated = jnp.broadcast_to(row, (BLOCK, row.shape[1]))
            turned = pltpu.roll(repeated, 0, 1, stride=1, stride_axis=0)
            column = lax.broadcasted_iota(jnp.int32, repeated.shape, 1)
            lag = lax.broadcasted_iota(jnp.int32, repeated.shape, 0)
            kept = jnp.where(column >= lag, turned, 0.0).astype(BF16)
            table_ref[at * BLOCK : (at + 1) * BLOCK, :] = kept

        stacked = jnp.concatenate(
            [
                signal[own, a * LANES : (a + 1) * LANES]
                for a in range(tiles)
                for signal in signals
            ],
            axis=0,
        )
        slot_of = lax.broadcasted_iota(jnp.int32, stacked.shape, 0) % SLOTS
        turned = stacked
        for slot in range(1, SLOTS):
            turned = jnp.where(slot_of == slot, lane_roll(stacked, BLOCK * slot), turned)
        spread = jnp.stack(
            [
                lane_roll(turned, -BLOCK * slot).reshape(tiles, block_rows, LANES)
                for slot in range(SLOTS)
            ],
            axis=1,
        ).reshape(rows, LANES)
        owner = lax.broadcasted_iota(jnp.int32, (rows, LANES), 0) % GROUP
        for half in range(GROUP // SLOTS):
            kept = jnp.where(owner == lane // BLOCK + half * SLOTS, spread, 0.0)
            left_ref[:, half * LANES : (half + 1) * LANES] = kept.astype(BF16)

        sums_ref[...] = jnp.zeros_like(sums_ref)
        if tiles <= 16:
            for at in range(tiles // 2):
                start = 2 * at * tile_rows
                partial = jnp.dot(
                    left_ref[: rows - start, :],
                    table_ref[:, at * pair : (at + 1) * pair],
                    preferred_element_type=F32,
                )
                sums_ref[start:rows, :] += partial[:, :LANES]
                sums_ref[start + tile_rows : rows, :] += partial[: rows - start - tile_rows, LANES:]
        else:

            def add(at, _):
                partial = jnp.dot(
                    left_ref[...],
                    table_ref[:, pl.ds(pl.multiple_of(at * pair, pair), pair)],
                    preferred_element_type=F32,
                )
                start = pl.multiple_of(2 * at * tile_rows, tile_rows)
                sums_ref[pl.ds(start, rows), :] += partial[:, :LANES]
                sums_ref[pl.ds(start + tile_rows, rows), :] += partial[:, LANES:]
                return 0

            lax.fori_loop(0, tiles // 2, add, 0)

        sums = sums_ref[:rows, :]
        landed = [0.0] * SLOTS
        for part in range(SLOTS):
            late = sums
            if part:
                ahead = jnp.zeros((part * block_rows, LANES), F32)
                late = jnp.concatenate([ahead, sums[: rows - part * block_rows]], axis=0)
            late = late.reshape(tiles, SLOTS, block_rows, LANES)
            for slot in range(SLOTS):
                moved = late[:, slot].reshape(tiles * block_rows, LANES)
                landed[slot] += lane_roll(moved, BLOCK * (slot - part))
        result = 0.0
        for slot in range(SLOTS):
            result += jnp.where(lane // BLOCK == slot, landed[slot], 0.0)
        result = result.reshape(tiles, cores, GROUP, LANES)
        for part in range(cores):
            done_ref[part * tiles : (part + 1) * tiles, own, :] = result[:, part]

    out_ref[...] = done_ref[:, :held, :].astype(BF16)


def out_kernel(gate_ref, before_ref, taps_ref, mixed_ref, source_ref, target_ref, weight_ref, held_ref, read_sems, write_sems):
    chunks, channels, step = weight_ref.shape
    reads = []
    for at in range(chunks):
        columns = source_ref.at[:, pl.ds(at * step, step)]
        reads.append(pltpu.make_async_copy(columns, weight_ref.at[at], read_sems.at[at]))
        reads[-1].start()
    gate = gate_ref[...].astype(F32)
    before = before_ref[...].astype(F32)
    extended = jnp.concatenate([before, gate], axis=0)
    gate_short = taps_ref[0:1, channels:] * gate
    for lag in range(1, 3):
        gate_short += taps_ref[lag : lag + 1, channels:] * extended[2 - lag : 2 - lag + gate.shape[0]]
    gated = (gate_short * mixed_ref[...].astype(F32).T).astype(BF16)
    writes = []
    for at in range(chunks):
        reads[at].wait()
        held_ref[at] = jnp.dot(gated, weight_ref[at], preferred_element_type=F32).astype(BF16)
        columns = target_ref.at[:, pl.ds(at * step, step)]
        writes.append(pltpu.make_async_copy(held_ref.at[at], columns, write_sems.at[at]))
        writes[-1].start()
    for write in writes:
        write.wait()


def exchanged(value, axis, step):
    return lax.ppermute(value, axis, [(i, i ^ step) for i in range(lax.axis_size(axis))])


def on_device(near, far, tokens, sign_in, sign_out, w_value, w_noise, w_gate, conv_taps, long_filter, w_out):
    rows, width = tokens.shape
    channels = w_gate.shape[1]
    cores = lax.axis_size("dp")
    count = near * far
    half = channels // cores
    held = half // count
    share = w_value.shape[0]
    depth = share * far
    length = count * rows
    far_at, near_at, core = lax.axis_index("far"), lax.axis_index("near"), lax.axis_index("dp")
    where = jnp.stack([core, far_at, near_at]).astype(jnp.int32)

    packed_width = depth + depth // 8 + channels // 8 + -(channels // 8) % LANES
    if share % LANES == 0 and far <= 8:
        weights, *chunks = pl.pallas_call(
            functools.partial(pack_kernel, near, far),
            in_specs=[SMEM] + [HBM] * 5,
            out_specs=[VMEM] * (1 + near),
            out_shape=[jax.ShapeDtypeStruct((share, 2 * half), BF16)]
            + [jax.ShapeDtypeStruct((rows, packed_width), BF16)] * near,
            scratch_shapes=[
                pltpu.VMEM(sign_in.shape, jnp.int32),
                pltpu.VMEM(sign_out.shape[::-1], jnp.int32),
                pltpu.SemaphoreType.DMA((2,)),
                pltpu.SemaphoreType.DMA((2,)),
                pltpu.SemaphoreType.DMA((near * far,)),
            ],
            compiler_params=params(16),
            cost_estimate=cost(2 * rows * 512 * 512, 3 * MIB),
            name="pack",
        )(where, *in_hbm(tokens, sign_in, sign_out.T, w_value, w_noise))
        pieces = [weights] * far
        for turn in sorted(range(1, far), key=lambda v: (v.bit_count(), -v)):
            top = 1 << (turn.bit_length() - 1)
            pieces[turn] = exchanged(pieces[top] if turn > top else weights, "far", turn - top or top)
    else:
        own = lax.dynamic_slice_in_dim(jnp.stack([w_value, w_noise]), core * half, half, axis=2)
        own = own.transpose(1, 0, 2).reshape(share, 2 * half)
        pieces = [lax.all_gather(own, "far", axis=0, tiled=True)]
        order = jnp.arange(near) ^ near_at

        def by_owner(array):
            parts = array.reshape(rows, far, near, -1).transpose(2, 0, 1, 3).reshape(near, rows, -1)
            return jnp.take(parts, order, axis=0)

        words = by_owner(sign_in)
        sent = jnp.broadcast_to(sign_out[None], (near, *sign_out.shape))
        spare = jnp.zeros((near, rows, -(channels // 8) % LANES), jnp.int32)
        signs = [words & 255, words >> 8, sent & 255, sent >> 8, spare]
        packed = [by_owner(tokens)] + [part.astype(BF16) for part in signs]
        chunks = list(jnp.concatenate(packed, axis=2))
    chunks = [chunks[0]] + [exchanged(chunks[step], "near", step) for step in range(1, near)]
    late = 1 % len(pieces)
    chunks[0], pieces[late] = lax.optimization_barrier((chunks[0], pieces[late]))
    chunks += [exchanged(chunk, "dp", 1) for chunk in chunks]

    first = core * half + (far_at * near + near_at) * held
    taps = lax.dynamic_slice_in_dim(conv_taps, first, held, axis=1).T
    pieces[0], taps = lax.optimization_barrier((pieces[0], taps))

    partial = pl.pallas_call(
        functools.partial(project_kernel, near, cores, far, depth),
        in_specs=[SMEM] + [VMEM] * (1 + len(chunks) + len(pieces)),
        out_specs=VMEM,
        out_shape=jax.ShapeDtypeStruct((half, (cores * near + 1) * rows), BF16),
        compiler_params=params(40),
        cost_estimate=cost(4 * cores * near * rows * depth * half, 6 * MIB),
        name="project",
    )(where, long_filter, *chunks, *pieces)
    parts = lax.all_to_all(partial, ("far", "near"), 0, 0, tiled=True)

    late_tokens, _ = lax.optimization_barrier((tokens, partial))
    gate_rows = jnp.dot(late_tokens, w_gate, preferred_element_type=F32).astype(BF16)
    before = lax.ppermute(
        gate_rows[rows - 2 :], ("far", "near"), [(i, i + 1) for i in range(count - 1)]
    )
    parts, gate_rows = lax.optimization_barrier((parts, gate_rows))

    tiles = length // LANES
    all_rows = tiles * SLOTS * cores * GROUP
    held_rows = max(held, GROUP)
    mixed = pl.pallas_call(
        functools.partial(mix_kernel, near, far, cores, held),
        in_specs=[VMEM] * 2,
        out_specs=VMEM,
        out_shape=jax.ShapeDtypeStruct((cores * tiles, held, LANES), BF16),
        scratch_shapes=[
            pltpu.VMEM((all_rows, GROUP * BLOCK), BF16),
            pltpu.VMEM((all_rows * (1 if tiles <= 16 else 2), LANES), F32),
            pltpu.VMEM((cores * tiles, held_rows, LANES), F32),
            pltpu.VMEM((GROUP * BLOCK, length), BF16),
        ],
        compiler_params=params(48),
        cost_estimate=cost(cores * held_rows * BLOCK * length * 256, 2 * MIB),
        name="mix",
    )(parts, taps)

    landed = lax.all_to_all(mixed, ("dp", "far", "near"), 0, 0, tiled=True).reshape(channels, rows)
    chunks = 8
    return pl.pallas_call(
        out_kernel,
        in_specs=[VMEM] * 4 + [HBM],
        out_specs=HBM,
        out_shape=jax.ShapeDtypeStruct((rows, width), BF16),
        scratch_shapes=[
            pltpu.VMEM((chunks, channels, width // chunks), BF16),
            pltpu.VMEM((chunks, rows, width // chunks), BF16),
            pltpu.SemaphoreType.DMA((chunks,)),
            pltpu.SemaphoreType.DMA((chunks,)),
        ],
        compiler_params=params(16),
        cost_estimate=cost(2 * rows * width * channels, 5 * MIB),
        name="project_out",
    )(gate_rows, before, conv_taps, landed, *in_hbm(w_out))


def solution(mesh):
    count = mesh.shape["seq"]
    near = 4 if count % 4 == 0 else 1
    far = count // near
    seq_at = mesh.axis_names.index("seq")
    shape = list(mesh.devices.shape)
    shape[seq_at : seq_at + 1] = [far, near]
    names = list(mesh.axis_names)
    names[seq_at : seq_at + 1] = ["far", "near"]
    inner = Mesh(mesh.devices.reshape(shape), tuple(names))
    by_token = P(("dp", "far", "near"), None)
    by_row = P(("far", "near"), None)
    placed = (by_token, by_token, by_token, by_row, by_row, P(), P(), by_row, P())
    return jax.shard_map(
        functools.partial(on_device, near, far),
        mesh=inner,
        in_specs=placed,
        out_specs=by_token,
        check_vma=False,
    )
```

```python
import functools

import jax
import jax.numpy as jnp
from jax import lax
from jax.experimental import pallas as pl
from jax.experimental.pallas import tpu as pltpu
from jax.sharding import Mesh, PartitionSpec as P

F32 = jnp.float32
BF16 = jnp.bfloat16
LANES = 128
GROUP = 8
BLOCK = 32
SLOTS = LANES // BLOCK
MIB = 1 << 20
VMEM = pl.BlockSpec(memory_space=pltpu.VMEM)
SMEM = pl.BlockSpec(memory_space=pltpu.SMEM)
HBM = pl.BlockSpec(memory_space=pltpu.HBM)


def params(mib):
    return pltpu.CompilerParams(vmem_limit_bytes=mib * MIB)


def cost(flops, accessed):
    return pl.CostEstimate(flops=flops, bytes_accessed=accessed, transcendentals=0)


def in_hbm(*arrays):
    return [pltpu.with_memory_space_constraint(array, pltpu.HBM) for array in arrays]


def sign_bytes(packed):
    parts = jnp.concatenate([packed & 255, packed >> 8], axis=1)
    return parts.astype(F32).astype(BF16)


def one_hot(rows, columns, source_of):
    at = lax.broadcasted_iota(jnp.int32, (rows, columns), 0)
    column = lax.broadcasted_iota(jnp.int32, (1, columns), 1)
    return (at == source_of(column)).astype(F32).astype(BF16)


def pack_kernel(
    near, far, where_ref, tokens_ref, in_ref, sent_ref, value_ref, noise_ref, weight_ref, *refs
):
    outs, (in_held, sent_held, read_sems, weight_sems, token_sems) = refs[:near], refs[near:]
    core, far_at, near_at = where_ref[0], where_ref[1], where_ref[2]
    half = weight_ref.shape[1] // 2
    share = weight_ref.shape[0]
    depth = share * far
    words = in_ref.shape[1]
    per_part = words // (near * far)
    own_words = per_part * far

    copies = []
    for at, source in enumerate((value_ref, noise_ref)):
        columns = pl.ds(pl.multiple_of(core * half, half), half)
        target = weight_ref.at[:, at * half : (at + 1) * half]
        copies.append(pltpu.make_async_copy(source.at[:, columns], target, weight_sems.at[at]))
    reads = [
        pltpu.make_async_copy(in_ref, in_held, read_sems.at[0]),
        pltpu.make_async_copy(sent_ref, sent_held, read_sems.at[1]),
    ]
    for step, out in enumerate(outs):
        for turn in range(far):
            start = ((far_at ^ turn) * near + (near_at ^ step)) * share
            columns = pl.ds(pl.multiple_of(start, share), share)
            target = out.at[:, turn * share : (turn + 1) * share]
            copies.append(
                pltpu.make_async_copy(tokens_ref.at[:, columns], target, token_sems.at[step * far + turn])
            )
    for copy in reads + copies:
        copy.start()

    def word_of(column):
        step, rest = column // (2 * own_words), column % (2 * own_words)
        part, word = rest // own_words, rest % own_words
        plane = (word // per_part) ^ far_at
        return part * words + (plane * near + (step ^ near_at)) * per_part + word % per_part

    by_word = one_hot(2 * words, 2 * words, word_of)
    reads[0].wait()
    moved = jnp.dot(sign_bytes(in_held[...]), by_word, preferred_element_type=F32).astype(BF16)
    reads[1].wait()
    sent = sign_bytes(sent_held[...].astype(F32).T.astype(jnp.int32))
    spare = -sent.shape[1] % LANES
    sent = jnp.concatenate([sent, jnp.zeros((sent.shape[0], spare), BF16)], axis=1)
    width = 2 * own_words
    for step, out in enumerate(outs):
        out[:, depth : depth + width] = moved[:, step * width : (step + 1) * width]
        out[:, depth + width :] = sent
    for copy in copies:
        copy.wait()


def spread_signs(pair, byte_of, columns):
    spread = jnp.dot(pair, one_hot(pair.shape[1], columns, byte_of), preferred_element_type=F32)
    mask = 1 << (lax.broadcasted_iota(jnp.int32, (1, columns), 1) & 7)
    return jnp.where((spread.astype(jnp.int32) & mask) != 0, 1.0, -1.0)


def project_kernel(near, cores, planes, depth, where_ref, lags_ref, *refs):
    chunks, pieces, out_ref = refs[: near * cores], refs[near * cores : -1], refs[-1]
    core, near_at = where_ref[0], where_ref[2]
    rows = chunks[0].shape[0]
    half = pieces[0].shape[1] // 2
    words = depth // 16
    sent_words = cores * half // 16
    sent_start = depth + 2 * words

    def in_byte(column):
        return (column >> 4) + words * ((column >> 3) & 1)

    def out_byte(column):
        return core * (half // 16) + (column >> 4) + sent_words * ((column >> 3) & 1)

    def joined(start, stop):
        return jnp.concatenate([chunk[:, start:stop] for chunk in chunks], axis=0)

    flip_in = spread_signs(joined(depth, sent_start), in_byte, depth).astype(BF16)
    flip_out = spread_signs(joined(sent_start, sent_start + 2 * sent_words), out_byte, half)
    mean_part, noise_part = 0.0, 0.0
    step = depth // len(pieces)
    for at, piece in enumerate(pieces):
        tokens = joined(at * step, (at + 1) * step)
        flipped = tokens * flip_in[:, at * step : (at + 1) * step]
        mean_part += jnp.dot(tokens, piece[:, :half], preferred_element_type=F32)
        noise_part += jnp.dot(flipped, piece[:, half:], preferred_element_type=F32)
    value = (mean_part + flip_out * noise_part).T.astype(BF16)
    for part in range(cores):
        for turn in range(near):
            at = part * near + turn
            target = ((core ^ part) * near + (near_at ^ turn)) * rows
            out_ref[:, pl.ds(pl.multiple_of(target, rows), rows)] = value[:, at * rows : (at + 1) * rows]
    lags = lags_ref[:, pl.ds(pl.multiple_of(core * half, half), half)]
    out_ref[:, cores * near * rows :] = lags.T.astype(BF16)


def shifted(values, steps):
    moved = pltpu.roll(values, steps, 1)
    at = lax.broadcasted_iota(jnp.int32, values.shape, 1)
    return jnp.where(at >= steps, moved, 0.0)


def lane_roll(values, steps):
    return pltpu.roll(values, steps % LANES, values.ndim - 1) if steps % LANES else values


def mix_kernel(near, far, cores, held, parts_ref, taps_ref, out_ref, left_ref, sums_ref, done_ref, table_ref):
    tiles = out_ref.shape[0] // cores
    block_rows = cores * GROUP
    tile_rows = SLOTS * block_rows
    rows = tiles * tile_rows
    lane = lax.broadcasted_iota(jnp.int32, (1, LANES), 1)
    pair = 2 * LANES
    span = near * LANES

    def padded(lines):
        if held >= GROUP:
            return lines
        return jnp.concatenate([lines, jnp.zeros((GROUP - held, lines.shape[1]), F32)], axis=0)

    signals = []
    for part in range(cores):
        planes = []
        for plane in range(far):
            total = 0.0
            for turn in range(near):
                start = (plane * near + turn) * held
                piece = parts_ref[start : start + held, part * span : (part + 1) * span]
                total += piece.astype(F32)
            planes.append(total)
        value = jnp.concatenate(planes, axis=1)
        signal = taps_ref[:, 0:1] * value
        for lag in range(1, 3):
            signal += taps_ref[:, lag : lag + 1] * shifted(value, lag)
        signals.append(padded(signal))
    lags = padded(
        jnp.concatenate(
            [
                parts_ref[at * held : (at + 1) * held, cores * span :].astype(F32)
                for at in range(near * far)
            ],
            axis=1,
        )
    )

    for group in range(max(held, GROUP) // GROUP):
        own = slice(group * GROUP, (group + 1) * GROUP)
        for at in range(GROUP):
            row = lags[group * GROUP + at : group * GROUP + at + 1, :]
            repeated = jnp.broadcast_to(row, (BLOCK, row.shape[1]))
            turned = pltpu.roll(repeated, 0, 1, stride=1, stride_axis=0)
            column = lax.broadcasted_iota(jnp.int32, repeated.shape, 1)
            lag = lax.broadcasted_iota(jnp.int32, repeated.shape, 0)
            kept = jnp.where(column >= lag, turned, 0.0).astype(BF16)
            table_ref[at * BLOCK : (at + 1) * BLOCK, :] = kept

        stacked = jnp.concatenate(
            [
                signal[own, a * LANES : (a + 1) * LANES]
                for a in range(tiles)
                for signal in signals
            ],
            axis=0,
        )
        slot_of = lax.broadcasted_iota(jnp.int32, stacked.shape, 0) % SLOTS
        turned = stacked
        for slot in range(1, SLOTS):
            turned = jnp.where(slot_of == slot, lane_roll(stacked, BLOCK * slot), turned)
        spread = jnp.stack(
            [
                lane_roll(turned, -BLOCK * slot).reshape(tiles, block_rows, LANES)
                for slot in range(SLOTS)
            ],
            axis=1,
        ).reshape(rows, LANES)
        owner = lax.broadcasted_iota(jnp.int32, (rows, LANES), 0) % GROUP
        for half in range(GROUP // SLOTS):
            kept = jnp.where(owner == lane // BLOCK + half * SLOTS, spread, 0.0)
            left_ref[:, half * LANES : (half + 1) * LANES] = kept.astype(BF16)

        sums_ref[...] = jnp.zeros_like(sums_ref)
        if tiles <= 16:
            for at in range(tiles // 2):
                start = 2 * at * tile_rows
                partial = jnp.dot(
                    left_ref[: rows - start, :],
                    table_ref[:, at * pair : (at + 1) * pair],
                    preferred_element_type=F32,
                )
                sums_ref[start:rows, :] += partial[:, :LANES]
                sums_ref[start + tile_rows : rows, :] += partial[: rows - start - tile_rows, LANES:]
        else:

            def add(at, _):
                partial = jnp.dot(
                    left_ref[...],
                    table_ref[:, pl.ds(pl.multiple_of(at * pair, pair), pair)],
                    preferred_element_type=F32,
                )
                start = pl.multiple_of(2 * at * tile_rows, tile_rows)
                sums_ref[pl.ds(start, rows), :] += partial[:, :LANES]
                sums_ref[pl.ds(start + tile_rows, rows), :] += partial[:, LANES:]
                return 0

            lax.fori_loop(0, tiles // 2, add, 0)

        sums = sums_ref[:rows, :]
        landed = [0.0] * SLOTS
        for part in range(SLOTS):
            late = sums
            if part:
                ahead = jnp.zeros((part * block_rows, LANES), F32)
                late = jnp.concatenate([ahead, sums[: rows - part * block_rows]], axis=0)
            late = late.reshape(tiles, SLOTS, block_rows, LANES)
            for slot in range(SLOTS):
                moved = late[:, slot].reshape(tiles * block_rows, LANES)
                landed[slot] += lane_roll(moved, BLOCK * (slot - part))
        result = 0.0
        for slot in range(SLOTS):
            result += jnp.where(lane // BLOCK == slot, landed[slot], 0.0)
        result = result.reshape(tiles, cores, GROUP, LANES)
        for part in range(cores):
            done_ref[part * tiles : (part + 1) * tiles, own, :] = result[:, part]

    out_ref[...] = done_ref[:, :held, :].astype(BF16)


def out_kernel(gate_ref, before_ref, taps_ref, mixed_ref, source_ref, target_ref, weight_ref, held_ref, read_sems, write_sems):
    chunks, channels, step = weight_ref.shape
    reads = []
    for at in range(chunks):
        columns = source_ref.at[:, pl.ds(at * step, step)]
        reads.append(pltpu.make_async_copy(columns, weight_ref.at[at], read_sems.at[at]))
        reads[-1].start()
    gate = gate_ref[...].astype(F32)
    before = before_ref[...].astype(F32)
    extended = jnp.concatenate([before, gate], axis=0)
    gate_short = taps_ref[0:1, channels:] * gate
    for lag in range(1, 3):
        gate_short += taps_ref[lag : lag + 1, channels:] * extended[2 - lag : 2 - lag + gate.shape[0]]
    gated = (gate_short * mixed_ref[...].astype(F32).T).astype(BF16)
    writes = []
    for at in range(chunks):
        reads[at].wait()
        held_ref[at] = jnp.dot(gated, weight_ref[at], preferred_element_type=F32).astype(BF16)
        columns = target_ref.at[:, pl.ds(at * step, step)]
        writes.append(pltpu.make_async_copy(held_ref.at[at], columns, write_sems.at[at]))
        writes[-1].start()
    for write in writes:
        write.wait()


def exchanged(value, axis, step):
    return lax.ppermute(value, axis, [(i, i ^ step) for i in range(lax.axis_size(axis))])


def on_device(near, far, tokens, sign_in, sign_out, w_value, w_noise, w_gate, conv_taps, long_filter, w_out):
    rows, width = tokens.shape
    channels = w_gate.shape[1]
    cores = lax.axis_size("dp")
    count = near * far
    half = channels // cores
    held = half // count
    share = w_value.shape[0]
    depth = share * far
    length = count * rows
    far_at, near_at, core = lax.axis_index("far"), lax.axis_index("near"), lax.axis_index("dp")
    where = jnp.stack([core, far_at, near_at]).astype(jnp.int32)

    packed_width = depth + depth // 8 + channels // 8 + -(channels // 8) % LANES
    if share % LANES == 0 and far == 4:
        weights, *chunks = pl.pallas_call(
            functools.partial(pack_kernel, near, far),
            in_specs=[SMEM] + [HBM] * 5,
            out_specs=[VMEM] * (1 + near),
            out_shape=[jax.ShapeDtypeStruct((share, 2 * half), BF16)]
            + [jax.ShapeDtypeStruct((rows, packed_width), BF16)] * near,
            scratch_shapes=[
                pltpu.VMEM(sign_in.shape, jnp.int32),
                pltpu.VMEM(sign_out.shape[::-1], jnp.int32),
                pltpu.SemaphoreType.DMA((2,)),
                pltpu.SemaphoreType.DMA((2,)),
                pltpu.SemaphoreType.DMA((near * far,)),
            ],
            compiler_params=params(16),
            cost_estimate=cost(2 * rows * 512 * 512, 3 * MIB),
            name="pack",
        )(where, *in_hbm(tokens, sign_in, sign_out.T, w_value, w_noise))
        pieces = [weights] * far
        for turn in (2, 1):
            pieces[turn] = exchanged(weights, "far", turn)
    else:
        own = lax.dynamic_slice_in_dim(jnp.stack([w_value, w_noise]), core * half, half, axis=2)
        own = own.transpose(1, 0, 2).reshape(share, 2 * half)
        pieces = [lax.all_gather(own, "far", axis=0, tiled=True)]
        order = jnp.arange(near) ^ near_at

        def by_owner(array):
            parts = array.reshape(rows, far, near, -1).transpose(2, 0, 1, 3).reshape(near, rows, -1)
            return jnp.take(parts, order, axis=0)

        words = by_owner(sign_in)
        sent = jnp.broadcast_to(sign_out[None], (near, *sign_out.shape))
        spare = jnp.zeros((near, rows, -(channels // 8) % LANES), jnp.int32)
        signs = [words & 255, words >> 8, sent & 255, sent >> 8, spare]
        packed = [by_owner(tokens)] + [part.astype(BF16) for part in signs]
        chunks = list(jnp.concatenate(packed, axis=2))
    late = 1 % len(pieces)
    chunks = [chunks[0]] + [exchanged(chunks[step], "near", step) for step in range(1, near)]

    late_tokens, pieces[late] = lax.optimization_barrier((tokens, pieces[late]))
    gate_rows = jnp.dot(late_tokens, w_gate, preferred_element_type=F32).astype(BF16)
    if len(pieces) > 1:
        pieces[2], chunks[0], gate_rows = lax.optimization_barrier((pieces[2], chunks[0], gate_rows))
        pieces[3] = exchanged(pieces[2], "far", 1)
    chunks += [exchanged(chunk, "dp", 1) for chunk in chunks]
    gate_rows, chunks[near] = lax.optimization_barrier((gate_rows, chunks[near]))
    before = lax.ppermute(
        gate_rows[rows - 2 :], ("far", "near"), [(i, i + 1) for i in range(count - 1)]
    )
    first = core * half + (far_at * near + near_at) * held
    taps = lax.dynamic_slice_in_dim(conv_taps, first, held, axis=1).T
    pieces[0], taps, before = lax.optimization_barrier((pieces[0], taps, before))

    partial = pl.pallas_call(
        functools.partial(project_kernel, near, cores, far, depth),
        in_specs=[SMEM] + [VMEM] * (1 + len(chunks) + len(pieces)),
        out_specs=VMEM,
        out_shape=jax.ShapeDtypeStruct((half, (cores * near + 1) * rows), BF16),
        compiler_params=params(40),
        cost_estimate=cost(4 * cores * near * rows * depth * half, 6 * MIB),
        name="project",
    )(where, long_filter, *chunks, *pieces)
    parts = lax.all_to_all(partial, ("far", "near"), 0, 0, tiled=True)

    tiles = length // LANES
    all_rows = tiles * SLOTS * cores * GROUP
    held_rows = max(held, GROUP)
    mixed = pl.pallas_call(
        functools.partial(mix_kernel, near, far, cores, held),
        in_specs=[VMEM] * 2,
        out_specs=VMEM,
        out_shape=jax.ShapeDtypeStruct((cores * tiles, held, LANES), BF16),
        scratch_shapes=[
            pltpu.VMEM((all_rows, GROUP * BLOCK), BF16),
            pltpu.VMEM((all_rows * (1 if tiles <= 16 else 2), LANES), F32),
            pltpu.VMEM((cores * tiles, held_rows, LANES), F32),
            pltpu.VMEM((GROUP * BLOCK, length), BF16),
        ],
        compiler_params=params(48),
        cost_estimate=cost(cores * held_rows * BLOCK * length * 256, 2 * MIB),
        name="mix",
    )(parts, taps)

    landed = lax.all_to_all(mixed, ("dp", "far", "near"), 0, 0, tiled=True).reshape(channels, rows)
    chunks = 8
    return pl.pallas_call(
        out_kernel,
        in_specs=[VMEM] * 4 + [HBM],
        out_specs=HBM,
        out_shape=jax.ShapeDtypeStruct((rows, width), BF16),
        scratch_shapes=[
            pltpu.VMEM((chunks, channels, width // chunks), BF16),
            pltpu.VMEM((chunks, rows, width // chunks), BF16),
            pltpu.SemaphoreType.DMA((chunks,)),
            pltpu.SemaphoreType.DMA((chunks,)),
        ],
        compiler_params=params(16),
        cost_estimate=cost(2 * rows * width * channels, 5 * MIB),
        name="project_out",
    )(gate_rows, before, conv_taps, landed, *in_hbm(w_out))


def solution(mesh):
    count = mesh.shape["seq"]
    near = 4 if count % 4 == 0 else 1
    far = count // near
    seq_at = mesh.axis_names.index("seq")
    shape = list(mesh.devices.shape)
    shape[seq_at : seq_at + 1] = [far, near]
    names = list(mesh.axis_names)
    names[seq_at : seq_at + 1] = ["far", "near"]
    inner = Mesh(mesh.devices.reshape(shape), tuple(names))
    by_token = P(("dp", "far", "near"), None)
    by_row = P(("far", "near"), None)
    placed = (by_token, by_token, by_token, by_row, by_row, P(), P(), by_row, P())
    return jax.shard_map(
        functools.partial(on_device, near, far),
        mesh=inner,
        in_specs=placed,
        out_specs=by_token,
        check_vma=False,
    )
```

```python
import functools

import jax
import jax.numpy as jnp
from jax import lax
from jax.experimental import pallas as pl
from jax.experimental.pallas import tpu as pltpu
from jax.sharding import Mesh, PartitionSpec as P

F32 = jnp.float32
BF16 = jnp.bfloat16
LANES = 128
GROUP = 8
BLOCK = 32
SLOTS = LANES // BLOCK
MIB = 1 << 20
VMEM = pl.BlockSpec(memory_space=pltpu.VMEM)
SMEM = pl.BlockSpec(memory_space=pltpu.SMEM)
HBM = pl.BlockSpec(memory_space=pltpu.HBM)


def params(mib):
    return pltpu.CompilerParams(vmem_limit_bytes=mib * MIB)


def cost(flops, accessed):
    return pl.CostEstimate(flops=flops, bytes_accessed=accessed, transcendentals=0)


def in_hbm(*arrays):
    return [pltpu.with_memory_space_constraint(array, pltpu.HBM) for array in arrays]


def sign_bytes(packed):
    parts = jnp.concatenate([packed & 255, packed >> 8], axis=1)
    return parts.astype(F32).astype(BF16)


def one_hot(rows, columns, source_of):
    at = lax.broadcasted_iota(jnp.int32, (rows, columns), 0)
    column = lax.broadcasted_iota(jnp.int32, (1, columns), 1)
    return (at == source_of(column)).astype(F32).astype(BF16)


def pack_kernel(
    near, far, where_ref, tokens_ref, in_ref, sent_ref, value_ref, noise_ref, weight_ref, *refs
):
    outs, (in_held, sent_held, read_sems, weight_sems, token_sems) = refs[:near], refs[near:]
    core, far_at, near_at = where_ref[0], where_ref[1], where_ref[2]
    half = weight_ref.shape[1] // 2
    share = weight_ref.shape[0]
    depth = share * far
    words = in_ref.shape[1]
    per_part = words // (near * far)
    own_words = per_part * far

    copies = []
    for at, source in enumerate((value_ref, noise_ref)):
        columns = pl.ds(pl.multiple_of(core * half, half), half)
        target = weight_ref.at[:, at * half : (at + 1) * half]
        copies.append(pltpu.make_async_copy(source.at[:, columns], target, weight_sems.at[at]))
    reads = [
        pltpu.make_async_copy(in_ref, in_held, read_sems.at[0]),
        pltpu.make_async_copy(sent_ref, sent_held, read_sems.at[1]),
    ]
    for step, out in enumerate(outs):
        for turn in range(far):
            start = ((far_at ^ turn) * near + (near_at ^ step)) * share
            columns = pl.ds(pl.multiple_of(start, share), share)
            target = out.at[:, turn * share : (turn + 1) * share]
            copies.append(
                pltpu.make_async_copy(tokens_ref.at[:, columns], target, token_sems.at[step * far + turn])
            )
    for copy in reads + copies:
        copy.start()

    def word_of(column):
        step, rest = column // (2 * own_words), column % (2 * own_words)
        part, word = rest // own_words, rest % own_words
        plane = (word // per_part) ^ far_at
        return part * words + (plane * near + (step ^ near_at)) * per_part + word % per_part

    by_word = one_hot(2 * words, 2 * words, word_of)
    reads[0].wait()
    moved = jnp.dot(sign_bytes(in_held[...]), by_word, preferred_element_type=F32).astype(BF16)
    reads[1].wait()
    sent = sign_bytes(sent_held[...].astype(F32).T.astype(jnp.int32))
    spare = -sent.shape[1] % LANES
    sent = jnp.concatenate([sent, jnp.zeros((sent.shape[0], spare), BF16)], axis=1)
    width = 2 * own_words
    for step, out in enumerate(outs):
        out[:, depth : depth + width] = moved[:, step * width : (step + 1) * width]
        out[:, depth + width :] = sent
    for copy in copies:
        copy.wait()


def spread_signs(pair, byte_of, columns):
    spread = jnp.dot(pair, one_hot(pair.shape[1], columns, byte_of), preferred_element_type=F32)
    mask = 1 << (lax.broadcasted_iota(jnp.int32, (1, columns), 1) & 7)
    return jnp.where((spread.astype(jnp.int32) & mask) != 0, 1.0, -1.0)


def project_kernel(near, cores, planes, depth, where_ref, lags_ref, *refs):
    chunks, pieces, out_ref = refs[: near * cores], refs[near * cores : -1], refs[-1]
    core, near_at = where_ref[0], where_ref[2]
    rows = chunks[0].shape[0]
    half = pieces[0].shape[1] // 2
    words = depth // 16
    sent_words = cores * half // 16
    sent_start = depth + 2 * words

    def in_byte(column):
        return (column >> 4) + words * ((column >> 3) & 1)

    def out_byte(column):
        return core * (half // 16) + (column >> 4) + sent_words * ((column >> 3) & 1)

    def joined(start, stop):
        return jnp.concatenate([chunk[:, start:stop] for chunk in chunks], axis=0)

    flip_in = spread_signs(joined(depth, sent_start), in_byte, depth).astype(BF16)
    flip_out = spread_signs(joined(sent_start, sent_start + 2 * sent_words), out_byte, half)
    mean_part, noise_part = 0.0, 0.0
    step = depth // len(pieces)
    for at, piece in enumerate(pieces):
        tokens = joined(at * step, (at + 1) * step)
        flipped = tokens * flip_in[:, at * step : (at + 1) * step]
        mean_part += jnp.dot(tokens, piece[:, :half], preferred_element_type=F32)
        noise_part += jnp.dot(flipped, piece[:, half:], preferred_element_type=F32)
    value = (mean_part + flip_out * noise_part).T.astype(BF16)
    for part in range(cores):
        for turn in range(near):
            at = part * near + turn
            target = ((core ^ part) * near + (near_at ^ turn)) * rows
            out_ref[:, pl.ds(pl.multiple_of(target, rows), rows)] = value[:, at * rows : (at + 1) * rows]
    lags = lags_ref[:, pl.ds(pl.multiple_of(core * half, half), half)]
    out_ref[:, cores * near * rows :] = lags.T.astype(BF16)


def shifted(values, steps):
    moved = pltpu.roll(values, steps, 1)
    at = lax.broadcasted_iota(jnp.int32, values.shape, 1)
    return jnp.where(at >= steps, moved, 0.0)


def lane_roll(values, steps):
    return pltpu.roll(values, steps % LANES, values.ndim - 1) if steps % LANES else values


def mix_kernel(near, far, cores, held, parts_ref, taps_ref, out_ref, left_ref, sums_ref, done_ref, table_ref):
    tiles = out_ref.shape[0] // cores
    block_rows = cores * GROUP
    tile_rows = SLOTS * block_rows
    rows = tiles * tile_rows
    lane = lax.broadcasted_iota(jnp.int32, (1, LANES), 1)
    pair = 2 * LANES
    span = near * LANES

    def padded(lines):
        if held >= GROUP:
            return lines
        return jnp.concatenate([lines, jnp.zeros((GROUP - held, lines.shape[1]), F32)], axis=0)

    signals = []
    for part in range(cores):
        planes = []
        for plane in range(far):
            total = 0.0
            for turn in range(near):
                start = (plane * near + turn) * held
                piece = parts_ref[start : start + held, part * span : (part + 1) * span]
                total += piece.astype(F32)
            planes.append(total)
        value = jnp.concatenate(planes, axis=1)
        signal = taps_ref[:, 0:1] * value
        for lag in range(1, 3):
            signal += taps_ref[:, lag : lag + 1] * shifted(value, lag)
        signals.append(padded(signal))
    lags = padded(
        jnp.concatenate(
            [
                parts_ref[at * held : (at + 1) * held, cores * span :].astype(F32)
                for at in range(near * far)
            ],
            axis=1,
        )
    )

    for group in range(max(held, GROUP) // GROUP):
        own = slice(group * GROUP, (group + 1) * GROUP)
        for at in range(GROUP):
            row = lags[group * GROUP + at : group * GROUP + at + 1, :]
            repeated = jnp.broadcast_to(row, (BLOCK, row.shape[1]))
            turned = pltpu.roll(repeated, 0, 1, stride=1, stride_axis=0)
            column = lax.broadcasted_iota(jnp.int32, repeated.shape, 1)
            lag = lax.broadcasted_iota(jnp.int32, repeated.shape, 0)
            kept = jnp.where(column >= lag, turned, 0.0).astype(BF16)
            table_ref[at * BLOCK : (at + 1) * BLOCK, :] = kept

        stacked = jnp.concatenate(
            [
                signal[own, a * LANES : (a + 1) * LANES]
                for a in range(tiles)
                for signal in signals
            ],
            axis=0,
        )
        slot_of = lax.broadcasted_iota(jnp.int32, stacked.shape, 0) % SLOTS
        turned = stacked
        for slot in range(1, SLOTS):
            turned = jnp.where(slot_of == slot, lane_roll(stacked, BLOCK * slot), turned)
        spread = jnp.stack(
            [
                lane_roll(turned, -BLOCK * slot).reshape(tiles, block_rows, LANES)
                for slot in range(SLOTS)
            ],
            axis=1,
        ).reshape(rows, LANES)
        owner = lax.broadcasted_iota(jnp.int32, (rows, LANES), 0) % GROUP
        for half in range(GROUP // SLOTS):
            kept = jnp.where(owner == lane // BLOCK + half * SLOTS, spread, 0.0)
            left_ref[:, half * LANES : (half + 1) * LANES] = kept.astype(BF16)

        sums_ref[...] = jnp.zeros_like(sums_ref)
        if tiles <= 16:
            for at in range(tiles // 2):
                start = 2 * at * tile_rows
                partial = jnp.dot(
                    left_ref[: rows - start, :],
                    table_ref[:, at * pair : (at + 1) * pair],
                    preferred_element_type=F32,
                )
                sums_ref[start:rows, :] += partial[:, :LANES]
                sums_ref[start + tile_rows : rows, :] += partial[: rows - start - tile_rows, LANES:]
        else:

            def add(at, _):
                partial = jnp.dot(
                    left_ref[...],
                    table_ref[:, pl.ds(pl.multiple_of(at * pair, pair), pair)],
                    preferred_element_type=F32,
                )
                start = pl.multiple_of(2 * at * tile_rows, tile_rows)
                sums_ref[pl.ds(start, rows), :] += partial[:, :LANES]
                sums_ref[pl.ds(start + tile_rows, rows), :] += partial[:, LANES:]
                return 0

            lax.fori_loop(0, tiles // 2, add, 0)

        sums = sums_ref[:rows, :]
        landed = [0.0] * SLOTS
        for part in range(SLOTS):
            late = sums
            if part:
                ahead = jnp.zeros((part * block_rows, LANES), F32)
                late = jnp.concatenate([ahead, sums[: rows - part * block_rows]], axis=0)
            late = late.reshape(tiles, SLOTS, block_rows, LANES)
            for slot in range(SLOTS):
                moved = late[:, slot].reshape(tiles * block_rows, LANES)
                landed[slot] += lane_roll(moved, BLOCK * (slot - part))
        result = 0.0
        for slot in range(SLOTS):
            result += jnp.where(lane // BLOCK == slot, landed[slot], 0.0)
        result = result.reshape(tiles, cores, GROUP, LANES)
        for part in range(cores):
            done_ref[part * tiles : (part + 1) * tiles, own, :] = result[:, part]

    out_ref[...] = done_ref[:, :held, :].astype(BF16)


def out_kernel(gate_ref, before_ref, taps_ref, mixed_ref, source_ref, target_ref, weight_ref, held_ref, read_sems, write_sems):
    chunks, channels, step = weight_ref.shape
    reads = []
    for at in range(chunks):
        columns = source_ref.at[:, pl.ds(at * step, step)]
        reads.append(pltpu.make_async_copy(columns, weight_ref.at[at], read_sems.at[at]))
        reads[-1].start()
    gate = gate_ref[...].astype(F32)
    before = before_ref[...].astype(F32)
    extended = jnp.concatenate([before, gate], axis=0)
    gate_short = taps_ref[0:1, channels:] * gate
    for lag in range(1, 3):
        gate_short += taps_ref[lag : lag + 1, channels:] * extended[2 - lag : 2 - lag + gate.shape[0]]
    gated = (gate_short * mixed_ref[...].astype(F32).T).astype(BF16)
    writes = []
    for at in range(chunks):
        reads[at].wait()
        held_ref[at] = jnp.dot(gated, weight_ref[at], preferred_element_type=F32).astype(BF16)
        columns = target_ref.at[:, pl.ds(at * step, step)]
        writes.append(pltpu.make_async_copy(held_ref.at[at], columns, write_sems.at[at]))
        writes[-1].start()
    for write in writes:
        write.wait()


def exchanged(value, axis, step):
    return lax.ppermute(value, axis, [(i, i ^ step) for i in range(lax.axis_size(axis))])


def on_device(near, far, tokens, sign_in, sign_out, w_value, w_noise, w_gate, conv_taps, long_filter, w_out):
    rows, width = tokens.shape
    channels = w_gate.shape[1]
    cores = lax.axis_size("dp")
    count = near * far
    half = channels // cores
    held = half // count
    share = w_value.shape[0]
    depth = share * far
    length = count * rows
    far_at, near_at, core = lax.axis_index("far"), lax.axis_index("near"), lax.axis_index("dp")
    where = jnp.stack([core, far_at, near_at]).astype(jnp.int32)

    packed_width = depth + depth // 8 + channels // 8 + -(channels // 8) % LANES
    if share % LANES == 0 and far == 4:
        weights, *chunks = pl.pallas_call(
            functools.partial(pack_kernel, near, far),
            in_specs=[SMEM] + [HBM] * 5,
            out_specs=[VMEM] * (1 + near),
            out_shape=[jax.ShapeDtypeStruct((share, 2 * half), BF16)]
            + [jax.ShapeDtypeStruct((rows, packed_width), BF16)] * near,
            scratch_shapes=[
                pltpu.VMEM(sign_in.shape, jnp.int32),
                pltpu.VMEM(sign_out.shape[::-1], jnp.int32),
                pltpu.SemaphoreType.DMA((2,)),
                pltpu.SemaphoreType.DMA((2,)),
                pltpu.SemaphoreType.DMA((near * far,)),
            ],
            compiler_params=params(16),
            cost_estimate=cost(2 * rows * 512 * 512, 3 * MIB),
            name="pack",
        )(where, *in_hbm(tokens, sign_in, sign_out.T, w_value, w_noise))
        pieces = [weights] * far
        for turn in (2, 1):
            pieces[turn] = exchanged(weights, "far", turn)
    else:
        own = lax.dynamic_slice_in_dim(jnp.stack([w_value, w_noise]), core * half, half, axis=2)
        own = own.transpose(1, 0, 2).reshape(share, 2 * half)
        pieces = [lax.all_gather(own, "far", axis=0, tiled=True)]
        order = jnp.arange(near) ^ near_at

        def by_owner(array):
            parts = array.reshape(rows, far, near, -1).transpose(2, 0, 1, 3).reshape(near, rows, -1)
            return jnp.take(parts, order, axis=0)

        words = by_owner(sign_in)
        sent = jnp.broadcast_to(sign_out[None], (near, *sign_out.shape))
        spare = jnp.zeros((near, rows, -(channels // 8) % LANES), jnp.int32)
        signs = [words & 255, words >> 8, sent & 255, sent >> 8, spare]
        packed = [by_owner(tokens)] + [part.astype(BF16) for part in signs]
        chunks = list(jnp.concatenate(packed, axis=2))
    chunks = [chunks[0]] + [exchanged(chunks[step], "near", step) for step in range(1, near)]

    late_tokens = tokens
    if len(pieces) > 1:
        late_tokens, pieces[2], chunks[0] = lax.optimization_barrier((tokens, pieces[2], chunks[0]))
        pieces[3] = exchanged(pieces[2], "far", 1)
        pieces[3], *chunks[2:] = lax.optimization_barrier((pieces[3], *chunks[2:]))
    chunks += [exchanged(chunk, "dp", 1) for chunk in chunks]

    gate_rows = jnp.dot(late_tokens, w_gate, preferred_element_type=F32).astype(BF16)
    gate_rows, chunks[near] = lax.optimization_barrier((gate_rows, chunks[near]))
    before = lax.ppermute(
        gate_rows[rows - 2 :], ("far", "near"), [(i, i + 1) for i in range(count - 1)]
    )
    first = core * half + (far_at * near + near_at) * held
    taps = lax.dynamic_slice_in_dim(conv_taps, first, held, axis=1).T
    pieces[0], taps, before = lax.optimization_barrier((pieces[0], taps, before))

    partial = pl.pallas_call(
        functools.partial(project_kernel, near, cores, far, depth),
        in_specs=[SMEM] + [VMEM] * (1 + len(chunks) + len(pieces)),
        out_specs=VMEM,
        out_shape=jax.ShapeDtypeStruct((half, (cores * near + 1) * rows), BF16),
        compiler_params=params(40),
        cost_estimate=cost(4 * cores * near * rows * depth * half, 6 * MIB),
        name="project",
    )(where, long_filter, *chunks, *pieces)
    parts = lax.all_to_all(partial, ("far", "near"), 0, 0, tiled=True)

    tiles = length // LANES
    all_rows = tiles * SLOTS * cores * GROUP
    held_rows = max(held, GROUP)
    mixed = pl.pallas_call(
        functools.partial(mix_kernel, near, far, cores, held),
        in_specs=[VMEM] * 2,
        out_specs=VMEM,
        out_shape=jax.ShapeDtypeStruct((cores * tiles, held, LANES), BF16),
        scratch_shapes=[
            pltpu.VMEM((all_rows, GROUP * BLOCK), BF16),
            pltpu.VMEM((all_rows * (1 if tiles <= 16 else 2), LANES), F32),
            pltpu.VMEM((cores * tiles, held_rows, LANES), F32),
            pltpu.VMEM((GROUP * BLOCK, length), BF16),
        ],
        compiler_params=params(48),
        cost_estimate=cost(cores * held_rows * BLOCK * length * 256, 2 * MIB),
        name="mix",
    )(parts, taps)

    landed = lax.all_to_all(mixed, ("dp", "far", "near"), 0, 0, tiled=True).reshape(channels, rows)
    chunks = 8
    return pl.pallas_call(
        out_kernel,
        in_specs=[VMEM] * 4 + [HBM],
        out_specs=HBM,
        out_shape=jax.ShapeDtypeStruct((rows, width), BF16),
        scratch_shapes=[
            pltpu.VMEM((chunks, channels, width // chunks), BF16),
            pltpu.VMEM((chunks, rows, width // chunks), BF16),
            pltpu.SemaphoreType.DMA((chunks,)),
            pltpu.SemaphoreType.DMA((chunks,)),
        ],
        compiler_params=params(16),
        cost_estimate=cost(2 * rows * width * channels, 5 * MIB),
        name="project_out",
    )(gate_rows, before, conv_taps, landed, *in_hbm(w_out))


def solution(mesh):
    count = mesh.shape["seq"]
    near = 4 if count % 4 == 0 else 1
    far = count // near
    seq_at = mesh.axis_names.index("seq")
    shape = list(mesh.devices.shape)
    shape[seq_at : seq_at + 1] = [far, near]
    names = list(mesh.axis_names)
    names[seq_at : seq_at + 1] = ["far", "near"]
    inner = Mesh(mesh.devices.reshape(shape), tuple(names))
    by_token = P(("dp", "far", "near"), None)
    by_row = P(("far", "near"), None)
    placed = (by_token, by_token, by_token, by_row, by_row, P(), P(), by_row, P())
    return jax.shard_map(
        functools.partial(on_device, near, far),
        mesh=inner,
        in_specs=placed,
        out_specs=by_token,
        check_vma=False,
    )
```

```python
import functools

import jax
import jax.numpy as jnp
from jax import lax
from jax.experimental import pallas as pl
from jax.experimental.pallas import tpu as pltpu
from jax.sharding import Mesh, PartitionSpec as P

F32 = jnp.float32
BF16 = jnp.bfloat16
LANES = 128
GROUP = 8
BLOCK = 32
SLOTS = LANES // BLOCK
MIB = 1 << 20
VMEM = pl.BlockSpec(memory_space=pltpu.VMEM)
SMEM = pl.BlockSpec(memory_space=pltpu.SMEM)
HBM = pl.BlockSpec(memory_space=pltpu.HBM)
ANY = pl.BlockSpec(memory_space=pl.ANY)


def params(mib):
    return pltpu.CompilerParams(vmem_limit_bytes=mib * MIB)


def cost(flops, accessed):
    return pl.CostEstimate(flops=flops, bytes_accessed=accessed, transcendentals=0)


def in_hbm(*arrays):
    return [pltpu.with_memory_space_constraint(array, pltpu.HBM) for array in arrays]


def sign_bytes(packed):
    parts = jnp.concatenate([packed & 255, packed >> 8], axis=1)
    return parts.astype(F32).astype(BF16)


def one_hot(rows, columns, source_of):
    at = lax.broadcasted_iota(jnp.int32, (rows, columns), 0)
    column = lax.broadcasted_iota(jnp.int32, (1, columns), 1)
    return (at == source_of(column)).astype(F32).astype(BF16)


def pack_kernel(
    near, far, where_ref, tokens_ref, in_ref, sent_ref, value_ref, noise_ref, weight_ref, *refs
):
    outs, (in_held, sent_held, read_sems, weight_sems, token_sems) = refs[:near], refs[near:]
    core, far_at, near_at = where_ref[0], where_ref[1], where_ref[2]
    half = weight_ref.shape[1] // 2
    share = weight_ref.shape[0]
    depth = share * far
    words = in_ref.shape[1]
    per_part = words // (near * far)
    own_words = per_part * far

    copies = []
    for at, source in enumerate((value_ref, noise_ref)):
        columns = pl.ds(pl.multiple_of(core * half, half), half)
        target = weight_ref.at[:, at * half : (at + 1) * half]
        copies.append(pltpu.make_async_copy(source.at[:, columns], target, weight_sems.at[at]))
    reads = [
        pltpu.make_async_copy(in_ref, in_held, read_sems.at[0]),
        pltpu.make_async_copy(sent_ref, sent_held, read_sems.at[1]),
    ]
    for step, out in enumerate(outs):
        for turn in range(far):
            start = ((far_at ^ turn) * near + (near_at ^ step)) * share
            columns = pl.ds(pl.multiple_of(start, share), share)
            target = out.at[:, turn * share : (turn + 1) * share]
            copies.append(
                pltpu.make_async_copy(tokens_ref.at[:, columns], target, token_sems.at[step * far + turn])
            )
    for copy in reads + copies:
        copy.start()

    def word_of(column):
        step, rest = column // (2 * own_words), column % (2 * own_words)
        part, word = rest // own_words, rest % own_words
        plane = (word // per_part) ^ far_at
        return part * words + (plane * near + (step ^ near_at)) * per_part + word % per_part

    by_word = one_hot(2 * words, 2 * words, word_of)
    reads[0].wait()
    moved = jnp.dot(sign_bytes(in_held[...]), by_word, preferred_element_type=F32).astype(BF16)
    reads[1].wait()
    sent = sign_bytes(sent_held[...].astype(F32).T.astype(jnp.int32))
    spare = -sent.shape[1] % LANES
    sent = jnp.concatenate([sent, jnp.zeros((sent.shape[0], spare), BF16)], axis=1)
    width = 2 * own_words
    for step, out in enumerate(outs):
        out[:, depth : depth + width] = moved[:, step * width : (step + 1) * width]
        out[:, depth + width :] = sent
    for copy in copies:
        copy.wait()


def spread_signs(pair, byte_of, columns):
    spread = jnp.dot(pair, one_hot(pair.shape[1], columns, byte_of), preferred_element_type=F32)
    mask = 1 << (lax.broadcasted_iota(jnp.int32, (1, columns), 1) & 7)
    return jnp.where((spread.astype(jnp.int32) & mask) != 0, 1.0, -1.0)


def project_kernel(near, cores, planes, depth, where_ref, lags_ref, *refs):
    chunks, pieces, (out_ref, lags_held, sem) = refs[: near * cores], refs[near * cores : -3], refs[-3:]
    core, near_at = where_ref[0], where_ref[2]
    rows = chunks[0].shape[0]
    half = pieces[0].shape[1] // 2
    own_lags = lags_ref.at[:, pl.ds(pl.multiple_of(core * half, half), half)]
    read = pltpu.make_async_copy(own_lags, lags_held, sem)
    read.start()
    words = depth // 16
    sent_words = cores * half // 16
    sent_start = depth + 2 * words

    def in_byte(column):
        return (column >> 4) + words * ((column >> 3) & 1)

    def out_byte(column):
        return core * (half // 16) + (column >> 4) + sent_words * ((column >> 3) & 1)

    def joined(start, stop):
        return jnp.concatenate([chunk[:, start:stop] for chunk in chunks], axis=0)

    flip_in = spread_signs(joined(depth, sent_start), in_byte, depth).astype(BF16)
    flip_out = spread_signs(joined(sent_start, sent_start + 2 * sent_words), out_byte, half)
    mean_part, noise_part = 0.0, 0.0
    step = depth // len(pieces)
    for at, piece in enumerate(pieces):
        tokens = joined(at * step, (at + 1) * step)
        flipped = tokens * flip_in[:, at * step : (at + 1) * step]
        mean_part += jnp.dot(tokens, piece[:, :half], preferred_element_type=F32)
        noise_part += jnp.dot(flipped, piece[:, half:], preferred_element_type=F32)
    value = (mean_part + flip_out * noise_part).T.astype(BF16)
    for part in range(cores):
        for turn in range(near):
            at = part * near + turn
            target = ((core ^ part) * near + (near_at ^ turn)) * rows
            out_ref[:, pl.ds(pl.multiple_of(target, rows), rows)] = value[:, at * rows : (at + 1) * rows]
    read.wait()
    out_ref[:, cores * near * rows :] = lags_held[...].T.astype(BF16)


def shifted(values, steps):
    moved = pltpu.roll(values, steps, 1)
    at = lax.broadcasted_iota(jnp.int32, values.shape, 1)
    return jnp.where(at >= steps, moved, 0.0)


def lane_roll(values, steps):
    return pltpu.roll(values, steps % LANES, values.ndim - 1) if steps % LANES else values


def mix_kernel(near, far, cores, held, where_ref, taps_ref, parts_ref, out_ref, left_ref, sums_ref, done_ref, table_ref):
    tiles = out_ref.shape[0] // cores
    block_rows = cores * GROUP
    tile_rows = SLOTS * block_rows
    rows = tiles * tile_rows
    lane = lax.broadcasted_iota(jnp.int32, (1, LANES), 1)
    pair = 2 * LANES
    span = near * LANES

    def padded(lines):
        if held >= GROUP:
            return lines
        return jnp.concatenate([lines, jnp.zeros((GROUP - held, lines.shape[1]), F32)], axis=0)

    half = held * near * far
    first = where_ref[0] * half + (where_ref[1] * near + where_ref[2]) * held
    channel = lax.broadcasted_iota(jnp.int32, (held, cores * half), 1) - first
    chosen = channel == lax.broadcasted_iota(jnp.int32, (held, cores * half), 0)
    taps = [
        jnp.sum(jnp.where(chosen, taps_ref[lag : lag + 1, : cores * half], 0.0), axis=1, keepdims=True)
        for lag in range(3)
    ]
    signals = []
    for part in range(cores):
        planes = []
        for plane in range(far):
            total = 0.0
            for turn in range(near):
                start = (plane * near + turn) * held
                piece = parts_ref[start : start + held, part * span : (part + 1) * span]
                total += piece.astype(F32)
            planes.append(total)
        value = jnp.concatenate(planes, axis=1)
        signal = taps[0] * value
        for lag in range(1, 3):
            signal += taps[lag] * shifted(value, lag)
        signals.append(padded(signal))
    lags = padded(
        jnp.concatenate(
            [
                parts_ref[at * held : (at + 1) * held, cores * span :].astype(F32)
                for at in range(near * far)
            ],
            axis=1,
        )
    )

    for group in range(max(held, GROUP) // GROUP):
        own = slice(group * GROUP, (group + 1) * GROUP)
        for at in range(GROUP):
            row = lags[group * GROUP + at : group * GROUP + at + 1, :]
            repeated = jnp.broadcast_to(row, (BLOCK, row.shape[1]))
            turned = pltpu.roll(repeated, 0, 1, stride=1, stride_axis=0)
            column = lax.broadcasted_iota(jnp.int32, repeated.shape, 1)
            lag = lax.broadcasted_iota(jnp.int32, repeated.shape, 0)
            kept = jnp.where(column >= lag, turned, 0.0).astype(BF16)
            table_ref[at * BLOCK : (at + 1) * BLOCK, :] = kept

        stacked = jnp.concatenate(
            [
                signal[own, a * LANES : (a + 1) * LANES]
                for a in range(tiles)
                for signal in signals
            ],
            axis=0,
        )
        slot_of = lax.broadcasted_iota(jnp.int32, stacked.shape, 0) % SLOTS
        turned = stacked
        for slot in range(1, SLOTS):
            turned = jnp.where(slot_of == slot, lane_roll(stacked, BLOCK * slot), turned)
        spread = jnp.stack(
            [
                lane_roll(turned, -BLOCK * slot).reshape(tiles, block_rows, LANES)
                for slot in range(SLOTS)
            ],
            axis=1,
        ).reshape(rows, LANES)
        owner = lax.broadcasted_iota(jnp.int32, (rows, LANES), 0) % GROUP
        for half in range(GROUP // SLOTS):
            kept = jnp.where(owner == lane // BLOCK + half * SLOTS, spread, 0.0)
            left_ref[:, half * LANES : (half + 1) * LANES] = kept.astype(BF16)

        sums_ref[...] = jnp.zeros_like(sums_ref)
        if tiles <= 16:
            for at in range(tiles // 2):
                start = 2 * at * tile_rows
                partial = jnp.dot(
                    left_ref[: rows - start, :],
                    table_ref[:, at * pair : (at + 1) * pair],
                    preferred_element_type=F32,
                )
                sums_ref[start:rows, :] += partial[:, :LANES]
                sums_ref[start + tile_rows : rows, :] += partial[: rows - start - tile_rows, LANES:]
        else:

            def add(at, _):
                partial = jnp.dot(
                    left_ref[...],
                    table_ref[:, pl.ds(pl.multiple_of(at * pair, pair), pair)],
                    preferred_element_type=F32,
                )
                start = pl.multiple_of(2 * at * tile_rows, tile_rows)
                sums_ref[pl.ds(start, rows), :] += partial[:, :LANES]
                sums_ref[pl.ds(start + tile_rows, rows), :] += partial[:, LANES:]
                return 0

            lax.fori_loop(0, tiles // 2, add, 0)

        sums = sums_ref[:rows, :]
        landed = [0.0] * SLOTS
        for part in range(SLOTS):
            late = sums
            if part:
                ahead = jnp.zeros((part * block_rows, LANES), F32)
                late = jnp.concatenate([ahead, sums[: rows - part * block_rows]], axis=0)
            late = late.reshape(tiles, SLOTS, block_rows, LANES)
            for slot in range(SLOTS):
                moved = late[:, slot].reshape(tiles * block_rows, LANES)
                landed[slot] += lane_roll(moved, BLOCK * (slot - part))
        result = 0.0
        for slot in range(SLOTS):
            result += jnp.where(lane // BLOCK == slot, landed[slot], 0.0)
        result = result.reshape(tiles, cores, GROUP, LANES)
        for part in range(cores):
            done_ref[part * tiles : (part + 1) * tiles, own, :] = result[:, part]

    out_ref[...] = done_ref[:, :held, :].astype(BF16)


def out_kernel(
    gate_ref, before_ref, taps_ref, mixed_ref, source_ref, target_ref,
    gate_held, before_held, taps_held, mixed_held, weight_ref, held_ref, small_sems, read_sems, write_sems,
):
    chunks, channels, step = weight_ref.shape
    small = [
        pltpu.make_async_copy(source, target, small_sems.at[at])
        for at, (source, target) in enumerate(
            (
                (gate_ref, gate_held),
                (before_ref, before_held),
                (taps_ref, taps_held),
                (mixed_ref, mixed_held),
            )
        )
    ]
    reads = [
        pltpu.make_async_copy(
            source_ref.at[:, pl.ds(at * step, step)], weight_ref.at[at], read_sems.at[at]
        )
        for at in range(chunks)
    ]
    for copy in small + reads:
        copy.start()
    for copy in small:
        copy.wait()
    gate = gate_held[...].astype(F32)
    extended = jnp.concatenate([before_held[...].astype(F32), gate], axis=0)
    gate_short = taps_held[0:1, channels:] * gate
    for lag in range(1, 3):
        gate_short += taps_held[lag : lag + 1, channels:] * extended[2 - lag : 2 - lag + gate.shape[0]]
    gated = (gate_short * mixed_held[...].astype(F32).T).astype(BF16)
    writes = []
    for at in range(chunks):
        reads[at].wait()
        held_ref[at] = jnp.dot(gated, weight_ref[at], preferred_element_type=F32).astype(BF16)
        columns = target_ref.at[:, pl.ds(at * step, step)]
        writes.append(pltpu.make_async_copy(held_ref.at[at], columns, write_sems.at[at]))
        writes[-1].start()
    for write in writes:
        write.wait()


def exchanged(value, axis, step):
    return lax.ppermute(value, axis, [(i, i ^ step) for i in range(lax.axis_size(axis))])


def on_device(near, far, tokens, sign_in, sign_out, w_value, w_noise, w_gate, conv_taps, long_filter, w_out):
    rows, width = tokens.shape
    channels = w_gate.shape[1]
    cores = lax.axis_size("dp")
    count = near * far
    half = channels // cores
    held = half // count
    share = w_value.shape[0]
    depth = share * far
    length = count * rows
    far_at, near_at, core = lax.axis_index("far"), lax.axis_index("near"), lax.axis_index("dp")
    where = jnp.stack([core, far_at, near_at]).astype(jnp.int32)

    packed_width = depth + depth // 8 + channels // 8 + -(channels // 8) % LANES
    if share % LANES == 0 and far == 4:
        weights, *chunks = pl.pallas_call(
            functools.partial(pack_kernel, near, far),
            in_specs=[SMEM] + [HBM] * 5,
            out_specs=[VMEM] * (1 + near),
            out_shape=[jax.ShapeDtypeStruct((share, 2 * half), BF16)]
            + [jax.ShapeDtypeStruct((rows, packed_width), BF16)] * near,
            scratch_shapes=[
                pltpu.VMEM(sign_in.shape, jnp.int32),
                pltpu.VMEM(sign_out.shape[::-1], jnp.int32),
                pltpu.SemaphoreType.DMA((2,)),
                pltpu.SemaphoreType.DMA((2,)),
                pltpu.SemaphoreType.DMA((near * far,)),
            ],
            compiler_params=params(16),
            cost_estimate=cost(2 * rows * 512 * 512, 3 * MIB),
            name="pack",
        )(where, *in_hbm(tokens, sign_in, sign_out.T, w_value, w_noise))
        pieces = [weights] * far
        for turn in (2, 1):
            pieces[turn] = exchanged(weights, "far", turn)
    else:
        own = lax.dynamic_slice_in_dim(jnp.stack([w_value, w_noise]), core * half, half, axis=2)
        own = own.transpose(1, 0, 2).reshape(share, 2 * half)
        pieces = [lax.all_gather(own, "far", axis=0, tiled=True)]
        order = jnp.arange(near) ^ near_at

        def by_owner(array):
            parts = array.reshape(rows, far, near, -1).transpose(2, 0, 1, 3).reshape(near, rows, -1)
            return jnp.take(parts, order, axis=0)

        words = by_owner(sign_in)
        sent = jnp.broadcast_to(sign_out[None], (near, *sign_out.shape))
        spare = jnp.zeros((near, rows, -(channels // 8) % LANES), jnp.int32)
        signs = [words & 255, words >> 8, sent & 255, sent >> 8, spare]
        packed = [by_owner(tokens)] + [part.astype(BF16) for part in signs]
        chunks = list(jnp.concatenate(packed, axis=2))
    chunks = [chunks[0]] + [exchanged(chunks[step], "near", step) for step in range(1, near)]

    def last_rows(gate_rows):
        return lax.ppermute(
            gate_rows[rows - 2 :], ("far", "near"), [(i, i + 1) for i in range(count - 1)]
        )

    if len(pieces) > 1:
        pieces[1], chunks[0] = lax.optimization_barrier((pieces[1], chunks[0]))
        late_tokens, pieces[2] = lax.optimization_barrier((tokens, pieces[2]))
        pieces[3] = exchanged(pieces[2], "far", 1)
        gate_rows = jnp.dot(late_tokens, w_gate, preferred_element_type=F32).astype(BF16)
        before = last_rows(gate_rows)
        before, pieces[3], *chunks[1:] = lax.optimization_barrier((before, pieces[3], *chunks[1:]))
    else:
        gate_rows = jnp.dot(tokens, w_gate, preferred_element_type=F32).astype(BF16)
        before = last_rows(gate_rows)
    chunks += [exchanged(chunk, "dp", 1) for chunk in chunks]
    pieces[0], before = lax.optimization_barrier((pieces[0], before))

    partial = pl.pallas_call(
        functools.partial(project_kernel, near, cores, far, depth),
        in_specs=[SMEM, HBM] + [VMEM] * (len(chunks) + len(pieces)),
        out_specs=VMEM,
        out_shape=jax.ShapeDtypeStruct((half, (cores * near + 1) * rows), BF16),
        scratch_shapes=[pltpu.VMEM((rows, half), F32), pltpu.SemaphoreType.DMA],
        compiler_params=params(40),
        cost_estimate=cost(4 * cores * near * rows * depth * half, 6 * MIB),
        name="project",
    )(where, *in_hbm(long_filter), *chunks, *pieces)
    parts = lax.all_to_all(partial, ("far", "near"), 0, 0, tiled=True)

    tiles = length // LANES
    all_rows = tiles * SLOTS * cores * GROUP
    held_rows = max(held, GROUP)
    mixed = pl.pallas_call(
        functools.partial(mix_kernel, near, far, cores, held),
        in_specs=[SMEM] + [VMEM] * 2,
        out_specs=VMEM,
        out_shape=jax.ShapeDtypeStruct((cores * tiles, held, LANES), BF16),
        scratch_shapes=[
            pltpu.VMEM((all_rows, GROUP * BLOCK), BF16),
            pltpu.VMEM((all_rows * (1 if tiles <= 16 else 2), LANES), F32),
            pltpu.VMEM((cores * tiles, held_rows, LANES), F32),
            pltpu.VMEM((GROUP * BLOCK, length), BF16),
        ],
        compiler_params=params(48),
        cost_estimate=cost(cores * held_rows * BLOCK * length * 256, 2 * MIB),
        name="mix",
    )(where, conv_taps, parts)

    landed = lax.all_to_all(mixed, ("dp", "far", "near"), 0, 0, tiled=True).reshape(channels, rows)
    chunks = 8
    return pl.pallas_call(
        out_kernel,
        in_specs=[ANY] * 4 + [HBM],
        out_specs=HBM,
        out_shape=jax.ShapeDtypeStruct((rows, width), BF16),
        scratch_shapes=[
            pltpu.VMEM(gate_rows.shape, BF16),
            pltpu.VMEM(before.shape, BF16),
            pltpu.VMEM(conv_taps.shape, F32),
            pltpu.VMEM(landed.shape, BF16),
            pltpu.VMEM((chunks, channels, width // chunks), BF16),
            pltpu.VMEM((chunks, rows, width // chunks), BF16),
            pltpu.SemaphoreType.DMA((4,)),
            pltpu.SemaphoreType.DMA((chunks,)),
            pltpu.SemaphoreType.DMA((chunks,)),
        ],
        compiler_params=params(16),
        cost_estimate=cost(2 * rows * width * channels, 5 * MIB),
        name="project_out",
    )(gate_rows, before, conv_taps, landed, *in_hbm(w_out))


def solution(mesh):
    count = mesh.shape["seq"]
    near = 4 if count % 4 == 0 else 1
    far = count // near
    seq_at = mesh.axis_names.index("seq")
    shape = list(mesh.devices.shape)
    shape[seq_at : seq_at + 1] = [far, near]
    names = list(mesh.axis_names)
    names[seq_at : seq_at + 1] = ["far", "near"]
    inner = Mesh(mesh.devices.reshape(shape), tuple(names))
    by_token = P(("dp", "far", "near"), None)
    by_row = P(("far", "near"), None)
    placed = (by_token, by_token, by_token, by_row, by_row, P(), P(), by_row, P())
    return jax.shard_map(
        functools.partial(on_device, near, far),
        mesh=inner,
        in_specs=placed,
        out_specs=by_token,
        check_vma=False,
    )
```

```python
import functools

import jax
import jax.numpy as jnp
from jax import lax
from jax.experimental import pallas as pl
from jax.experimental.pallas import tpu as pltpu
from jax.sharding import Mesh, PartitionSpec as P

F32 = jnp.float32
BF16 = jnp.bfloat16
LANES = 128
GROUP = 8
BLOCK = 32
SLOTS = LANES // BLOCK
MIB = 1 << 20
VMEM = pl.BlockSpec(memory_space=pltpu.VMEM)
SMEM = pl.BlockSpec(memory_space=pltpu.SMEM)
HBM = pl.BlockSpec(memory_space=pltpu.HBM)
ANY = pl.BlockSpec(memory_space=pl.ANY)


def params(mib):
    return pltpu.CompilerParams(vmem_limit_bytes=mib * MIB)


def cost(flops, accessed):
    return pl.CostEstimate(flops=flops, bytes_accessed=accessed, transcendentals=0)


def in_hbm(*arrays):
    return [pltpu.with_memory_space_constraint(array, pltpu.HBM) for array in arrays]


def sign_bytes(packed):
    parts = jnp.concatenate([packed & 255, packed >> 8], axis=1)
    return parts.astype(F32).astype(BF16)


def one_hot(rows, columns, source_of):
    at = lax.broadcasted_iota(jnp.int32, (rows, columns), 0)
    column = lax.broadcasted_iota(jnp.int32, (1, columns), 1)
    return (at == source_of(column)).astype(F32).astype(BF16)


def pack_kernel(
    near, far, tokens_ref, in_ref, sent_ref, value_ref, noise_ref, weight_ref, *refs
):
    outs, (in_held, sent_held, read_sems, weight_sems, token_sems) = refs[:near], refs[near:]
    core, far_at, near_at = lax.axis_index("dp"), lax.axis_index("far"), lax.axis_index("near")
    half = weight_ref.shape[1] // 2
    share = weight_ref.shape[0]
    depth = share * far
    words = in_ref.shape[1]
    per_part = words // (near * far)
    own_words = per_part * far

    copies = []
    for at, source in enumerate((value_ref, noise_ref)):
        columns = pl.ds(pl.multiple_of(core * half, half), half)
        target = weight_ref.at[:, at * half : (at + 1) * half]
        copies.append(pltpu.make_async_copy(source.at[:, columns], target, weight_sems.at[at]))
    reads = [
        pltpu.make_async_copy(in_ref, in_held, read_sems.at[0]),
        pltpu.make_async_copy(sent_ref, sent_held, read_sems.at[1]),
    ]
    for step, out in enumerate(outs):
        for turn in range(far):
            start = ((far_at ^ turn) * near + (near_at ^ step)) * share
            columns = pl.ds(pl.multiple_of(start, share), share)
            target = out.at[:, turn * share : (turn + 1) * share]
            copies.append(
                pltpu.make_async_copy(tokens_ref.at[:, columns], target, token_sems.at[step * far + turn])
            )
    for copy in reads + copies:
        copy.start()

    def word_of(column):
        step, rest = column // (2 * own_words), column % (2 * own_words)
        part, word = rest // own_words, rest % own_words
        plane = (word // per_part) ^ far_at
        return part * words + (plane * near + (step ^ near_at)) * per_part + word % per_part

    by_word = one_hot(2 * words, 2 * words, word_of)
    reads[0].wait()
    moved = jnp.dot(sign_bytes(in_held[...]), by_word, preferred_element_type=F32).astype(BF16)
    reads[1].wait()
    sent = sign_bytes(sent_held[...].astype(F32).T.astype(jnp.int32))
    spare = -sent.shape[1] % LANES
    sent = jnp.concatenate([sent, jnp.zeros((sent.shape[0], spare), BF16)], axis=1)
    width = 2 * own_words
    for step, out in enumerate(outs):
        out[:, depth : depth + width] = moved[:, step * width : (step + 1) * width]
        out[:, depth + width :] = sent
    for copy in copies:
        copy.wait()


def spread_signs(pair, byte_of, columns):
    spread = jnp.dot(pair, one_hot(pair.shape[1], columns, byte_of), preferred_element_type=F32)
    mask = 1 << (lax.broadcasted_iota(jnp.int32, (1, columns), 1) & 7)
    return jnp.where((spread.astype(jnp.int32) & mask) != 0, 1.0, -1.0)


def project_kernel(near, cores, depth, lags_ref, *refs):
    chunks, pieces, (out_ref, lags_held, sem) = refs[: near * cores], refs[near * cores : -3], refs[-3:]
    core, near_at = lax.axis_index("dp"), lax.axis_index("near")
    rows = chunks[0].shape[0]
    half = pieces[0].shape[1] // 2
    own_lags = lags_ref.at[:, pl.ds(pl.multiple_of(core * half, half), half)]
    read = pltpu.make_async_copy(own_lags, lags_held, sem)
    read.start()
    words = depth // 16
    sent_words = cores * half // 16
    sent_start = depth + 2 * words

    def in_byte(column):
        return (column >> 4) + words * ((column >> 3) & 1)

    def out_byte(column):
        return core * (half // 16) + (column >> 4) + sent_words * ((column >> 3) & 1)

    def joined(start, stop):
        return jnp.concatenate([chunk[:, start:stop] for chunk in chunks], axis=0)

    flip_in = spread_signs(joined(depth, sent_start), in_byte, depth).astype(BF16)
    flip_out = spread_signs(joined(sent_start, sent_start + 2 * sent_words), out_byte, half)
    mean_part, noise_part = 0.0, 0.0
    step = depth // len(pieces)
    for at, piece in enumerate(pieces):
        tokens = joined(at * step, (at + 1) * step)
        flipped = tokens * flip_in[:, at * step : (at + 1) * step]
        mean_part += jnp.dot(tokens, piece[:, :half], preferred_element_type=F32)
        noise_part += jnp.dot(flipped, piece[:, half:], preferred_element_type=F32)
    value = (mean_part + flip_out * noise_part).T.astype(BF16)
    for part in range(cores):
        for turn in range(near):
            at = part * near + turn
            target = ((core ^ part) * near + (near_at ^ turn)) * rows
            out_ref[:, pl.ds(pl.multiple_of(target, rows), rows)] = value[:, at * rows : (at + 1) * rows]
    read.wait()
    out_ref[:, cores * near * rows :] = lags_held[...].T.astype(BF16)


def shifted(values, steps):
    moved = pltpu.roll(values, steps, 1)
    at = lax.broadcasted_iota(jnp.int32, values.shape, 1)
    return jnp.where(at >= steps, moved, 0.0)


def lane_roll(values, steps):
    return pltpu.roll(values, steps % LANES, values.ndim - 1) if steps % LANES else values


def mix_kernel(near, far, cores, held, taps_ref, parts_ref, out_ref, left_ref, sums_ref, done_ref, table_ref):
    tiles = out_ref.shape[0] // cores
    block_rows = cores * GROUP
    tile_rows = SLOTS * block_rows
    rows = tiles * tile_rows
    lane = lax.broadcasted_iota(jnp.int32, (1, LANES), 1)
    pair = 2 * LANES
    span = near * LANES

    def padded(lines):
        if held >= GROUP:
            return lines
        return jnp.concatenate([lines, jnp.zeros((GROUP - held, lines.shape[1]), F32)], axis=0)

    half = held * near * far
    position = lax.axis_index("far") * near + lax.axis_index("near")
    first = lax.axis_index("dp") * half + position * held
    channel = lax.broadcasted_iota(jnp.int32, (held, cores * half), 1) - first
    chosen = channel == lax.broadcasted_iota(jnp.int32, (held, cores * half), 0)
    taps = [
        jnp.sum(jnp.where(chosen, taps_ref[lag : lag + 1, : cores * half], 0.0), axis=1, keepdims=True)
        for lag in range(3)
    ]
    signals = []
    for part in range(cores):
        planes = []
        for plane in range(far):
            total = 0.0
            for turn in range(near):
                start = (plane * near + turn) * held
                piece = parts_ref[start : start + held, part * span : (part + 1) * span]
                total += piece.astype(F32)
            planes.append(total)
        value = jnp.concatenate(planes, axis=1)
        signal = taps[0] * value
        for lag in range(1, 3):
            signal += taps[lag] * shifted(value, lag)
        signals.append(padded(signal))
    lags = padded(
        jnp.concatenate(
            [
                parts_ref[at * held : (at + 1) * held, cores * span :].astype(F32)
                for at in range(near * far)
            ],
            axis=1,
        )
    )

    for group in range(max(held, GROUP) // GROUP):
        own = slice(group * GROUP, (group + 1) * GROUP)
        for at in range(GROUP):
            row = lags[group * GROUP + at : group * GROUP + at + 1, :]
            repeated = jnp.broadcast_to(row, (BLOCK, row.shape[1]))
            turned = pltpu.roll(repeated, 0, 1, stride=1, stride_axis=0)
            column = lax.broadcasted_iota(jnp.int32, repeated.shape, 1)
            lag = lax.broadcasted_iota(jnp.int32, repeated.shape, 0)
            kept = jnp.where(column >= lag, turned, 0.0).astype(BF16)
            table_ref[at * BLOCK : (at + 1) * BLOCK, :] = kept

        stacked = jnp.concatenate(
            [
                signal[own, a * LANES : (a + 1) * LANES]
                for a in range(tiles)
                for signal in signals
            ],
            axis=0,
        )
        slot_of = lax.broadcasted_iota(jnp.int32, stacked.shape, 0) % SLOTS
        turned = stacked
        for slot in range(1, SLOTS):
            turned = jnp.where(slot_of == slot, lane_roll(stacked, BLOCK * slot), turned)
        spread = jnp.stack(
            [
                lane_roll(turned, -BLOCK * slot).reshape(tiles, block_rows, LANES)
                for slot in range(SLOTS)
            ],
            axis=1,
        ).reshape(rows, LANES)
        owner = lax.broadcasted_iota(jnp.int32, (rows, LANES), 0) % GROUP
        for half in range(GROUP // SLOTS):
            kept = jnp.where(owner == lane // BLOCK + half * SLOTS, spread, 0.0)
            left_ref[:, half * LANES : (half + 1) * LANES] = kept.astype(BF16)

        sums_ref[...] = jnp.zeros_like(sums_ref)
        if tiles <= 16:
            for at in range(tiles // 2):
                start = 2 * at * tile_rows
                partial = jnp.dot(
                    left_ref[: rows - start, :],
                    table_ref[:, at * pair : (at + 1) * pair],
                    preferred_element_type=F32,
                )
                sums_ref[start:rows, :] += partial[:, :LANES]
                sums_ref[start + tile_rows : rows, :] += partial[: rows - start - tile_rows, LANES:]
        else:

            def add(at, _):
                partial = jnp.dot(
                    left_ref[...],
                    table_ref[:, pl.ds(pl.multiple_of(at * pair, pair), pair)],
                    preferred_element_type=F32,
                )
                start = pl.multiple_of(2 * at * tile_rows, tile_rows)
                sums_ref[pl.ds(start, rows), :] += partial[:, :LANES]
                sums_ref[pl.ds(start + tile_rows, rows), :] += partial[:, LANES:]
                return 0

            lax.fori_loop(0, tiles // 2, add, 0)

        sums = sums_ref[:rows, :]
        landed = [0.0] * SLOTS
        for part in range(SLOTS):
            late = sums
            if part:
                ahead = jnp.zeros((part * block_rows, LANES), F32)
                late = jnp.concatenate([ahead, sums[: rows - part * block_rows]], axis=0)
            late = late.reshape(tiles, SLOTS, block_rows, LANES)
            for slot in range(SLOTS):
                moved = late[:, slot].reshape(tiles * block_rows, LANES)
                landed[slot] += lane_roll(moved, BLOCK * (slot - part))
        result = 0.0
        for slot in range(SLOTS):
            result += jnp.where(lane // BLOCK == slot, landed[slot], 0.0)
        result = result.reshape(tiles, cores, GROUP, LANES)
        for part in range(cores):
            done_ref[part * tiles : (part + 1) * tiles, own, :] = result[:, part]

    out_ref[...] = done_ref[:, :held, :].astype(BF16)


def out_kernel(
    gate_ref, before_ref, taps_ref, mixed_ref, source_ref, target_ref,
    gate_held, before_held, taps_held, mixed_held, weight_ref, held_ref, small_sems, read_sems, write_sems,
):
    chunks, channels, step = weight_ref.shape
    small = [
        pltpu.make_async_copy(source, target, small_sems.at[at])
        for at, (source, target) in enumerate(
            (
                (gate_ref, gate_held),
                (before_ref, before_held),
                (taps_ref, taps_held),
                (mixed_ref, mixed_held),
            )
        )
    ]
    reads = [
        pltpu.make_async_copy(
            source_ref.at[:, pl.ds(at * step, step)], weight_ref.at[at], read_sems.at[at]
        )
        for at in range(chunks)
    ]
    for copy in small + reads:
        copy.start()
    for copy in small:
        copy.wait()
    gate = gate_held[...].astype(F32)
    extended = jnp.concatenate([before_held[...].astype(F32), gate], axis=0)
    gate_short = taps_held[0:1, channels:] * gate
    for lag in range(1, 3):
        gate_short += taps_held[lag : lag + 1, channels:] * extended[2 - lag : 2 - lag + gate.shape[0]]
    gated = (gate_short * mixed_held[...].astype(F32).T).astype(BF16)
    writes = []
    for at in range(chunks):
        reads[at].wait()
        held_ref[at] = jnp.dot(gated, weight_ref[at], preferred_element_type=F32).astype(BF16)
        columns = target_ref.at[:, pl.ds(at * step, step)]
        writes.append(pltpu.make_async_copy(held_ref.at[at], columns, write_sems.at[at]))
        writes[-1].start()
    for write in writes:
        write.wait()


def exchanged(value, axis, step):
    return lax.ppermute(value, axis, [(i, i ^ step) for i in range(lax.axis_size(axis))])


def on_device(near, far, tokens, sign_in, sign_out, w_value, w_noise, w_gate, conv_taps, long_filter, w_out):
    rows, width = tokens.shape
    channels = w_gate.shape[1]
    cores = lax.axis_size("dp")
    count = near * far
    half = channels // cores
    held = half // count
    share = w_value.shape[0]
    depth = share * far
    length = count * rows
    near_at, core = lax.axis_index("near"), lax.axis_index("dp")

    packed_width = depth + depth // 8 + channels // 8 + -(channels // 8) % LANES
    if share % LANES == 0 and far == 4:
        weights, *chunks = pl.pallas_call(
            functools.partial(pack_kernel, near, far),
            in_specs=[HBM] * 5,
            out_specs=[VMEM] * (1 + near),
            out_shape=[jax.ShapeDtypeStruct((share, 2 * half), BF16)]
            + [jax.ShapeDtypeStruct((rows, packed_width), BF16)] * near,
            scratch_shapes=[
                pltpu.VMEM(sign_in.shape, jnp.int32),
                pltpu.VMEM(sign_out.shape[::-1], jnp.int32),
                pltpu.SemaphoreType.DMA((2,)),
                pltpu.SemaphoreType.DMA((2,)),
                pltpu.SemaphoreType.DMA((near * far,)),
            ],
            compiler_params=params(16),
            cost_estimate=cost(2 * rows * 512 * 512, 3 * MIB),
            name="pack",
        )(*in_hbm(tokens, sign_in, sign_out.T, w_value, w_noise))
        pieces = [weights] * far
        for turn in (2, 1):
            pieces[turn] = exchanged(weights, "far", turn)
    else:
        own = lax.dynamic_slice_in_dim(jnp.stack([w_value, w_noise]), core * half, half, axis=2)
        own = own.transpose(1, 0, 2).reshape(share, 2 * half)
        pieces = [lax.all_gather(own, "far", axis=0, tiled=True)]
        order = jnp.arange(near) ^ near_at

        def by_owner(array):
            parts = array.reshape(rows, far, near, -1).transpose(2, 0, 1, 3).reshape(near, rows, -1)
            return jnp.take(parts, order, axis=0)

        words = by_owner(sign_in)
        sent = jnp.broadcast_to(sign_out[None], (near, *sign_out.shape))
        spare = jnp.zeros((near, rows, -(channels // 8) % LANES), jnp.int32)
        signs = [words & 255, words >> 8, sent & 255, sent >> 8, spare]
        packed = [by_owner(tokens)] + [part.astype(BF16) for part in signs]
        chunks = list(jnp.concatenate(packed, axis=2))
    chunks = [chunks[0]] + [exchanged(chunks[step], "near", step) for step in range(1, near)]

    late_tokens = tokens
    if len(pieces) > 1:
        pieces[1], chunks[0] = lax.optimization_barrier((pieces[1], chunks[0]))
        late_tokens, pieces[2] = lax.optimization_barrier((tokens, pieces[2]))
        pieces[3] = exchanged(pieces[2], "far", 1)
    gate_rows = jnp.dot(late_tokens, w_gate, preferred_element_type=F32).astype(BF16)
    gate_rows, pieces[-1], *chunks[1:] = lax.optimization_barrier((gate_rows, pieces[-1], *chunks[1:]))
    chunks += [exchanged(chunk, "dp", 1) for chunk in chunks]

    partial = pl.pallas_call(
        functools.partial(project_kernel, near, cores, depth),
        in_specs=[HBM] + [VMEM] * (len(chunks) + len(pieces)),
        out_specs=VMEM,
        out_shape=jax.ShapeDtypeStruct((half, (cores * near + 1) * rows), BF16),
        scratch_shapes=[pltpu.VMEM((rows, half), F32), pltpu.SemaphoreType.DMA],
        compiler_params=params(40),
        cost_estimate=cost(4 * cores * near * rows * depth * half, 6 * MIB),
        name="project",
    )(*in_hbm(long_filter), *chunks, *pieces)
    parts = lax.all_to_all(partial, ("far", "near"), 0, 0, tiled=True)

    tiles = length // LANES
    all_rows = tiles * SLOTS * cores * GROUP
    held_rows = max(held, GROUP)
    mixed = pl.pallas_call(
        functools.partial(mix_kernel, near, far, cores, held),
        in_specs=[VMEM] * 2,
        out_specs=VMEM,
        out_shape=jax.ShapeDtypeStruct((cores * tiles, held, LANES), BF16),
        scratch_shapes=[
            pltpu.VMEM((all_rows, GROUP * BLOCK), BF16),
            pltpu.VMEM((all_rows * (1 if tiles <= 16 else 2), LANES), F32),
            pltpu.VMEM((cores * tiles, held_rows, LANES), F32),
            pltpu.VMEM((GROUP * BLOCK, length), BF16),
        ],
        compiler_params=params(48),
        cost_estimate=cost(cores * held_rows * BLOCK * length * 256, 2 * MIB),
        name="mix",
    )(conv_taps, parts)

    last_rows, _ = lax.optimization_barrier((gate_rows[rows - 2 :], mixed))
    before = lax.ppermute(last_rows, ("far", "near"), [(i, i + 1) for i in range(count - 1)])
    landed = lax.all_to_all(mixed, ("dp", "far", "near"), 0, 0, tiled=True).reshape(channels, rows)
    chunks = 8
    return pl.pallas_call(
        out_kernel,
        in_specs=[ANY] * 4 + [HBM],
        out_specs=HBM,
        out_shape=jax.ShapeDtypeStruct((rows, width), BF16),
        scratch_shapes=[
            pltpu.VMEM(gate_rows.shape, BF16),
            pltpu.VMEM(before.shape, BF16),
            pltpu.VMEM(conv_taps.shape, F32),
            pltpu.VMEM(landed.shape, BF16),
            pltpu.VMEM((chunks, channels, width // chunks), BF16),
            pltpu.VMEM((chunks, rows, width // chunks), BF16),
            pltpu.SemaphoreType.DMA((4,)),
            pltpu.SemaphoreType.DMA((chunks,)),
            pltpu.SemaphoreType.DMA((chunks,)),
        ],
        compiler_params=params(16),
        cost_estimate=cost(2 * rows * width * channels, 5 * MIB),
        name="project_out",
    )(gate_rows, before, conv_taps, landed, *in_hbm(w_out))


def solution(mesh):
    count = mesh.shape["seq"]
    near = 4 if count % 4 == 0 else 1
    far = count // near
    seq_at = mesh.axis_names.index("seq")
    shape = list(mesh.devices.shape)
    shape[seq_at : seq_at + 1] = [far, near]
    names = list(mesh.axis_names)
    names[seq_at : seq_at + 1] = ["far", "near"]
    inner = Mesh(mesh.devices.reshape(shape), tuple(names))
    by_token = P(("dp", "far", "near"), None)
    by_row = P(("far", "near"), None)
    placed = (by_token, by_token, by_token, by_row, by_row, P(), P(), by_row, P())
    return jax.shard_map(
        functools.partial(on_device, near, far),
        mesh=inner,
        in_specs=placed,
        out_specs=by_token,
        check_vma=False,
    )
```

```python
import functools

import jax
import jax.numpy as jnp
from jax import lax
from jax.experimental import pallas as pl
from jax.experimental.pallas import tpu as pltpu
from jax.sharding import Mesh, PartitionSpec as P

F32 = jnp.float32
BF16 = jnp.bfloat16
LANES = 128
GROUP = 8
BLOCK = 32
SLOTS = LANES // BLOCK
MIB = 1 << 20
VMEM = pl.BlockSpec(memory_space=pltpu.VMEM)
SMEM = pl.BlockSpec(memory_space=pltpu.SMEM)
HBM = pl.BlockSpec(memory_space=pltpu.HBM)
ANY = pl.BlockSpec(memory_space=pl.ANY)


def params(mib):
    return pltpu.CompilerParams(vmem_limit_bytes=mib * MIB)


def cost(flops, accessed):
    return pl.CostEstimate(flops=flops, bytes_accessed=accessed, transcendentals=0)


def in_hbm(*arrays):
    return [pltpu.with_memory_space_constraint(array, pltpu.HBM) for array in arrays]


def sign_bytes(packed):
    parts = jnp.concatenate([packed & 255, packed >> 8], axis=1)
    return parts.astype(F32).astype(BF16)


def one_hot(rows, columns, source_of):
    at = lax.broadcasted_iota(jnp.int32, (rows, columns), 0)
    column = lax.broadcasted_iota(jnp.int32, (1, columns), 1)
    return (at == source_of(column)).astype(F32).astype(BF16)


def pack_kernel(
    near, far, tokens_ref, in_ref, sent_ref, value_ref, noise_ref, weight_ref, *refs
):
    outs, (in_held, sent_held, read_sems, weight_sems, token_sems) = refs[:near], refs[near:]
    core, far_at, near_at = lax.axis_index("dp"), lax.axis_index("far"), lax.axis_index("near")
    half = weight_ref.shape[1] // 2
    share = weight_ref.shape[0]
    depth = share * far
    words = in_ref.shape[1]
    per_part = words // (near * far)
    own_words = per_part * far

    copies = []
    for at, source in enumerate((value_ref, noise_ref)):
        columns = pl.ds(pl.multiple_of(core * half, half), half)
        target = weight_ref.at[:, at * half : (at + 1) * half]
        copies.append(pltpu.make_async_copy(source.at[:, columns], target, weight_sems.at[at]))
    reads = [
        pltpu.make_async_copy(in_ref, in_held, read_sems.at[0]),
        pltpu.make_async_copy(sent_ref, sent_held, read_sems.at[1]),
    ]
    for step, out in enumerate(outs):
        for turn in range(far):
            start = ((far_at ^ turn) * near + (near_at ^ step)) * share
            columns = pl.ds(pl.multiple_of(start, share), share)
            target = out.at[:, turn * share : (turn + 1) * share]
            copies.append(
                pltpu.make_async_copy(tokens_ref.at[:, columns], target, token_sems.at[step * far + turn])
            )
    for copy in reads + copies:
        copy.start()

    def word_of(column):
        step, rest = column // (2 * own_words), column % (2 * own_words)
        part, word = rest // own_words, rest % own_words
        plane = (word // per_part) ^ far_at
        return part * words + (plane * near + (step ^ near_at)) * per_part + word % per_part

    by_word = one_hot(2 * words, 2 * words, word_of)
    reads[0].wait()
    moved = jnp.dot(sign_bytes(in_held[...]), by_word, preferred_element_type=F32).astype(BF16)
    reads[1].wait()
    sent = sign_bytes(sent_held[...].astype(F32).T.astype(jnp.int32))
    spare = -sent.shape[1] % LANES
    sent = jnp.concatenate([sent, jnp.zeros((sent.shape[0], spare), BF16)], axis=1)
    width = 2 * own_words
    for step, out in enumerate(outs):
        out[:, depth : depth + width] = moved[:, step * width : (step + 1) * width]
        out[:, depth + width :] = sent
    for copy in copies:
        copy.wait()


def spread_signs(pair, byte_of, columns):
    spread = jnp.dot(pair, one_hot(pair.shape[1], columns, byte_of), preferred_element_type=F32)
    mask = 1 << (lax.broadcasted_iota(jnp.int32, (1, columns), 1) & 7)
    return jnp.where((spread.astype(jnp.int32) & mask) != 0, 1.0, -1.0)


def spaced(lines, held):
    if held >= GROUP:
        return lines
    spare = jnp.zeros((GROUP - held, lines.shape[1]), F32)
    split = [lines[at : at + held] for at in range(0, lines.shape[0], held)]
    return jnp.concatenate([part for own in split for part in (own, spare)], axis=0)


def project_kernel(near, far, cores, depth, lags_ref, *refs):
    outs, (whole_ref, lags_held, sem) = refs[-3 - near : -3], refs[-3:]
    chunks, pieces = refs[: near * cores], refs[near * cores : -3 - near]
    core, near_at = lax.axis_index("dp"), lax.axis_index("near")
    rows = chunks[0].shape[0]
    half = pieces[0].shape[1] // 2
    own_lags = lags_ref.at[:, pl.ds(pl.multiple_of(core * half, half), half)]
    read = pltpu.make_async_copy(own_lags, lags_held, sem)
    read.start()
    words = depth // 16
    sent_words = cores * half // 16
    sent_start = depth + 2 * words

    def in_byte(column):
        return (column >> 4) + words * ((column >> 3) & 1)

    def out_byte(column):
        return core * (half // 16) + (column >> 4) + sent_words * ((column >> 3) & 1)

    def joined(start, stop):
        return jnp.concatenate([chunk[:, start:stop] for chunk in chunks], axis=0)

    flip_in = spread_signs(joined(depth, sent_start), in_byte, depth).astype(BF16)
    flip_out = spread_signs(joined(sent_start, sent_start + 2 * sent_words), out_byte, half)
    mean_part, noise_part = 0.0, 0.0
    step = depth // len(pieces)
    for at, piece in enumerate(pieces):
        tokens = joined(at * step, (at + 1) * step)
        flipped = tokens * flip_in[:, at * step : (at + 1) * step]
        mean_part += jnp.dot(tokens, piece[:, :half], preferred_element_type=F32)
        noise_part += jnp.dot(flipped, piece[:, half:], preferred_element_type=F32)
    held = half // (near * far)
    stride = max(held, GROUP)
    value = spaced((mean_part + flip_out * noise_part).T, held)
    for part in range(cores):
        for turn in range(near):
            at = part * near + turn
            target = ((core ^ part) * near + (near_at ^ turn)) * rows
            whole_ref[:, pl.ds(pl.multiple_of(target, rows), rows)] = value[:, at * rows : (at + 1) * rows]
    read.wait()
    whole_ref[:, cores * near * rows :] = spaced(lags_held[...].T, held)
    for turn, out in enumerate(outs):
        for plane in range(far):
            at = pl.multiple_of((plane * near + (near_at ^ turn)) * stride, stride)
            out[plane * held : (plane + 1) * held, :] = whole_ref[pl.ds(at, held), :].astype(BF16)


def sum_kernel(near, far, rows, *refs):
    parts, outs, whole_ref = refs[:near], refs[near : near + far], refs[-1]
    far_at, near_at = lax.axis_index("far"), lax.axis_index("near")
    held = outs[0].shape[0]
    stride = max(held, GROUP)
    span = parts[0].shape[1] - rows
    total = 0.0
    for turn, part in enumerate(parts):
        total += part[:, :span].astype(F32)
        at = pl.multiple_of(span + (near_at ^ turn) * rows, rows)
        whole_ref[:, pl.ds(at, rows)] = spaced(part[:, span:].astype(F32), held)
    whole_ref[:, :span] = spaced(total, held)
    for turn, out in enumerate(outs):
        at = pl.multiple_of((far_at ^ turn) * stride, stride)
        out[...] = whole_ref[pl.ds(at, held), :].astype(BF16)


def shifted(values, steps):
    moved = pltpu.roll(values, steps, 1)
    at = lax.broadcasted_iota(jnp.int32, values.shape, 1)
    return jnp.where(at >= steps, moved, 0.0)


def lane_roll(values, steps):
    return pltpu.roll(values, steps % LANES, values.ndim - 1) if steps % LANES else values


def mix_kernel(near, far, cores, held, taps_ref, *refs):
    parts, (out_ref, left_ref, sums_ref, done_ref, table_ref, lines_ref) = refs[:-6], refs[-6:]
    tiles = out_ref.shape[0] // cores
    block_rows = cores * GROUP
    tile_rows = SLOTS * block_rows
    rows = tiles * tile_rows
    lane = lax.broadcasted_iota(jnp.int32, (1, LANES), 1)
    pair = 2 * LANES
    span = near * LANES

    def padded(lines):
        if held >= GROUP:
            return lines
        return jnp.concatenate([lines, jnp.zeros((GROUP - held, lines.shape[1]), F32)], axis=0)

    for turn, part in enumerate(parts):
        for plane in range(far // len(parts)):
            own = slice(plane * held, (plane + 1) * held)
            target = pl.multiple_of(((lax.axis_index("far") if len(parts) > 1 else plane) ^ turn) * span, span)
            for line in range(cores + 1):
                piece = part[own, line * span : (line + 1) * span]
                lines_ref[line, :, pl.ds(target, span)] = piece.astype(F32)
    half = held * near * far
    position = lax.axis_index("far") * near + lax.axis_index("near")
    first = lax.axis_index("dp") * half + position * held
    channel = lax.broadcasted_iota(jnp.int32, (held, cores * half), 1) - first
    chosen = channel == lax.broadcasted_iota(jnp.int32, (held, cores * half), 0)
    taps = [
        jnp.sum(jnp.where(chosen, taps_ref[lag : lag + 1, : cores * half], 0.0), axis=1, keepdims=True)
        for lag in range(3)
    ]
    signals = []
    for part in range(cores):
        value = lines_ref[part]
        signal = taps[0] * value
        for lag in range(1, 3):
            signal += taps[lag] * shifted(value, lag)
        signals.append(padded(signal))
    lags = padded(lines_ref[cores])

    for group in range(max(held, GROUP) // GROUP):
        own = slice(group * GROUP, (group + 1) * GROUP)
        for at in range(GROUP):
            row = lags[group * GROUP + at : group * GROUP + at + 1, :]
            repeated = jnp.broadcast_to(row, (BLOCK, row.shape[1]))
            turned = pltpu.roll(repeated, 0, 1, stride=1, stride_axis=0)
            column = lax.broadcasted_iota(jnp.int32, repeated.shape, 1)
            lag = lax.broadcasted_iota(jnp.int32, repeated.shape, 0)
            kept = jnp.where(column >= lag, turned, 0.0).astype(BF16)
            table_ref[at * BLOCK : (at + 1) * BLOCK, :] = kept

        stacked = jnp.concatenate(
            [
                signal[own, a * LANES : (a + 1) * LANES]
                for a in range(tiles)
                for signal in signals
            ],
            axis=0,
        )
        slot_of = lax.broadcasted_iota(jnp.int32, stacked.shape, 0) % SLOTS
        turned = stacked
        for slot in range(1, SLOTS):
            turned = jnp.where(slot_of == slot, lane_roll(stacked, BLOCK * slot), turned)
        spread = jnp.stack(
            [
                lane_roll(turned, -BLOCK * slot).reshape(tiles, block_rows, LANES)
                for slot in range(SLOTS)
            ],
            axis=1,
        ).reshape(rows, LANES)
        owner = lax.broadcasted_iota(jnp.int32, (rows, LANES), 0) % GROUP
        for half in range(GROUP // SLOTS):
            kept = jnp.where(owner == lane // BLOCK + half * SLOTS, spread, 0.0)
            left_ref[:, half * LANES : (half + 1) * LANES] = kept.astype(BF16)

        sums_ref[...] = jnp.zeros_like(sums_ref)
        if tiles <= 16:
            for at in range(tiles // 2):
                start = 2 * at * tile_rows
                partial = jnp.dot(
                    left_ref[: rows - start, :],
                    table_ref[:, at * pair : (at + 1) * pair],
                    preferred_element_type=F32,
                )
                sums_ref[start:rows, :] += partial[:, :LANES]
                sums_ref[start + tile_rows : rows, :] += partial[: rows - start - tile_rows, LANES:]
        else:

            def add(at, _):
                partial = jnp.dot(
                    left_ref[...],
                    table_ref[:, pl.ds(pl.multiple_of(at * pair, pair), pair)],
                    preferred_element_type=F32,
                )
                start = pl.multiple_of(2 * at * tile_rows, tile_rows)
                sums_ref[pl.ds(start, rows), :] += partial[:, :LANES]
                sums_ref[pl.ds(start + tile_rows, rows), :] += partial[:, LANES:]
                return 0

            lax.fori_loop(0, tiles // 2, add, 0)

        sums = sums_ref[:rows, :]
        landed = [0.0] * SLOTS
        for part in range(SLOTS):
            late = sums
            if part:
                ahead = jnp.zeros((part * block_rows, LANES), F32)
                late = jnp.concatenate([ahead, sums[: rows - part * block_rows]], axis=0)
            late = late.reshape(tiles, SLOTS, block_rows, LANES)
            for slot in range(SLOTS):
                moved = late[:, slot].reshape(tiles * block_rows, LANES)
                landed[slot] += lane_roll(moved, BLOCK * (slot - part))
        result = 0.0
        for slot in range(SLOTS):
            result += jnp.where(lane // BLOCK == slot, landed[slot], 0.0)
        result = result.reshape(tiles, cores, GROUP, LANES)
        for part in range(cores):
            done_ref[part * tiles : (part + 1) * tiles, own, :] = result[:, part]

    out_ref[...] = done_ref[:, :held, :].astype(BF16)


def out_kernel(
    gate_ref, before_ref, taps_ref, mixed_ref, source_ref, target_ref,
    gate_held, before_held, taps_held, mixed_held, weight_ref, held_ref, small_sems, read_sems, write_sems,
):
    chunks, channels, step = weight_ref.shape
    small = [
        pltpu.make_async_copy(source, target, small_sems.at[at])
        for at, (source, target) in enumerate(
            (
                (gate_ref, gate_held),
                (before_ref, before_held),
                (taps_ref, taps_held),
                (mixed_ref, mixed_held),
            )
        )
    ]
    reads = [
        pltpu.make_async_copy(
            source_ref.at[:, pl.ds(at * step, step)], weight_ref.at[at], read_sems.at[at]
        )
        for at in range(chunks)
    ]
    for copy in small + reads:
        copy.start()
    for copy in small:
        copy.wait()
    gate = gate_held[...].astype(F32)
    extended = jnp.concatenate([before_held[...].astype(F32), gate], axis=0)
    gate_short = taps_held[0:1, channels:] * gate
    for lag in range(1, 3):
        gate_short += taps_held[lag : lag + 1, channels:] * extended[2 - lag : 2 - lag + gate.shape[0]]
    gated = (gate_short * mixed_held[...].astype(F32).T).astype(BF16)
    writes = []
    for at in range(chunks):
        reads[at].wait()
        held_ref[at] = jnp.dot(gated, weight_ref[at], preferred_element_type=F32).astype(BF16)
        columns = target_ref.at[:, pl.ds(at * step, step)]
        writes.append(pltpu.make_async_copy(held_ref.at[at], columns, write_sems.at[at]))
        writes[-1].start()
    for write in writes:
        write.wait()


def exchanged(value, axis, step):
    return lax.ppermute(value, axis, [(i, i ^ step) for i in range(lax.axis_size(axis))])


def on_device(near, far, tokens, sign_in, sign_out, w_value, w_noise, w_gate, conv_taps, long_filter, w_out):
    rows, width = tokens.shape
    channels = w_gate.shape[1]
    cores = lax.axis_size("dp")
    count = near * far
    half = channels // cores
    held = half // count
    share = w_value.shape[0]
    depth = share * far
    length = count * rows
    near_at, core = lax.axis_index("near"), lax.axis_index("dp")

    packed_width = depth + depth // 8 + channels // 8 + -(channels // 8) % LANES
    if share % LANES == 0 and far == 4:
        weights, *chunks = pl.pallas_call(
            functools.partial(pack_kernel, near, far),
            in_specs=[HBM] * 5,
            out_specs=[VMEM] * (1 + near),
            out_shape=[jax.ShapeDtypeStruct((share, 2 * half), BF16)]
            + [jax.ShapeDtypeStruct((rows, packed_width), BF16)] * near,
            scratch_shapes=[
                pltpu.VMEM(sign_in.shape, jnp.int32),
                pltpu.VMEM(sign_out.shape[::-1], jnp.int32),
                pltpu.SemaphoreType.DMA((2,)),
                pltpu.SemaphoreType.DMA((2,)),
                pltpu.SemaphoreType.DMA((near * far,)),
            ],
            compiler_params=params(16),
            cost_estimate=cost(2 * rows * 512 * 512, 3 * MIB),
            name="pack",
        )(*in_hbm(tokens, sign_in, sign_out.T, w_value, w_noise))
        pieces = [weights] * far
        for turn in (2, 1):
            pieces[turn] = exchanged(weights, "far", turn)
    else:
        own = lax.dynamic_slice_in_dim(jnp.stack([w_value, w_noise]), core * half, half, axis=2)
        own = own.transpose(1, 0, 2).reshape(share, 2 * half)
        pieces = [lax.all_gather(own, "far", axis=0, tiled=True)]
        order = jnp.arange(near) ^ near_at

        def by_owner(array):
            parts = array.reshape(rows, far, near, -1).transpose(2, 0, 1, 3).reshape(near, rows, -1)
            return jnp.take(parts, order, axis=0)

        words = by_owner(sign_in)
        sent = jnp.broadcast_to(sign_out[None], (near, *sign_out.shape))
        spare = jnp.zeros((near, rows, -(channels // 8) % LANES), jnp.int32)
        signs = [words & 255, words >> 8, sent & 255, sent >> 8, spare]
        packed = [by_owner(tokens)] + [part.astype(BF16) for part in signs]
        chunks = list(jnp.concatenate(packed, axis=2))
    chunks = [chunks[0]] + [exchanged(chunks[step], "near", step) for step in range(1, near)]

    late_tokens = tokens
    if len(pieces) > 1:
        pieces[1], chunks[0] = lax.optimization_barrier((pieces[1], chunks[0]))
        late_tokens, pieces[2] = lax.optimization_barrier((tokens, pieces[2]))
        pieces[3] = exchanged(pieces[2], "far", 1)
    gate_rows = jnp.dot(late_tokens, w_gate, preferred_element_type=F32).astype(BF16)
    gate_rows, pieces[-1], *chunks[1:] = lax.optimization_barrier((gate_rows, pieces[-1], *chunks[1:]))
    chunks += [exchanged(chunk, "dp", 1) for chunk in chunks]

    near_shape = jax.ShapeDtypeStruct((far * held, (cores * near + 1) * rows), BF16)
    partial = pl.pallas_call(
        functools.partial(project_kernel, near, far, cores, depth),
        in_specs=[HBM] + [VMEM] * (len(chunks) + len(pieces)),
        out_specs=[VMEM] * near,
        out_shape=[near_shape] * near,
        scratch_shapes=[
            pltpu.VMEM((count * max(held, GROUP), near_shape.shape[1]), F32),
            pltpu.VMEM((rows, half), F32),
            pltpu.SemaphoreType.DMA,
        ],
        compiler_params=params(40),
        cost_estimate=cost(4 * cores * near * rows * depth * half, 6 * MIB),
        name="project",
    )(*in_hbm(long_filter), *chunks, *pieces)
    partial = list(partial)
    last_rows, partial[0] = lax.optimization_barrier((gate_rows[rows - 2 :], partial[0]))
    before = lax.ppermute(last_rows, ("far", "near"), [(i, i + 1) for i in range(count - 1)])
    partial = [partial[0]] + [exchanged(partial[step], "near", step) for step in range(1, near)]

    far_shape = (held, (cores + 1) * near * rows)
    parts = pl.pallas_call(
        functools.partial(sum_kernel, near, far, rows),
        in_specs=[VMEM] * near,
        out_specs=[VMEM] * far,
        out_shape=[jax.ShapeDtypeStruct(far_shape, BF16)] * far,
        scratch_shapes=[pltpu.VMEM((far * max(held, GROUP), far_shape[1]), F32)],
        compiler_params=params(16),
        cost_estimate=cost(MIB, MIB),
        name="sum",
    )(*partial)
    if far == 4:
        parts = [parts[0]] + [exchanged(parts[turn], "far", turn) for turn in range(1, far)]
    else:
        order = jnp.arange(far) ^ lax.axis_index("far")
        parts = lax.all_to_all(jnp.take(jnp.stack(parts), order, axis=0), "far", 0, 0, tiled=True)
        parts = [parts.reshape(far * held, far_shape[1])]
    before, parts[0] = lax.optimization_barrier((before, parts[0]))

    tiles = length // LANES
    all_rows = tiles * SLOTS * cores * GROUP
    held_rows = max(held, GROUP)
    mixed = pl.pallas_call(
        functools.partial(mix_kernel, near, far, cores, held),
        in_specs=[VMEM] * (1 + len(parts)),
        out_specs=VMEM,
        out_shape=jax.ShapeDtypeStruct((cores * tiles, held, LANES), BF16),
        scratch_shapes=[
            pltpu.VMEM((all_rows, GROUP * BLOCK), BF16),
            pltpu.VMEM((all_rows * (1 if tiles <= 16 else 2), LANES), F32),
            pltpu.VMEM((cores * tiles, held_rows, LANES), F32),
            pltpu.VMEM((GROUP * BLOCK, length), BF16),
            pltpu.VMEM((cores + 1, held, length), F32),
        ],
        compiler_params=params(48),
        cost_estimate=cost(cores * held_rows * BLOCK * length * 256, 2 * MIB),
        name="mix",
    )(conv_taps, *parts)

    landed = lax.all_to_all(mixed, ("dp", "far", "near"), 0, 0, tiled=True).reshape(channels, rows)
    chunks = 8
    return pl.pallas_call(
        out_kernel,
        in_specs=[ANY] * 4 + [HBM],
        out_specs=HBM,
        out_shape=jax.ShapeDtypeStruct((rows, width), BF16),
        scratch_shapes=[
            pltpu.VMEM(gate_rows.shape, BF16),
            pltpu.VMEM(before.shape, BF16),
            pltpu.VMEM(conv_taps.shape, F32),
            pltpu.VMEM(landed.shape, BF16),
            pltpu.VMEM((chunks, channels, width // chunks), BF16),
            pltpu.VMEM((chunks, rows, width // chunks), BF16),
            pltpu.SemaphoreType.DMA((4,)),
            pltpu.SemaphoreType.DMA((chunks,)),
            pltpu.SemaphoreType.DMA((chunks,)),
        ],
        compiler_params=params(16),
        cost_estimate=cost(2 * rows * width * channels, 5 * MIB),
        name="project_out",
    )(gate_rows, before, conv_taps, landed, *in_hbm(w_out))


def solution(mesh):
    count = mesh.shape["seq"]
    near = 4 if count % 4 == 0 else 1
    far = count // near
    seq_at = mesh.axis_names.index("seq")
    shape = list(mesh.devices.shape)
    shape[seq_at : seq_at + 1] = [far, near]
    names = list(mesh.axis_names)
    names[seq_at : seq_at + 1] = ["far", "near"]
    inner = Mesh(mesh.devices.reshape(shape), tuple(names))
    by_token = P(("dp", "far", "near"), None)
    by_row = P(("far", "near"), None)
    placed = (by_token, by_token, by_token, by_row, by_row, P(), P(), by_row, P())
    return jax.shard_map(
        functools.partial(on_device, near, far),
        mesh=inner,
        in_specs=placed,
        out_specs=by_token,
        check_vma=False,
    )
```

```python
import functools

import jax
import jax.numpy as jnp
from jax import lax
from jax.experimental import pallas as pl
from jax.experimental.pallas import tpu as pltpu
from jax.sharding import Mesh, PartitionSpec as P

F32 = jnp.float32
BF16 = jnp.bfloat16
LANES = 128
GROUP = 8
BLOCK = 32
SLOTS = LANES // BLOCK
MIB = 1 << 20
VMEM = pl.BlockSpec(memory_space=pltpu.VMEM)
SMEM = pl.BlockSpec(memory_space=pltpu.SMEM)
HBM = pl.BlockSpec(memory_space=pltpu.HBM)
ANY = pl.BlockSpec(memory_space=pl.ANY)


def params(mib):
    return pltpu.CompilerParams(vmem_limit_bytes=mib * MIB)


def cost(flops, accessed):
    return pl.CostEstimate(flops=flops, bytes_accessed=accessed, transcendentals=0)


def in_hbm(*arrays):
    return [pltpu.with_memory_space_constraint(array, pltpu.HBM) for array in arrays]


def sign_bytes(packed):
    parts = jnp.concatenate([packed & 255, packed >> 8], axis=1)
    return parts.astype(F32).astype(BF16)


def one_hot(rows, columns, source_of):
    at = lax.broadcasted_iota(jnp.int32, (rows, columns), 0)
    column = lax.broadcasted_iota(jnp.int32, (1, columns), 1)
    return (at == source_of(column)).astype(F32).astype(BF16)


def pack_kernel(
    near, far, tokens_ref, in_ref, sent_ref, value_ref, noise_ref, weight_ref, *refs
):
    outs, (in_held, sent_held, read_sems, weight_sems, token_sems) = refs[:near], refs[near:]
    core, far_at, near_at = lax.axis_index("dp"), lax.axis_index("far"), lax.axis_index("near")
    half = weight_ref.shape[1] // 2
    share = weight_ref.shape[0]
    depth = share * far
    words = in_ref.shape[1]
    per_part = words // (near * far)
    own_words = per_part * far

    copies = []
    for at, source in enumerate((value_ref, noise_ref)):
        columns = pl.ds(pl.multiple_of(core * half, half), half)
        target = weight_ref.at[:, at * half : (at + 1) * half]
        copies.append(pltpu.make_async_copy(source.at[:, columns], target, weight_sems.at[at]))
    reads = [
        pltpu.make_async_copy(in_ref, in_held, read_sems.at[0]),
        pltpu.make_async_copy(sent_ref, sent_held, read_sems.at[1]),
    ]
    for step, out in enumerate(outs):
        for turn in range(far):
            start = ((far_at ^ turn) * near + (near_at ^ step)) * share
            columns = pl.ds(pl.multiple_of(start, share), share)
            target = out.at[:, turn * share : (turn + 1) * share]
            copies.append(
                pltpu.make_async_copy(tokens_ref.at[:, columns], target, token_sems.at[step * far + turn])
            )
    for copy in reads + copies:
        copy.start()

    def word_of(column):
        step, rest = column // (2 * own_words), column % (2 * own_words)
        part, word = rest // own_words, rest % own_words
        plane = (word // per_part) ^ far_at
        return part * words + (plane * near + (step ^ near_at)) * per_part + word % per_part

    by_word = one_hot(2 * words, 2 * words, word_of)
    reads[0].wait()
    moved = jnp.dot(sign_bytes(in_held[...]), by_word, preferred_element_type=F32).astype(BF16)
    reads[1].wait()
    sent = sign_bytes(sent_held[...].astype(F32).T.astype(jnp.int32))
    spare = -sent.shape[1] % LANES
    sent = jnp.concatenate([sent, jnp.zeros((sent.shape[0], spare), BF16)], axis=1)
    width = 2 * own_words
    for step, out in enumerate(outs):
        out[:, depth : depth + width] = moved[:, step * width : (step + 1) * width]
        out[:, depth + width :] = sent
    for copy in copies:
        copy.wait()


def spread_signs(pair, byte_of, columns):
    spread = jnp.dot(pair, one_hot(pair.shape[1], columns, byte_of), preferred_element_type=F32)
    mask = 1 << (lax.broadcasted_iota(jnp.int32, (1, columns), 1) & 7)
    return jnp.where((spread.astype(jnp.int32) & mask) != 0, 1.0, -1.0)


def spaced(lines, held):
    if held >= GROUP:
        return lines
    spare = jnp.zeros((GROUP - held, lines.shape[1]), F32)
    split = [lines[at : at + held] for at in range(0, lines.shape[0], held)]
    return jnp.concatenate([part for own in split for part in (own, spare)], axis=0)


def project_kernel(near, far, cores, depth, lags_ref, *refs):
    outs, (whole_ref, lags_held, sem) = refs[-3 - near : -3], refs[-3:]
    chunks, pieces = refs[: near * cores], refs[near * cores : -3 - near]
    core, near_at = lax.axis_index("dp"), lax.axis_index("near")
    rows = chunks[0].shape[0]
    half = pieces[0].shape[1] // 2
    own_lags = lags_ref.at[:, pl.ds(pl.multiple_of(core * half, half), half)]
    read = pltpu.make_async_copy(own_lags, lags_held, sem)
    read.start()
    words = depth // 16
    sent_words = cores * half // 16
    sent_start = depth + 2 * words

    def in_byte(column):
        return (column >> 4) + words * ((column >> 3) & 1)

    def out_byte(column):
        return core * (half // 16) + (column >> 4) + sent_words * ((column >> 3) & 1)

    def joined(start, stop):
        return jnp.concatenate([chunk[:, start:stop] for chunk in chunks], axis=0)

    flip_in = spread_signs(joined(depth, sent_start), in_byte, depth).astype(BF16)
    flip_out = spread_signs(joined(sent_start, sent_start + 2 * sent_words), out_byte, half)
    mean_part, noise_part = 0.0, 0.0
    step = depth // len(pieces)
    for at, piece in enumerate(pieces):
        tokens = joined(at * step, (at + 1) * step)
        flipped = tokens * flip_in[:, at * step : (at + 1) * step]
        mean_part += jnp.dot(tokens, piece[:, :half], preferred_element_type=F32)
        noise_part += jnp.dot(flipped, piece[:, half:], preferred_element_type=F32)
    held = half // (near * far)
    stride = max(held, GROUP)
    value = spaced((mean_part + flip_out * noise_part).T, held)
    for part in range(cores):
        for turn in range(near):
            at = part * near + turn
            target = ((core ^ part) * near + (near_at ^ turn)) * rows
            whole_ref[:, pl.ds(pl.multiple_of(target, rows), rows)] = value[:, at * rows : (at + 1) * rows]
    read.wait()
    whole_ref[:, cores * near * rows :] = spaced(lags_held[...].T, held)
    for turn, out in enumerate(outs):
        for plane in range(far):
            at = pl.multiple_of((plane * near + (near_at ^ turn)) * stride, stride)
            out[plane * held : (plane + 1) * held, :] = whole_ref[pl.ds(at, held), :].astype(BF16)


def sum_kernel(near, far, rows, *refs):
    parts, outs, whole_ref = refs[:near], refs[near : near + far], refs[-1]
    far_at, near_at = lax.axis_index("far"), lax.axis_index("near")
    held = outs[0].shape[0]
    stride = max(held, GROUP)
    span = parts[0].shape[1] - rows
    total = 0.0
    for turn, part in enumerate(parts):
        total += part[:, :span].astype(F32)
        at = pl.multiple_of(span + (near_at ^ turn) * rows, rows)
        whole_ref[:, pl.ds(at, rows)] = spaced(part[:, span:].astype(F32), held)
    whole_ref[:, :span] = spaced(total, held)
    for turn, out in enumerate(outs):
        at = pl.multiple_of((far_at ^ turn) * stride, stride)
        out[...] = whole_ref[pl.ds(at, held), :].astype(BF16)


def shifted(values, steps):
    moved = pltpu.roll(values, steps, 1)
    at = lax.broadcasted_iota(jnp.int32, values.shape, 1)
    return jnp.where(at >= steps, moved, 0.0)


def lane_roll(values, steps):
    return pltpu.roll(values, steps % LANES, values.ndim - 1) if steps % LANES else values


def mix_kernel(near, far, cores, held, taps_ref, *refs):
    parts, (out_ref, left_ref, sums_ref, done_ref, table_ref, lines_ref) = refs[:-6], refs[-6:]
    tiles = out_ref.shape[0] // cores
    block_rows = cores * GROUP
    tile_rows = SLOTS * block_rows
    rows = tiles * tile_rows
    lane = lax.broadcasted_iota(jnp.int32, (1, LANES), 1)
    pair = 2 * LANES
    span = near * LANES

    def padded(lines):
        if held >= GROUP:
            return lines
        return jnp.concatenate([lines, jnp.zeros((GROUP - held, lines.shape[1]), F32)], axis=0)

    for turn, part in enumerate(parts):
        for plane in range(far // len(parts)):
            own = slice(plane * held, (plane + 1) * held)
            target = pl.multiple_of(((lax.axis_index("far") if len(parts) > 1 else plane) ^ turn) * span, span)
            for line in range(cores + 1):
                piece = part[own, line * span : (line + 1) * span]
                lines_ref[line, :, pl.ds(target, span)] = piece.astype(F32)
    half = held * near * far
    position = lax.axis_index("far") * near + lax.axis_index("near")
    first = lax.axis_index("dp") * half + position * held
    channel = lax.broadcasted_iota(jnp.int32, (held, cores * half), 1) - first
    chosen = channel == lax.broadcasted_iota(jnp.int32, (held, cores * half), 0)
    taps = [
        jnp.sum(jnp.where(chosen, taps_ref[lag : lag + 1, : cores * half], 0.0), axis=1, keepdims=True)
        for lag in range(3)
    ]
    signals = []
    for part in range(cores):
        value = lines_ref[part]
        signal = taps[0] * value
        for lag in range(1, 3):
            signal += taps[lag] * shifted(value, lag)
        signals.append(padded(signal))
    lags = padded(lines_ref[cores])

    for group in range(max(held, GROUP) // GROUP):
        own = slice(group * GROUP, (group + 1) * GROUP)
        for at in range(GROUP):
            row = lags[group * GROUP + at : group * GROUP + at + 1, :]
            repeated = jnp.broadcast_to(row, (BLOCK, row.shape[1]))
            turned = pltpu.roll(repeated, 0, 1, stride=1, stride_axis=0)
            column = lax.broadcasted_iota(jnp.int32, repeated.shape, 1)
            lag = lax.broadcasted_iota(jnp.int32, repeated.shape, 0)
            kept = jnp.where(column >= lag, turned, 0.0).astype(BF16)
            table_ref[at * BLOCK : (at + 1) * BLOCK, :] = kept

        stacked = jnp.concatenate(
            [
                signal[own, a * LANES : (a + 1) * LANES]
                for a in range(tiles)
                for signal in signals
            ],
            axis=0,
        )
        slot_of = lax.broadcasted_iota(jnp.int32, stacked.shape, 0) % SLOTS
        turned = stacked
        for slot in range(1, SLOTS):
            turned = jnp.where(slot_of == slot, lane_roll(stacked, BLOCK * slot), turned)
        spread = jnp.stack(
            [
                lane_roll(turned, -BLOCK * slot).reshape(tiles, block_rows, LANES)
                for slot in range(SLOTS)
            ],
            axis=1,
        ).reshape(rows, LANES)
        owner = lax.broadcasted_iota(jnp.int32, (rows, LANES), 0) % GROUP
        for half in range(GROUP // SLOTS):
            kept = jnp.where(owner == lane // BLOCK + half * SLOTS, spread, 0.0)
            left_ref[:, half * LANES : (half + 1) * LANES] = kept.astype(BF16)

        sums_ref[...] = jnp.zeros_like(sums_ref)
        if tiles <= 16:
            for at in range(tiles // 2):
                start = 2 * at * tile_rows
                partial = jnp.dot(
                    left_ref[: rows - start, :],
                    table_ref[:, at * pair : (at + 1) * pair],
                    preferred_element_type=F32,
                )
                sums_ref[start:rows, :] += partial[:, :LANES]
                sums_ref[start + tile_rows : rows, :] += partial[: rows - start - tile_rows, LANES:]
        else:

            def add(at, _):
                partial = jnp.dot(
                    left_ref[...],
                    table_ref[:, pl.ds(pl.multiple_of(at * pair, pair), pair)],
                    preferred_element_type=F32,
                )
                start = pl.multiple_of(2 * at * tile_rows, tile_rows)
                sums_ref[pl.ds(start, rows), :] += partial[:, :LANES]
                sums_ref[pl.ds(start + tile_rows, rows), :] += partial[:, LANES:]
                return 0

            lax.fori_loop(0, tiles // 2, add, 0)

        sums = sums_ref[:rows, :]
        landed = [0.0] * SLOTS
        for part in range(SLOTS):
            late = sums
            if part:
                ahead = jnp.zeros((part * block_rows, LANES), F32)
                late = jnp.concatenate([ahead, sums[: rows - part * block_rows]], axis=0)
            late = late.reshape(tiles, SLOTS, block_rows, LANES)
            for slot in range(SLOTS):
                moved = late[:, slot].reshape(tiles * block_rows, LANES)
                landed[slot] += lane_roll(moved, BLOCK * (slot - part))
        result = 0.0
        for slot in range(SLOTS):
            result += jnp.where(lane // BLOCK == slot, landed[slot], 0.0)
        result = result.reshape(tiles, cores, GROUP, LANES)
        for part in range(cores):
            done_ref[part * tiles : (part + 1) * tiles, own, :] = result[:, part]

    out_ref[...] = done_ref[:, :held, :].astype(BF16)


def out_kernel(
    gate_ref, before_ref, taps_ref, mixed_ref, source_ref, target_ref,
    gate_held, before_held, taps_held, mixed_held, weight_ref, held_ref, small_sems, read_sems, write_sems,
):
    chunks, channels, step = weight_ref.shape
    small = [
        pltpu.make_async_copy(source, target, small_sems.at[at])
        for at, (source, target) in enumerate(
            (
                (gate_ref, gate_held),
                (before_ref, before_held),
                (taps_ref, taps_held),
                (mixed_ref, mixed_held),
            )
        )
    ]
    reads = [
        pltpu.make_async_copy(
            source_ref.at[:, pl.ds(at * step, step)], weight_ref.at[at], read_sems.at[at]
        )
        for at in range(chunks)
    ]
    for copy in small + reads:
        copy.start()
    for copy in small:
        copy.wait()
    gate = gate_held[...].astype(F32)
    extended = jnp.concatenate([before_held[...].astype(F32), gate], axis=0)
    gate_short = taps_held[0:1, channels:] * gate
    for lag in range(1, 3):
        gate_short += taps_held[lag : lag + 1, channels:] * extended[2 - lag : 2 - lag + gate.shape[0]]
    gated = (gate_short * mixed_held[...].astype(F32).T).astype(BF16)
    writes = []
    for at in range(chunks):
        reads[at].wait()
        held_ref[at] = jnp.dot(gated, weight_ref[at], preferred_element_type=F32).astype(BF16)
        columns = target_ref.at[:, pl.ds(at * step, step)]
        writes.append(pltpu.make_async_copy(held_ref.at[at], columns, write_sems.at[at]))
        writes[-1].start()
    for write in writes:
        write.wait()


def exchanged(value, axis, step):
    return lax.ppermute(value, axis, [(i, i ^ step) for i in range(lax.axis_size(axis))])


def on_device(near, far, tokens, sign_in, sign_out, w_value, w_noise, w_gate, conv_taps, long_filter, w_out):
    rows, width = tokens.shape
    channels = w_gate.shape[1]
    cores = lax.axis_size("dp")
    count = near * far
    half = channels // cores
    held = half // count
    share = w_value.shape[0]
    depth = share * far
    length = count * rows
    near_at, core = lax.axis_index("near"), lax.axis_index("dp")

    packed_width = depth + depth // 8 + channels // 8 + -(channels // 8) % LANES
    if share % LANES == 0 and far == 4:
        weights, *chunks = pl.pallas_call(
            functools.partial(pack_kernel, near, far),
            in_specs=[HBM] * 5,
            out_specs=[VMEM] * (1 + near),
            out_shape=[jax.ShapeDtypeStruct((share, 2 * half), BF16)]
            + [jax.ShapeDtypeStruct((rows, packed_width), BF16)] * near,
            scratch_shapes=[
                pltpu.VMEM(sign_in.shape, jnp.int32),
                pltpu.VMEM(sign_out.shape[::-1], jnp.int32),
                pltpu.SemaphoreType.DMA((2,)),
                pltpu.SemaphoreType.DMA((2,)),
                pltpu.SemaphoreType.DMA((near * far,)),
            ],
            compiler_params=params(16),
            cost_estimate=cost(2 * rows * 512 * 512, 3 * MIB),
            name="pack",
        )(*in_hbm(tokens, sign_in, sign_out.T, w_value, w_noise))
        pieces = [weights] * far
        for turn in (2, 1):
            pieces[turn] = exchanged(weights, "far", turn)
    else:
        own = lax.dynamic_slice_in_dim(jnp.stack([w_value, w_noise]), core * half, half, axis=2)
        own = own.transpose(1, 0, 2).reshape(share, 2 * half)
        pieces = [lax.all_gather(own, "far", axis=0, tiled=True)]
        order = jnp.arange(near) ^ near_at

        def by_owner(array):
            parts = array.reshape(rows, far, near, -1).transpose(2, 0, 1, 3).reshape(near, rows, -1)
            return jnp.take(parts, order, axis=0)

        words = by_owner(sign_in)
        sent = jnp.broadcast_to(sign_out[None], (near, *sign_out.shape))
        spare = jnp.zeros((near, rows, -(channels // 8) % LANES), jnp.int32)
        signs = [words & 255, words >> 8, sent & 255, sent >> 8, spare]
        packed = [by_owner(tokens)] + [part.astype(BF16) for part in signs]
        chunks = list(jnp.concatenate(packed, axis=2))
    chunks = [chunks[0]] + [exchanged(chunks[step], "near", step) for step in range(1, near)]

    late_tokens = tokens
    if len(pieces) > 1:
        pieces[1], chunks[0] = lax.optimization_barrier((pieces[1], chunks[0]))
        late_tokens, pieces[2] = lax.optimization_barrier((tokens, pieces[2]))
        pieces[3] = exchanged(pieces[2], "far", 1)
    gate_rows = jnp.dot(late_tokens, w_gate, preferred_element_type=F32).astype(BF16)
    gate_rows, *chunks[1:] = lax.optimization_barrier((gate_rows, *chunks[1:]))
    pieces[-1], chunks[-1] = lax.optimization_barrier((pieces[-1], chunks[-1]))
    chunks += [exchanged(chunk, "dp", 1) for chunk in chunks]

    near_shape = jax.ShapeDtypeStruct((far * held, (cores * near + 1) * rows), BF16)
    partial = pl.pallas_call(
        functools.partial(project_kernel, near, far, cores, depth),
        in_specs=[HBM] + [VMEM] * (len(chunks) + len(pieces)),
        out_specs=[VMEM] * near,
        out_shape=[near_shape] * near,
        scratch_shapes=[
            pltpu.VMEM((count * max(held, GROUP), near_shape.shape[1]), F32),
            pltpu.VMEM((rows, half), F32),
            pltpu.SemaphoreType.DMA,
        ],
        compiler_params=params(40),
        cost_estimate=cost(4 * cores * near * rows * depth * half, 6 * MIB),
        name="project",
    )(*in_hbm(long_filter), *chunks, *pieces)
    partial = list(partial)
    last_rows, partial[0] = lax.optimization_barrier((gate_rows[rows - 2 :], partial[0]))
    before = lax.ppermute(last_rows, ("far", "near"), [(i, i + 1) for i in range(count - 1)])
    partial = [partial[0]] + [exchanged(partial[step], "near", step) for step in range(1, near)]
    before, *partial = lax.optimization_barrier((before, *partial))

    far_shape = (held, (cores + 1) * near * rows)
    parts = pl.pallas_call(
        functools.partial(sum_kernel, near, far, rows),
        in_specs=[VMEM] * near,
        out_specs=[VMEM] * far,
        out_shape=[jax.ShapeDtypeStruct(far_shape, BF16)] * far,
        scratch_shapes=[pltpu.VMEM((far * max(held, GROUP), far_shape[1]), F32)],
        compiler_params=params(16),
        cost_estimate=cost(MIB, MIB),
        name="sum",
    )(*partial)
    if far == 4:
        parts = [parts[0]] + [exchanged(parts[turn], "far", turn) for turn in range(1, far)]
    else:
        order = jnp.arange(far) ^ lax.axis_index("far")
        parts = lax.all_to_all(jnp.take(jnp.stack(parts), order, axis=0), "far", 0, 0, tiled=True)
        parts = [parts.reshape(far * held, far_shape[1])]

    tiles = length // LANES
    all_rows = tiles * SLOTS * cores * GROUP
    held_rows = max(held, GROUP)
    mixed = pl.pallas_call(
        functools.partial(mix_kernel, near, far, cores, held),
        in_specs=[VMEM] * (1 + len(parts)),
        out_specs=VMEM,
        out_shape=jax.ShapeDtypeStruct((cores * tiles, held, LANES), BF16),
        scratch_shapes=[
            pltpu.VMEM((all_rows, GROUP * BLOCK), BF16),
            pltpu.VMEM((all_rows * (1 if tiles <= 16 else 2), LANES), F32),
            pltpu.VMEM((cores * tiles, held_rows, LANES), F32),
            pltpu.VMEM((GROUP * BLOCK, length), BF16),
            pltpu.VMEM((cores + 1, held, length), F32),
        ],
        compiler_params=params(48),
        cost_estimate=cost(cores * held_rows * BLOCK * length * 256, 2 * MIB),
        name="mix",
    )(conv_taps, *parts)

    landed = lax.all_to_all(mixed, ("dp", "far", "near"), 0, 0, tiled=True).reshape(channels, rows)
    chunks = 8
    return pl.pallas_call(
        out_kernel,
        in_specs=[ANY] * 4 + [HBM],
        out_specs=HBM,
        out_shape=jax.ShapeDtypeStruct((rows, width), BF16),
        scratch_shapes=[
            pltpu.VMEM(gate_rows.shape, BF16),
            pltpu.VMEM(before.shape, BF16),
            pltpu.VMEM(conv_taps.shape, F32),
            pltpu.VMEM(landed.shape, BF16),
            pltpu.VMEM((chunks, channels, width // chunks), BF16),
            pltpu.VMEM((chunks, rows, width // chunks), BF16),
            pltpu.SemaphoreType.DMA((4,)),
            pltpu.SemaphoreType.DMA((chunks,)),
            pltpu.SemaphoreType.DMA((chunks,)),
        ],
        compiler_params=params(16),
        cost_estimate=cost(2 * rows * width * channels, 5 * MIB),
        name="project_out",
    )(gate_rows, before, conv_taps, landed, *in_hbm(w_out))


def solution(mesh):
    count = mesh.shape["seq"]
    near = 4 if count % 4 == 0 else 1
    far = count // near
    seq_at = mesh.axis_names.index("seq")
    shape = list(mesh.devices.shape)
    shape[seq_at : seq_at + 1] = [far, near]
    names = list(mesh.axis_names)
    names[seq_at : seq_at + 1] = ["far", "near"]
    inner = Mesh(mesh.devices.reshape(shape), tuple(names))
    by_token = P(("dp", "far", "near"), None)
    by_row = P(("far", "near"), None)
    placed = (by_token, by_token, by_token, by_row, by_row, P(), P(), by_row, P())
    return jax.shard_map(
        functools.partial(on_device, near, far),
        mesh=inner,
        in_specs=placed,
        out_specs=by_token,
        check_vma=False,
    )
```

```python
import functools

import jax
import jax.numpy as jnp
from jax import lax
from jax.experimental import pallas as pl
from jax.experimental.pallas import tpu as pltpu
from jax.sharding import Mesh, PartitionSpec as P

F32 = jnp.float32
BF16 = jnp.bfloat16
LANES = 128
GROUP = 8
BLOCK = 32
SLOTS = LANES // BLOCK
MIB = 1 << 20
VMEM = pl.BlockSpec(memory_space=pltpu.VMEM)
SMEM = pl.BlockSpec(memory_space=pltpu.SMEM)
HBM = pl.BlockSpec(memory_space=pltpu.HBM)
ANY = pl.BlockSpec(memory_space=pl.ANY)


def params(mib):
    return pltpu.CompilerParams(vmem_limit_bytes=mib * MIB)


def cost(flops, accessed):
    return pl.CostEstimate(flops=flops, bytes_accessed=accessed, transcendentals=0)


def in_hbm(*arrays):
    return [pltpu.with_memory_space_constraint(array, pltpu.HBM) for array in arrays]


def sign_bytes(packed):
    parts = jnp.concatenate([packed & 255, packed >> 8], axis=1)
    return parts.astype(F32).astype(BF16)


def one_hot(rows, columns, source_of):
    at = lax.broadcasted_iota(jnp.int32, (rows, columns), 0)
    column = lax.broadcasted_iota(jnp.int32, (1, columns), 1)
    return (at == source_of(column)).astype(F32).astype(BF16)


def pack_kernel(
    near, far, tokens_ref, in_ref, sent_ref, value_ref, noise_ref, mean_ref, spread_ref, weight_ref, *refs
):
    outs, (in_held, sent_held, read_sems, weight_sems, token_sems) = refs[:near], refs[near:]
    core, far_at, near_at = lax.axis_index("dp"), lax.axis_index("far"), lax.axis_index("near")
    half = weight_ref.shape[1] // 2
    share = weight_ref.shape[0]
    depth = share * far
    words = in_ref.shape[1]
    per_part = words // (near * far)
    own_words = per_part * far

    copies = []
    columns = pl.ds(pl.multiple_of(core * half, half), half)
    for at, (source, alone) in enumerate(((value_ref, mean_ref), (noise_ref, spread_ref))):
        both = weight_ref.at[:, at * half : (at + 1) * half]
        copies.append(pltpu.make_async_copy(source.at[:, columns], alone, weight_sems.at[at]))
        copies.append(pltpu.make_async_copy(source.at[:, columns], both, weight_sems.at[2 + at]))
    reads = [
        pltpu.make_async_copy(in_ref, in_held, read_sems.at[0]),
        pltpu.make_async_copy(sent_ref, sent_held, read_sems.at[1]),
    ]
    for step, out in enumerate(outs):
        for turn in range(far):
            start = ((far_at ^ turn) * near + (near_at ^ step)) * share
            columns = pl.ds(pl.multiple_of(start, share), share)
            target = out.at[:, turn * share : (turn + 1) * share]
            copies.append(
                pltpu.make_async_copy(tokens_ref.at[:, columns], target, token_sems.at[step * far + turn])
            )
    for copy in reads + copies:
        copy.start()

    def word_of(column):
        step, rest = column // (2 * own_words), column % (2 * own_words)
        part, word = rest // own_words, rest % own_words
        plane = (word // per_part) ^ far_at
        return part * words + (plane * near + (step ^ near_at)) * per_part + word % per_part

    by_word = one_hot(2 * words, 2 * words, word_of)
    reads[0].wait()
    moved = jnp.dot(sign_bytes(in_held[...]), by_word, preferred_element_type=F32).astype(BF16)
    reads[1].wait()
    sent = sign_bytes(sent_held[...].astype(F32).T.astype(jnp.int32))
    spare = -sent.shape[1] % LANES
    sent = jnp.concatenate([sent, jnp.zeros((sent.shape[0], spare), BF16)], axis=1)
    width = 2 * own_words
    for step, out in enumerate(outs):
        out[:, depth : depth + width] = moved[:, step * width : (step + 1) * width]
        out[:, depth + width :] = sent
    for copy in copies:
        copy.wait()


def spread_signs(pair, byte_of, columns):
    spread = jnp.dot(pair, one_hot(pair.shape[1], columns, byte_of), preferred_element_type=F32)
    mask = 1 << (lax.broadcasted_iota(jnp.int32, (1, columns), 1) & 7)
    return jnp.where((spread.astype(jnp.int32) & mask) != 0, 1.0, -1.0)


def spaced(lines, held):
    if held >= GROUP:
        return lines
    spare = jnp.zeros((GROUP - held, lines.shape[1]), F32)
    split = [lines[at : at + held] for at in range(0, lines.shape[0], held)]
    return jnp.concatenate([part for own in split for part in (own, spare)], axis=0)


def project_kernel(near, far, cores, depth, half, split, lags_ref, *refs):
    outs, (whole_ref, lags_held, sem) = refs[-3 - near : -3], refs[-3:]
    chunks, flat = refs[: near * cores], refs[near * cores : -3 - near]
    core, near_at = lax.axis_index("dp"), lax.axis_index("near")
    rows = chunks[0].shape[0]
    flat = list(flat)
    pieces = []
    for parts in split:
        own = [flat.pop(0) for _ in range(parts)]
        pieces.append(own if parts > 1 else (own[0].at[:, :half], own[0].at[:, half:]))
    own_lags = lags_ref.at[:, pl.ds(pl.multiple_of(core * half, half), half)]
    read = pltpu.make_async_copy(own_lags, lags_held, sem)
    read.start()
    words = depth // 16
    sent_words = cores * half // 16
    sent_start = depth + 2 * words

    def in_byte(column):
        return (column >> 4) + words * ((column >> 3) & 1)

    def out_byte(column):
        return core * (half // 16) + (column >> 4) + sent_words * ((column >> 3) & 1)

    def joined(start, stop):
        return jnp.concatenate([chunk[:, start:stop] for chunk in chunks], axis=0)

    flip_in = spread_signs(joined(depth, sent_start), in_byte, depth).astype(BF16)
    flip_out = spread_signs(joined(sent_start, sent_start + 2 * sent_words), out_byte, half)
    mean_part, noise_part = 0.0, 0.0
    step = depth // len(pieces)
    for at, (mean, spread) in enumerate(pieces):
        tokens = joined(at * step, (at + 1) * step)
        flipped = tokens * flip_in[:, at * step : (at + 1) * step]
        mean_part += jnp.dot(tokens, mean[...], preferred_element_type=F32)
        noise_part += jnp.dot(flipped, spread[...], preferred_element_type=F32)
    held = half // (near * far)
    stride = max(held, GROUP)
    value = spaced((mean_part + flip_out * noise_part).T, held)
    for part in range(cores):
        for turn in range(near):
            at = part * near + turn
            target = ((core ^ part) * near + (near_at ^ turn)) * rows
            whole_ref[:, pl.ds(pl.multiple_of(target, rows), rows)] = value[:, at * rows : (at + 1) * rows]
    read.wait()
    whole_ref[:, cores * near * rows :] = spaced(lags_held[...].T, held)
    for turn, out in enumerate(outs):
        for plane in range(far):
            at = pl.multiple_of((plane * near + (near_at ^ turn)) * stride, stride)
            out[plane * held : (plane + 1) * held, :] = whole_ref[pl.ds(at, held), :].astype(BF16)


def sum_kernel(near, far, rows, *refs):
    parts, outs, whole_ref = refs[:near], refs[near : near + far], refs[-1]
    far_at, near_at = lax.axis_index("far"), lax.axis_index("near")
    held = outs[0].shape[0]
    stride = max(held, GROUP)
    span = parts[0].shape[1] - rows
    total = 0.0
    for turn, part in enumerate(parts):
        total += part[:, :span].astype(F32)
        at = pl.multiple_of(span + (near_at ^ turn) * rows, rows)
        whole_ref[:, pl.ds(at, rows)] = spaced(part[:, span:].astype(F32), held)
    whole_ref[:, :span] = spaced(total, held)
    for turn, out in enumerate(outs):
        at = pl.multiple_of((far_at ^ turn) * stride, stride)
        out[...] = whole_ref[pl.ds(at, held), :].astype(BF16)


def shifted(values, steps):
    moved = pltpu.roll(values, steps, 1)
    at = lax.broadcasted_iota(jnp.int32, values.shape, 1)
    return jnp.where(at >= steps, moved, 0.0)


def lane_roll(values, steps):
    return pltpu.roll(values, steps % LANES, values.ndim - 1) if steps % LANES else values


def mix_kernel(near, far, cores, held, taps_ref, *refs):
    parts, (out_ref, left_ref, sums_ref, done_ref, table_ref, lines_ref) = refs[:-6], refs[-6:]
    tiles = out_ref.shape[0] // cores
    block_rows = cores * GROUP
    tile_rows = SLOTS * block_rows
    rows = tiles * tile_rows
    lane = lax.broadcasted_iota(jnp.int32, (1, LANES), 1)
    pair = 2 * LANES
    span = near * LANES

    def padded(lines):
        if held >= GROUP:
            return lines
        return jnp.concatenate([lines, jnp.zeros((GROUP - held, lines.shape[1]), F32)], axis=0)

    for turn, part in enumerate(parts):
        for plane in range(far // len(parts)):
            own = slice(plane * held, (plane + 1) * held)
            target = pl.multiple_of(((lax.axis_index("far") if len(parts) > 1 else plane) ^ turn) * span, span)
            for line in range(cores + 1):
                piece = part[own, line * span : (line + 1) * span]
                lines_ref[line, :, pl.ds(target, span)] = piece.astype(F32)
    half = held * near * far
    position = lax.axis_index("far") * near + lax.axis_index("near")
    first = lax.axis_index("dp") * half + position * held
    channel = lax.broadcasted_iota(jnp.int32, (held, cores * half), 1) - first
    chosen = channel == lax.broadcasted_iota(jnp.int32, (held, cores * half), 0)
    taps = [
        jnp.sum(jnp.where(chosen, taps_ref[lag : lag + 1, : cores * half], 0.0), axis=1, keepdims=True)
        for lag in range(3)
    ]
    signals = []
    for part in range(cores):
        value = lines_ref[part]
        signal = taps[0] * value
        for lag in range(1, 3):
            signal += taps[lag] * shifted(value, lag)
        signals.append(padded(signal))
    lags = padded(lines_ref[cores])

    for group in range(max(held, GROUP) // GROUP):
        own = slice(group * GROUP, (group + 1) * GROUP)
        for at in range(GROUP):
            row = lags[group * GROUP + at : group * GROUP + at + 1, :]
            repeated = jnp.broadcast_to(row, (BLOCK, row.shape[1]))
            turned = pltpu.roll(repeated, 0, 1, stride=1, stride_axis=0)
            column = lax.broadcasted_iota(jnp.int32, repeated.shape, 1)
            lag = lax.broadcasted_iota(jnp.int32, repeated.shape, 0)
            kept = jnp.where(column >= lag, turned, 0.0).astype(BF16)
            table_ref[at * BLOCK : (at + 1) * BLOCK, :] = kept

        stacked = jnp.concatenate(
            [
                signal[own, a * LANES : (a + 1) * LANES]
                for a in range(tiles)
                for signal in signals
            ],
            axis=0,
        )
        slot_of = lax.broadcasted_iota(jnp.int32, stacked.shape, 0) % SLOTS
        turned = stacked
        for slot in range(1, SLOTS):
            turned = jnp.where(slot_of == slot, lane_roll(stacked, BLOCK * slot), turned)
        spread = jnp.stack(
            [
                lane_roll(turned, -BLOCK * slot).reshape(tiles, block_rows, LANES)
                for slot in range(SLOTS)
            ],
            axis=1,
        ).reshape(rows, LANES)
        owner = lax.broadcasted_iota(jnp.int32, (rows, LANES), 0) % GROUP
        for half in range(GROUP // SLOTS):
            kept = jnp.where(owner == lane // BLOCK + half * SLOTS, spread, 0.0)
            left_ref[:, half * LANES : (half + 1) * LANES] = kept.astype(BF16)

        sums_ref[...] = jnp.zeros_like(sums_ref)
        if tiles <= 16:
            for at in range(tiles // 2):
                start = 2 * at * tile_rows
                partial = jnp.dot(
                    left_ref[: rows - start, :],
                    table_ref[:, at * pair : (at + 1) * pair],
                    preferred_element_type=F32,
                )
                sums_ref[start:rows, :] += partial[:, :LANES]
                sums_ref[start + tile_rows : rows, :] += partial[: rows - start - tile_rows, LANES:]
        else:

            def add(at, _):
                partial = jnp.dot(
                    left_ref[...],
                    table_ref[:, pl.ds(pl.multiple_of(at * pair, pair), pair)],
                    preferred_element_type=F32,
                )
                start = pl.multiple_of(2 * at * tile_rows, tile_rows)
                sums_ref[pl.ds(start, rows), :] += partial[:, :LANES]
                sums_ref[pl.ds(start + tile_rows, rows), :] += partial[:, LANES:]
                return 0

            lax.fori_loop(0, tiles // 2, add, 0)

        sums = sums_ref[:rows, :]
        landed = [0.0] * SLOTS
        for part in range(SLOTS):
            late = sums
            if part:
                ahead = jnp.zeros((part * block_rows, LANES), F32)
                late = jnp.concatenate([ahead, sums[: rows - part * block_rows]], axis=0)
            late = late.reshape(tiles, SLOTS, block_rows, LANES)
            for slot in range(SLOTS):
                moved = late[:, slot].reshape(tiles * block_rows, LANES)
                landed[slot] += lane_roll(moved, BLOCK * (slot - part))
        result = 0.0
        for slot in range(SLOTS):
            result += jnp.where(lane // BLOCK == slot, landed[slot], 0.0)
        result = result.reshape(tiles, cores, GROUP, LANES)
        for part in range(cores):
            done_ref[part * tiles : (part + 1) * tiles, own, :] = result[:, part]

    out_ref[...] = done_ref[:, :held, :].astype(BF16)


def out_kernel(
    gate_ref, before_ref, taps_ref, mixed_ref, source_ref, target_ref,
    gate_held, before_held, taps_held, mixed_held, weight_ref, held_ref, small_sems, read_sems, write_sems,
):
    chunks, channels, step = weight_ref.shape
    small = [
        pltpu.make_async_copy(source, target, small_sems.at[at])
        for at, (source, target) in enumerate(
            (
                (gate_ref, gate_held),
                (before_ref, before_held),
                (taps_ref, taps_held),
                (mixed_ref, mixed_held),
            )
        )
    ]
    reads = [
        pltpu.make_async_copy(
            source_ref.at[:, pl.ds(at * step, step)], weight_ref.at[at], read_sems.at[at]
        )
        for at in range(chunks)
    ]
    for copy in small + reads:
        copy.start()
    for copy in small:
        copy.wait()
    gate = gate_held[...].astype(F32)
    extended = jnp.concatenate([before_held[...].astype(F32), gate], axis=0)
    gate_short = taps_held[0:1, channels:] * gate
    for lag in range(1, 3):
        gate_short += taps_held[lag : lag + 1, channels:] * extended[2 - lag : 2 - lag + gate.shape[0]]
    gated = (gate_short * mixed_held[...].astype(F32).T).astype(BF16)
    writes = []
    for at in range(chunks):
        reads[at].wait()
        held_ref[at] = jnp.dot(gated, weight_ref[at], preferred_element_type=F32).astype(BF16)
        columns = target_ref.at[:, pl.ds(at * step, step)]
        writes.append(pltpu.make_async_copy(held_ref.at[at], columns, write_sems.at[at]))
        writes[-1].start()
    for write in writes:
        write.wait()


def exchanged(value, axis, step):
    return lax.ppermute(value, axis, [(i, i ^ step) for i in range(lax.axis_size(axis))])


def on_device(near, far, tokens, sign_in, sign_out, w_value, w_noise, w_gate, conv_taps, long_filter, w_out):
    rows, width = tokens.shape
    channels = w_gate.shape[1]
    cores = lax.axis_size("dp")
    count = near * far
    half = channels // cores
    held = half // count
    share = w_value.shape[0]
    depth = share * far
    length = count * rows
    near_at, core = lax.axis_index("near"), lax.axis_index("dp")

    packed_width = depth + depth // 8 + channels // 8 + -(channels // 8) % LANES
    if share % LANES == 0 and far == 4:
        mean, spread, weights, *chunks = pl.pallas_call(
            functools.partial(pack_kernel, near, far),
            in_specs=[HBM] * 5,
            out_specs=[VMEM] * (3 + near),
            out_shape=[jax.ShapeDtypeStruct((share, half), BF16)] * 2
            + [jax.ShapeDtypeStruct((share, 2 * half), BF16)]
            + [jax.ShapeDtypeStruct((rows, packed_width), BF16)] * near,
            scratch_shapes=[
                pltpu.VMEM(sign_in.shape, jnp.int32),
                pltpu.VMEM(sign_out.shape[::-1], jnp.int32),
                pltpu.SemaphoreType.DMA((2,)),
                pltpu.SemaphoreType.DMA((4,)),
                pltpu.SemaphoreType.DMA((near * far,)),
            ],
            compiler_params=params(16),
            cost_estimate=cost(2 * rows * 512 * 512, 3 * MIB),
            name="pack",
        )(*in_hbm(tokens, sign_in, sign_out.T, w_value, w_noise))
        mean_far = exchanged(mean, "far", 2)
        spread_far = exchanged(spread, "far", 2)
        late_weights, mean_far = lax.optimization_barrier((weights, mean_far))
        pieces = [(weights,), (exchanged(late_weights, "far", 1),), (mean_far, spread_far)]
    else:
        own = lax.dynamic_slice_in_dim(jnp.stack([w_value, w_noise]), core * half, half, axis=2)
        own = own.transpose(1, 0, 2).reshape(share, 2 * half)
        pieces = [(lax.all_gather(own, "far", axis=0, tiled=True),)]
        order = jnp.arange(near) ^ near_at

        def by_owner(array):
            parts = array.reshape(rows, far, near, -1).transpose(2, 0, 1, 3).reshape(near, rows, -1)
            return jnp.take(parts, order, axis=0)

        words = by_owner(sign_in)
        sent = jnp.broadcast_to(sign_out[None], (near, *sign_out.shape))
        spare = jnp.zeros((near, rows, -(channels // 8) % LANES), jnp.int32)
        signs = [words & 255, words >> 8, sent & 255, sent >> 8, spare]
        packed = [by_owner(tokens)] + [part.astype(BF16) for part in signs]
        chunks = list(jnp.concatenate(packed, axis=2))
    chunks = [chunks[0]] + [exchanged(chunks[step], "near", step) for step in range(1, near)]

    late_tokens = tokens
    if len(pieces) > 1:
        late_tokens, mean_far = lax.optimization_barrier((tokens, mean_far))
        mean_last = exchanged(mean_far, "far", 1)
    gate_rows = jnp.dot(late_tokens, w_gate, preferred_element_type=F32).astype(BF16)
    if len(pieces) > 1:
        gate_rows, spread_far, chunks[0] = lax.optimization_barrier((gate_rows, spread_far, chunks[0]))
        pieces[2] = (mean_far, spread_far)
        pieces.append((mean_last, exchanged(spread_far, "far", 1)))
    gate_rows, pieces[1 % len(pieces)], *chunks[1:] = lax.optimization_barrier(
        (gate_rows, pieces[1 % len(pieces)], *chunks[1:])
    )
    pieces[-1], chunks[-1] = lax.optimization_barrier((pieces[-1], chunks[-1]))
    chunks += [exchanged(chunk, "dp", 1) for chunk in chunks]

    near_shape = jax.ShapeDtypeStruct((far * held, (cores * near + 1) * rows), BF16)
    split = tuple(len(parts) for parts in pieces)
    partial = pl.pallas_call(
        functools.partial(project_kernel, near, far, cores, depth, half, split),
        in_specs=[HBM] + [VMEM] * (len(chunks) + sum(split)),
        out_specs=[VMEM] * near,
        out_shape=[near_shape] * near,
        scratch_shapes=[
            pltpu.VMEM((count * max(held, GROUP), near_shape.shape[1]), F32),
            pltpu.VMEM((rows, half), F32),
            pltpu.SemaphoreType.DMA,
        ],
        compiler_params=params(40),
        cost_estimate=cost(4 * cores * near * rows * depth * half, 6 * MIB),
        name="project",
    )(*in_hbm(long_filter), *chunks, *(part for parts in pieces for part in parts))
    partial = list(partial)
    last_rows, partial[0] = lax.optimization_barrier((gate_rows[rows - 2 :], partial[0]))
    before = lax.ppermute(last_rows, ("far", "near"), [(i, i + 1) for i in range(count - 1)])
    partial = [partial[0]] + [exchanged(partial[step], "near", step) for step in range(1, near)]
    before, *partial = lax.optimization_barrier((before, *partial))

    far_shape = (held, (cores + 1) * near * rows)
    parts = pl.pallas_call(
        functools.partial(sum_kernel, near, far, rows),
        in_specs=[VMEM] * near,
        out_specs=[VMEM] * far,
        out_shape=[jax.ShapeDtypeStruct(far_shape, BF16)] * far,
        scratch_shapes=[pltpu.VMEM((far * max(held, GROUP), far_shape[1]), F32)],
        compiler_params=params(16),
        cost_estimate=cost(MIB, MIB),
        name="sum",
    )(*partial)
    if far == 4:
        parts = [parts[0]] + [exchanged(parts[turn], "far", turn) for turn in range(1, far)]
    else:
        order = jnp.arange(far) ^ lax.axis_index("far")
        parts = lax.all_to_all(jnp.take(jnp.stack(parts), order, axis=0), "far", 0, 0, tiled=True)
        parts = [parts.reshape(far * held, far_shape[1])]

    tiles = length // LANES
    all_rows = tiles * SLOTS * cores * GROUP
    held_rows = max(held, GROUP)
    mixed = pl.pallas_call(
        functools.partial(mix_kernel, near, far, cores, held),
        in_specs=[VMEM] * (1 + len(parts)),
        out_specs=VMEM,
        out_shape=jax.ShapeDtypeStruct((cores * tiles, held, LANES), BF16),
        scratch_shapes=[
            pltpu.VMEM((all_rows, GROUP * BLOCK), BF16),
            pltpu.VMEM((all_rows * (1 if tiles <= 16 else 2), LANES), F32),
            pltpu.VMEM((cores * tiles, held_rows, LANES), F32),
            pltpu.VMEM((GROUP * BLOCK, length), BF16),
            pltpu.VMEM((cores + 1, held, length), F32),
        ],
        compiler_params=params(48),
        cost_estimate=cost(cores * held_rows * BLOCK * length * 256, 2 * MIB),
        name="mix",
    )(conv_taps, *parts)

    landed = lax.all_to_all(mixed, ("dp", "far", "near"), 0, 0, tiled=True).reshape(channels, rows)
    chunks = 8
    return pl.pallas_call(
        out_kernel,
        in_specs=[ANY] * 4 + [HBM],
        out_specs=HBM,
        out_shape=jax.ShapeDtypeStruct((rows, width), BF16),
        scratch_shapes=[
            pltpu.VMEM(gate_rows.shape, BF16),
            pltpu.VMEM(before.shape, BF16),
            pltpu.VMEM(conv_taps.shape, F32),
            pltpu.VMEM(landed.shape, BF16),
            pltpu.VMEM((chunks, channels, width // chunks), BF16),
            pltpu.VMEM((chunks, rows, width // chunks), BF16),
            pltpu.SemaphoreType.DMA((4,)),
            pltpu.SemaphoreType.DMA((chunks,)),
            pltpu.SemaphoreType.DMA((chunks,)),
        ],
        compiler_params=params(16),
        cost_estimate=cost(2 * rows * width * channels, 5 * MIB),
        name="project_out",
    )(gate_rows, before, conv_taps, landed, *in_hbm(w_out))


def solution(mesh):
    count = mesh.shape["seq"]
    near = 4 if count % 4 == 0 else 1
    far = count // near
    seq_at = mesh.axis_names.index("seq")
    shape = list(mesh.devices.shape)
    shape[seq_at : seq_at + 1] = [far, near]
    names = list(mesh.axis_names)
    names[seq_at : seq_at + 1] = ["far", "near"]
    inner = Mesh(mesh.devices.reshape(shape), tuple(names))
    by_token = P(("dp", "far", "near"), None)
    by_row = P(("far", "near"), None)
    placed = (by_token, by_token, by_token, by_row, by_row, P(), P(), by_row, P())
    return jax.shard_map(
        functools.partial(on_device, near, far),
        mesh=inner,
        in_specs=placed,
        out_specs=by_token,
        check_vma=False,
    )
```

```python
import functools

import jax
import jax.numpy as jnp
from jax import lax
from jax.experimental import pallas as pl
from jax.experimental.pallas import tpu as pltpu
from jax.sharding import Mesh, PartitionSpec as P

F32 = jnp.float32
BF16 = jnp.bfloat16
LANES = 128
GROUP = 8
BLOCK = 32
SLOTS = LANES // BLOCK
MIB = 1 << 20
VMEM = pl.BlockSpec(memory_space=pltpu.VMEM)
SMEM = pl.BlockSpec(memory_space=pltpu.SMEM)
HBM = pl.BlockSpec(memory_space=pltpu.HBM)
ANY = pl.BlockSpec(memory_space=pl.ANY)


def params(mib):
    return pltpu.CompilerParams(vmem_limit_bytes=mib * MIB)


def cost(flops, accessed):
    return pl.CostEstimate(flops=flops, bytes_accessed=accessed, transcendentals=0)


def in_hbm(*arrays):
    return [pltpu.with_memory_space_constraint(array, pltpu.HBM) for array in arrays]


def sign_bytes(packed):
    parts = jnp.concatenate([packed & 255, packed >> 8], axis=1)
    return parts.astype(F32).astype(BF16)


def one_hot(rows, columns, source_of):
    at = lax.broadcasted_iota(jnp.int32, (rows, columns), 0)
    column = lax.broadcasted_iota(jnp.int32, (1, columns), 1)
    return (at == source_of(column)).astype(F32).astype(BF16)


def weights_kernel(value_ref, noise_ref, weight_ref, sems):
    half = weight_ref.shape[1] // 2
    columns = pl.ds(pl.multiple_of(lax.axis_index("dp") * half, half), half)
    copies = []
    for at, source in enumerate((value_ref, noise_ref)):
        target = weight_ref.at[:, at * half : (at + 1) * half]
        copies.append(pltpu.make_async_copy(source.at[:, columns], target, sems.at[at]))
        copies[-1].start()
    for copy in copies:
        copy.wait()


def pack_kernel(
    near, far, tokens_ref, in_ref, sent_ref, value_ref, noise_ref, weight_ref, *refs
):
    outs, (in_held, sent_held, read_sems, weight_sems, token_sems) = refs[:near], refs[near:]
    core, far_at, near_at = lax.axis_index("dp"), lax.axis_index("far"), lax.axis_index("near")
    half = weight_ref.shape[1] // 2
    share = weight_ref.shape[0]
    depth = share * far
    words = in_ref.shape[1]
    per_part = words // (near * far)
    own_words = per_part * far

    copies = []
    for at, source in enumerate((value_ref, noise_ref)):
        columns = pl.ds(pl.multiple_of(core * half, half), half)
        target = weight_ref.at[:, at * half : (at + 1) * half]
        copies.append(pltpu.make_async_copy(source.at[:, columns], target, weight_sems.at[at]))
    reads = [
        pltpu.make_async_copy(in_ref, in_held, read_sems.at[0]),
        pltpu.make_async_copy(sent_ref, sent_held, read_sems.at[1]),
    ]
    for step, out in enumerate(outs):
        for turn in range(far):
            start = ((far_at ^ turn) * near + (near_at ^ step)) * share
            columns = pl.ds(pl.multiple_of(start, share), share)
            target = out.at[:, turn * share : (turn + 1) * share]
            copies.append(
                pltpu.make_async_copy(tokens_ref.at[:, columns], target, token_sems.at[step * far + turn])
            )
    for copy in reads + copies:
        copy.start()

    def word_of(column):
        step, rest = column // (2 * own_words), column % (2 * own_words)
        part, word = rest // own_words, rest % own_words
        plane = (word // per_part) ^ far_at
        return part * words + (plane * near + (step ^ near_at)) * per_part + word % per_part

    by_word = one_hot(2 * words, 2 * words, word_of)
    reads[0].wait()
    moved = jnp.dot(sign_bytes(in_held[...]), by_word, preferred_element_type=F32).astype(BF16)
    reads[1].wait()
    sent = sign_bytes(sent_held[...].astype(F32).T.astype(jnp.int32))
    spare = -sent.shape[1] % LANES
    sent = jnp.concatenate([sent, jnp.zeros((sent.shape[0], spare), BF16)], axis=1)
    width = 2 * own_words
    for step, out in enumerate(outs):
        out[:, depth : depth + width] = moved[:, step * width : (step + 1) * width]
        out[:, depth + width :] = sent
    for copy in copies:
        copy.wait()


def spread_signs(pair, byte_of, columns):
    spread = jnp.dot(pair, one_hot(pair.shape[1], columns, byte_of), preferred_element_type=F32)
    mask = 1 << (lax.broadcasted_iota(jnp.int32, (1, columns), 1) & 7)
    return jnp.where((spread.astype(jnp.int32) & mask) != 0, 1.0, -1.0)


def spaced(lines, held):
    if held >= GROUP:
        return lines
    spare = jnp.zeros((GROUP - held, lines.shape[1]), F32)
    split = [lines[at : at + held] for at in range(0, lines.shape[0], held)]
    return jnp.concatenate([part for own in split for part in (own, spare)], axis=0)


def project_kernel(near, far, cores, depth, lags_ref, *refs):
    outs, (whole_ref, lags_held, sem) = refs[-3 - near : -3], refs[-3:]
    chunks, pieces = refs[: near * cores], refs[near * cores : -3 - near]
    core, near_at = lax.axis_index("dp"), lax.axis_index("near")
    rows = chunks[0].shape[0]
    half = pieces[0].shape[1] // 2
    own_lags = lags_ref.at[:, pl.ds(pl.multiple_of(core * half, half), half)]
    read = pltpu.make_async_copy(own_lags, lags_held, sem)
    read.start()
    words = depth // 16
    sent_words = cores * half // 16
    sent_start = depth + 2 * words

    def in_byte(column):
        return (column >> 4) + words * ((column >> 3) & 1)

    def out_byte(column):
        return core * (half // 16) + (column >> 4) + sent_words * ((column >> 3) & 1)

    def joined(start, stop):
        return jnp.concatenate([chunk[:, start:stop] for chunk in chunks], axis=0)

    flip_in = spread_signs(joined(depth, sent_start), in_byte, depth).astype(BF16)
    flip_out = spread_signs(joined(sent_start, sent_start + 2 * sent_words), out_byte, half)
    mean_part, noise_part = 0.0, 0.0
    step = depth // len(pieces)
    for at, piece in enumerate(pieces):
        tokens = joined(at * step, (at + 1) * step)
        flipped = tokens * flip_in[:, at * step : (at + 1) * step]
        mean_part += jnp.dot(tokens, piece[:, :half], preferred_element_type=F32)
        noise_part += jnp.dot(flipped, piece[:, half:], preferred_element_type=F32)
    held = half // (near * far)
    stride = max(held, GROUP)
    value = spaced((mean_part + flip_out * noise_part).T, held)
    for part in range(cores):
        for turn in range(near):
            at = part * near + turn
            target = ((core ^ part) * near + (near_at ^ turn)) * rows
            whole_ref[:, pl.ds(pl.multiple_of(target, rows), rows)] = value[:, at * rows : (at + 1) * rows]
    read.wait()
    whole_ref[:, cores * near * rows :] = spaced(lags_held[...].T, held)
    for turn, out in enumerate(outs):
        for plane in range(far):
            at = pl.multiple_of((plane * near + (near_at ^ turn)) * stride, stride)
            out[plane * held : (plane + 1) * held, :] = whole_ref[pl.ds(at, held), :].astype(BF16)


def sum_kernel(near, far, rows, *refs):
    parts, outs, whole_ref = refs[:near], refs[near : near + far], refs[-1]
    far_at, near_at = lax.axis_index("far"), lax.axis_index("near")
    held = outs[0].shape[0]
    stride = max(held, GROUP)
    span = parts[0].shape[1] - rows
    total = 0.0
    for turn, part in enumerate(parts):
        total += part[:, :span].astype(F32)
        at = pl.multiple_of(span + (near_at ^ turn) * rows, rows)
        whole_ref[:, pl.ds(at, rows)] = spaced(part[:, span:].astype(F32), held)
    whole_ref[:, :span] = spaced(total, held)
    for turn, out in enumerate(outs):
        at = pl.multiple_of((far_at ^ turn) * stride, stride)
        out[...] = whole_ref[pl.ds(at, held), :].astype(BF16)


def shifted(values, steps):
    moved = pltpu.roll(values, steps, 1)
    at = lax.broadcasted_iota(jnp.int32, values.shape, 1)
    return jnp.where(at >= steps, moved, 0.0)


def lane_roll(values, steps):
    return pltpu.roll(values, steps % LANES, values.ndim - 1) if steps % LANES else values


def mix_kernel(near, far, cores, held, taps_ref, *refs):
    parts, (out_ref, left_ref, sums_ref, done_ref, table_ref, lines_ref) = refs[:-6], refs[-6:]
    tiles = out_ref.shape[0] // cores
    block_rows = cores * GROUP
    tile_rows = SLOTS * block_rows
    rows = tiles * tile_rows
    lane = lax.broadcasted_iota(jnp.int32, (1, LANES), 1)
    pair = 2 * LANES
    span = near * LANES

    def padded(lines):
        if held >= GROUP:
            return lines
        return jnp.concatenate([lines, jnp.zeros((GROUP - held, lines.shape[1]), F32)], axis=0)

    for turn, part in enumerate(parts):
        for plane in range(far // len(parts)):
            own = slice(plane * held, (plane + 1) * held)
            target = pl.multiple_of(((lax.axis_index("far") if len(parts) > 1 else plane) ^ turn) * span, span)
            for line in range(cores + 1):
                piece = part[own, line * span : (line + 1) * span]
                lines_ref[line, :, pl.ds(target, span)] = piece.astype(F32)
    half = held * near * far
    position = lax.axis_index("far") * near + lax.axis_index("near")
    first = lax.axis_index("dp") * half + position * held
    channel = lax.broadcasted_iota(jnp.int32, (held, cores * half), 1) - first
    chosen = channel == lax.broadcasted_iota(jnp.int32, (held, cores * half), 0)
    taps = [
        jnp.sum(jnp.where(chosen, taps_ref[lag : lag + 1, : cores * half], 0.0), axis=1, keepdims=True)
        for lag in range(3)
    ]
    signals = []
    for part in range(cores):
        value = lines_ref[part]
        signal = taps[0] * value
        for lag in range(1, 3):
            signal += taps[lag] * shifted(value, lag)
        signals.append(padded(signal))
    lags = padded(lines_ref[cores])

    for group in range(max(held, GROUP) // GROUP):
        own = slice(group * GROUP, (group + 1) * GROUP)
        for at in range(GROUP):
            row = lags[group * GROUP + at : group * GROUP + at + 1, :]
            repeated = jnp.broadcast_to(row, (BLOCK, row.shape[1]))
            turned = pltpu.roll(repeated, 0, 1, stride=1, stride_axis=0)
            column = lax.broadcasted_iota(jnp.int32, repeated.shape, 1)
            lag = lax.broadcasted_iota(jnp.int32, repeated.shape, 0)
            kept = jnp.where(column >= lag, turned, 0.0).astype(BF16)
            table_ref[at * BLOCK : (at + 1) * BLOCK, :] = kept

        stacked = jnp.concatenate(
            [
                signal[own, a * LANES : (a + 1) * LANES]
                for a in range(tiles)
                for signal in signals
            ],
            axis=0,
        )
        slot_of = lax.broadcasted_iota(jnp.int32, stacked.shape, 0) % SLOTS
        turned = stacked
        for slot in range(1, SLOTS):
            turned = jnp.where(slot_of == slot, lane_roll(stacked, BLOCK * slot), turned)
        spread = jnp.stack(
            [
                lane_roll(turned, -BLOCK * slot).reshape(tiles, block_rows, LANES)
                for slot in range(SLOTS)
            ],
            axis=1,
        ).reshape(rows, LANES)
        owner = lax.broadcasted_iota(jnp.int32, (rows, LANES), 0) % GROUP
        for half in range(GROUP // SLOTS):
            kept = jnp.where(owner == lane // BLOCK + half * SLOTS, spread, 0.0)
            left_ref[:, half * LANES : (half + 1) * LANES] = kept.astype(BF16)

        sums_ref[...] = jnp.zeros_like(sums_ref)
        if tiles <= 16:
            for at in range(tiles // 2):
                start = 2 * at * tile_rows
                partial = jnp.dot(
                    left_ref[: rows - start, :],
                    table_ref[:, at * pair : (at + 1) * pair],
                    preferred_element_type=F32,
                )
                sums_ref[start:rows, :] += partial[:, :LANES]
                sums_ref[start + tile_rows : rows, :] += partial[: rows - start - tile_rows, LANES:]
        else:

            def add(at, _):
                partial = jnp.dot(
                    left_ref[...],
                    table_ref[:, pl.ds(pl.multiple_of(at * pair, pair), pair)],
                    preferred_element_type=F32,
                )
                start = pl.multiple_of(2 * at * tile_rows, tile_rows)
                sums_ref[pl.ds(start, rows), :] += partial[:, :LANES]
                sums_ref[pl.ds(start + tile_rows, rows), :] += partial[:, LANES:]
                return 0

            lax.fori_loop(0, tiles // 2, add, 0)

        sums = sums_ref[:rows, :]
        landed = [0.0] * SLOTS
        for part in range(SLOTS):
            late = sums
            if part:
                ahead = jnp.zeros((part * block_rows, LANES), F32)
                late = jnp.concatenate([ahead, sums[: rows - part * block_rows]], axis=0)
            late = late.reshape(tiles, SLOTS, block_rows, LANES)
            for slot in range(SLOTS):
                moved = late[:, slot].reshape(tiles * block_rows, LANES)
                landed[slot] += lane_roll(moved, BLOCK * (slot - part))
        result = 0.0
        for slot in range(SLOTS):
            result += jnp.where(lane // BLOCK == slot, landed[slot], 0.0)
        result = result.reshape(tiles, cores, GROUP, LANES)
        for part in range(cores):
            done_ref[part * tiles : (part + 1) * tiles, own, :] = result[:, part]

    out_ref[...] = done_ref[:, :held, :].astype(BF16)


def out_kernel(
    gate_ref, before_ref, taps_ref, mixed_ref, source_ref, target_ref,
    gate_held, before_held, taps_held, mixed_held, weight_ref, held_ref, small_sems, read_sems, write_sems,
):
    chunks, channels, step = weight_ref.shape
    small = [
        pltpu.make_async_copy(source, target, small_sems.at[at])
        for at, (source, target) in enumerate(
            (
                (gate_ref, gate_held),
                (before_ref, before_held),
                (taps_ref, taps_held),
                (mixed_ref, mixed_held),
            )
        )
    ]
    reads = [
        pltpu.make_async_copy(
            source_ref.at[:, pl.ds(at * step, step)], weight_ref.at[at], read_sems.at[at]
        )
        for at in range(chunks)
    ]
    for copy in small + reads:
        copy.start()
    for copy in small:
        copy.wait()
    gate = gate_held[...].astype(F32)
    extended = jnp.concatenate([before_held[...].astype(F32), gate], axis=0)
    gate_short = taps_held[0:1, channels:] * gate
    for lag in range(1, 3):
        gate_short += taps_held[lag : lag + 1, channels:] * extended[2 - lag : 2 - lag + gate.shape[0]]
    gated = (gate_short * mixed_held[...].astype(F32).T).astype(BF16)
    writes = []
    for at in range(chunks):
        reads[at].wait()
        held_ref[at] = jnp.dot(gated, weight_ref[at], preferred_element_type=F32).astype(BF16)
        columns = target_ref.at[:, pl.ds(at * step, step)]
        writes.append(pltpu.make_async_copy(held_ref.at[at], columns, write_sems.at[at]))
        writes[-1].start()
    for write in writes:
        write.wait()


def exchanged(value, axis, step):
    return lax.ppermute(value, axis, [(i, i ^ step) for i in range(lax.axis_size(axis))])


def on_device(near, far, tokens, sign_in, sign_out, w_value, w_noise, w_gate, conv_taps, long_filter, w_out):
    rows, width = tokens.shape
    channels = w_gate.shape[1]
    cores = lax.axis_size("dp")
    count = near * far
    half = channels // cores
    held = half // count
    share = w_value.shape[0]
    depth = share * far
    length = count * rows
    near_at, core = lax.axis_index("near"), lax.axis_index("dp")

    packed_width = depth + depth // 8 + channels // 8 + -(channels // 8) % LANES
    if share % LANES == 0 and far == 4:
        first = pl.pallas_call(
            weights_kernel,
            in_specs=[HBM] * 2,
            out_specs=VMEM,
            out_shape=jax.ShapeDtypeStruct((share, 2 * half), BF16),
            scratch_shapes=[pltpu.SemaphoreType.DMA((2,))],
            compiler_params=params(2),
            cost_estimate=cost(0, MIB // 2),
            name="weights",
        )(*in_hbm(w_value, w_noise))
        far_weights = exchanged(first, "far", 2)
        late_tokens, first = lax.optimization_barrier((tokens, first))
        weights, *chunks = pl.pallas_call(
            functools.partial(pack_kernel, near, far),
            in_specs=[HBM] * 5,
            out_specs=[VMEM] * (1 + near),
            out_shape=[jax.ShapeDtypeStruct((share, 2 * half), BF16)]
            + [jax.ShapeDtypeStruct((rows, packed_width), BF16)] * near,
            scratch_shapes=[
                pltpu.VMEM(sign_in.shape, jnp.int32),
                pltpu.VMEM(sign_out.shape[::-1], jnp.int32),
                pltpu.SemaphoreType.DMA((2,)),
                pltpu.SemaphoreType.DMA((2,)),
                pltpu.SemaphoreType.DMA((near * far,)),
            ],
            compiler_params=params(16),
            cost_estimate=cost(2 * rows * 512 * 512, 3 * MIB),
            name="pack",
        )(*in_hbm(late_tokens, sign_in, sign_out.T, w_value, w_noise))
        pieces = [weights, exchanged(weights, "far", 1), far_weights, None]
    else:
        own = lax.dynamic_slice_in_dim(jnp.stack([w_value, w_noise]), core * half, half, axis=2)
        own = own.transpose(1, 0, 2).reshape(share, 2 * half)
        pieces = [lax.all_gather(own, "far", axis=0, tiled=True)]
        order = jnp.arange(near) ^ near_at

        def by_owner(array):
            parts = array.reshape(rows, far, near, -1).transpose(2, 0, 1, 3).reshape(near, rows, -1)
            return jnp.take(parts, order, axis=0)

        words = by_owner(sign_in)
        sent = jnp.broadcast_to(sign_out[None], (near, *sign_out.shape))
        spare = jnp.zeros((near, rows, -(channels // 8) % LANES), jnp.int32)
        signs = [words & 255, words >> 8, sent & 255, sent >> 8, spare]
        packed = [by_owner(tokens)] + [part.astype(BF16) for part in signs]
        chunks = list(jnp.concatenate(packed, axis=2))
    chunks = [chunks[0]] + [exchanged(chunks[step], "near", step) for step in range(1, near)]

    late_tokens = tokens
    if len(pieces) > 1:
        pieces[1], chunks[0] = lax.optimization_barrier((pieces[1], chunks[0]))
        late_tokens, pieces[2] = lax.optimization_barrier((tokens, pieces[2]))
        pieces[3] = exchanged(pieces[2], "far", 1)
    gate_rows = jnp.dot(late_tokens, w_gate, preferred_element_type=F32).astype(BF16)
    gate_rows, *chunks[1:] = lax.optimization_barrier((gate_rows, *chunks[1:]))
    pieces[-1], chunks[-1] = lax.optimization_barrier((pieces[-1], chunks[-1]))
    chunks += [exchanged(chunk, "dp", 1) for chunk in chunks]

    near_shape = jax.ShapeDtypeStruct((far * held, (cores * near + 1) * rows), BF16)
    partial = pl.pallas_call(
        functools.partial(project_kernel, near, far, cores, depth),
        in_specs=[HBM] + [VMEM] * (len(chunks) + len(pieces)),
        out_specs=[VMEM] * near,
        out_shape=[near_shape] * near,
        scratch_shapes=[
            pltpu.VMEM((count * max(held, GROUP), near_shape.shape[1]), F32),
            pltpu.VMEM((rows, half), F32),
            pltpu.SemaphoreType.DMA,
        ],
        compiler_params=params(40),
        cost_estimate=cost(4 * cores * near * rows * depth * half, 6 * MIB),
        name="project",
    )(*in_hbm(long_filter), *chunks, *pieces)
    partial = list(partial)
    last_rows, partial[0] = lax.optimization_barrier((gate_rows[rows - 2 :], partial[0]))
    before = lax.ppermute(last_rows, ("far", "near"), [(i, i + 1) for i in range(count - 1)])
    partial = [partial[0]] + [exchanged(partial[step], "near", step) for step in range(1, near)]
    before, *partial = lax.optimization_barrier((before, *partial))

    far_shape = (held, (cores + 1) * near * rows)
    parts = pl.pallas_call(
        functools.partial(sum_kernel, near, far, rows),
        in_specs=[VMEM] * near,
        out_specs=[VMEM] * far,
        out_shape=[jax.ShapeDtypeStruct(far_shape, BF16)] * far,
        scratch_shapes=[pltpu.VMEM((far * max(held, GROUP), far_shape[1]), F32)],
        compiler_params=params(16),
        cost_estimate=cost(MIB, MIB),
        name="sum",
    )(*partial)
    if far == 4:
        parts = [parts[0]] + [exchanged(parts[turn], "far", turn) for turn in range(1, far)]
    else:
        order = jnp.arange(far) ^ lax.axis_index("far")
        parts = lax.all_to_all(jnp.take(jnp.stack(parts), order, axis=0), "far", 0, 0, tiled=True)
        parts = [parts.reshape(far * held, far_shape[1])]

    tiles = length // LANES
    all_rows = tiles * SLOTS * cores * GROUP
    held_rows = max(held, GROUP)
    mixed = pl.pallas_call(
        functools.partial(mix_kernel, near, far, cores, held),
        in_specs=[VMEM] * (1 + len(parts)),
        out_specs=VMEM,
        out_shape=jax.ShapeDtypeStruct((cores * tiles, held, LANES), BF16),
        scratch_shapes=[
            pltpu.VMEM((all_rows, GROUP * BLOCK), BF16),
            pltpu.VMEM((all_rows * (1 if tiles <= 16 else 2), LANES), F32),
            pltpu.VMEM((cores * tiles, held_rows, LANES), F32),
            pltpu.VMEM((GROUP * BLOCK, length), BF16),
            pltpu.VMEM((cores + 1, held, length), F32),
        ],
        compiler_params=params(48),
        cost_estimate=cost(cores * held_rows * BLOCK * length * 256, 2 * MIB),
        name="mix",
    )(conv_taps, *parts)

    landed = lax.all_to_all(mixed, ("dp", "far", "near"), 0, 0, tiled=True).reshape(channels, rows)
    chunks = 8
    return pl.pallas_call(
        out_kernel,
        in_specs=[ANY] * 4 + [HBM],
        out_specs=HBM,
        out_shape=jax.ShapeDtypeStruct((rows, width), BF16),
        scratch_shapes=[
            pltpu.VMEM(gate_rows.shape, BF16),
            pltpu.VMEM(before.shape, BF16),
            pltpu.VMEM(conv_taps.shape, F32),
            pltpu.VMEM(landed.shape, BF16),
            pltpu.VMEM((chunks, channels, width // chunks), BF16),
            pltpu.VMEM((chunks, rows, width // chunks), BF16),
            pltpu.SemaphoreType.DMA((4,)),
            pltpu.SemaphoreType.DMA((chunks,)),
            pltpu.SemaphoreType.DMA((chunks,)),
        ],
        compiler_params=params(16),
        cost_estimate=cost(2 * rows * width * channels, 5 * MIB),
        name="project_out",
    )(gate_rows, before, conv_taps, landed, *in_hbm(w_out))


def solution(mesh):
    count = mesh.shape["seq"]
    near = 4 if count % 4 == 0 else 1
    far = count // near
    seq_at = mesh.axis_names.index("seq")
    shape = list(mesh.devices.shape)
    shape[seq_at : seq_at + 1] = [far, near]
    names = list(mesh.axis_names)
    names[seq_at : seq_at + 1] = ["far", "near"]
    inner = Mesh(mesh.devices.reshape(shape), tuple(names))
    by_token = P(("dp", "far", "near"), None)
    by_row = P(("far", "near"), None)
    placed = (by_token, by_token, by_token, by_row, by_row, P(), P(), by_row, P())
    return jax.shard_map(
        functools.partial(on_device, near, far),
        mesh=inner,
        in_specs=placed,
        out_specs=by_token,
        check_vma=False,
    )
```

```python
import functools

import jax
import jax.numpy as jnp
from jax import lax
from jax.experimental import pallas as pl
from jax.experimental.pallas import tpu as pltpu
from jax.sharding import Mesh, PartitionSpec as P

F32 = jnp.float32
BF16 = jnp.bfloat16
LANES = 128
GROUP = 8
BLOCK = 32
SLOTS = LANES // BLOCK
MIB = 1 << 20
VMEM = pl.BlockSpec(memory_space=pltpu.VMEM)
SMEM = pl.BlockSpec(memory_space=pltpu.SMEM)
HBM = pl.BlockSpec(memory_space=pltpu.HBM)
ANY = pl.BlockSpec(memory_space=pl.ANY)


def params(mib):
    return pltpu.CompilerParams(vmem_limit_bytes=mib * MIB)


def cost(flops, accessed):
    return pl.CostEstimate(flops=flops, bytes_accessed=accessed, transcendentals=0)


def in_hbm(*arrays):
    return [pltpu.with_memory_space_constraint(array, pltpu.HBM) for array in arrays]


def sign_bytes(packed):
    parts = jnp.concatenate([packed & 255, packed >> 8], axis=1)
    return parts.astype(F32).astype(BF16)


def one_hot(rows, columns, source_of):
    at = lax.broadcasted_iota(jnp.int32, (rows, columns), 0)
    column = lax.broadcasted_iota(jnp.int32, (1, columns), 1)
    return (at == source_of(column)).astype(F32).astype(BF16)


def weights_kernel(value_ref, noise_ref, weight_ref, sems):
    half = weight_ref.shape[1] // 2
    columns = pl.ds(pl.multiple_of(lax.axis_index("dp") * half, half), half)
    copies = []
    for at, source in enumerate((value_ref, noise_ref)):
        target = weight_ref.at[:, at * half : (at + 1) * half]
        copies.append(pltpu.make_async_copy(source.at[:, columns], target, sems.at[at]))
        copies[-1].start()
    for copy in copies:
        copy.wait()


def pack_kernel(
    near, far, tokens_ref, in_ref, sent_ref, lags_ref, value_ref, noise_ref, weight_ref, *refs
):
    outs, (in_held, sent_held, lags_held, read_sems, weight_sems, token_sems) = refs[:near], refs[near:]
    core, far_at, near_at = lax.axis_index("dp"), lax.axis_index("far"), lax.axis_index("near")
    half = weight_ref.shape[1] // 2
    share = weight_ref.shape[0]
    depth = share * far
    words = in_ref.shape[1]
    per_part = words // (near * far)
    own_words = per_part * far

    copies = []
    for at, source in enumerate((value_ref, noise_ref)):
        columns = pl.ds(pl.multiple_of(core * half, half), half)
        target = weight_ref.at[:, at * half : (at + 1) * half]
        copies.append(pltpu.make_async_copy(source.at[:, columns], target, weight_sems.at[at]))
    reads = [
        pltpu.make_async_copy(in_ref, in_held, read_sems.at[0]),
        pltpu.make_async_copy(sent_ref, sent_held, read_sems.at[1]),
        pltpu.make_async_copy(
            lags_ref.at[:, pl.ds(pl.multiple_of(core * half, half), half)], lags_held, read_sems.at[2]
        ),
    ]
    for step, out in enumerate(outs):
        for turn in range(far):
            start = ((far_at ^ turn) * near + (near_at ^ step)) * share
            columns = pl.ds(pl.multiple_of(start, share), share)
            target = out.at[:, turn * share : (turn + 1) * share]
            copies.append(
                pltpu.make_async_copy(tokens_ref.at[:, columns], target, token_sems.at[step * far + turn])
            )
    for copy in reads + copies:
        copy.start()

    def word_of(column):
        step, rest = column // (2 * own_words), column % (2 * own_words)
        part, word = rest // own_words, rest % own_words
        plane = (word // per_part) ^ far_at
        return part * words + (plane * near + (step ^ near_at)) * per_part + word % per_part

    by_word = one_hot(2 * words, 2 * words, word_of)
    reads[0].wait()
    moved = jnp.dot(sign_bytes(in_held[...]), by_word, preferred_element_type=F32).astype(BF16)
    reads[1].wait()
    sent = sign_bytes(sent_held[...].astype(F32).T.astype(jnp.int32))
    held = half // (near * far)

    def channel_of(column):
        step, rest = column // (far * held), column % (far * held)
        return (rest // held * near + (step ^ near_at)) * held + rest % held

    reads[2].wait()
    lags = jnp.dot(
        lags_held[...].astype(BF16), one_hot(half, half, channel_of), preferred_element_type=F32
    ).astype(BF16)
    width, own_lags = 2 * own_words, far * held
    for step, out in enumerate(outs):
        out[:, depth : depth + width] = moved[:, step * width : (step + 1) * width]
        out[:, depth + width :] = jnp.concatenate(
            [sent, lags[:, step * own_lags : (step + 1) * own_lags]], axis=1
        )
    for copy in copies:
        copy.wait()


def spread_signs(pair, byte_of, columns):
    spread = jnp.dot(pair, one_hot(pair.shape[1], columns, byte_of), preferred_element_type=F32)
    mask = 1 << (lax.broadcasted_iota(jnp.int32, (1, columns), 1) & 7)
    return jnp.where((spread.astype(jnp.int32) & mask) != 0, 1.0, -1.0)


def spaced(lines, held):
    if held >= GROUP:
        return lines
    spare = jnp.zeros((GROUP - held, lines.shape[1]), F32)
    split = [lines[at : at + held] for at in range(0, lines.shape[0], held)]
    return jnp.concatenate([part for own in split for part in (own, spare)], axis=0)


def project_kernel(near, far, cores, depth, *refs):
    outs, (out_lags_ref, whole_ref) = refs[-2 - near : -2], refs[-2:]
    chunks, pieces = refs[: near * cores][::-1], refs[near * cores : -2 - near]
    core, near_at = lax.axis_index("dp"), lax.axis_index("near")
    rows = chunks[0].shape[0]
    half = pieces[0].shape[1] // 2
    words = depth // 16
    sent_words = cores * half // 16
    sent_start = depth + 2 * words

    def in_byte(column):
        return (column >> 4) + words * ((column >> 3) & 1)

    def out_byte(column):
        return core * (half // 16) + (column >> 4) + sent_words * ((column >> 3) & 1)

    def joined(start, stop):
        return jnp.concatenate([chunk[:, start:stop] for chunk in chunks], axis=0)

    flip_in = spread_signs(joined(depth, sent_start), in_byte, depth).astype(BF16)
    flip_out = spread_signs(joined(sent_start, sent_start + 2 * sent_words), out_byte, half)
    mean_part, noise_part = 0.0, 0.0
    step = depth // len(pieces)
    for at, piece in enumerate(pieces):
        tokens = joined(at * step, (at + 1) * step)
        flipped = tokens * flip_in[:, at * step : (at + 1) * step]
        mean_part += jnp.dot(tokens, piece[:, :half], preferred_element_type=F32)
        noise_part += jnp.dot(flipped, piece[:, half:], preferred_element_type=F32)
    held = half // (near * far)
    stride = max(held, GROUP)
    value = spaced((mean_part + flip_out * noise_part).T, held)
    for part in range(cores):
        for turn in range(near):
            at = part * near + turn
            target = ((core ^ part) * near + (near_at ^ turn)) * rows
            whole_ref[:, pl.ds(pl.multiple_of(target, rows), rows)] = value[:, at * rows : (at + 1) * rows]
    for turn in range(near):
        own_lags = chunks[turn][:, sent_start + 2 * sent_words :].astype(F32).T
        at = pl.multiple_of((near_at ^ turn) * rows, rows)
        out_lags_ref[:, pl.ds(at, rows)] = own_lags
    for turn, out in enumerate(outs):
        for plane in range(far):
            at = pl.multiple_of((plane * near + (near_at ^ turn)) * stride, stride)
            out[plane * held : (plane + 1) * held, :] = whole_ref[pl.ds(at, held), :].astype(BF16)


def sum_kernel(near, far, lags_ref, *refs):
    parts, outs, whole_ref = refs[:near], refs[near : near + far], refs[-1]
    far_at = lax.axis_index("far")
    held = outs[0].shape[0]
    stride = max(held, GROUP)
    span = parts[0].shape[1]
    total = 0.0
    for part in parts:
        total += part[...].astype(F32)
    whole_ref[:, :span] = spaced(total, held)
    whole_ref[:, span:] = spaced(lags_ref[...], held)
    for turn, out in enumerate(outs):
        at = pl.multiple_of((far_at ^ turn) * stride, stride)
        out[...] = whole_ref[pl.ds(at, held), :].astype(BF16)


def shifted(values, steps):
    moved = pltpu.roll(values, steps, 1)
    at = lax.broadcasted_iota(jnp.int32, values.shape, 1)
    return jnp.where(at >= steps, moved, 0.0)


def lane_roll(values, steps):
    return pltpu.roll(values, steps % LANES, values.ndim - 1) if steps % LANES else values


def mix_kernel(near, far, cores, held, taps_ref, *refs):
    parts, (out_ref, left_ref, sums_ref, done_ref, table_ref, lines_ref) = refs[:-6][::-1], refs[-6:]
    tiles = out_ref.shape[0] // cores
    block_rows = cores * GROUP
    tile_rows = SLOTS * block_rows
    rows = tiles * tile_rows
    lane = lax.broadcasted_iota(jnp.int32, (1, LANES), 1)
    pair = 2 * LANES
    span = near * LANES

    def padded(lines):
        if held >= GROUP:
            return lines
        return jnp.concatenate([lines, jnp.zeros((GROUP - held, lines.shape[1]), F32)], axis=0)

    for turn, part in enumerate(parts):
        for plane in range(far // len(parts)):
            own = slice(plane * held, (plane + 1) * held)
            target = pl.multiple_of(((lax.axis_index("far") if len(parts) > 1 else plane) ^ turn) * span, span)
            for line in range(cores + 1):
                piece = part[own, line * span : (line + 1) * span]
                lines_ref[line, :, pl.ds(target, span)] = piece.astype(F32)
    half = held * near * far
    position = lax.axis_index("far") * near + lax.axis_index("near")
    first = lax.axis_index("dp") * half + position * held
    channel = lax.broadcasted_iota(jnp.int32, (held, cores * half), 1) - first
    chosen = channel == lax.broadcasted_iota(jnp.int32, (held, cores * half), 0)
    taps = [
        jnp.sum(jnp.where(chosen, taps_ref[lag : lag + 1, : cores * half], 0.0), axis=1, keepdims=True)
        for lag in range(3)
    ]
    signals = []
    for part in range(cores):
        value = lines_ref[part]
        signal = taps[0] * value
        for lag in range(1, 3):
            signal += taps[lag] * shifted(value, lag)
        signals.append(padded(signal))
    lags = padded(lines_ref[cores])

    for group in range(max(held, GROUP) // GROUP):
        own = slice(group * GROUP, (group + 1) * GROUP)
        for at in range(GROUP):
            row = lags[group * GROUP + at : group * GROUP + at + 1, :]
            repeated = jnp.broadcast_to(row, (BLOCK, row.shape[1]))
            turned = pltpu.roll(repeated, 0, 1, stride=1, stride_axis=0)
            column = lax.broadcasted_iota(jnp.int32, repeated.shape, 1)
            lag = lax.broadcasted_iota(jnp.int32, repeated.shape, 0)
            kept = jnp.where(column >= lag, turned, 0.0).astype(BF16)
            table_ref[at * BLOCK : (at + 1) * BLOCK, :] = kept

        stacked = jnp.concatenate(
            [
                signal[own, a * LANES : (a + 1) * LANES]
                for a in range(tiles)
                for signal in signals
            ],
            axis=0,
        )
        slot_of = lax.broadcasted_iota(jnp.int32, stacked.shape, 0) % SLOTS
        turned = stacked
        for slot in range(1, SLOTS):
            turned = jnp.where(slot_of == slot, lane_roll(stacked, BLOCK * slot), turned)
        spread = jnp.stack(
            [
                lane_roll(turned, -BLOCK * slot).reshape(tiles, block_rows, LANES)
                for slot in range(SLOTS)
            ],
            axis=1,
        ).reshape(rows, LANES)
        owner = lax.broadcasted_iota(jnp.int32, (rows, LANES), 0) % GROUP
        for half in range(GROUP // SLOTS):
            kept = jnp.where(owner == lane // BLOCK + half * SLOTS, spread, 0.0)
            left_ref[:, half * LANES : (half + 1) * LANES] = kept.astype(BF16)

        sums_ref[...] = jnp.zeros_like(sums_ref)
        if tiles <= 16:
            for at in range(tiles // 2):
                start = 2 * at * tile_rows
                partial = jnp.dot(
                    left_ref[: rows - start, :],
                    table_ref[:, at * pair : (at + 1) * pair],
                    preferred_element_type=F32,
                )
                sums_ref[start:rows, :] += partial[:, :LANES]
                sums_ref[start + tile_rows : rows, :] += partial[: rows - start - tile_rows, LANES:]
        else:

            def add(at, _):
                partial = jnp.dot(
                    left_ref[...],
                    table_ref[:, pl.ds(pl.multiple_of(at * pair, pair), pair)],
                    preferred_element_type=F32,
                )
                start = pl.multiple_of(2 * at * tile_rows, tile_rows)
                sums_ref[pl.ds(start, rows), :] += partial[:, :LANES]
                sums_ref[pl.ds(start + tile_rows, rows), :] += partial[:, LANES:]
                return 0

            lax.fori_loop(0, tiles // 2, add, 0)

        sums = sums_ref[:rows, :]
        landed = [0.0] * SLOTS
        for part in range(SLOTS):
            late = sums
            if part:
                ahead = jnp.zeros((part * block_rows, LANES), F32)
                late = jnp.concatenate([ahead, sums[: rows - part * block_rows]], axis=0)
            late = late.reshape(tiles, SLOTS, block_rows, LANES)
            for slot in range(SLOTS):
                moved = late[:, slot].reshape(tiles * block_rows, LANES)
                landed[slot] += lane_roll(moved, BLOCK * (slot - part))
        result = 0.0
        for slot in range(SLOTS):
            result += jnp.where(lane // BLOCK == slot, landed[slot], 0.0)
        result = result.reshape(tiles, cores, GROUP, LANES)
        for part in range(cores):
            done_ref[part * tiles : (part + 1) * tiles, own, :] = result[:, part]

    out_ref[...] = done_ref[:, :held, :].astype(BF16)


def out_kernel(
    gate_ref, before_ref, taps_ref, mixed_ref, source_ref, target_ref,
    gate_held, before_held, taps_held, mixed_held, weight_ref, held_ref, small_sems, read_sems, write_sems,
):
    chunks, channels, step = weight_ref.shape
    small = [
        pltpu.make_async_copy(source, target, small_sems.at[at])
        for at, (source, target) in enumerate(
            (
                (gate_ref, gate_held),
                (before_ref, before_held),
                (taps_ref, taps_held),
                (mixed_ref, mixed_held),
            )
        )
    ]
    reads = [
        pltpu.make_async_copy(
            source_ref.at[:, pl.ds(at * step, step)], weight_ref.at[at], read_sems.at[at]
        )
        for at in range(chunks)
    ]
    for copy in small + reads:
        copy.start()
    for copy in small:
        copy.wait()
    gate = gate_held[...].astype(F32)
    extended = jnp.concatenate([before_held[...].astype(F32), gate], axis=0)
    gate_short = taps_held[0:1, channels:] * gate
    for lag in range(1, 3):
        gate_short += taps_held[lag : lag + 1, channels:] * extended[2 - lag : 2 - lag + gate.shape[0]]
    gated = (gate_short * mixed_held[...].astype(F32).T).astype(BF16)
    writes = []
    for at in range(chunks):
        reads[at].wait()
        held_ref[at] = jnp.dot(gated, weight_ref[at], preferred_element_type=F32).astype(BF16)
        columns = target_ref.at[:, pl.ds(at * step, step)]
        writes.append(pltpu.make_async_copy(held_ref.at[at], columns, write_sems.at[at]))
        writes[-1].start()
    for write in writes:
        write.wait()


def exchanged(value, axis, step):
    return lax.ppermute(value, axis, [(i, i ^ step) for i in range(lax.axis_size(axis))])


def all_exchanged(values, axis):
    result = list(values)
    for step in reversed(range(1, len(values))):
        result[step] = exchanged(values[step], axis, step)
    return result


def on_device(near, far, tokens, sign_in, sign_out, w_value, w_noise, w_gate, conv_taps, long_filter, w_out):
    rows, width = tokens.shape
    channels = w_gate.shape[1]
    cores = lax.axis_size("dp")
    count = near * far
    half = channels // cores
    held = half // count
    share = w_value.shape[0]
    depth = share * far
    length = count * rows
    near_at, core = lax.axis_index("near"), lax.axis_index("dp")

    lags_start = depth + depth // 8 + channels // 8
    packed_width = lags_start + far * held
    if share % LANES == 0 and far == 4:
        first = pl.pallas_call(
            weights_kernel,
            in_specs=[HBM] * 2,
            out_specs=VMEM,
            out_shape=jax.ShapeDtypeStruct((share, 2 * half), BF16),
            scratch_shapes=[pltpu.SemaphoreType.DMA((2,))],
            compiler_params=params(2),
            cost_estimate=cost(0, MIB // 2),
            name="weights",
        )(*in_hbm(w_value, w_noise))
        far_weights = exchanged(first, "far", 2)
        late_tokens, first = lax.optimization_barrier((tokens, first))
        weights, *chunks = pl.pallas_call(
            functools.partial(pack_kernel, near, far),
            in_specs=[HBM] * 6,
            out_specs=[VMEM] * (1 + near),
            out_shape=[jax.ShapeDtypeStruct((share, 2 * half), BF16)]
            + [jax.ShapeDtypeStruct((rows, packed_width), BF16)] * near,
            scratch_shapes=[
                pltpu.VMEM(sign_in.shape, jnp.int32),
                pltpu.VMEM(sign_out.shape[::-1], jnp.int32),
                pltpu.VMEM((rows, half), F32),
                pltpu.SemaphoreType.DMA((3,)),
                pltpu.SemaphoreType.DMA((2,)),
                pltpu.SemaphoreType.DMA((near * far,)),
            ],
            compiler_params=params(16),
            cost_estimate=cost(2 * rows * 512 * 512, 3 * MIB),
            name="pack",
        )(*in_hbm(late_tokens, sign_in, sign_out.T, long_filter, w_value, w_noise))
        pieces = [weights, exchanged(weights, "far", 1), far_weights, None]
    else:
        own = lax.dynamic_slice_in_dim(jnp.stack([w_value, w_noise]), core * half, half, axis=2)
        own = own.transpose(1, 0, 2).reshape(share, 2 * half)
        pieces = [lax.all_gather(own, "far", axis=0, tiled=True)]
        order = jnp.arange(near) ^ near_at

        def by_owner(array):
            parts = array.reshape(rows, far, near, -1).transpose(2, 0, 1, 3).reshape(near, rows, -1)
            return jnp.take(parts, order, axis=0)

        words = by_owner(sign_in)
        sent = jnp.broadcast_to(sign_out[None], (near, *sign_out.shape))
        own_lags = lax.dynamic_slice_in_dim(long_filter, core * half, half, axis=1)
        signs = [words & 255, words >> 8, sent & 255, sent >> 8, by_owner(own_lags)]
        packed = [by_owner(tokens)] + [part.astype(BF16) for part in signs]
        chunks = list(jnp.concatenate(packed, axis=2))
    chunks = all_exchanged(chunks, "near")

    late_tokens = tokens
    if len(pieces) > 1:
        pieces[1], chunks[0] = lax.optimization_barrier((pieces[1], chunks[0]))
        late_tokens, pieces[2] = lax.optimization_barrier((tokens, pieces[2]))
        pieces[3] = exchanged(pieces[2], "far", 1)
    gate_rows = jnp.dot(late_tokens, w_gate, preferred_element_type=F32).astype(BF16)
    *chunks[:0:-1], gate_rows = lax.optimization_barrier((*chunks[:0:-1], gate_rows))
    pieces[-1], chunks[-1] = lax.optimization_barrier((pieces[-1], chunks[-1]))
    chunks += [exchanged(chunk, "dp", 1) for chunk in chunks]

    near_shape = jax.ShapeDtypeStruct((far * held, cores * near * rows), BF16)
    partial = pl.pallas_call(
        functools.partial(project_kernel, near, far, cores, depth),
        in_specs=[VMEM] * (len(chunks) + len(pieces)),
        out_specs=[VMEM] * (near + 1),
        out_shape=[near_shape] * near + [jax.ShapeDtypeStruct((far * held, near * rows), F32)],
        scratch_shapes=[pltpu.VMEM((count * max(held, GROUP), near_shape.shape[1]), F32)],
        compiler_params=params(40),
        cost_estimate=cost(4 * cores * near * rows * depth * half, 6 * MIB),
        name="project",
    )(*chunks[::-1], *pieces)
    *partial, lags = partial
    last_rows, partial[0] = lax.optimization_barrier((gate_rows[rows - 2 :], partial[0]))
    before = lax.ppermute(last_rows, ("far", "near"), [(i, i + 1) for i in range(count - 1)])
    partial = all_exchanged(partial, "near")
    *partial[::-1], before = lax.optimization_barrier((*partial[::-1], before))

    far_shape = (held, (cores + 1) * near * rows)
    parts = pl.pallas_call(
        functools.partial(sum_kernel, near, far),
        in_specs=[VMEM] * (1 + near),
        out_specs=[VMEM] * far,
        out_shape=[jax.ShapeDtypeStruct(far_shape, BF16)] * far,
        scratch_shapes=[pltpu.VMEM((far * max(held, GROUP), far_shape[1]), F32)],
        compiler_params=params(16),
        cost_estimate=cost(MIB, MIB),
        name="sum",
    )(lags, *partial[::-1])
    if far == 4:
        parts = all_exchanged(parts, "far")
    else:
        order = jnp.arange(far) ^ lax.axis_index("far")
        parts = lax.all_to_all(jnp.take(jnp.stack(parts), order, axis=0), "far", 0, 0, tiled=True)
        parts = [parts.reshape(far * held, far_shape[1])]

    tiles = length // LANES
    all_rows = tiles * SLOTS * cores * GROUP
    held_rows = max(held, GROUP)
    mixed = pl.pallas_call(
        functools.partial(mix_kernel, near, far, cores, held),
        in_specs=[VMEM] * (1 + len(parts)),
        out_specs=VMEM,
        out_shape=jax.ShapeDtypeStruct((cores * tiles, held, LANES), BF16),
        scratch_shapes=[
            pltpu.VMEM((all_rows, GROUP * BLOCK), BF16),
            pltpu.VMEM((all_rows * (1 if tiles <= 16 else 2), LANES), F32),
            pltpu.VMEM((cores * tiles, held_rows, LANES), F32),
            pltpu.VMEM((GROUP * BLOCK, length), BF16),
            pltpu.VMEM((cores + 1, held, length), F32),
        ],
        compiler_params=params(48),
        cost_estimate=cost(cores * held_rows * BLOCK * length * 256, 2 * MIB),
        name="mix",
    )(conv_taps, *parts[::-1])

    landed = lax.all_to_all(mixed, ("dp", "far", "near"), 0, 0, tiled=True).reshape(channels, rows)
    chunks = 8
    return pl.pallas_call(
        out_kernel,
        in_specs=[ANY] * 4 + [HBM],
        out_specs=HBM,
        out_shape=jax.ShapeDtypeStruct((rows, width), BF16),
        scratch_shapes=[
            pltpu.VMEM(gate_rows.shape, BF16),
            pltpu.VMEM(before.shape, BF16),
            pltpu.VMEM(conv_taps.shape, F32),
            pltpu.VMEM(landed.shape, BF16),
            pltpu.VMEM((chunks, channels, width // chunks), BF16),
            pltpu.VMEM((chunks, rows, width // chunks), BF16),
            pltpu.SemaphoreType.DMA((4,)),
            pltpu.SemaphoreType.DMA((chunks,)),
            pltpu.SemaphoreType.DMA((chunks,)),
        ],
        compiler_params=params(16),
        cost_estimate=cost(2 * rows * width * channels, 5 * MIB),
        name="project_out",
    )(gate_rows, before, conv_taps, landed, *in_hbm(w_out))


def solution(mesh):
    count = mesh.shape["seq"]
    near = 4 if count % 4 == 0 else 1
    far = count // near
    seq_at = mesh.axis_names.index("seq")
    shape = list(mesh.devices.shape)
    shape[seq_at : seq_at + 1] = [far, near]
    names = list(mesh.axis_names)
    names[seq_at : seq_at + 1] = ["far", "near"]
    inner = Mesh(mesh.devices.reshape(shape), tuple(names))
    by_token = P(("dp", "far", "near"), None)
    by_row = P(("far", "near"), None)
    placed = (by_token, by_token, by_token, by_row, by_row, P(), P(), by_row, P())
    return jax.shard_map(
        functools.partial(on_device, near, far),
        mesh=inner,
        in_specs=placed,
        out_specs=by_token,
        check_vma=False,
    )
```

```python
import functools

import jax
import jax.numpy as jnp
from jax import lax
from jax.experimental import pallas as pl
from jax.experimental.pallas import tpu as pltpu
from jax.sharding import Mesh, PartitionSpec as P

F32 = jnp.float32
BF16 = jnp.bfloat16
LANES = 128
GROUP = 8
BLOCK = 32
SLOTS = LANES // BLOCK
MIB = 1 << 20
VMEM = pl.BlockSpec(memory_space=pltpu.VMEM)
SMEM = pl.BlockSpec(memory_space=pltpu.SMEM)
HBM = pl.BlockSpec(memory_space=pltpu.HBM)
ANY = pl.BlockSpec(memory_space=pl.ANY)


def params(mib):
    return pltpu.CompilerParams(vmem_limit_bytes=mib * MIB)


def cost(flops, accessed):
    return pl.CostEstimate(flops=flops, bytes_accessed=accessed, transcendentals=0)


def in_hbm(*arrays):
    return [pltpu.with_memory_space_constraint(array, pltpu.HBM) for array in arrays]


def sign_bytes(packed):
    parts = jnp.concatenate([packed & 255, packed >> 8], axis=1)
    return parts.astype(F32).astype(BF16)


def one_hot(rows, columns, source_of):
    at = lax.broadcasted_iota(jnp.int32, (rows, columns), 0)
    column = lax.broadcasted_iota(jnp.int32, (1, columns), 1)
    return (at == source_of(column)).astype(F32).astype(BF16)


def weights_kernel(value_ref, noise_ref, weight_ref, sems):
    half = weight_ref.shape[1] // 2
    columns = pl.ds(pl.multiple_of(lax.axis_index("dp") * half, half), half)
    copies = []
    for at, source in enumerate((value_ref, noise_ref)):
        target = weight_ref.at[:, at * half : (at + 1) * half]
        copies.append(pltpu.make_async_copy(source.at[:, columns], target, sems.at[at]))
        copies[-1].start()
    for copy in copies:
        copy.wait()


def pack_kernel(
    near, far, tokens_ref, in_ref, sent_ref, lags_ref, value_ref, noise_ref, weight_ref, *refs
):
    outs, (in_held, sent_held, lags_held, read_sems, weight_sems, token_sems) = refs[:near], refs[near:]
    core, far_at, near_at = lax.axis_index("dp"), lax.axis_index("far"), lax.axis_index("near")
    half = weight_ref.shape[1] // 2
    share = weight_ref.shape[0]
    depth = share * far
    words = in_ref.shape[1]
    per_part = words // (near * far)
    own_words = per_part * far

    copies = []
    for at, source in enumerate((value_ref, noise_ref)):
        columns = pl.ds(pl.multiple_of(core * half, half), half)
        target = weight_ref.at[:, at * half : (at + 1) * half]
        copies.append(pltpu.make_async_copy(source.at[:, columns], target, weight_sems.at[at]))
    reads = [
        pltpu.make_async_copy(in_ref, in_held, read_sems.at[0]),
        pltpu.make_async_copy(sent_ref, sent_held, read_sems.at[1]),
        pltpu.make_async_copy(
            lags_ref.at[:, pl.ds(pl.multiple_of(core * half, half), half)], lags_held, read_sems.at[2]
        ),
    ]
    for step, out in enumerate(outs):
        for turn in range(far):
            start = ((far_at ^ turn) * near + (near_at ^ step)) * share
            columns = pl.ds(pl.multiple_of(start, share), share)
            target = out.at[:, turn * share : (turn + 1) * share]
            copies.append(
                pltpu.make_async_copy(tokens_ref.at[:, columns], target, token_sems.at[step * far + turn])
            )
    for copy in reads + copies:
        copy.start()

    def word_of(column):
        step, rest = column // (2 * own_words), column % (2 * own_words)
        part, word = rest // own_words, rest % own_words
        plane = (word // per_part) ^ far_at
        return part * words + (plane * near + (step ^ near_at)) * per_part + word % per_part

    by_word = one_hot(2 * words, 2 * words, word_of)
    reads[0].wait()
    moved = jnp.dot(sign_bytes(in_held[...]), by_word, preferred_element_type=F32).astype(BF16)
    reads[1].wait()
    sent = sign_bytes(sent_held[...].astype(F32).T.astype(jnp.int32))
    held = half // (near * far)

    def channel_of(column):
        step, rest = column // (far * held), column % (far * held)
        return (rest // held * near + (step ^ near_at)) * held + rest % held

    reads[2].wait()
    lags = jnp.dot(
        lags_held[...].astype(BF16), one_hot(half, half, channel_of), preferred_element_type=F32
    ).astype(BF16)
    width, own_lags = 2 * own_words, far * held
    for step, out in enumerate(outs):
        out[:, depth : depth + width] = moved[:, step * width : (step + 1) * width]
        out[:, depth + width :] = jnp.concatenate(
            [sent, lags[:, step * own_lags : (step + 1) * own_lags]], axis=1
        )
    for copy in copies:
        copy.wait()


def spread_signs(pair, byte_of, columns):
    spread = jnp.dot(pair, one_hot(pair.shape[1], columns, byte_of), preferred_element_type=F32)
    mask = 1 << (lax.broadcasted_iota(jnp.int32, (1, columns), 1) & 7)
    return jnp.where((spread.astype(jnp.int32) & mask) != 0, 1.0, -1.0)


def spaced(lines, held):
    if held >= GROUP:
        return lines
    spare = jnp.zeros((GROUP - held, lines.shape[1]), F32)
    split = [lines[at : at + held] for at in range(0, lines.shape[0], held)]
    return jnp.concatenate([part for own in split for part in (own, spare)], axis=0)


def project_kernel(near, far, cores, depth, *refs):
    whole_ref, lines_ref = refs[-2:]
    outs, lag_outs = refs[-2 - near - far : -2 - far], refs[-2 - far : -2]
    chunks, pieces = refs[: near * cores][::-1], refs[near * cores : -2 - near - far]
    core, near_at = lax.axis_index("dp"), lax.axis_index("near")
    rows = chunks[0].shape[0]
    half = pieces[0].shape[1] // 2
    words = depth // 16
    sent_words = cores * half // 16
    sent_start = depth + 2 * words

    def in_byte(column):
        return (column >> 4) + words * ((column >> 3) & 1)

    def out_byte(column):
        return core * (half // 16) + (column >> 4) + sent_words * ((column >> 3) & 1)

    def joined(start, stop):
        return jnp.concatenate([chunk[:, start:stop] for chunk in chunks], axis=0)

    flip_in = spread_signs(joined(depth, sent_start), in_byte, depth).astype(BF16)
    flip_out = spread_signs(joined(sent_start, sent_start + 2 * sent_words), out_byte, half)
    mean_part, noise_part = 0.0, 0.0
    step = depth // len(pieces)
    for at, piece in enumerate(pieces):
        tokens = joined(at * step, (at + 1) * step)
        flipped = tokens * flip_in[:, at * step : (at + 1) * step]
        mean_part += jnp.dot(tokens, piece[:, :half], preferred_element_type=F32)
        noise_part += jnp.dot(flipped, piece[:, half:], preferred_element_type=F32)
    held = half // (near * far)
    stride = max(held, GROUP)
    value = spaced((mean_part + flip_out * noise_part).T, held)
    for part in range(cores):
        for turn in range(near):
            at = part * near + turn
            target = ((core ^ part) * near + (near_at ^ turn)) * rows
            whole_ref[:, pl.ds(pl.multiple_of(target, rows), rows)] = value[:, at * rows : (at + 1) * rows]
    for turn in range(near):
        own_lags = chunks[turn][:, sent_start + 2 * sent_words :].astype(F32).T
        at = pl.multiple_of((near_at ^ turn) * rows, rows)
        lines_ref[:, pl.ds(at, rows)] = spaced(own_lags, held)
    for turn, out in enumerate(lag_outs):
        at = pl.multiple_of((lax.axis_index("far") ^ turn) * stride, stride)
        out[...] = lines_ref[pl.ds(at, held), :].astype(BF16)
    for turn, out in enumerate(outs):
        for plane in range(far):
            at = pl.multiple_of((plane * near + (near_at ^ turn)) * stride, stride)
            out[plane * held : (plane + 1) * held, :] = whole_ref[pl.ds(at, held), :].astype(BF16)


def sum_kernel(near, far, *refs):
    parts, outs, whole_ref = refs[:near], refs[near : near + far], refs[-1]
    far_at = lax.axis_index("far")
    held = outs[0].shape[0]
    stride = max(held, GROUP)
    total = 0.0
    for part in parts:
        total += part[...].astype(F32)
    whole_ref[...] = spaced(total, held)
    for turn, out in enumerate(outs):
        at = pl.multiple_of((far_at ^ turn) * stride, stride)
        out[...] = whole_ref[pl.ds(at, held), :].astype(BF16)


def shifted(values, steps):
    moved = pltpu.roll(values, steps, 1)
    at = lax.broadcasted_iota(jnp.int32, values.shape, 1)
    return jnp.where(at >= steps, moved, 0.0)


def lane_roll(values, steps):
    return pltpu.roll(values, steps % LANES, values.ndim - 1) if steps % LANES else values


def laid_out(far, held, parts, lines_ref):
    span = lines_ref.shape[2] // far
    for turn, part in enumerate(parts):
        for plane in range(far // len(parts)):
            own = slice(plane * held, (plane + 1) * held)
            target = ((lax.axis_index("far") if len(parts) > 1 else plane) ^ turn) * span
            for line in range(lines_ref.shape[0]):
                piece = part[own, line * span : (line + 1) * span]
                lines_ref[line, :, pl.ds(pl.multiple_of(target, span), span)] = piece.astype(F32)


def padded(lines):
    if lines.shape[0] >= GROUP:
        return lines
    spare = jnp.zeros((GROUP - lines.shape[0], lines.shape[1]), F32)
    return jnp.concatenate([lines, spare], axis=0)


def table_kernel(far, held, *refs):
    parts, (out_ref, lines_ref) = refs[:-2][::-1], refs[-2:]
    laid_out(far, held, parts, lines_ref)
    lags = padded(lines_ref[0])
    for at in range(lags.shape[0]):
        repeated = jnp.broadcast_to(lags[at : at + 1, :], (BLOCK, lags.shape[1]))
        turned = pltpu.roll(repeated, 0, 1, stride=1, stride_axis=0)
        column = lax.broadcasted_iota(jnp.int32, repeated.shape, 1)
        lag = lax.broadcasted_iota(jnp.int32, repeated.shape, 0)
        kept = jnp.where(column >= lag, turned, 0.0).astype(BF16)
        out_ref[at * BLOCK : (at + 1) * BLOCK, :] = kept


def mix_kernel(near, far, cores, held, taps_ref, full_ref, *refs):
    parts, (out_ref, left_ref, sums_ref, done_ref, lines_ref) = refs[:-5][::-1], refs[-5:]
    tiles = out_ref.shape[0] // cores
    block_rows = cores * GROUP
    tile_rows = SLOTS * block_rows
    rows = tiles * tile_rows
    lane = lax.broadcasted_iota(jnp.int32, (1, LANES), 1)
    pair = 2 * LANES
    laid_out(far, held, parts, lines_ref)
    half = held * near * far
    position = lax.axis_index("far") * near + lax.axis_index("near")
    first = lax.axis_index("dp") * half + position * held
    channel = lax.broadcasted_iota(jnp.int32, (held, cores * half), 1) - first
    chosen = channel == lax.broadcasted_iota(jnp.int32, (held, cores * half), 0)
    taps = [
        jnp.sum(jnp.where(chosen, taps_ref[lag : lag + 1, : cores * half], 0.0), axis=1, keepdims=True)
        for lag in range(3)
    ]
    signals = []
    for part in range(cores):
        value = lines_ref[part]
        signal = taps[0] * value
        for lag in range(1, 3):
            signal += taps[lag] * shifted(value, lag)
        signals.append(padded(signal))

    for group in range(max(held, GROUP) // GROUP):
        own = slice(group * GROUP, (group + 1) * GROUP)
        table_ref = full_ref.at[group * GROUP * BLOCK : (group + 1) * GROUP * BLOCK]
        stacked = jnp.concatenate(
            [
                signal[own, a * LANES : (a + 1) * LANES]
                for a in range(tiles)
                for signal in signals
            ],
            axis=0,
        )
        slot_of = lax.broadcasted_iota(jnp.int32, stacked.shape, 0) % SLOTS
        turned = stacked
        for slot in range(1, SLOTS):
            turned = jnp.where(slot_of == slot, lane_roll(stacked, BLOCK * slot), turned)
        spread = jnp.stack(
            [
                lane_roll(turned, -BLOCK * slot).reshape(tiles, block_rows, LANES)
                for slot in range(SLOTS)
            ],
            axis=1,
        ).reshape(rows, LANES)
        owner = lax.broadcasted_iota(jnp.int32, (rows, LANES), 0) % GROUP
        for half in range(GROUP // SLOTS):
            kept = jnp.where(owner == lane // BLOCK + half * SLOTS, spread, 0.0)
            left_ref[:, half * LANES : (half + 1) * LANES] = kept.astype(BF16)

        sums_ref[...] = jnp.zeros_like(sums_ref)
        if tiles <= 16:
            for at in range(tiles // 2):
                start = 2 * at * tile_rows
                partial = jnp.dot(
                    left_ref[: rows - start, :],
                    table_ref[:, at * pair : (at + 1) * pair],
                    preferred_element_type=F32,
                )
                sums_ref[start:rows, :] += partial[:, :LANES]
                sums_ref[start + tile_rows : rows, :] += partial[: rows - start - tile_rows, LANES:]
        else:

            def add(at, _):
                partial = jnp.dot(
                    left_ref[...],
                    table_ref[:, pl.ds(pl.multiple_of(at * pair, pair), pair)],
                    preferred_element_type=F32,
                )
                start = pl.multiple_of(2 * at * tile_rows, tile_rows)
                sums_ref[pl.ds(start, rows), :] += partial[:, :LANES]
                sums_ref[pl.ds(start + tile_rows, rows), :] += partial[:, LANES:]
                return 0

            lax.fori_loop(0, tiles // 2, add, 0)

        sums = sums_ref[:rows, :]
        landed = [0.0] * SLOTS
        for part in range(SLOTS):
            late = sums
            if part:
                ahead = jnp.zeros((part * block_rows, LANES), F32)
                late = jnp.concatenate([ahead, sums[: rows - part * block_rows]], axis=0)
            late = late.reshape(tiles, SLOTS, block_rows, LANES)
            for slot in range(SLOTS):
                moved = late[:, slot].reshape(tiles * block_rows, LANES)
                landed[slot] += lane_roll(moved, BLOCK * (slot - part))
        result = 0.0
        for slot in range(SLOTS):
            result += jnp.where(lane // BLOCK == slot, landed[slot], 0.0)
        result = result.reshape(tiles, cores, GROUP, LANES)
        for part in range(cores):
            done_ref[part * tiles : (part + 1) * tiles, own, :] = result[:, part]

    out_ref[...] = done_ref[:, :held, :].astype(BF16)


def out_kernel(
    gate_ref, before_ref, taps_ref, mixed_ref, source_ref, target_ref,
    gate_held, before_held, taps_held, mixed_held, weight_ref, held_ref, small_sems, read_sems, write_sems,
):
    chunks, channels, step = weight_ref.shape
    small = [
        pltpu.make_async_copy(source, target, small_sems.at[at])
        for at, (source, target) in enumerate(
            (
                (gate_ref, gate_held),
                (before_ref, before_held),
                (taps_ref, taps_held),
                (mixed_ref, mixed_held),
            )
        )
    ]
    reads = [
        pltpu.make_async_copy(
            source_ref.at[:, pl.ds(at * step, step)], weight_ref.at[at], read_sems.at[at]
        )
        for at in range(chunks)
    ]
    for copy in small + reads:
        copy.start()
    for copy in small:
        copy.wait()
    gate = gate_held[...].astype(F32)
    extended = jnp.concatenate([before_held[...].astype(F32), gate], axis=0)
    gate_short = taps_held[0:1, channels:] * gate
    for lag in range(1, 3):
        gate_short += taps_held[lag : lag + 1, channels:] * extended[2 - lag : 2 - lag + gate.shape[0]]
    gated = (gate_short * mixed_held[...].astype(F32).T).astype(BF16)
    writes = []
    for at in range(chunks):
        reads[at].wait()
        held_ref[at] = jnp.dot(gated, weight_ref[at], preferred_element_type=F32).astype(BF16)
        columns = target_ref.at[:, pl.ds(at * step, step)]
        writes.append(pltpu.make_async_copy(held_ref.at[at], columns, write_sems.at[at]))
        writes[-1].start()
    for write in writes:
        write.wait()


def exchanged(value, axis, step):
    return lax.ppermute(value, axis, [(i, i ^ step) for i in range(lax.axis_size(axis))])


def over_far(values):
    if len(values) == 4:
        return all_exchanged(values, "far")
    order = jnp.arange(len(values)) ^ lax.axis_index("far")
    moved = lax.all_to_all(jnp.take(jnp.stack(values), order, axis=0), "far", 0, 0, tiled=True)
    return [moved.reshape(-1, moved.shape[2])]


def all_exchanged(values, axis):
    result = list(values)
    for step in reversed(range(1, len(values))):
        result[step] = exchanged(values[step], axis, step)
    return result


def on_device(near, far, tokens, sign_in, sign_out, w_value, w_noise, w_gate, conv_taps, long_filter, w_out):
    rows, width = tokens.shape
    channels = w_gate.shape[1]
    cores = lax.axis_size("dp")
    count = near * far
    half = channels // cores
    held = half // count
    share = w_value.shape[0]
    depth = share * far
    length = count * rows
    near_at, core = lax.axis_index("near"), lax.axis_index("dp")

    lags_start = depth + depth // 8 + channels // 8
    packed_width = lags_start + far * held
    if share % LANES == 0 and far == 4:
        first = pl.pallas_call(
            weights_kernel,
            in_specs=[HBM] * 2,
            out_specs=VMEM,
            out_shape=jax.ShapeDtypeStruct((share, 2 * half), BF16),
            scratch_shapes=[pltpu.SemaphoreType.DMA((2,))],
            compiler_params=params(2),
            cost_estimate=cost(0, MIB // 2),
            name="weights",
        )(*in_hbm(w_value, w_noise))
        far_weights = exchanged(first, "far", 2)
        late_tokens, first = lax.optimization_barrier((tokens, first))
        weights, *chunks = pl.pallas_call(
            functools.partial(pack_kernel, near, far),
            in_specs=[HBM] * 6,
            out_specs=[VMEM] * (1 + near),
            out_shape=[jax.ShapeDtypeStruct((share, 2 * half), BF16)]
            + [jax.ShapeDtypeStruct((rows, packed_width), BF16)] * near,
            scratch_shapes=[
                pltpu.VMEM(sign_in.shape, jnp.int32),
                pltpu.VMEM(sign_out.shape[::-1], jnp.int32),
                pltpu.VMEM((rows, half), F32),
                pltpu.SemaphoreType.DMA((3,)),
                pltpu.SemaphoreType.DMA((2,)),
                pltpu.SemaphoreType.DMA((near * far,)),
            ],
            compiler_params=params(16),
            cost_estimate=cost(2 * rows * 512 * 512, 3 * MIB),
            name="pack",
        )(*in_hbm(late_tokens, sign_in, sign_out.T, long_filter, w_value, w_noise))
        pieces = [weights, exchanged(weights, "far", 1), far_weights, None]
    else:
        own = lax.dynamic_slice_in_dim(jnp.stack([w_value, w_noise]), core * half, half, axis=2)
        own = own.transpose(1, 0, 2).reshape(share, 2 * half)
        pieces = [lax.all_gather(own, "far", axis=0, tiled=True)]
        order = jnp.arange(near) ^ near_at

        def by_owner(array):
            parts = array.reshape(rows, far, near, -1).transpose(2, 0, 1, 3).reshape(near, rows, -1)
            return jnp.take(parts, order, axis=0)

        words = by_owner(sign_in)
        sent = jnp.broadcast_to(sign_out[None], (near, *sign_out.shape))
        own_lags = lax.dynamic_slice_in_dim(long_filter, core * half, half, axis=1)
        signs = [words & 255, words >> 8, sent & 255, sent >> 8, by_owner(own_lags)]
        packed = [by_owner(tokens)] + [part.astype(BF16) for part in signs]
        chunks = list(jnp.concatenate(packed, axis=2))
    chunks = all_exchanged(chunks, "near")

    late_tokens = tokens
    if len(pieces) > 1:
        pieces[1], chunks[0] = lax.optimization_barrier((pieces[1], chunks[0]))
        late_tokens, pieces[2] = lax.optimization_barrier((tokens, pieces[2]))
        pieces[3] = exchanged(pieces[2], "far", 1)
    gate_rows = jnp.dot(late_tokens, w_gate, preferred_element_type=F32).astype(BF16)
    *chunks[:0:-1], gate_rows = lax.optimization_barrier((*chunks[:0:-1], gate_rows))
    pieces[-1], chunks[-1] = lax.optimization_barrier((pieces[-1], chunks[-1]))
    chunks += [exchanged(chunk, "dp", 1) for chunk in chunks]

    near_shape = jax.ShapeDtypeStruct((far * held, cores * near * rows), BF16)
    partial = pl.pallas_call(
        functools.partial(project_kernel, near, far, cores, depth),
        in_specs=[VMEM] * (len(chunks) + len(pieces)),
        out_specs=[VMEM] * (near + far),
        out_shape=[near_shape] * near + [jax.ShapeDtypeStruct((held, near * rows), BF16)] * far,
        scratch_shapes=[
            pltpu.VMEM((count * max(held, GROUP), near_shape.shape[1]), F32),
            pltpu.VMEM((far * max(held, GROUP), near * rows), F32),
        ],
        compiler_params=params(40),
        cost_estimate=cost(4 * cores * near * rows * depth * half, 6 * MIB),
        name="project",
    )(*chunks[::-1], *pieces)
    partial, lags = list(partial[:near]), partial[near:]
    lags = over_far(lags)
    last_rows, partial[0] = lax.optimization_barrier((gate_rows[rows - 2 :], partial[0]))
    before = lax.ppermute(last_rows, ("far", "near"), [(i, i + 1) for i in range(count - 1)])
    partial = all_exchanged(partial, "near")
    *partial[::-1], before = lax.optimization_barrier((*partial[::-1], before))

    far_shape = (held, cores * near * rows)
    parts = pl.pallas_call(
        functools.partial(sum_kernel, near, far),
        in_specs=[VMEM] * near,
        out_specs=[VMEM] * far,
        out_shape=[jax.ShapeDtypeStruct(far_shape, BF16)] * far,
        scratch_shapes=[pltpu.VMEM((far * max(held, GROUP), far_shape[1]), F32)],
        compiler_params=params(16),
        cost_estimate=cost(MIB, MIB),
        name="sum",
    )(*partial[::-1])
    parts = over_far(parts)
    held_rows = max(held, GROUP)
    table = pl.pallas_call(
        functools.partial(table_kernel, far, held),
        in_specs=[VMEM] * len(lags),
        out_specs=VMEM,
        out_shape=jax.ShapeDtypeStruct((held_rows * BLOCK, length), BF16),
        scratch_shapes=[pltpu.VMEM((1, held, length), F32)],
        compiler_params=params(16),
        cost_estimate=cost(held_rows * BLOCK * length * 4, 3 * MIB),
        name="table",
    )(*lags[::-1])

    tiles = length // LANES
    all_rows = tiles * SLOTS * cores * GROUP
    mixed = pl.pallas_call(
        functools.partial(mix_kernel, near, far, cores, held),
        in_specs=[VMEM] * (2 + len(parts)),
        out_specs=VMEM,
        out_shape=jax.ShapeDtypeStruct((cores * tiles, held, LANES), BF16),
        scratch_shapes=[
            pltpu.VMEM((all_rows, GROUP * BLOCK), BF16),
            pltpu.VMEM((all_rows * (1 if tiles <= 16 else 2), LANES), F32),
            pltpu.VMEM((cores * tiles, held_rows, LANES), F32),
            pltpu.VMEM((cores, held, length), F32),
        ],
        compiler_params=params(48),
        cost_estimate=cost(cores * held_rows * BLOCK * length * 256, 2 * MIB),
        name="mix",
    )(conv_taps, table, *parts[::-1])

    landed = lax.all_to_all(mixed, ("dp", "far", "near"), 0, 0, tiled=True).reshape(channels, rows)
    chunks = 8
    return pl.pallas_call(
        out_kernel,
        in_specs=[ANY] * 4 + [HBM],
        out_specs=HBM,
        out_shape=jax.ShapeDtypeStruct((rows, width), BF16),
        scratch_shapes=[
            pltpu.VMEM(gate_rows.shape, BF16),
            pltpu.VMEM(before.shape, BF16),
            pltpu.VMEM(conv_taps.shape, F32),
            pltpu.VMEM(landed.shape, BF16),
            pltpu.VMEM((chunks, channels, width // chunks), BF16),
            pltpu.VMEM((chunks, rows, width // chunks), BF16),
            pltpu.SemaphoreType.DMA((4,)),
            pltpu.SemaphoreType.DMA((chunks,)),
            pltpu.SemaphoreType.DMA((chunks,)),
        ],
        compiler_params=params(16),
        cost_estimate=cost(2 * rows * width * channels, 5 * MIB),
        name="project_out",
    )(gate_rows, before, conv_taps, landed, *in_hbm(w_out))


def solution(mesh):
    count = mesh.shape["seq"]
    near = 4 if count % 4 == 0 else 1
    far = count // near
    seq_at = mesh.axis_names.index("seq")
    shape = list(mesh.devices.shape)
    shape[seq_at : seq_at + 1] = [far, near]
    names = list(mesh.axis_names)
    names[seq_at : seq_at + 1] = ["far", "near"]
    inner = Mesh(mesh.devices.reshape(shape), tuple(names))
    by_token = P(("dp", "far", "near"), None)
    by_row = P(("far", "near"), None)
    placed = (by_token, by_token, by_token, by_row, by_row, P(), P(), by_row, P())
    return jax.shard_map(
        functools.partial(on_device, near, far),
        mesh=inner,
        in_specs=placed,
        out_specs=by_token,
        check_vma=False,
    )
```

```python
import functools

import jax
import jax.numpy as jnp
from jax import lax
from jax.experimental import pallas as pl
from jax.experimental.pallas import tpu as pltpu
from jax.sharding import Mesh, PartitionSpec as P

F32 = jnp.float32
BF16 = jnp.bfloat16
LANES = 128
GROUP = 8
BLOCK = 32
SLOTS = LANES // BLOCK
MIB = 1 << 20
VMEM = pl.BlockSpec(memory_space=pltpu.VMEM)
SMEM = pl.BlockSpec(memory_space=pltpu.SMEM)
HBM = pl.BlockSpec(memory_space=pltpu.HBM)
ANY = pl.BlockSpec(memory_space=pl.ANY)


def params(mib):
    return pltpu.CompilerParams(vmem_limit_bytes=mib * MIB)


def cost(flops, accessed):
    return pl.CostEstimate(flops=flops, bytes_accessed=accessed, transcendentals=0)


def in_hbm(*arrays):
    return [pltpu.with_memory_space_constraint(array, pltpu.HBM) for array in arrays]


def sign_bytes(packed):
    parts = jnp.concatenate([packed & 255, packed >> 8], axis=1)
    return parts.astype(F32).astype(BF16)


def one_hot(rows, columns, source_of):
    at = lax.broadcasted_iota(jnp.int32, (rows, columns), 0)
    column = lax.broadcasted_iota(jnp.int32, (1, columns), 1)
    return (at == source_of(column)).astype(F32).astype(BF16)


def weights_kernel(value_ref, noise_ref, weight_ref, sems):
    half = weight_ref.shape[1] // 2
    columns = pl.ds(pl.multiple_of(lax.axis_index("dp") * half, half), half)
    copies = []
    for at, source in enumerate((value_ref, noise_ref)):
        target = weight_ref.at[:, at * half : (at + 1) * half]
        copies.append(pltpu.make_async_copy(source.at[:, columns], target, sems.at[at]))
        copies[-1].start()
    for copy in copies:
        copy.wait()


def pack_kernel(
    near, far, tokens_ref, in_ref, sent_ref, lags_ref, value_ref, noise_ref, weight_ref, *refs
):
    outs, (in_held, sent_held, lags_held, read_sems, weight_sems, token_sems) = refs[:near], refs[near:]
    core, far_at, near_at = lax.axis_index("dp"), lax.axis_index("far"), lax.axis_index("near")
    half = weight_ref.shape[1] // 2
    share = weight_ref.shape[0]
    depth = share * far
    words = in_ref.shape[1]
    per_part = words // (near * far)
    own_words = per_part * far

    copies = []
    for at, source in enumerate((value_ref, noise_ref)):
        columns = pl.ds(pl.multiple_of(core * half, half), half)
        target = weight_ref.at[:, at * half : (at + 1) * half]
        copies.append(pltpu.make_async_copy(source.at[:, columns], target, weight_sems.at[at]))
    reads = [
        pltpu.make_async_copy(in_ref, in_held, read_sems.at[0]),
        pltpu.make_async_copy(sent_ref, sent_held, read_sems.at[1]),
        pltpu.make_async_copy(
            lags_ref.at[:, pl.ds(pl.multiple_of(core * half, half), half)], lags_held, read_sems.at[2]
        ),
    ]
    for step, out in enumerate(outs):
        for turn in range(far):
            start = ((far_at ^ turn) * near + (near_at ^ step)) * share
            columns = pl.ds(pl.multiple_of(start, share), share)
            target = out.at[:, turn * share : (turn + 1) * share]
            copies.append(
                pltpu.make_async_copy(tokens_ref.at[:, columns], target, token_sems.at[step * far + turn])
            )
    for copy in reads + copies:
        copy.start()

    def word_of(column):
        step, rest = column // (2 * own_words), column % (2 * own_words)
        part, word = rest // own_words, rest % own_words
        plane = (word // per_part) ^ far_at
        return part * words + (plane * near + (step ^ near_at)) * per_part + word % per_part

    by_word = one_hot(2 * words, 2 * words, word_of)
    reads[0].wait()
    moved = jnp.dot(sign_bytes(in_held[...]), by_word, preferred_element_type=F32).astype(BF16)
    reads[1].wait()
    sent = sign_bytes(sent_held[...].astype(F32).T.astype(jnp.int32))
    held = half // (near * far)

    def channel_of(column):
        step, rest = column // (far * held), column % (far * held)
        return (rest // held * near + (step ^ near_at)) * held + rest % held

    reads[2].wait()
    lags = jnp.dot(
        lags_held[...].astype(BF16), one_hot(half, half, channel_of), preferred_element_type=F32
    ).astype(BF16)
    width, own_lags = 2 * own_words, far * held
    for step, out in enumerate(outs):
        out[:, depth : depth + width] = moved[:, step * width : (step + 1) * width]
        out[:, depth + width :] = jnp.concatenate(
            [sent, lags[:, step * own_lags : (step + 1) * own_lags]], axis=1
        )
    for copy in copies:
        copy.wait()


def spread_signs(pair, byte_of, columns):
    spread = jnp.dot(pair, one_hot(pair.shape[1], columns, byte_of), preferred_element_type=F32)
    mask = 1 << (lax.broadcasted_iota(jnp.int32, (1, columns), 1) & 7)
    return jnp.where((spread.astype(jnp.int32) & mask) != 0, 1.0, -1.0)


def spaced(lines, held):
    if held >= GROUP:
        return lines
    spare = jnp.zeros((GROUP - held, lines.shape[1]), F32)
    split = [lines[at : at + held] for at in range(0, lines.shape[0], held)]
    return jnp.concatenate([part for own in split for part in (own, spare)], axis=0)


def project_kernel(near, far, cores, depth, *refs):
    outs, (out_lags_ref, whole_ref) = refs[-2 - near : -2], refs[-2:]
    chunks, pieces = refs[: near * cores][::-1], refs[near * cores : -2 - near]
    core, near_at = lax.axis_index("dp"), lax.axis_index("near")
    rows = chunks[0].shape[0]
    half = pieces[0].shape[1] // 2
    words = depth // 16
    sent_words = cores * half // 16
    sent_start = depth + 2 * words

    def in_byte(column):
        return (column >> 4) + words * ((column >> 3) & 1)

    def out_byte(column):
        return core * (half // 16) + (column >> 4) + sent_words * ((column >> 3) & 1)

    def joined(start, stop):
        return jnp.concatenate([chunk[:, start:stop] for chunk in chunks], axis=0)

    flip_in = spread_signs(joined(depth, sent_start), in_byte, depth).astype(BF16)
    flip_out = spread_signs(joined(sent_start, sent_start + 2 * sent_words), out_byte, half)
    mean_part, noise_part = 0.0, 0.0
    step = depth // len(pieces)
    for at, piece in enumerate(pieces):
        tokens = joined(at * step, (at + 1) * step)
        flipped = tokens * flip_in[:, at * step : (at + 1) * step]
        mean_part += jnp.dot(tokens, piece[:, :half], preferred_element_type=F32)
        noise_part += jnp.dot(flipped, piece[:, half:], preferred_element_type=F32)
    held = half // (near * far)
    stride = max(held, GROUP)
    value = spaced((mean_part + flip_out * noise_part).T, held)
    for part in range(cores):
        for turn in range(near):
            at = part * near + turn
            target = ((core ^ part) * near + (near_at ^ turn)) * rows
            whole_ref[:, pl.ds(pl.multiple_of(target, rows), rows)] = value[:, at * rows : (at + 1) * rows]
    for turn in range(near):
        own_lags = chunks[turn][:, sent_start + 2 * sent_words :].astype(F32).T
        at = pl.multiple_of((near_at ^ turn) * rows, rows)
        out_lags_ref[:, pl.ds(at, rows)] = own_lags
    for turn, out in enumerate(outs):
        for plane in range(far):
            at = pl.multiple_of((plane * near + (near_at ^ turn)) * stride, stride)
            out[plane * held : (plane + 1) * held, :] = whole_ref[pl.ds(at, held), :].astype(BF16)


def sum_kernel(near, far, lags_ref, *refs):
    parts, outs, whole_ref = refs[:near], refs[near : near + far], refs[-1]
    far_at = lax.axis_index("far")
    held = outs[0].shape[0]
    stride = max(held, GROUP)
    span = parts[0].shape[1]
    total = 0.0
    for part in parts:
        total += part[...].astype(F32)
    whole_ref[:, :span] = spaced(total, held)
    whole_ref[:, span:] = spaced(lags_ref[...], held)
    for turn, out in enumerate(outs):
        at = pl.multiple_of((far_at ^ turn) * stride, stride)
        out[...] = whole_ref[pl.ds(at, held), :].astype(BF16)


def shifted(values, steps):
    moved = pltpu.roll(values, steps, 1)
    at = lax.broadcasted_iota(jnp.int32, values.shape, 1)
    return jnp.where(at >= steps, moved, 0.0)


def lane_roll(values, steps):
    return pltpu.roll(values, steps % LANES, values.ndim - 1) if steps % LANES else values


def mix_kernel(near, far, cores, held, taps_ref, *refs):
    parts, (out_ref, left_ref, sums_ref, done_ref, table_ref, lines_ref) = refs[:-6][::-1], refs[-6:]
    tiles = out_ref.shape[0] // cores
    block_rows = cores * GROUP
    tile_rows = SLOTS * block_rows
    rows = tiles * tile_rows
    lane = lax.broadcasted_iota(jnp.int32, (1, LANES), 1)
    pair = 2 * LANES
    span = near * LANES

    def padded(lines):
        if held >= GROUP:
            return lines
        return jnp.concatenate([lines, jnp.zeros((GROUP - held, lines.shape[1]), F32)], axis=0)

    for turn, part in enumerate(parts):
        for plane in range(far // len(parts)):
            own = slice(plane * held, (plane + 1) * held)
            target = pl.multiple_of(((lax.axis_index("far") if len(parts) > 1 else plane) ^ turn) * span, span)
            for line in range(cores + 1):
                piece = part[own, line * span : (line + 1) * span]
                lines_ref[line, :, pl.ds(target, span)] = piece.astype(F32)
    half = held * near * far
    position = lax.axis_index("far") * near + lax.axis_index("near")
    first = lax.axis_index("dp") * half + position * held
    channel = lax.broadcasted_iota(jnp.int32, (held, cores * half), 1) - first
    chosen = channel == lax.broadcasted_iota(jnp.int32, (held, cores * half), 0)
    taps = [
        jnp.sum(jnp.where(chosen, taps_ref[lag : lag + 1, : cores * half], 0.0), axis=1, keepdims=True)
        for lag in range(3)
    ]
    signals = []
    for part in range(cores):
        value = lines_ref[part]
        signal = taps[0] * value
        for lag in range(1, 3):
            signal += taps[lag] * shifted(value, lag)
        signals.append(padded(signal))
    lags = padded(lines_ref[cores])

    for group in range(max(held, GROUP) // GROUP):
        own = slice(group * GROUP, (group + 1) * GROUP)
        for at in range(GROUP):
            row = lags[group * GROUP + at : group * GROUP + at + 1, :]
            repeated = jnp.broadcast_to(row, (BLOCK, row.shape[1]))
            turned = pltpu.roll(repeated, 0, 1, stride=1, stride_axis=0)
            column = lax.broadcasted_iota(jnp.int32, repeated.shape, 1)
            lag = lax.broadcasted_iota(jnp.int32, repeated.shape, 0)
            kept = jnp.where(column >= lag, turned, 0.0).astype(BF16)
            table_ref[at * BLOCK : (at + 1) * BLOCK, :] = kept

        stacked = jnp.concatenate(
            [
                signal[own, a * LANES : (a + 1) * LANES]
                for a in range(tiles)
                for signal in signals
            ],
            axis=0,
        )
        slot_of = lax.broadcasted_iota(jnp.int32, stacked.shape, 0) % SLOTS
        turned = stacked
        for slot in range(1, SLOTS):
            turned = jnp.where(slot_of == slot, lane_roll(stacked, BLOCK * slot), turned)
        spread = jnp.stack(
            [
                lane_roll(turned, -BLOCK * slot).reshape(tiles, block_rows, LANES)
                for slot in range(SLOTS)
            ],
            axis=1,
        ).reshape(rows, LANES)
        owner = lax.broadcasted_iota(jnp.int32, (rows, LANES), 0) % GROUP
        for half in range(GROUP // SLOTS):
            kept = jnp.where(owner == lane // BLOCK + half * SLOTS, spread, 0.0)
            left_ref[:, half * LANES : (half + 1) * LANES] = kept.astype(BF16)

        sums_ref[...] = jnp.zeros_like(sums_ref)
        if tiles <= 16:
            for at in range(tiles // 2):
                start = 2 * at * tile_rows
                partial = jnp.dot(
                    left_ref[: rows - start, :],
                    table_ref[:, at * pair : (at + 1) * pair],
                    preferred_element_type=F32,
                )
                sums_ref[start:rows, :] += partial[:, :LANES]
                sums_ref[start + tile_rows : rows, :] += partial[: rows - start - tile_rows, LANES:]
        else:

            def add(at, _):
                partial = jnp.dot(
                    left_ref[...],
                    table_ref[:, pl.ds(pl.multiple_of(at * pair, pair), pair)],
                    preferred_element_type=F32,
                )
                start = pl.multiple_of(2 * at * tile_rows, tile_rows)
                sums_ref[pl.ds(start, rows), :] += partial[:, :LANES]
                sums_ref[pl.ds(start + tile_rows, rows), :] += partial[:, LANES:]
                return 0

            lax.fori_loop(0, tiles // 2, add, 0)

        sums = sums_ref[:rows, :]
        landed = [0.0] * SLOTS
        for part in range(SLOTS):
            late = sums
            if part:
                ahead = jnp.zeros((part * block_rows, LANES), F32)
                late = jnp.concatenate([ahead, sums[: rows - part * block_rows]], axis=0)
            late = late.reshape(tiles, SLOTS, block_rows, LANES)
            for slot in range(SLOTS):
                moved = late[:, slot].reshape(tiles * block_rows, LANES)
                landed[slot] += lane_roll(moved, BLOCK * (slot - part))
        result = 0.0
        for slot in range(SLOTS):
            result += jnp.where(lane // BLOCK == slot, landed[slot], 0.0)
        result = result.reshape(tiles, cores, GROUP, LANES)
        for part in range(cores):
            done_ref[part * tiles : (part + 1) * tiles, own, :] = result[:, part]

    out_ref[...] = done_ref[:, :held, :].astype(BF16)


def out_kernel(
    gate_ref, even_ref, odd_ref, taps_ref, mixed_ref, source_ref, target_ref,
    gate_held, even_held, odd_held, taps_held, mixed_held, weight_ref, held_ref, small_sems, read_sems, write_sems,
):
    chunks, channels, step = weight_ref.shape
    small = [
        pltpu.make_async_copy(source, target, small_sems.at[at])
        for at, (source, target) in enumerate(
            (
                (gate_ref, gate_held),
                (even_ref, even_held),
                (odd_ref, odd_held),
                (taps_ref, taps_held),
                (mixed_ref, mixed_held),
            )
        )
    ]
    reads = [
        pltpu.make_async_copy(
            source_ref.at[:, pl.ds(at * step, step)], weight_ref.at[at], read_sems.at[at]
        )
        for at in range(chunks)
    ]
    for copy in small + reads:
        copy.start()
    for copy in small:
        copy.wait()
    gate = gate_held[...].astype(F32)
    position = lax.axis_index("far") * lax.axis_size("near") + lax.axis_index("near")
    odd = jnp.full((1, 1), position & 1, jnp.int32) != 0
    before = jnp.where(odd, odd_held[...].astype(F32), even_held[...].astype(F32))
    extended = jnp.concatenate([before, gate], axis=0)
    gate_short = taps_held[0:1, channels:] * gate
    for lag in range(1, 3):
        gate_short += taps_held[lag : lag + 1, channels:] * extended[2 - lag : 2 - lag + gate.shape[0]]
    gated = (gate_short * mixed_held[...].astype(F32).T).astype(BF16)
    writes = []
    for at in range(chunks):
        reads[at].wait()
        held_ref[at] = jnp.dot(gated, weight_ref[at], preferred_element_type=F32).astype(BF16)
        columns = target_ref.at[:, pl.ds(at * step, step)]
        writes.append(pltpu.make_async_copy(held_ref.at[at], columns, write_sems.at[at]))
        writes[-1].start()
    for write in writes:
        write.wait()


def exchanged(value, axis, step):
    return lax.ppermute(value, axis, [(i, i ^ step) for i in range(lax.axis_size(axis))])


def all_exchanged(values, axis):
    result = list(values)
    for step in reversed(range(1, len(values))):
        result[step] = exchanged(values[step], axis, step)
    return result


def on_device(near, far, tokens, sign_in, sign_out, w_value, w_noise, w_gate, conv_taps, long_filter, w_out):
    rows, width = tokens.shape
    channels = w_gate.shape[1]
    cores = lax.axis_size("dp")
    count = near * far
    half = channels // cores
    held = half // count
    share = w_value.shape[0]
    depth = share * far
    length = count * rows
    near_at, core = lax.axis_index("near"), lax.axis_index("dp")

    lags_start = depth + depth // 8 + channels // 8
    packed_width = lags_start + far * held
    if share % LANES == 0 and far == 4:
        first = pl.pallas_call(
            weights_kernel,
            in_specs=[HBM] * 2,
            out_specs=VMEM,
            out_shape=jax.ShapeDtypeStruct((share, 2 * half), BF16),
            scratch_shapes=[pltpu.SemaphoreType.DMA((2,))],
            compiler_params=params(2),
            cost_estimate=cost(0, MIB // 2),
            name="weights",
        )(*in_hbm(w_value, w_noise))
        far_weights = exchanged(first, "far", 2)
        late_tokens, first = lax.optimization_barrier((tokens, first))
        weights, *chunks = pl.pallas_call(
            functools.partial(pack_kernel, near, far),
            in_specs=[HBM] * 6,
            out_specs=[VMEM] * (1 + near),
            out_shape=[jax.ShapeDtypeStruct((share, 2 * half), BF16)]
            + [jax.ShapeDtypeStruct((rows, packed_width), BF16)] * near,
            scratch_shapes=[
                pltpu.VMEM(sign_in.shape, jnp.int32),
                pltpu.VMEM(sign_out.shape[::-1], jnp.int32),
                pltpu.VMEM((rows, half), F32),
                pltpu.SemaphoreType.DMA((3,)),
                pltpu.SemaphoreType.DMA((2,)),
                pltpu.SemaphoreType.DMA((near * far,)),
            ],
            compiler_params=params(16),
            cost_estimate=cost(2 * rows * 512 * 512, 3 * MIB),
            name="pack",
        )(*in_hbm(late_tokens, sign_in, sign_out.T, long_filter, w_value, w_noise))
        pieces = [weights, exchanged(weights, "far", 1), far_weights, None]
    else:
        own = lax.dynamic_slice_in_dim(jnp.stack([w_value, w_noise]), core * half, half, axis=2)
        own = own.transpose(1, 0, 2).reshape(share, 2 * half)
        pieces = [lax.all_gather(own, "far", axis=0, tiled=True)]
        order = jnp.arange(near) ^ near_at

        def by_owner(array):
            parts = array.reshape(rows, far, near, -1).transpose(2, 0, 1, 3).reshape(near, rows, -1)
            return jnp.take(parts, order, axis=0)

        words = by_owner(sign_in)
        sent = jnp.broadcast_to(sign_out[None], (near, *sign_out.shape))
        own_lags = lax.dynamic_slice_in_dim(long_filter, core * half, half, axis=1)
        signs = [words & 255, words >> 8, sent & 255, sent >> 8, by_owner(own_lags)]
        packed = [by_owner(tokens)] + [part.astype(BF16) for part in signs]
        chunks = list(jnp.concatenate(packed, axis=2))
    chunks = all_exchanged(chunks, "near")

    late_tokens = tokens
    if len(pieces) > 1:
        pieces[1], chunks[0] = lax.optimization_barrier((pieces[1], chunks[0]))
        late_tokens, pieces[2] = lax.optimization_barrier((tokens, pieces[2]))
        pieces[3] = exchanged(pieces[2], "far", 1)
    gate_rows = jnp.dot(late_tokens, w_gate, preferred_element_type=F32).astype(BF16)
    *chunks[:0:-1], gate_rows = lax.optimization_barrier((*chunks[:0:-1], gate_rows))
    pieces[-1], chunks[-1] = lax.optimization_barrier((pieces[-1], chunks[-1]))
    chunks += [exchanged(chunk, "dp", 1) for chunk in chunks]

    near_shape = jax.ShapeDtypeStruct((far * held, cores * near * rows), BF16)
    partial = pl.pallas_call(
        functools.partial(project_kernel, near, far, cores, depth),
        in_specs=[VMEM] * (len(chunks) + len(pieces)),
        out_specs=[VMEM] * (near + 1),
        out_shape=[near_shape] * near + [jax.ShapeDtypeStruct((far * held, near * rows), F32)],
        scratch_shapes=[pltpu.VMEM((count * max(held, GROUP), near_shape.shape[1]), F32)],
        compiler_params=params(40),
        cost_estimate=cost(4 * cores * near * rows * depth * half, 6 * MIB),
        name="project",
    )(*chunks[::-1], *pieces)
    *partial, lags = partial
    last_rows, partial[0] = lax.optimization_barrier((gate_rows[rows - 2 :], partial[0]))
    pairs = [(i, i + 1) for i in range(count - 1)]
    before = [
        lax.ppermute(
            last_rows, ("far", "near"), [pair for i, j in pairs[first::2] for pair in ((i, j), (j, i))]
        )
        for first in (1, 0)
    ]
    partial = all_exchanged(partial, "near")
    *partial[::-1], before = lax.optimization_barrier((*partial[::-1], before))

    far_shape = (held, (cores + 1) * near * rows)
    parts = pl.pallas_call(
        functools.partial(sum_kernel, near, far),
        in_specs=[VMEM] * (1 + near),
        out_specs=[VMEM] * far,
        out_shape=[jax.ShapeDtypeStruct(far_shape, BF16)] * far,
        scratch_shapes=[pltpu.VMEM((far * max(held, GROUP), far_shape[1]), F32)],
        compiler_params=params(16),
        cost_estimate=cost(MIB, MIB),
        name="sum",
    )(lags, *partial[::-1])
    if far == 4:
        parts = all_exchanged(parts, "far")
    else:
        order = jnp.arange(far) ^ lax.axis_index("far")
        parts = lax.all_to_all(jnp.take(jnp.stack(parts), order, axis=0), "far", 0, 0, tiled=True)
        parts = [parts.reshape(far * held, far_shape[1])]

    tiles = length // LANES
    all_rows = tiles * SLOTS * cores * GROUP
    held_rows = max(held, GROUP)
    mixed = pl.pallas_call(
        functools.partial(mix_kernel, near, far, cores, held),
        in_specs=[VMEM] * (1 + len(parts)),
        out_specs=VMEM,
        out_shape=jax.ShapeDtypeStruct((cores * tiles, held, LANES), BF16),
        scratch_shapes=[
            pltpu.VMEM((all_rows, GROUP * BLOCK), BF16),
            pltpu.VMEM((all_rows * (1 if tiles <= 16 else 2), LANES), F32),
            pltpu.VMEM((cores * tiles, held_rows, LANES), F32),
            pltpu.VMEM((GROUP * BLOCK, length), BF16),
            pltpu.VMEM((cores + 1, held, length), F32),
        ],
        compiler_params=params(48),
        cost_estimate=cost(cores * held_rows * BLOCK * length * 256, 2 * MIB),
        name="mix",
    )(conv_taps, *parts[::-1])

    landed = lax.all_to_all(mixed, ("dp", "far", "near"), 0, 0, tiled=True).reshape(channels, rows)
    chunks = 8
    return pl.pallas_call(
        out_kernel,
        in_specs=[ANY] * 5 + [HBM],
        out_specs=HBM,
        out_shape=jax.ShapeDtypeStruct((rows, width), BF16),
        scratch_shapes=[
            pltpu.VMEM(gate_rows.shape, BF16),
            pltpu.VMEM(before[0].shape, BF16),
            pltpu.VMEM(before[1].shape, BF16),
            pltpu.VMEM(conv_taps.shape, F32),
            pltpu.VMEM(landed.shape, BF16),
            pltpu.VMEM((chunks, channels, width // chunks), BF16),
            pltpu.VMEM((chunks, rows, width // chunks), BF16),
            pltpu.SemaphoreType.DMA((5,)),
            pltpu.SemaphoreType.DMA((chunks,)),
            pltpu.SemaphoreType.DMA((chunks,)),
        ],
        compiler_params=params(16),
        cost_estimate=cost(2 * rows * width * channels, 5 * MIB),
        name="project_out",
    )(gate_rows, *before, conv_taps, landed, *in_hbm(w_out))


def solution(mesh):
    count = mesh.shape["seq"]
    near = 4 if count % 4 == 0 else 1
    far = count // near
    seq_at = mesh.axis_names.index("seq")
    shape = list(mesh.devices.shape)
    shape[seq_at : seq_at + 1] = [far, near]
    names = list(mesh.axis_names)
    names[seq_at : seq_at + 1] = ["far", "near"]
    inner = Mesh(mesh.devices.reshape(shape), tuple(names))
    by_token = P(("dp", "far", "near"), None)
    by_row = P(("far", "near"), None)
    placed = (by_token, by_token, by_token, by_row, by_row, P(), P(), by_row, P())
    return jax.shard_map(
        functools.partial(on_device, near, far),
        mesh=inner,
        in_specs=placed,
        out_specs=by_token,
        check_vma=False,
    )
```

```python
import functools

import jax
import jax.numpy as jnp
from jax import lax
from jax.experimental import pallas as pl
from jax.experimental.pallas import tpu as pltpu
from jax.sharding import Mesh, PartitionSpec as P

F32 = jnp.float32
BF16 = jnp.bfloat16
LANES = 128
GROUP = 8
BLOCK = 32
SLOTS = LANES // BLOCK
MIB = 1 << 20
VMEM = pl.BlockSpec(memory_space=pltpu.VMEM)
SMEM = pl.BlockSpec(memory_space=pltpu.SMEM)
HBM = pl.BlockSpec(memory_space=pltpu.HBM)
ANY = pl.BlockSpec(memory_space=pl.ANY)


def params(mib):
    return pltpu.CompilerParams(vmem_limit_bytes=mib * MIB)


def cost(flops, accessed):
    return pl.CostEstimate(flops=flops, bytes_accessed=accessed, transcendentals=0)


def in_hbm(*arrays):
    return [pltpu.with_memory_space_constraint(array, pltpu.HBM) for array in arrays]


def sign_bytes(packed):
    parts = jnp.concatenate([packed & 255, packed >> 8], axis=1)
    return parts.astype(F32).astype(BF16)


def one_hot(rows, columns, source_of):
    at = lax.broadcasted_iota(jnp.int32, (rows, columns), 0)
    column = lax.broadcasted_iota(jnp.int32, (1, columns), 1)
    return (at == source_of(column)).astype(F32).astype(BF16)


def weights_kernel(value_ref, noise_ref, weight_ref, sems):
    half = weight_ref.shape[1] // 2
    columns = pl.ds(pl.multiple_of(lax.axis_index("dp") * half, half), half)
    copies = []
    for at, source in enumerate((value_ref, noise_ref)):
        target = weight_ref.at[:, at * half : (at + 1) * half]
        copies.append(pltpu.make_async_copy(source.at[:, columns], target, sems.at[at]))
        copies[-1].start()
    for copy in copies:
        copy.wait()


def pack_kernel(
    near, far, tokens_ref, in_ref, sent_ref, lags_ref, value_ref, noise_ref, weight_ref, *refs
):
    outs, (in_held, sent_held, lags_held, read_sems, weight_sems, token_sems) = refs[:near], refs[near:]
    core, far_at, near_at = lax.axis_index("dp"), lax.axis_index("far"), lax.axis_index("near")
    half = weight_ref.shape[1] // 2
    share = weight_ref.shape[0]
    depth = share * far
    words = in_ref.shape[1]
    per_part = words // (near * far)
    own_words = per_part * far

    copies = []
    for at, source in enumerate((value_ref, noise_ref)):
        columns = pl.ds(pl.multiple_of(core * half, half), half)
        target = weight_ref.at[:, at * half : (at + 1) * half]
        copies.append(pltpu.make_async_copy(source.at[:, columns], target, weight_sems.at[at]))
    reads = [
        pltpu.make_async_copy(in_ref, in_held, read_sems.at[0]),
        pltpu.make_async_copy(sent_ref, sent_held, read_sems.at[1]),
        pltpu.make_async_copy(
            lags_ref.at[:, pl.ds(pl.multiple_of(core * half, half), half)], lags_held, read_sems.at[2]
        ),
    ]
    for step, out in enumerate(outs):
        for turn in range(far):
            start = ((far_at ^ turn) * near + (near_at ^ step)) * share
            columns = pl.ds(pl.multiple_of(start, share), share)
            target = out.at[:, turn * share : (turn + 1) * share]
            copies.append(
                pltpu.make_async_copy(tokens_ref.at[:, columns], target, token_sems.at[step * far + turn])
            )
    for copy in reads + copies:
        copy.start()

    def word_of(column):
        step, rest = column // (2 * own_words), column % (2 * own_words)
        part, word = rest // own_words, rest % own_words
        plane = (word // per_part) ^ far_at
        return part * words + (plane * near + (step ^ near_at)) * per_part + word % per_part

    by_word = one_hot(2 * words, 2 * words, word_of)
    reads[0].wait()
    moved = jnp.dot(sign_bytes(in_held[...]), by_word, preferred_element_type=F32).astype(BF16)
    reads[1].wait()
    sent = sign_bytes(sent_held[...].astype(F32).T.astype(jnp.int32))
    held = half // (near * far)

    def channel_of(column):
        step, rest = column // (far * held), column % (far * held)
        return (rest // held * near + (step ^ near_at)) * held + rest % held

    reads[2].wait()
    lags = jnp.dot(
        lags_held[...].astype(BF16), one_hot(half, half, channel_of), preferred_element_type=F32
    ).astype(BF16)
    width, own_lags = 2 * own_words, far * held
    for step, out in enumerate(outs):
        out[:, depth : depth + width] = moved[:, step * width : (step + 1) * width]
        out[:, depth + width :] = jnp.concatenate(
            [sent, lags[:, step * own_lags : (step + 1) * own_lags]], axis=1
        )
    for copy in copies:
        copy.wait()


def spread_signs(pair, byte_of, columns):
    spread = jnp.dot(pair, one_hot(pair.shape[1], columns, byte_of), preferred_element_type=F32)
    mask = 1 << (lax.broadcasted_iota(jnp.int32, (1, columns), 1) & 7)
    return jnp.where((spread.astype(jnp.int32) & mask) != 0, 1.0, -1.0)


def spaced(lines, held):
    if held >= GROUP:
        return lines
    spare = jnp.zeros((GROUP - held, lines.shape[1]), F32)
    split = [lines[at : at + held] for at in range(0, lines.shape[0], held)]
    return jnp.concatenate([part for own in split for part in (own, spare)], axis=0)


def joined(chunks, start, stop):
    return jnp.concatenate([chunk[:, start:stop] for chunk in chunks], axis=0)


def flips(chunks, depth, cores, half):
    core = lax.axis_index("dp")
    words = depth // 16
    sent_words = cores * half // 16
    sent_start = depth + 2 * words

    def in_byte(column):
        return (column >> 4) + words * ((column >> 3) & 1)

    def out_byte(column):
        return core * (half // 16) + (column >> 4) + sent_words * ((column >> 3) & 1)

    flip_in = spread_signs(joined(chunks, depth, sent_start), in_byte, depth).astype(BF16)
    sent = joined(chunks, sent_start, sent_start + 2 * sent_words)
    return flip_in, spread_signs(sent, out_byte, half)


def products(chunks, flip_in, pieces, half):
    mean_part, noise_part = 0.0, 0.0
    for at, piece in enumerate(pieces):
        own = slice(at * piece.shape[0], (at + 1) * piece.shape[0])
        tokens = joined(chunks, own.start, own.stop)
        mean_part += jnp.dot(tokens, piece[:, :half], preferred_element_type=F32)
        noise_part += jnp.dot(tokens * flip_in[:, own], piece[:, half:], preferred_element_type=F32)
    return mean_part, noise_part


def project_kernel(near, cores, depth, *refs):
    mean_ref, noise_ref, flip_ref, flipped_ref, lags_ref = refs[-5:]
    count = near * cores - 1
    chunks, pieces = refs[:count][::-1], refs[count:-5]
    rows = chunks[0].shape[0]
    half = pieces[0].shape[1] // 2
    step = pieces[0].shape[0]
    flip_in, flip_out = flips(chunks, depth, cores, half)
    flip_ref[...] = flip_out.astype(BF16)
    flipped_ref[...] = joined(chunks, depth - step, depth) * flip_in[:, depth - step :]
    mean_ref[...], noise_ref[...] = products(chunks, flip_in, pieces, half)
    for turn in range(near):
        own_lags = chunks[turn][:, chunks[turn].shape[1] - lags_ref.shape[0] :].astype(F32).T
        at = pl.multiple_of((lax.axis_index("near") ^ turn) * rows, rows)
        lags_ref[:, pl.ds(at, rows)] = own_lags


def finish_kernel(near, far, cores, depth, mean_ref, noise_ref, flip_ref, flipped_ref, *refs):
    outs, whole_ref = refs[-1 - near : -1], refs[-1]
    chunks, pieces = refs[: near * cores][::-1], refs[near * cores : -1 - near]
    core, near_at = lax.axis_index("dp"), lax.axis_index("near")
    rows = chunks[0].shape[0]
    step, half = pieces[0].shape[0], pieces[0].shape[1] // 2
    last = pieces[-1]
    flip_in, flip_out = flips(chunks[-1:], depth, cores, half)
    mean_late, noise_late = products(chunks[-1:], flip_in, pieces, half)
    tokens = joined(chunks[:-1], depth - step, depth)
    mean_part = mean_ref[...] + jnp.dot(tokens, last[:, :half], preferred_element_type=F32)
    noise_part = noise_ref[...] + jnp.dot(flipped_ref[...], last[:, half:], preferred_element_type=F32)
    held = half // (near * far)
    stride = max(held, GROUP)
    value = jnp.concatenate(
        [mean_part + flip_ref[...].astype(F32) * noise_part, mean_late + flip_out * noise_late], axis=0
    )
    value = spaced(value.T, held)
    for part in range(cores):
        for turn in range(near):
            at = part * near + turn
            target = ((core ^ part) * near + (near_at ^ turn)) * rows
            whole_ref[:, pl.ds(pl.multiple_of(target, rows), rows)] = value[:, at * rows : (at + 1) * rows]
    for turn, out in enumerate(outs):
        for plane in range(far):
            at = pl.multiple_of((plane * near + (near_at ^ turn)) * stride, stride)
            out[plane * held : (plane + 1) * held, :] = whole_ref[pl.ds(at, held), :].astype(BF16)


def sum_kernel(near, far, lags_ref, *refs):
    parts, outs, whole_ref = refs[:near], refs[near : near + far], refs[-1]
    far_at = lax.axis_index("far")
    held = outs[0].shape[0]
    stride = max(held, GROUP)
    span = parts[0].shape[1]
    total = 0.0
    for part in parts:
        total += part[...].astype(F32)
    whole_ref[:, :span] = spaced(total, held)
    whole_ref[:, span:] = spaced(lags_ref[...], held)
    for turn, out in enumerate(outs):
        at = pl.multiple_of((far_at ^ turn) * stride, stride)
        out[...] = whole_ref[pl.ds(at, held), :].astype(BF16)


def shifted(values, steps):
    moved = pltpu.roll(values, steps, 1)
    at = lax.broadcasted_iota(jnp.int32, values.shape, 1)
    return jnp.where(at >= steps, moved, 0.0)


def lane_roll(values, steps):
    return pltpu.roll(values, steps % LANES, values.ndim - 1) if steps % LANES else values


def mix_kernel(near, far, cores, held, taps_ref, *refs):
    parts, (out_ref, left_ref, sums_ref, done_ref, table_ref, lines_ref) = refs[:-6][::-1], refs[-6:]
    tiles = out_ref.shape[0] // cores
    block_rows = cores * GROUP
    tile_rows = SLOTS * block_rows
    rows = tiles * tile_rows
    lane = lax.broadcasted_iota(jnp.int32, (1, LANES), 1)
    pair = 2 * LANES
    span = near * LANES

    def padded(lines):
        if held >= GROUP:
            return lines
        return jnp.concatenate([lines, jnp.zeros((GROUP - held, lines.shape[1]), F32)], axis=0)

    for turn, part in enumerate(parts):
        for plane in range(far // len(parts)):
            own = slice(plane * held, (plane + 1) * held)
            target = pl.multiple_of(((lax.axis_index("far") if len(parts) > 1 else plane) ^ turn) * span, span)
            for line in range(cores + 1):
                piece = part[own, line * span : (line + 1) * span]
                lines_ref[line, :, pl.ds(target, span)] = piece.astype(F32)
    half = held * near * far
    position = lax.axis_index("far") * near + lax.axis_index("near")
    first = lax.axis_index("dp") * half + position * held
    channel = lax.broadcasted_iota(jnp.int32, (held, cores * half), 1) - first
    chosen = channel == lax.broadcasted_iota(jnp.int32, (held, cores * half), 0)
    taps = [
        jnp.sum(jnp.where(chosen, taps_ref[lag : lag + 1, : cores * half], 0.0), axis=1, keepdims=True)
        for lag in range(3)
    ]
    signals = []
    for part in range(cores):
        value = lines_ref[part]
        signal = taps[0] * value
        for lag in range(1, 3):
            signal += taps[lag] * shifted(value, lag)
        signals.append(padded(signal))
    lags = padded(lines_ref[cores])

    for group in range(max(held, GROUP) // GROUP):
        own = slice(group * GROUP, (group + 1) * GROUP)
        for at in range(GROUP):
            row = lags[group * GROUP + at : group * GROUP + at + 1, :]
            repeated = jnp.broadcast_to(row, (BLOCK, row.shape[1]))
            turned = pltpu.roll(repeated, 0, 1, stride=1, stride_axis=0)
            column = lax.broadcasted_iota(jnp.int32, repeated.shape, 1)
            lag = lax.broadcasted_iota(jnp.int32, repeated.shape, 0)
            kept = jnp.where(column >= lag, turned, 0.0).astype(BF16)
            table_ref[at * BLOCK : (at + 1) * BLOCK, :] = kept

        stacked = jnp.concatenate(
            [
                signal[own, a * LANES : (a + 1) * LANES]
                for a in range(tiles)
                for signal in signals
            ],
            axis=0,
        )
        slot_of = lax.broadcasted_iota(jnp.int32, stacked.shape, 0) % SLOTS
        turned = stacked
        for slot in range(1, SLOTS):
            turned = jnp.where(slot_of == slot, lane_roll(stacked, BLOCK * slot), turned)
        spread = jnp.stack(
            [
                lane_roll(turned, -BLOCK * slot).reshape(tiles, block_rows, LANES)
                for slot in range(SLOTS)
            ],
            axis=1,
        ).reshape(rows, LANES)
        owner = lax.broadcasted_iota(jnp.int32, (rows, LANES), 0) % GROUP
        for half in range(GROUP // SLOTS):
            kept = jnp.where(owner == lane // BLOCK + half * SLOTS, spread, 0.0)
            left_ref[:, half * LANES : (half + 1) * LANES] = kept.astype(BF16)

        sums_ref[...] = jnp.zeros_like(sums_ref)
        if tiles <= 16:
            for at in range(tiles // 2):
                start = 2 * at * tile_rows
                partial = jnp.dot(
                    left_ref[: rows - start, :],
                    table_ref[:, at * pair : (at + 1) * pair],
                    preferred_element_type=F32,
                )
                sums_ref[start:rows, :] += partial[:, :LANES]
                sums_ref[start + tile_rows : rows, :] += partial[: rows - start - tile_rows, LANES:]
        else:

            def add(at, _):
                partial = jnp.dot(
                    left_ref[...],
                    table_ref[:, pl.ds(pl.multiple_of(at * pair, pair), pair)],
                    preferred_element_type=F32,
                )
                start = pl.multiple_of(2 * at * tile_rows, tile_rows)
                sums_ref[pl.ds(start, rows), :] += partial[:, :LANES]
                sums_ref[pl.ds(start + tile_rows, rows), :] += partial[:, LANES:]
                return 0

            lax.fori_loop(0, tiles // 2, add, 0)

        sums = sums_ref[:rows, :]
        landed = [0.0] * SLOTS
        for part in range(SLOTS):
            late = sums
            if part:
                ahead = jnp.zeros((part * block_rows, LANES), F32)
                late = jnp.concatenate([ahead, sums[: rows - part * block_rows]], axis=0)
            late = late.reshape(tiles, SLOTS, block_rows, LANES)
            for slot in range(SLOTS):
                moved = late[:, slot].reshape(tiles * block_rows, LANES)
                landed[slot] += lane_roll(moved, BLOCK * (slot - part))
        result = 0.0
        for slot in range(SLOTS):
            result += jnp.where(lane // BLOCK == slot, landed[slot], 0.0)
        result = result.reshape(tiles, cores, GROUP, LANES)
        for part in range(cores):
            done_ref[part * tiles : (part + 1) * tiles, own, :] = result[:, part]

    out_ref[...] = done_ref[:, :held, :].astype(BF16)


def out_kernel(
    gate_ref, before_ref, taps_ref, mixed_ref, source_ref, target_ref,
    gate_held, before_held, taps_held, mixed_held, weight_ref, held_ref, small_sems, read_sems, write_sems,
):
    chunks, channels, step = weight_ref.shape
    small = [
        pltpu.make_async_copy(source, target, small_sems.at[at])
        for at, (source, target) in enumerate(
            (
                (gate_ref, gate_held),
                (before_ref, before_held),
                (taps_ref, taps_held),
                (mixed_ref, mixed_held),
            )
        )
    ]
    reads = [
        pltpu.make_async_copy(
            source_ref.at[:, pl.ds(at * step, step)], weight_ref.at[at], read_sems.at[at]
        )
        for at in range(chunks)
    ]
    for copy in small + reads:
        copy.start()
    for copy in small:
        copy.wait()
    gate = gate_held[...].astype(F32)
    extended = jnp.concatenate([before_held[...].astype(F32), gate], axis=0)
    gate_short = taps_held[0:1, channels:] * gate
    for lag in range(1, 3):
        gate_short += taps_held[lag : lag + 1, channels:] * extended[2 - lag : 2 - lag + gate.shape[0]]
    gated = (gate_short * mixed_held[...].astype(F32).T).astype(BF16)
    writes = []
    for at in range(chunks):
        reads[at].wait()
        held_ref[at] = jnp.dot(gated, weight_ref[at], preferred_element_type=F32).astype(BF16)
        columns = target_ref.at[:, pl.ds(at * step, step)]
        writes.append(pltpu.make_async_copy(held_ref.at[at], columns, write_sems.at[at]))
        writes[-1].start()
    for write in writes:
        write.wait()


def exchanged(value, axis, step):
    return lax.ppermute(value, axis, [(i, i ^ step) for i in range(lax.axis_size(axis))])


def all_exchanged(values, axis):
    result = list(values)
    for step in reversed(range(1, len(values))):
        result[step] = exchanged(values[step], axis, step)
    return result


def on_device(near, far, tokens, sign_in, sign_out, w_value, w_noise, w_gate, conv_taps, long_filter, w_out):
    rows, width = tokens.shape
    channels = w_gate.shape[1]
    cores = lax.axis_size("dp")
    count = near * far
    half = channels // cores
    held = half // count
    share = w_value.shape[0]
    depth = share * far
    length = count * rows
    near_at, core = lax.axis_index("near"), lax.axis_index("dp")

    lags_start = depth + depth // 8 + channels // 8
    packed_width = lags_start + far * held
    if share % LANES == 0 and far == 4:
        first = pl.pallas_call(
            weights_kernel,
            in_specs=[HBM] * 2,
            out_specs=VMEM,
            out_shape=jax.ShapeDtypeStruct((share, 2 * half), BF16),
            scratch_shapes=[pltpu.SemaphoreType.DMA((2,))],
            compiler_params=params(2),
            cost_estimate=cost(0, MIB // 2),
            name="weights",
        )(*in_hbm(w_value, w_noise))
        far_weights = exchanged(first, "far", 2)
        late_tokens, first = lax.optimization_barrier((tokens, first))
        weights, *chunks = pl.pallas_call(
            functools.partial(pack_kernel, near, far),
            in_specs=[HBM] * 6,
            out_specs=[VMEM] * (1 + near),
            out_shape=[jax.ShapeDtypeStruct((share, 2 * half), BF16)]
            + [jax.ShapeDtypeStruct((rows, packed_width), BF16)] * near,
            scratch_shapes=[
                pltpu.VMEM(sign_in.shape, jnp.int32),
                pltpu.VMEM(sign_out.shape[::-1], jnp.int32),
                pltpu.VMEM((rows, half), F32),
                pltpu.SemaphoreType.DMA((3,)),
                pltpu.SemaphoreType.DMA((2,)),
                pltpu.SemaphoreType.DMA((near * far,)),
            ],
            compiler_params=params(16),
            cost_estimate=cost(2 * rows * 512 * 512, 3 * MIB),
            name="pack",
        )(*in_hbm(late_tokens, sign_in, sign_out.T, long_filter, w_value, w_noise))
        pieces = [weights, exchanged(weights, "far", 1), far_weights, None]
    else:
        own = lax.dynamic_slice_in_dim(jnp.stack([w_value, w_noise]), core * half, half, axis=2)
        own = own.transpose(1, 0, 2).reshape(share, 2 * half)
        pieces = [lax.all_gather(own, "far", axis=0, tiled=True)]
        order = jnp.arange(near) ^ near_at

        def by_owner(array):
            parts = array.reshape(rows, far, near, -1).transpose(2, 0, 1, 3).reshape(near, rows, -1)
            return jnp.take(parts, order, axis=0)

        words = by_owner(sign_in)
        sent = jnp.broadcast_to(sign_out[None], (near, *sign_out.shape))
        own_lags = lax.dynamic_slice_in_dim(long_filter, core * half, half, axis=1)
        signs = [words & 255, words >> 8, sent & 255, sent >> 8, by_owner(own_lags)]
        packed = [by_owner(tokens)] + [part.astype(BF16) for part in signs]
        chunks = list(jnp.concatenate(packed, axis=2))
    chunks = all_exchanged(chunks, "near")

    late_tokens = tokens
    if len(pieces) > 1:
        late_tokens, pieces[2] = lax.optimization_barrier((tokens, pieces[2]))
        pieces[3] = exchanged(pieces[2], "far", 1)
    gate_rows = jnp.dot(late_tokens, w_gate, preferred_element_type=F32).astype(BF16)
    late = 1 % len(pieces)
    *chunks[::-1], gate_rows, pieces[late] = lax.optimization_barrier((*chunks[::-1], gate_rows, pieces[late]))
    pieces[-1], chunks[-1] = lax.optimization_barrier((pieces[-1], chunks[-1]))
    chunks += [exchanged(chunk, "dp", 1) for chunk in chunks]

    if len(pieces) == 1:
        pieces = [pieces[0][: depth // 2], pieces[0][depth // 2 :]]
    step = depth // len(pieces)
    early = (cores * near - 1) * rows
    *kept, lags = pl.pallas_call(
        functools.partial(project_kernel, near, cores, depth),
        in_specs=[VMEM] * (len(chunks) + len(pieces) - 2),
        out_specs=[VMEM] * 5,
        out_shape=[
            jax.ShapeDtypeStruct((early, half), F32),
            jax.ShapeDtypeStruct((early, half), F32),
            jax.ShapeDtypeStruct((early, half), BF16),
            jax.ShapeDtypeStruct((early, step), BF16),
            jax.ShapeDtypeStruct((far * held, near * rows), F32),
        ],
        compiler_params=params(32),
        cost_estimate=cost(4 * early * (depth - step) * half, 5 * MIB),
        name="project",
    )(*chunks[-2::-1], *pieces[:-1])
    near_shape = jax.ShapeDtypeStruct((far * held, cores * near * rows), BF16)
    partial = pl.pallas_call(
        functools.partial(finish_kernel, near, far, cores, depth),
        in_specs=[VMEM] * (4 + len(chunks) + len(pieces)),
        out_specs=[VMEM] * near,
        out_shape=[near_shape] * near,
        scratch_shapes=[pltpu.VMEM((count * max(held, GROUP), near_shape.shape[1]), F32)],
        compiler_params=params(32),
        cost_estimate=cost(4 * (early * step + rows * depth) * half, 3 * MIB),
        name="finish",
    )(*kept, *chunks[::-1], *pieces)
    partial = list(partial)
    last_rows, partial[0] = lax.optimization_barrier((gate_rows[rows - 2 :], partial[0]))
    before = lax.ppermute(last_rows, ("far", "near"), [(i, i + 1) for i in range(count - 1)])
    partial = all_exchanged(partial, "near")
    *partial[::-1], before = lax.optimization_barrier((*partial[::-1], before))

    far_shape = (held, (cores + 1) * near * rows)
    parts = pl.pallas_call(
        functools.partial(sum_kernel, near, far),
        in_specs=[VMEM] * (1 + near),
        out_specs=[VMEM] * far,
        out_shape=[jax.ShapeDtypeStruct(far_shape, BF16)] * far,
        scratch_shapes=[pltpu.VMEM((far * max(held, GROUP), far_shape[1]), F32)],
        compiler_params=params(16),
        cost_estimate=cost(MIB, MIB),
        name="sum",
    )(lags, *partial[::-1])
    if far == 4:
        parts = all_exchanged(parts, "far")
    else:
        order = jnp.arange(far) ^ lax.axis_index("far")
        parts = lax.all_to_all(jnp.take(jnp.stack(parts), order, axis=0), "far", 0, 0, tiled=True)
        parts = [parts.reshape(far * held, far_shape[1])]

    tiles = length // LANES
    all_rows = tiles * SLOTS * cores * GROUP
    held_rows = max(held, GROUP)
    mixed = pl.pallas_call(
        functools.partial(mix_kernel, near, far, cores, held),
        in_specs=[VMEM] * (1 + len(parts)),
        out_specs=VMEM,
        out_shape=jax.ShapeDtypeStruct((cores * tiles, held, LANES), BF16),
        scratch_shapes=[
            pltpu.VMEM((all_rows, GROUP * BLOCK), BF16),
            pltpu.VMEM((all_rows * (1 if tiles <= 16 else 2), LANES), F32),
            pltpu.VMEM((cores * tiles, held_rows, LANES), F32),
            pltpu.VMEM((GROUP * BLOCK, length), BF16),
            pltpu.VMEM((cores + 1, held, length), F32),
        ],
        compiler_params=params(48),
        cost_estimate=cost(cores * held_rows * BLOCK * length * 256, 2 * MIB),
        name="mix",
    )(conv_taps, *parts[::-1])

    landed = lax.all_to_all(mixed, ("dp", "far", "near"), 0, 0, tiled=True).reshape(channels, rows)
    chunks = 8
    return pl.pallas_call(
        out_kernel,
        in_specs=[ANY] * 4 + [HBM],
        out_specs=HBM,
        out_shape=jax.ShapeDtypeStruct((rows, width), BF16),
        scratch_shapes=[
            pltpu.VMEM(gate_rows.shape, BF16),
            pltpu.VMEM(before.shape, BF16),
            pltpu.VMEM(conv_taps.shape, F32),
            pltpu.VMEM(landed.shape, BF16),
            pltpu.VMEM((chunks, channels, width // chunks), BF16),
            pltpu.VMEM((chunks, rows, width // chunks), BF16),
            pltpu.SemaphoreType.DMA((4,)),
            pltpu.SemaphoreType.DMA((chunks,)),
            pltpu.SemaphoreType.DMA((chunks,)),
        ],
        compiler_params=params(16),
        cost_estimate=cost(2 * rows * width * channels, 5 * MIB),
        name="project_out",
    )(gate_rows, before, conv_taps, landed, *in_hbm(w_out))


def solution(mesh):
    count = mesh.shape["seq"]
    near = 4 if count % 4 == 0 else 1
    far = count // near
    seq_at = mesh.axis_names.index("seq")
    shape = list(mesh.devices.shape)
    shape[seq_at : seq_at + 1] = [far, near]
    names = list(mesh.axis_names)
    names[seq_at : seq_at + 1] = ["far", "near"]
    inner = Mesh(mesh.devices.reshape(shape), tuple(names))
    by_token = P(("dp", "far", "near"), None)
    by_row = P(("far", "near"), None)
    placed = (by_token, by_token, by_token, by_row, by_row, P(), P(), by_row, P())
    return jax.shard_map(
        functools.partial(on_device, near, far),
        mesh=inner,
        in_specs=placed,
        out_specs=by_token,
        check_vma=False,
    )
```

```python
import functools

import jax
import jax.numpy as jnp
from jax import lax
from jax.experimental import pallas as pl
from jax.experimental.pallas import tpu as pltpu
from jax.sharding import Mesh, PartitionSpec as P

F32 = jnp.float32
BF16 = jnp.bfloat16
LANES = 128
GROUP = 8
BLOCK = 32
SLOTS = LANES // BLOCK
MIB = 1 << 20
VMEM = pl.BlockSpec(memory_space=pltpu.VMEM)
SMEM = pl.BlockSpec(memory_space=pltpu.SMEM)
HBM = pl.BlockSpec(memory_space=pltpu.HBM)
ANY = pl.BlockSpec(memory_space=pl.ANY)


def params(mib):
    return pltpu.CompilerParams(vmem_limit_bytes=mib * MIB)


def cost(flops, accessed):
    return pl.CostEstimate(flops=flops, bytes_accessed=accessed, transcendentals=0)


def in_hbm(*arrays):
    return [pltpu.with_memory_space_constraint(array, pltpu.HBM) for array in arrays]


def sign_bytes(packed):
    parts = jnp.concatenate([packed & 255, packed >> 8], axis=1)
    return parts.astype(F32).astype(BF16)


def one_hot(rows, columns, source_of):
    at = lax.broadcasted_iota(jnp.int32, (rows, columns), 0)
    column = lax.broadcasted_iota(jnp.int32, (1, columns), 1)
    return (at == source_of(column)).astype(F32).astype(BF16)


def weights_kernel(value_ref, noise_ref, weight_ref, sems):
    half = weight_ref.shape[1] // 2
    columns = pl.ds(pl.multiple_of(lax.axis_index("dp") * half, half), half)
    copies = []
    for at, source in enumerate((value_ref, noise_ref)):
        target = weight_ref.at[:, at * half : (at + 1) * half]
        copies.append(pltpu.make_async_copy(source.at[:, columns], target, sems.at[at]))
        copies[-1].start()
    for copy in copies:
        copy.wait()


def pack_kernel(
    near, far, tokens_ref, in_ref, sent_ref, lags_ref, value_ref, noise_ref, weight_ref, *refs
):
    outs, (in_held, sent_held, lags_held, read_sems, weight_sems, token_sems) = refs[:near], refs[near:]
    core, far_at, near_at = lax.axis_index("dp"), lax.axis_index("far"), lax.axis_index("near")
    half = weight_ref.shape[1] // 2
    share = weight_ref.shape[0]
    depth = share * far
    words = in_ref.shape[1]
    per_part = words // (near * far)
    own_words = per_part * far

    copies = []
    for at, source in enumerate((value_ref, noise_ref)):
        columns = pl.ds(pl.multiple_of(core * half, half), half)
        target = weight_ref.at[:, at * half : (at + 1) * half]
        copies.append(pltpu.make_async_copy(source.at[:, columns], target, weight_sems.at[at]))
    reads = [
        pltpu.make_async_copy(in_ref, in_held, read_sems.at[0]),
        pltpu.make_async_copy(sent_ref, sent_held, read_sems.at[1]),
        pltpu.make_async_copy(
            lags_ref.at[:, pl.ds(pl.multiple_of(core * half, half), half)], lags_held, read_sems.at[2]
        ),
    ]
    for step, out in enumerate(outs):
        for turn in range(far):
            start = ((far_at ^ turn) * near + (near_at ^ step)) * share
            columns = pl.ds(pl.multiple_of(start, share), share)
            target = out.at[:, turn * share : (turn + 1) * share]
            copies.append(
                pltpu.make_async_copy(tokens_ref.at[:, columns], target, token_sems.at[step * far + turn])
            )
    for copy in reads + copies:
        copy.start()

    def word_of(column):
        step, rest = column // (2 * own_words), column % (2 * own_words)
        part, word = rest // own_words, rest % own_words
        plane = (word // per_part) ^ far_at
        return part * words + (plane * near + (step ^ near_at)) * per_part + word % per_part

    by_word = one_hot(2 * words, 2 * words, word_of)
    reads[0].wait()
    moved = jnp.dot(sign_bytes(in_held[...]), by_word, preferred_element_type=F32).astype(BF16)
    reads[1].wait()
    sent = sign_bytes(sent_held[...].astype(F32).T.astype(jnp.int32))
    held = half // (near * far)

    def channel_of(column):
        step, rest = column // (far * held), column % (far * held)
        return (rest // held * near + (step ^ near_at)) * held + rest % held

    reads[2].wait()
    lags = jnp.dot(
        lags_held[...].astype(BF16), one_hot(half, half, channel_of), preferred_element_type=F32
    ).astype(BF16)
    width, own_lags = 2 * own_words, far * held
    for step, out in enumerate(outs):
        out[:, depth : depth + width] = moved[:, step * width : (step + 1) * width]
        out[:, depth + width :] = jnp.concatenate(
            [sent, lags[:, step * own_lags : (step + 1) * own_lags]], axis=1
        )
    for copy in copies:
        copy.wait()


def spread_signs(pair, byte_of, columns):
    spread = jnp.dot(pair, one_hot(pair.shape[1], columns, byte_of), preferred_element_type=F32)
    mask = 1 << (lax.broadcasted_iota(jnp.int32, (1, columns), 1) & 7)
    return jnp.where((spread.astype(jnp.int32) & mask) != 0, 1.0, -1.0)


def spaced(lines, held):
    if held >= GROUP:
        return lines
    spare = jnp.zeros((GROUP - held, lines.shape[1]), F32)
    split = [lines[at : at + held] for at in range(0, lines.shape[0], held)]
    return jnp.concatenate([part for own in split for part in (own, spare)], axis=0)


def joined(chunks, start, stop):
    return jnp.concatenate([chunk[:, start:stop] for chunk in chunks], axis=0)


def flips(chunks, depth, cores, half):
    core = lax.axis_index("dp")
    words = depth // 16
    sent_words = cores * half // 16
    sent_start = depth + 2 * words

    def in_byte(column):
        return (column >> 4) + words * ((column >> 3) & 1)

    def out_byte(column):
        return core * (half // 16) + (column >> 4) + sent_words * ((column >> 3) & 1)

    flip_in = spread_signs(joined(chunks, depth, sent_start), in_byte, depth).astype(BF16)
    sent = joined(chunks, sent_start, sent_start + 2 * sent_words)
    return flip_in, spread_signs(sent, out_byte, half)


def products(chunks, flip_in, pieces, half):
    mean_part, noise_part = 0.0, 0.0
    for at, piece in enumerate(pieces):
        own = slice(at * piece.shape[0], (at + 1) * piece.shape[0])
        tokens = joined(chunks, own.start, own.stop)
        mean_part += jnp.dot(tokens, piece[:, :half], preferred_element_type=F32)
        noise_part += jnp.dot(tokens * flip_in[:, own], piece[:, half:], preferred_element_type=F32)
    return mean_part, noise_part


def project_kernel(near, cores, depth, *refs):
    mean_ref, noise_ref, flip_ref, flipped_ref, lags_ref = refs[-5:]
    count = near * cores - 1
    chunks, pieces = refs[:count][::-1], refs[count:-5]
    rows = chunks[0].shape[0]
    half = pieces[0].shape[1] // 2
    step = pieces[0].shape[0]
    flip_in, flip_out = flips(chunks, depth, cores, half)
    flip_ref[...] = flip_out.astype(BF16)
    flipped_ref[...] = joined(chunks, depth - step, depth) * flip_in[:, depth - step :]
    mean_ref[...], noise_ref[...] = products(chunks, flip_in, pieces, half)
    for turn in range(near):
        own_lags = chunks[turn][:, chunks[turn].shape[1] - lags_ref.shape[0] :].astype(F32).T
        at = pl.multiple_of((lax.axis_index("near") ^ turn) * rows, rows)
        lags_ref[:, pl.ds(at, rows)] = own_lags


def finish_kernel(near, far, cores, depth, mean_ref, noise_ref, flip_ref, flipped_ref, *refs):
    outs, whole_ref = refs[-1 - near : -1], refs[-1]
    chunks, pieces = refs[: near * cores][::-1], refs[near * cores : -1 - near]
    core, near_at = lax.axis_index("dp"), lax.axis_index("near")
    rows = chunks[0].shape[0]
    step, half = pieces[0].shape[0], pieces[0].shape[1] // 2
    last = pieces[-1]
    flip_in, flip_out = flips(chunks[-1:], depth, cores, half)
    mean_late, noise_late = products(chunks[-1:], flip_in, pieces, half)
    tokens = joined(chunks[:-1], depth - step, depth)
    mean_part = mean_ref[...] + jnp.dot(tokens, last[:, :half], preferred_element_type=F32)
    noise_part = noise_ref[...] + jnp.dot(flipped_ref[...], last[:, half:], preferred_element_type=F32)
    held = half // (near * far)
    stride = max(held, GROUP)
    value = jnp.concatenate(
        [mean_part + flip_ref[...].astype(F32) * noise_part, mean_late + flip_out * noise_late], axis=0
    )
    value = spaced(value.T, held)
    for part in range(cores):
        for turn in range(near):
            at = part * near + turn
            target = ((core ^ part) * near + (near_at ^ turn)) * rows
            whole_ref[:, pl.ds(pl.multiple_of(target, rows), rows)] = value[:, at * rows : (at + 1) * rows]
    for turn, out in enumerate(outs):
        for plane in range(far):
            at = pl.multiple_of((plane * near + (near_at ^ turn)) * stride, stride)
            out[plane * held : (plane + 1) * held, :] = whole_ref[pl.ds(at, held), :].astype(BF16)


def sum_kernel(near, far, lags_ref, *refs):
    parts, outs, whole_ref = refs[:near], refs[near : near + far], refs[-1]
    far_at = lax.axis_index("far")
    held = outs[0].shape[0]
    stride = max(held, GROUP)
    span = parts[0].shape[1]
    total = 0.0
    for part in parts:
        total += part[...].astype(F32)
    whole_ref[:, :span] = spaced(total, held)
    whole_ref[:, span:] = spaced(lags_ref[...], held)
    for turn, out in enumerate(outs):
        at = pl.multiple_of((far_at ^ turn) * stride, stride)
        out[...] = whole_ref[pl.ds(at, held), :].astype(BF16)


def shifted(values, steps):
    moved = pltpu.roll(values, steps, 1)
    at = lax.broadcasted_iota(jnp.int32, values.shape, 1)
    return jnp.where(at >= steps, moved, 0.0)


def lane_roll(values, steps):
    return pltpu.roll(values, steps % LANES, values.ndim - 1) if steps % LANES else values


def mix_kernel(near, far, cores, held, taps_ref, *refs):
    parts, (out_ref, left_ref, sums_ref, done_ref, table_ref, lines_ref) = refs[:-6][::-1], refs[-6:]
    tiles = out_ref.shape[0] // cores
    block_rows = cores * GROUP
    tile_rows = SLOTS * block_rows
    rows = tiles * tile_rows
    lane = lax.broadcasted_iota(jnp.int32, (1, LANES), 1)
    pair = 2 * LANES
    span = near * LANES

    def padded(lines):
        if held >= GROUP:
            return lines
        return jnp.concatenate([lines, jnp.zeros((GROUP - held, lines.shape[1]), F32)], axis=0)

    for turn, part in enumerate(parts):
        for plane in range(far // len(parts)):
            own = slice(plane * held, (plane + 1) * held)
            target = pl.multiple_of(((lax.axis_index("far") if len(parts) > 1 else plane) ^ turn) * span, span)
            for line in range(cores + 1):
                piece = part[own, line * span : (line + 1) * span]
                lines_ref[line, :, pl.ds(target, span)] = piece.astype(F32)
    half = held * near * far
    position = lax.axis_index("far") * near + lax.axis_index("near")
    first = lax.axis_index("dp") * half + position * held
    channel = lax.broadcasted_iota(jnp.int32, (held, cores * half), 1) - first
    chosen = channel == lax.broadcasted_iota(jnp.int32, (held, cores * half), 0)
    taps = [
        jnp.sum(jnp.where(chosen, taps_ref[lag : lag + 1, : cores * half], 0.0), axis=1, keepdims=True)
        for lag in range(3)
    ]
    signals = []
    for part in range(cores):
        value = lines_ref[part]
        signal = taps[0] * value
        for lag in range(1, 3):
            signal += taps[lag] * shifted(value, lag)
        signals.append(padded(signal))
    lags = padded(lines_ref[cores])

    for group in range(max(held, GROUP) // GROUP):
        own = slice(group * GROUP, (group + 1) * GROUP)
        for at in range(GROUP):
            row = lags[group * GROUP + at : group * GROUP + at + 1, :]
            repeated = jnp.broadcast_to(row, (BLOCK, row.shape[1]))
            turned = pltpu.roll(repeated, 0, 1, stride=1, stride_axis=0)
            column = lax.broadcasted_iota(jnp.int32, repeated.shape, 1)
            lag = lax.broadcasted_iota(jnp.int32, repeated.shape, 0)
            kept = jnp.where(column >= lag, turned, 0.0).astype(BF16)
            table_ref[at * BLOCK : (at + 1) * BLOCK, :] = kept

        stacked = jnp.concatenate(
            [
                signal[own, a * LANES : (a + 1) * LANES]
                for a in range(tiles)
                for signal in signals
            ],
            axis=0,
        )
        slot_of = lax.broadcasted_iota(jnp.int32, stacked.shape, 0) % SLOTS
        turned = stacked
        for slot in range(1, SLOTS):
            turned = jnp.where(slot_of == slot, lane_roll(stacked, BLOCK * slot), turned)
        spread = jnp.stack(
            [
                lane_roll(turned, -BLOCK * slot).reshape(tiles, block_rows, LANES)
                for slot in range(SLOTS)
            ],
            axis=1,
        ).reshape(rows, LANES)
        owner = lax.broadcasted_iota(jnp.int32, (rows, LANES), 0) % GROUP
        for half in range(GROUP // SLOTS):
            kept = jnp.where(owner == lane // BLOCK + half * SLOTS, spread, 0.0)
            left_ref[:, half * LANES : (half + 1) * LANES] = kept.astype(BF16)

        sums_ref[...] = jnp.zeros_like(sums_ref)
        if tiles <= 16:
            for at in range(tiles // 2):
                start = 2 * at * tile_rows
                partial = jnp.dot(
                    left_ref[: rows - start, :],
                    table_ref[:, at * pair : (at + 1) * pair],
                    preferred_element_type=F32,
                )
                sums_ref[start:rows, :] += partial[:, :LANES]
                sums_ref[start + tile_rows : rows, :] += partial[: rows - start - tile_rows, LANES:]
        else:

            def add(at, _):
                partial = jnp.dot(
                    left_ref[...],
                    table_ref[:, pl.ds(pl.multiple_of(at * pair, pair), pair)],
                    preferred_element_type=F32,
                )
                start = pl.multiple_of(2 * at * tile_rows, tile_rows)
                sums_ref[pl.ds(start, rows), :] += partial[:, :LANES]
                sums_ref[pl.ds(start + tile_rows, rows), :] += partial[:, LANES:]
                return 0

            lax.fori_loop(0, tiles // 2, add, 0)

        sums = sums_ref[:rows, :]
        landed = [0.0] * SLOTS
        for part in range(SLOTS):
            late = sums
            if part:
                ahead = jnp.zeros((part * block_rows, LANES), F32)
                late = jnp.concatenate([ahead, sums[: rows - part * block_rows]], axis=0)
            late = late.reshape(tiles, SLOTS, block_rows, LANES)
            for slot in range(SLOTS):
                moved = late[:, slot].reshape(tiles * block_rows, LANES)
                landed[slot] += lane_roll(moved, BLOCK * (slot - part))
        result = 0.0
        for slot in range(SLOTS):
            result += jnp.where(lane // BLOCK == slot, landed[slot], 0.0)
        result = result.reshape(tiles, cores, GROUP, LANES)
        for part in range(cores):
            done_ref[part * tiles : (part + 1) * tiles, own, :] = result[:, part]

    out_ref[...] = done_ref[:, :held, :].astype(BF16)


def out_kernel(
    gate_ref, before_ref, taps_ref, mixed_ref, source_ref, target_ref,
    gate_held, before_held, taps_held, mixed_held, weight_ref, held_ref, small_sems, read_sems, write_sems,
):
    chunks, channels, step = weight_ref.shape
    small = [
        pltpu.make_async_copy(source, target, small_sems.at[at])
        for at, (source, target) in enumerate(
            (
                (gate_ref, gate_held),
                (before_ref, before_held),
                (taps_ref, taps_held),
                (mixed_ref, mixed_held),
            )
        )
    ]
    reads = [
        pltpu.make_async_copy(
            source_ref.at[:, pl.ds(at * step, step)], weight_ref.at[at], read_sems.at[at]
        )
        for at in range(chunks)
    ]
    for copy in small + reads:
        copy.start()
    for copy in small:
        copy.wait()
    gate = gate_held[...].astype(F32)
    extended = jnp.concatenate([before_held[...].astype(F32), gate], axis=0)
    gate_short = taps_held[0:1, channels:] * gate
    for lag in range(1, 3):
        gate_short += taps_held[lag : lag + 1, channels:] * extended[2 - lag : 2 - lag + gate.shape[0]]
    gated = (gate_short * mixed_held[...].astype(F32).T).astype(BF16)
    writes = []
    for at in range(chunks):
        reads[at].wait()
        held_ref[at] = jnp.dot(gated, weight_ref[at], preferred_element_type=F32).astype(BF16)
        columns = target_ref.at[:, pl.ds(at * step, step)]
        writes.append(pltpu.make_async_copy(held_ref.at[at], columns, write_sems.at[at]))
        writes[-1].start()
    for write in writes:
        write.wait()


def exchanged(value, axis, step):
    return lax.ppermute(value, axis, [(i, i ^ step) for i in range(lax.axis_size(axis))])


def all_exchanged(values, axis):
    result = list(values)
    for step in reversed(range(1, len(values))):
        result[step] = exchanged(values[step], axis, step)
    return result


def on_device(near, far, tokens, sign_in, sign_out, w_value, w_noise, w_gate, conv_taps, long_filter, w_out):
    rows, width = tokens.shape
    channels = w_gate.shape[1]
    cores = lax.axis_size("dp")
    count = near * far
    half = channels // cores
    held = half // count
    share = w_value.shape[0]
    depth = share * far
    length = count * rows
    near_at, core = lax.axis_index("near"), lax.axis_index("dp")

    lags_start = depth + depth // 8 + channels // 8
    packed_width = lags_start + far * held
    if share % LANES == 0 and far == 4:
        first = pl.pallas_call(
            weights_kernel,
            in_specs=[HBM] * 2,
            out_specs=VMEM,
            out_shape=jax.ShapeDtypeStruct((share, 2 * half), BF16),
            scratch_shapes=[pltpu.SemaphoreType.DMA((2,))],
            compiler_params=params(2),
            cost_estimate=cost(0, MIB // 2),
            name="weights",
        )(*in_hbm(w_value, w_noise))
        far_weights = exchanged(first, "far", 2)
        late_tokens, first = lax.optimization_barrier((tokens, first))
        weights, *chunks = pl.pallas_call(
            functools.partial(pack_kernel, near, far),
            in_specs=[HBM] * 6,
            out_specs=[VMEM] * (1 + near),
            out_shape=[jax.ShapeDtypeStruct((share, 2 * half), BF16)]
            + [jax.ShapeDtypeStruct((rows, packed_width), BF16)] * near,
            scratch_shapes=[
                pltpu.VMEM(sign_in.shape, jnp.int32),
                pltpu.VMEM(sign_out.shape[::-1], jnp.int32),
                pltpu.VMEM((rows, half), F32),
                pltpu.SemaphoreType.DMA((3,)),
                pltpu.SemaphoreType.DMA((2,)),
                pltpu.SemaphoreType.DMA((near * far,)),
            ],
            compiler_params=params(16),
            cost_estimate=cost(2 * rows * 512 * 512, 3 * MIB),
            name="pack",
        )(*in_hbm(late_tokens, sign_in, sign_out.T, long_filter, w_value, w_noise))
        pieces = [weights, exchanged(weights, "far", 1), far_weights, None]
    else:
        own = lax.dynamic_slice_in_dim(jnp.stack([w_value, w_noise]), core * half, half, axis=2)
        own = own.transpose(1, 0, 2).reshape(share, 2 * half)
        pieces = [lax.all_gather(own, "far", axis=0, tiled=True)]
        order = jnp.arange(near) ^ near_at

        def by_owner(array):
            parts = array.reshape(rows, far, near, -1).transpose(2, 0, 1, 3).reshape(near, rows, -1)
            return jnp.take(parts, order, axis=0)

        words = by_owner(sign_in)
        sent = jnp.broadcast_to(sign_out[None], (near, *sign_out.shape))
        own_lags = lax.dynamic_slice_in_dim(long_filter, core * half, half, axis=1)
        signs = [words & 255, words >> 8, sent & 255, sent >> 8, by_owner(own_lags)]
        packed = [by_owner(tokens)] + [part.astype(BF16) for part in signs]
        chunks = list(jnp.concatenate(packed, axis=2))
    chunks = all_exchanged(chunks, "near")

    late_tokens = tokens
    if len(pieces) > 1:
        late_tokens, pieces[2] = lax.optimization_barrier((tokens, pieces[2]))
        pieces[3] = exchanged(pieces[2], "far", 1)
    gate_rows = jnp.dot(late_tokens, w_gate, preferred_element_type=F32).astype(BF16)
    late = 1 % len(pieces)
    pieces[late], *chunks[::-1], gate_rows = lax.optimization_barrier((pieces[late], *chunks[::-1], gate_rows))
    pieces[-1], chunks[-1] = lax.optimization_barrier((pieces[-1], chunks[-1]))
    chunks += [exchanged(chunk, "dp", 1) for chunk in chunks]

    if len(pieces) == 1:
        pieces = [pieces[0][: depth // 2], pieces[0][depth // 2 :]]
    step = depth // len(pieces)
    early = (cores * near - 1) * rows
    *kept, lags = pl.pallas_call(
        functools.partial(project_kernel, near, cores, depth),
        in_specs=[VMEM] * (len(chunks) + len(pieces) - 2),
        out_specs=[VMEM] * 5,
        out_shape=[
            jax.ShapeDtypeStruct((early, half), F32),
            jax.ShapeDtypeStruct((early, half), F32),
            jax.ShapeDtypeStruct((early, half), BF16),
            jax.ShapeDtypeStruct((early, step), BF16),
            jax.ShapeDtypeStruct((far * held, near * rows), F32),
        ],
        compiler_params=params(32),
        cost_estimate=cost(4 * early * (depth - step) * half, 5 * MIB),
        name="project",
    )(*chunks[-2::-1], *pieces[:-1])
    near_shape = jax.ShapeDtypeStruct((far * held, cores * near * rows), BF16)
    partial = pl.pallas_call(
        functools.partial(finish_kernel, near, far, cores, depth),
        in_specs=[VMEM] * (4 + len(chunks) + len(pieces)),
        out_specs=[VMEM] * near,
        out_shape=[near_shape] * near,
        scratch_shapes=[pltpu.VMEM((count * max(held, GROUP), near_shape.shape[1]), F32)],
        compiler_params=params(32),
        cost_estimate=cost(4 * (early * step + rows * depth) * half, 3 * MIB),
        name="finish",
    )(*kept, *chunks[::-1], *pieces)
    partial = list(partial)
    last_rows, partial[0] = lax.optimization_barrier((gate_rows[rows - 2 :], partial[0]))
    before = lax.ppermute(last_rows, ("far", "near"), [(i, i + 1) for i in range(count - 1)])
    partial = all_exchanged(partial, "near")
    *partial[::-1], before = lax.optimization_barrier((*partial[::-1], before))

    far_shape = (held, (cores + 1) * near * rows)
    parts = pl.pallas_call(
        functools.partial(sum_kernel, near, far),
        in_specs=[VMEM] * (1 + near),
        out_specs=[VMEM] * far,
        out_shape=[jax.ShapeDtypeStruct(far_shape, BF16)] * far,
        scratch_shapes=[pltpu.VMEM((far * max(held, GROUP), far_shape[1]), F32)],
        compiler_params=params(16),
        cost_estimate=cost(MIB, MIB),
        name="sum",
    )(lags, *partial[::-1])
    if far == 4:
        parts = all_exchanged(parts, "far")
    else:
        order = jnp.arange(far) ^ lax.axis_index("far")
        parts = lax.all_to_all(jnp.take(jnp.stack(parts), order, axis=0), "far", 0, 0, tiled=True)
        parts = [parts.reshape(far * held, far_shape[1])]

    tiles = length // LANES
    all_rows = tiles * SLOTS * cores * GROUP
    held_rows = max(held, GROUP)
    mixed = pl.pallas_call(
        functools.partial(mix_kernel, near, far, cores, held),
        in_specs=[VMEM] * (1 + len(parts)),
        out_specs=VMEM,
        out_shape=jax.ShapeDtypeStruct((cores * tiles, held, LANES), BF16),
        scratch_shapes=[
            pltpu.VMEM((all_rows, GROUP * BLOCK), BF16),
            pltpu.VMEM((all_rows * (1 if tiles <= 16 else 2), LANES), F32),
            pltpu.VMEM((cores * tiles, held_rows, LANES), F32),
            pltpu.VMEM((GROUP * BLOCK, length), BF16),
            pltpu.VMEM((cores + 1, held, length), F32),
        ],
        compiler_params=params(48),
        cost_estimate=cost(cores * held_rows * BLOCK * length * 256, 2 * MIB),
        name="mix",
    )(conv_taps, *parts[::-1])

    landed = lax.all_to_all(mixed, ("dp", "far", "near"), 0, 0, tiled=True).reshape(channels, rows)
    chunks = 8
    return pl.pallas_call(
        out_kernel,
        in_specs=[ANY] * 4 + [HBM],
        out_specs=HBM,
        out_shape=jax.ShapeDtypeStruct((rows, width), BF16),
        scratch_shapes=[
            pltpu.VMEM(gate_rows.shape, BF16),
            pltpu.VMEM(before.shape, BF16),
            pltpu.VMEM(conv_taps.shape, F32),
            pltpu.VMEM(landed.shape, BF16),
            pltpu.VMEM((chunks, channels, width // chunks), BF16),
            pltpu.VMEM((chunks, rows, width // chunks), BF16),
            pltpu.SemaphoreType.DMA((4,)),
            pltpu.SemaphoreType.DMA((chunks,)),
            pltpu.SemaphoreType.DMA((chunks,)),
        ],
        compiler_params=params(16),
        cost_estimate=cost(2 * rows * width * channels, 5 * MIB),
        name="project_out",
    )(gate_rows, before, conv_taps, landed, *in_hbm(w_out))


def solution(mesh):
    count = mesh.shape["seq"]
    near = 4 if count % 4 == 0 else 1
    far = count // near
    seq_at = mesh.axis_names.index("seq")
    shape = list(mesh.devices.shape)
    shape[seq_at : seq_at + 1] = [far, near]
    names = list(mesh.axis_names)
    names[seq_at : seq_at + 1] = ["far", "near"]
    inner = Mesh(mesh.devices.reshape(shape), tuple(names))
    by_token = P(("dp", "far", "near"), None)
    by_row = P(("far", "near"), None)
    placed = (by_token, by_token, by_token, by_row, by_row, P(), P(), by_row, P())
    return jax.shard_map(
        functools.partial(on_device, near, far),
        mesh=inner,
        in_specs=placed,
        out_specs=by_token,
        check_vma=False,
    )
```

```python
import functools

import jax
import jax.numpy as jnp
from jax import lax
from jax.experimental import pallas as pl
from jax.experimental.pallas import tpu as pltpu
from jax.sharding import Mesh, PartitionSpec as P

F32 = jnp.float32
BF16 = jnp.bfloat16
LANES = 128
GROUP = 8
BLOCK = 32
SLOTS = LANES // BLOCK
MIB = 1 << 20
VMEM = pl.BlockSpec(memory_space=pltpu.VMEM)
SMEM = pl.BlockSpec(memory_space=pltpu.SMEM)
HBM = pl.BlockSpec(memory_space=pltpu.HBM)
ANY = pl.BlockSpec(memory_space=pl.ANY)


def params(mib):
    return pltpu.CompilerParams(vmem_limit_bytes=mib * MIB)


def cost(flops, accessed):
    return pl.CostEstimate(flops=flops, bytes_accessed=accessed, transcendentals=0)


def in_hbm(*arrays):
    return [pltpu.with_memory_space_constraint(array, pltpu.HBM) for array in arrays]


def sign_bytes(packed):
    parts = jnp.concatenate([packed & 255, packed >> 8], axis=1)
    return parts.astype(F32).astype(BF16)


def one_hot(rows, columns, source_of):
    at = lax.broadcasted_iota(jnp.int32, (rows, columns), 0)
    column = lax.broadcasted_iota(jnp.int32, (1, columns), 1)
    return (at == source_of(column)).astype(F32).astype(BF16)


def weights_kernel(value_ref, noise_ref, weight_ref, sems):
    half = weight_ref.shape[1] // 2
    columns = pl.ds(pl.multiple_of(lax.axis_index("dp") * half, half), half)
    copies = []
    for at, source in enumerate((value_ref, noise_ref)):
        target = weight_ref.at[:, at * half : (at + 1) * half]
        copies.append(pltpu.make_async_copy(source.at[:, columns], target, sems.at[at]))
        copies[-1].start()
    for copy in copies:
        copy.wait()


def pack_kernel(
    near, far, tokens_ref, in_ref, sent_ref, lags_ref, value_ref, noise_ref, weight_ref, *refs
):
    outs, (in_held, sent_held, lags_held, read_sems, weight_sems, token_sems) = refs[:near], refs[near:]
    core, far_at, near_at = lax.axis_index("dp"), lax.axis_index("far"), lax.axis_index("near")
    half = weight_ref.shape[1] // 2
    share = weight_ref.shape[0]
    depth = share * far
    words = in_ref.shape[1]
    per_part = words // (near * far)
    own_words = per_part * far

    copies = []
    for at, source in enumerate((value_ref, noise_ref)):
        columns = pl.ds(pl.multiple_of(core * half, half), half)
        target = weight_ref.at[:, at * half : (at + 1) * half]
        copies.append(pltpu.make_async_copy(source.at[:, columns], target, weight_sems.at[at]))
    reads = [
        pltpu.make_async_copy(in_ref, in_held, read_sems.at[0]),
        pltpu.make_async_copy(sent_ref, sent_held, read_sems.at[1]),
        pltpu.make_async_copy(
            lags_ref.at[:, pl.ds(pl.multiple_of(core * half, half), half)], lags_held, read_sems.at[2]
        ),
    ]
    for step, out in enumerate(outs):
        for turn in range(far):
            start = ((far_at ^ turn) * near + (near_at ^ step)) * share
            columns = pl.ds(pl.multiple_of(start, share), share)
            target = out.at[:, turn * share : (turn + 1) * share]
            copies.append(
                pltpu.make_async_copy(tokens_ref.at[:, columns], target, token_sems.at[step * far + turn])
            )
    for copy in reads + copies:
        copy.start()

    def word_of(column):
        step, rest = column // (2 * own_words), column % (2 * own_words)
        part, word = rest // own_words, rest % own_words
        plane = (word // per_part) ^ far_at
        return part * words + (plane * near + (step ^ near_at)) * per_part + word % per_part

    by_word = one_hot(2 * words, 2 * words, word_of)
    reads[0].wait()
    moved = jnp.dot(sign_bytes(in_held[...]), by_word, preferred_element_type=F32).astype(BF16)
    reads[1].wait()
    sent = sign_bytes(sent_held[...].astype(F32).T.astype(jnp.int32))
    held = half // (near * far)

    def channel_of(column):
        step, rest = column // (far * held), column % (far * held)
        return (rest // held * near + (step ^ near_at)) * held + rest % held

    reads[2].wait()
    lags = jnp.dot(
        lags_held[...].astype(BF16), one_hot(half, half, channel_of), preferred_element_type=F32
    ).astype(BF16)
    width, own_lags = 2 * own_words, far * held
    for step, out in enumerate(outs):
        out[:, depth : depth + width] = moved[:, step * width : (step + 1) * width]
        out[:, depth + width :] = jnp.concatenate(
            [sent, lags[:, step * own_lags : (step + 1) * own_lags]], axis=1
        )
    for copy in copies:
        copy.wait()


def spread_signs(pair, byte_of, columns):
    spread = jnp.dot(pair, one_hot(pair.shape[1], columns, byte_of), preferred_element_type=F32)
    mask = 1 << (lax.broadcasted_iota(jnp.int32, (1, columns), 1) & 7)
    return jnp.where((spread.astype(jnp.int32) & mask) != 0, 1.0, -1.0)


def spaced(lines, held):
    if held >= GROUP:
        return lines
    spare = jnp.zeros((GROUP - held, lines.shape[1]), F32)
    split = [lines[at : at + held] for at in range(0, lines.shape[0], held)]
    return jnp.concatenate([part for own in split for part in (own, spare)], axis=0)


def joined(chunks, start, stop):
    return jnp.concatenate([chunk[:, start:stop] for chunk in chunks], axis=0)


def flips(chunks, depth, cores, half):
    core = lax.axis_index("dp")
    words = depth // 16
    sent_words = cores * half // 16
    sent_start = depth + 2 * words

    def in_byte(column):
        return (column >> 4) + words * ((column >> 3) & 1)

    def out_byte(column):
        return core * (half // 16) + (column >> 4) + sent_words * ((column >> 3) & 1)

    flip_in = spread_signs(joined(chunks, depth, sent_start), in_byte, depth).astype(BF16)
    sent = joined(chunks, sent_start, sent_start + 2 * sent_words)
    return flip_in, spread_signs(sent, out_byte, half)


def products(chunks, flip_in, pieces, half):
    mean_part, noise_part = 0.0, 0.0
    for at, piece in enumerate(pieces):
        own = slice(at * piece.shape[0], (at + 1) * piece.shape[0])
        tokens = joined(chunks, own.start, own.stop)
        mean_part += jnp.dot(tokens, piece[:, :half], preferred_element_type=F32)
        noise_part += jnp.dot(tokens * flip_in[:, own], piece[:, half:], preferred_element_type=F32)
    return mean_part, noise_part


def project_kernel(near, cores, depth, *refs):
    mean_ref, noise_ref, flip_ref, flipped_ref, lags_ref = refs[-5:]
    count = near * cores - 1
    chunks, pieces = refs[:count][::-1], refs[count:-5]
    rows = chunks[0].shape[0]
    half = pieces[0].shape[1] // 2
    step = pieces[0].shape[0]
    flip_in, flip_out = flips(chunks, depth, cores, half)
    flip_ref[...] = flip_out.astype(BF16)
    flipped_ref[...] = joined(chunks, depth - step, depth) * flip_in[:, depth - step :]
    mean_ref[...], noise_ref[...] = products(chunks, flip_in, pieces, half)
    for turn in range(near):
        own_lags = chunks[turn][:, chunks[turn].shape[1] - lags_ref.shape[0] :].astype(F32).T
        at = pl.multiple_of((lax.axis_index("near") ^ turn) * rows, rows)
        lags_ref[:, pl.ds(at, rows)] = own_lags


def finish_kernel(near, far, cores, depth, mean_ref, noise_ref, flip_ref, flipped_ref, *refs):
    outs, whole_ref = refs[-1 - near : -1], refs[-1]
    chunks, pieces = refs[: near * cores][::-1], refs[near * cores : -1 - near]
    core, near_at = lax.axis_index("dp"), lax.axis_index("near")
    rows = chunks[0].shape[0]
    step, half = pieces[0].shape[0], pieces[0].shape[1] // 2
    last = pieces[-1]
    flip_in, flip_out = flips(chunks[-1:], depth, cores, half)
    mean_late, noise_late = products(chunks[-1:], flip_in, pieces, half)
    tokens = joined(chunks[:-1], depth - step, depth)
    mean_part = mean_ref[...] + jnp.dot(tokens, last[:, :half], preferred_element_type=F32)
    noise_part = noise_ref[...] + jnp.dot(flipped_ref[...], last[:, half:], preferred_element_type=F32)
    held = half // (near * far)
    stride = max(held, GROUP)
    value = jnp.concatenate(
        [mean_part + flip_ref[...].astype(F32) * noise_part, mean_late + flip_out * noise_late], axis=0
    )
    value = spaced(value.T, held)
    for part in range(cores):
        for turn in range(near):
            at = part * near + turn
            target = ((core ^ part) * near + (near_at ^ turn)) * rows
            whole_ref[:, pl.ds(pl.multiple_of(target, rows), rows)] = value[:, at * rows : (at + 1) * rows]
    for turn, out in enumerate(outs):
        for plane in range(far):
            at = pl.multiple_of((plane * near + (near_at ^ turn)) * stride, stride)
            out[plane * held : (plane + 1) * held, :] = whole_ref[pl.ds(at, held), :].astype(BF16)


def sum_kernel(near, far, lags_ref, *refs):
    parts, outs, whole_ref = refs[:near], refs[near : near + far], refs[-1]
    far_at = lax.axis_index("far")
    held = outs[0].shape[0]
    stride = max(held, GROUP)
    span = parts[0].shape[1]
    total = 0.0
    for part in parts:
        total += part[...].astype(F32)
    whole_ref[:, :span] = spaced(total, held)
    whole_ref[:, span:] = spaced(lags_ref[...], held)
    for turn, out in enumerate(outs):
        at = pl.multiple_of((far_at ^ turn) * stride, stride)
        out[...] = whole_ref[pl.ds(at, held), :].astype(BF16)


def shifted(values, steps):
    moved = pltpu.roll(values, steps, 1)
    at = lax.broadcasted_iota(jnp.int32, values.shape, 1)
    return jnp.where(at >= steps, moved, 0.0)


def lane_roll(values, steps):
    return pltpu.roll(values, steps % LANES, values.ndim - 1) if steps % LANES else values


def mix_kernel(near, far, cores, held, taps_ref, *refs):
    parts, (out_ref, left_ref, sums_ref, done_ref, table_ref, lines_ref) = refs[:-6][::-1], refs[-6:]
    tiles = out_ref.shape[0] // cores
    block_rows = cores * GROUP
    tile_rows = SLOTS * block_rows
    rows = tiles * tile_rows
    lane = lax.broadcasted_iota(jnp.int32, (1, LANES), 1)
    pair = 2 * LANES
    span = near * LANES

    def padded(lines):
        if held >= GROUP:
            return lines
        return jnp.concatenate([lines, jnp.zeros((GROUP - held, lines.shape[1]), F32)], axis=0)

    for turn, part in enumerate(parts):
        for plane in range(far // len(parts)):
            own = slice(plane * held, (plane + 1) * held)
            target = pl.multiple_of(((lax.axis_index("far") if len(parts) > 1 else plane) ^ turn) * span, span)
            for line in range(cores + 1):
                piece = part[own, line * span : (line + 1) * span]
                lines_ref[line, :, pl.ds(target, span)] = piece.astype(F32)
    half = held * near * far
    position = lax.axis_index("far") * near + lax.axis_index("near")
    first = lax.axis_index("dp") * half + position * held
    channel = lax.broadcasted_iota(jnp.int32, (held, cores * half), 1) - first
    chosen = channel == lax.broadcasted_iota(jnp.int32, (held, cores * half), 0)
    taps = [
        jnp.sum(jnp.where(chosen, taps_ref[lag : lag + 1, : cores * half], 0.0), axis=1, keepdims=True)
        for lag in range(3)
    ]
    signals = []
    for part in range(cores):
        value = lines_ref[part]
        signal = taps[0] * value
        for lag in range(1, 3):
            signal += taps[lag] * shifted(value, lag)
        signals.append(padded(signal))
    lags = padded(lines_ref[cores])

    for group in range(max(held, GROUP) // GROUP):
        own = slice(group * GROUP, (group + 1) * GROUP)
        for at in range(GROUP):
            row = lags[group * GROUP + at : group * GROUP + at + 1, :]
            repeated = jnp.broadcast_to(row, (BLOCK, row.shape[1]))
            turned = pltpu.roll(repeated, 0, 1, stride=1, stride_axis=0)
            column = lax.broadcasted_iota(jnp.int32, repeated.shape, 1)
            lag = lax.broadcasted_iota(jnp.int32, repeated.shape, 0)
            kept = jnp.where(column >= lag, turned, 0.0).astype(BF16)
            table_ref[at * BLOCK : (at + 1) * BLOCK, :] = kept

        stacked = jnp.concatenate(
            [
                signal[own, a * LANES : (a + 1) * LANES]
                for a in range(tiles)
                for signal in signals
            ],
            axis=0,
        )
        slot_of = lax.broadcasted_iota(jnp.int32, stacked.shape, 0) % SLOTS
        turned = stacked
        for slot in range(1, SLOTS):
            turned = jnp.where(slot_of == slot, lane_roll(stacked, BLOCK * slot), turned)
        spread = jnp.stack(
            [
                lane_roll(turned, -BLOCK * slot).reshape(tiles, block_rows, LANES)
                for slot in range(SLOTS)
            ],
            axis=1,
        ).reshape(rows, LANES)
        owner = lax.broadcasted_iota(jnp.int32, (rows, LANES), 0) % GROUP
        for half in range(GROUP // SLOTS):
            kept = jnp.where(owner == lane // BLOCK + half * SLOTS, spread, 0.0)
            left_ref[:, half * LANES : (half + 1) * LANES] = kept.astype(BF16)

        sums_ref[...] = jnp.zeros_like(sums_ref)
        if tiles <= 16:
            for at in range(tiles // 2):
                start = 2 * at * tile_rows
                partial = jnp.dot(
                    left_ref[: rows - start, :],
                    table_ref[:, at * pair : (at + 1) * pair],
                    preferred_element_type=F32,
                )
                sums_ref[start:rows, :] += partial[:, :LANES]
                sums_ref[start + tile_rows : rows, :] += partial[: rows - start - tile_rows, LANES:]
        else:

            def add(at, _):
                partial = jnp.dot(
                    left_ref[...],
                    table_ref[:, pl.ds(pl.multiple_of(at * pair, pair), pair)],
                    preferred_element_type=F32,
                )
                start = pl.multiple_of(2 * at * tile_rows, tile_rows)
                sums_ref[pl.ds(start, rows), :] += partial[:, :LANES]
                sums_ref[pl.ds(start + tile_rows, rows), :] += partial[:, LANES:]
                return 0

            lax.fori_loop(0, tiles // 2, add, 0)

        sums = sums_ref[:rows, :]
        landed = [0.0] * SLOTS
        for part in range(SLOTS):
            late = sums
            if part:
                ahead = jnp.zeros((part * block_rows, LANES), F32)
                late = jnp.concatenate([ahead, sums[: rows - part * block_rows]], axis=0)
            late = late.reshape(tiles, SLOTS, block_rows, LANES)
            for slot in range(SLOTS):
                moved = late[:, slot].reshape(tiles * block_rows, LANES)
                landed[slot] += lane_roll(moved, BLOCK * (slot - part))
        result = 0.0
        for slot in range(SLOTS):
            result += jnp.where(lane // BLOCK == slot, landed[slot], 0.0)
        result = result.reshape(tiles, cores, GROUP, LANES)
        for part in range(cores):
            done_ref[part * tiles : (part + 1) * tiles, own, :] = result[:, part]

    out_ref[...] = done_ref[:, :held, :].astype(BF16)


def out_kernel(
    gate_ref, before_ref, taps_ref, mixed_ref, source_ref, target_ref,
    gate_held, before_held, taps_held, mixed_held, weight_ref, held_ref, small_sems, read_sems, write_sems,
):
    chunks, channels, step = weight_ref.shape
    small = [
        pltpu.make_async_copy(source, target, small_sems.at[at])
        for at, (source, target) in enumerate(
            (
                (gate_ref, gate_held),
                (before_ref, before_held),
                (taps_ref, taps_held),
                (mixed_ref, mixed_held),
            )
        )
    ]
    reads = [
        pltpu.make_async_copy(
            source_ref.at[:, pl.ds(at * step, step)], weight_ref.at[at], read_sems.at[at]
        )
        for at in range(chunks)
    ]
    for copy in small + reads:
        copy.start()
    for copy in small:
        copy.wait()
    gate = gate_held[...].astype(F32)
    extended = jnp.concatenate([before_held[...].astype(F32), gate], axis=0)
    gate_short = taps_held[0:1, channels:] * gate
    for lag in range(1, 3):
        gate_short += taps_held[lag : lag + 1, channels:] * extended[2 - lag : 2 - lag + gate.shape[0]]
    gated = (gate_short * mixed_held[...].astype(F32).T).astype(BF16)
    writes = []
    for at in range(chunks):
        reads[at].wait()
        held_ref[at] = jnp.dot(gated, weight_ref[at], preferred_element_type=F32).astype(BF16)
        columns = target_ref.at[:, pl.ds(at * step, step)]
        writes.append(pltpu.make_async_copy(held_ref.at[at], columns, write_sems.at[at]))
        writes[-1].start()
    for write in writes:
        write.wait()


def exchanged(value, axis, step):
    return lax.ppermute(value, axis, [(i, i ^ step) for i in range(lax.axis_size(axis))])


def all_exchanged(values, axis):
    result = list(values)
    for step in reversed(range(1, len(values))):
        result[step] = exchanged(values[step], axis, step)
    return result


def on_device(near, far, tokens, sign_in, sign_out, w_value, w_noise, w_gate, conv_taps, long_filter, w_out):
    rows, width = tokens.shape
    channels = w_gate.shape[1]
    cores = lax.axis_size("dp")
    count = near * far
    half = channels // cores
    held = half // count
    share = w_value.shape[0]
    depth = share * far
    length = count * rows
    near_at, core = lax.axis_index("near"), lax.axis_index("dp")

    lags_start = depth + depth // 8 + channels // 8
    packed_width = lags_start + far * held
    if share % LANES == 0 and far == 4:
        first = pl.pallas_call(
            weights_kernel,
            in_specs=[HBM] * 2,
            out_specs=VMEM,
            out_shape=jax.ShapeDtypeStruct((share, 2 * half), BF16),
            scratch_shapes=[pltpu.SemaphoreType.DMA((2,))],
            compiler_params=params(2),
            cost_estimate=cost(0, MIB // 2),
            name="weights",
        )(*in_hbm(w_value, w_noise))
        far_weights = exchanged(first, "far", 2)
        late_tokens, first = lax.optimization_barrier((tokens, first))
        weights, *chunks = pl.pallas_call(
            functools.partial(pack_kernel, near, far),
            in_specs=[HBM] * 6,
            out_specs=[VMEM] * (1 + near),
            out_shape=[jax.ShapeDtypeStruct((share, 2 * half), BF16)]
            + [jax.ShapeDtypeStruct((rows, packed_width), BF16)] * near,
            scratch_shapes=[
                pltpu.VMEM(sign_in.shape, jnp.int32),
                pltpu.VMEM(sign_out.shape[::-1], jnp.int32),
                pltpu.VMEM((rows, half), F32),
                pltpu.SemaphoreType.DMA((3,)),
                pltpu.SemaphoreType.DMA((2,)),
                pltpu.SemaphoreType.DMA((near * far,)),
            ],
            compiler_params=params(16),
            cost_estimate=cost(2 * rows * 512 * 512, 3 * MIB),
            name="pack",
        )(*in_hbm(late_tokens, sign_in, sign_out.T, long_filter, w_value, w_noise))
        pieces = [weights, exchanged(weights, "far", 1), far_weights, None]
    else:
        own = lax.dynamic_slice_in_dim(jnp.stack([w_value, w_noise]), core * half, half, axis=2)
        own = own.transpose(1, 0, 2).reshape(share, 2 * half)
        pieces = [lax.all_gather(own, "far", axis=0, tiled=True)]
        order = jnp.arange(near) ^ near_at

        def by_owner(array):
            parts = array.reshape(rows, far, near, -1).transpose(2, 0, 1, 3).reshape(near, rows, -1)
            return jnp.take(parts, order, axis=0)

        words = by_owner(sign_in)
        sent = jnp.broadcast_to(sign_out[None], (near, *sign_out.shape))
        own_lags = lax.dynamic_slice_in_dim(long_filter, core * half, half, axis=1)
        signs = [words & 255, words >> 8, sent & 255, sent >> 8, by_owner(own_lags)]
        packed = [by_owner(tokens)] + [part.astype(BF16) for part in signs]
        chunks = list(jnp.concatenate(packed, axis=2))
    chunks = all_exchanged(chunks, "near")

    late_tokens = tokens
    if len(pieces) > 1:
        late_tokens, pieces[2] = lax.optimization_barrier((tokens, pieces[2]))
        pieces[3] = exchanged(pieces[2], "far", 1)
    gate_rows = jnp.dot(late_tokens, w_gate, preferred_element_type=F32).astype(BF16)
    late = 1 % len(pieces)
    pieces[late], chunks[0], gate_rows = lax.optimization_barrier((pieces[late], chunks[0], gate_rows))
    for step in range(1, near):
        chunks[step], _ = lax.optimization_barrier((chunks[step], gate_rows))
    pieces[-1], chunks[-1] = lax.optimization_barrier((pieces[-1], chunks[-1]))
    chunks += [exchanged(chunk, "dp", 1) for chunk in chunks]

    if len(pieces) == 1:
        pieces = [pieces[0][: depth // 2], pieces[0][depth // 2 :]]
    step = depth // len(pieces)
    early = (cores * near - 1) * rows
    *kept, lags = pl.pallas_call(
        functools.partial(project_kernel, near, cores, depth),
        in_specs=[VMEM] * (len(chunks) + len(pieces) - 2),
        out_specs=[VMEM] * 5,
        out_shape=[
            jax.ShapeDtypeStruct((early, half), F32),
            jax.ShapeDtypeStruct((early, half), F32),
            jax.ShapeDtypeStruct((early, half), BF16),
            jax.ShapeDtypeStruct((early, step), BF16),
            jax.ShapeDtypeStruct((far * held, near * rows), F32),
        ],
        compiler_params=params(32),
        cost_estimate=cost(4 * early * (depth - step) * half, 5 * MIB),
        name="project",
    )(*chunks[-2::-1], *pieces[:-1])
    near_shape = jax.ShapeDtypeStruct((far * held, cores * near * rows), BF16)
    partial = pl.pallas_call(
        functools.partial(finish_kernel, near, far, cores, depth),
        in_specs=[VMEM] * (4 + len(chunks) + len(pieces)),
        out_specs=[VMEM] * near,
        out_shape=[near_shape] * near,
        scratch_shapes=[pltpu.VMEM((count * max(held, GROUP), near_shape.shape[1]), F32)],
        compiler_params=params(32),
        cost_estimate=cost(4 * (early * step + rows * depth) * half, 3 * MIB),
        name="finish",
    )(*kept, *chunks[::-1], *pieces)
    partial = list(partial)
    last_rows, partial[0] = lax.optimization_barrier((gate_rows[rows - 2 :], partial[0]))
    before = lax.ppermute(last_rows, ("far", "near"), [(i, i + 1) for i in range(count - 1)])
    partial = all_exchanged(partial, "near")
    *partial[::-1], before = lax.optimization_barrier((*partial[::-1], before))

    far_shape = (held, (cores + 1) * near * rows)
    parts = pl.pallas_call(
        functools.partial(sum_kernel, near, far),
        in_specs=[VMEM] * (1 + near),
        out_specs=[VMEM] * far,
        out_shape=[jax.ShapeDtypeStruct(far_shape, BF16)] * far,
        scratch_shapes=[pltpu.VMEM((far * max(held, GROUP), far_shape[1]), F32)],
        compiler_params=params(16),
        cost_estimate=cost(MIB, MIB),
        name="sum",
    )(lags, *partial[::-1])
    if far == 4:
        parts = all_exchanged(parts, "far")
    else:
        order = jnp.arange(far) ^ lax.axis_index("far")
        parts = lax.all_to_all(jnp.take(jnp.stack(parts), order, axis=0), "far", 0, 0, tiled=True)
        parts = [parts.reshape(far * held, far_shape[1])]

    tiles = length // LANES
    all_rows = tiles * SLOTS * cores * GROUP
    held_rows = max(held, GROUP)
    mixed = pl.pallas_call(
        functools.partial(mix_kernel, near, far, cores, held),
        in_specs=[VMEM] * (1 + len(parts)),
        out_specs=VMEM,
        out_shape=jax.ShapeDtypeStruct((cores * tiles, held, LANES), BF16),
        scratch_shapes=[
            pltpu.VMEM((all_rows, GROUP * BLOCK), BF16),
            pltpu.VMEM((all_rows * (1 if tiles <= 16 else 2), LANES), F32),
            pltpu.VMEM((cores * tiles, held_rows, LANES), F32),
            pltpu.VMEM((GROUP * BLOCK, length), BF16),
            pltpu.VMEM((cores + 1, held, length), F32),
        ],
        compiler_params=params(48),
        cost_estimate=cost(cores * held_rows * BLOCK * length * 256, 2 * MIB),
        name="mix",
    )(conv_taps, *parts[::-1])

    landed = lax.all_to_all(mixed, ("dp", "far", "near"), 0, 0, tiled=True).reshape(channels, rows)
    chunks = 8
    return pl.pallas_call(
        out_kernel,
        in_specs=[ANY] * 4 + [HBM],
        out_specs=HBM,
        out_shape=jax.ShapeDtypeStruct((rows, width), BF16),
        scratch_shapes=[
            pltpu.VMEM(gate_rows.shape, BF16),
            pltpu.VMEM(before.shape, BF16),
            pltpu.VMEM(conv_taps.shape, F32),
            pltpu.VMEM(landed.shape, BF16),
            pltpu.VMEM((chunks, channels, width // chunks), BF16),
            pltpu.VMEM((chunks, rows, width // chunks), BF16),
            pltpu.SemaphoreType.DMA((4,)),
            pltpu.SemaphoreType.DMA((chunks,)),
            pltpu.SemaphoreType.DMA((chunks,)),
        ],
        compiler_params=params(16),
        cost_estimate=cost(2 * rows * width * channels, 5 * MIB),
        name="project_out",
    )(gate_rows, before, conv_taps, landed, *in_hbm(w_out))


def solution(mesh):
    count = mesh.shape["seq"]
    near = 4 if count % 4 == 0 else 1
    far = count // near
    seq_at = mesh.axis_names.index("seq")
    shape = list(mesh.devices.shape)
    shape[seq_at : seq_at + 1] = [far, near]
    names = list(mesh.axis_names)
    names[seq_at : seq_at + 1] = ["far", "near"]
    inner = Mesh(mesh.devices.reshape(shape), tuple(names))
    by_token = P(("dp", "far", "near"), None)
    by_row = P(("far", "near"), None)
    placed = (by_token, by_token, by_token, by_row, by_row, P(), P(), by_row, P())
    return jax.shard_map(
        functools.partial(on_device, near, far),
        mesh=inner,
        in_specs=placed,
        out_specs=by_token,
        check_vma=False,
    )
```

```python
import functools

import jax
import jax.numpy as jnp
from jax import lax
from jax.experimental import pallas as pl
from jax.experimental.pallas import tpu as pltpu
from jax.sharding import Mesh, PartitionSpec as P

F32 = jnp.float32
BF16 = jnp.bfloat16
LANES = 128
GROUP = 8
BLOCK = 32
SLOTS = LANES // BLOCK
MIB = 1 << 20
VMEM = pl.BlockSpec(memory_space=pltpu.VMEM)
HBM = pl.BlockSpec(memory_space=pltpu.HBM)


def params(mib):
    return pltpu.CompilerParams(vmem_limit_bytes=mib * MIB)


def cost(flops, accessed):
    return pl.CostEstimate(flops=flops, bytes_accessed=accessed, transcendentals=0)


def in_hbm(*arrays):
    return [pltpu.with_memory_space_constraint(array, pltpu.HBM) for array in arrays]


def sign_bytes(packed):
    parts = jnp.concatenate([packed & 255, packed >> 8], axis=1)
    return parts.astype(F32).astype(BF16)


def one_hot(rows, columns, source_of):
    at = lax.broadcasted_iota(jnp.int32, (rows, columns), 0)
    column = lax.broadcasted_iota(jnp.int32, (1, columns), 1)
    return (at == source_of(column)).astype(F32).astype(BF16)


def weights_kernel(value_ref, noise_ref, weight_ref, sems):
    half = weight_ref.shape[1] // 2
    columns = pl.ds(pl.multiple_of(lax.axis_index("dp") * half, half), half)
    copies = []
    for at, source in enumerate((value_ref, noise_ref)):
        target = weight_ref.at[:, at * half : (at + 1) * half]
        copies.append(pltpu.make_async_copy(source.at[:, columns], target, sems.at[at]))
        copies[-1].start()
    for copy in copies:
        copy.wait()


def pack_kernel(
    near, far, tokens_ref, in_ref, sent_ref, lags_ref, value_ref, noise_ref, weight_ref, *refs
):
    outs, (in_held, sent_held, lags_held, read_sems, weight_sems, token_sems) = refs[:near], refs[near:]
    core, far_at, near_at = lax.axis_index("dp"), lax.axis_index("far"), lax.axis_index("near")
    half = weight_ref.shape[1] // 2
    share = weight_ref.shape[0]
    depth = share * far
    words = in_ref.shape[1]
    per_part = words // (near * far)
    own_words = per_part * far

    copies = []
    for at, source in enumerate((value_ref, noise_ref)):
        columns = pl.ds(pl.multiple_of(core * half, half), half)
        target = weight_ref.at[:, at * half : (at + 1) * half]
        copies.append(pltpu.make_async_copy(source.at[:, columns], target, weight_sems.at[at]))
    reads = [
        pltpu.make_async_copy(in_ref, in_held, read_sems.at[0]),
        pltpu.make_async_copy(sent_ref, sent_held, read_sems.at[1]),
        pltpu.make_async_copy(
            lags_ref.at[:, pl.ds(pl.multiple_of(core * half, half), half)], lags_held, read_sems.at[2]
        ),
    ]
    for step, out in enumerate(outs):
        for turn in range(far):
            start = ((far_at ^ turn) * near + (near_at ^ step)) * share
            columns = pl.ds(pl.multiple_of(start, share), share)
            target = out.at[:, turn * share : (turn + 1) * share]
            copies.append(
                pltpu.make_async_copy(tokens_ref.at[:, columns], target, token_sems.at[step * far + turn])
            )
    for copy in reads + copies:
        copy.start()

    def word_of(column):
        step, rest = column // (2 * own_words), column % (2 * own_words)
        part, word = rest // own_words, rest % own_words
        plane = (word // per_part) ^ far_at
        return part * words + (plane * near + (step ^ near_at)) * per_part + word % per_part

    by_word = one_hot(2 * words, 2 * words, word_of)
    reads[0].wait()
    moved = jnp.dot(sign_bytes(in_held[...]), by_word, preferred_element_type=F32).astype(BF16)
    reads[1].wait()
    sent = sign_bytes(sent_held[...].astype(F32).T.astype(jnp.int32))
    held = half // (near * far)

    def channel_of(column):
        step, rest = column // (far * held), column % (far * held)
        return (rest // held * near + (step ^ near_at)) * held + rest % held

    reads[2].wait()
    lags = jnp.dot(
        lags_held[...].astype(BF16), one_hot(half, half, channel_of), preferred_element_type=F32
    ).astype(BF16)
    width, own_lags = 2 * own_words, far * held
    for step, out in enumerate(outs):
        out[:, depth : depth + width] = moved[:, step * width : (step + 1) * width]
        out[:, depth + width :] = jnp.concatenate(
            [sent, lags[:, step * own_lags : (step + 1) * own_lags]], axis=1
        )
    for copy in copies:
        copy.wait()


def spread_signs(pair, byte_of, columns):
    spread = jnp.dot(pair, one_hot(pair.shape[1], columns, byte_of), preferred_element_type=F32)
    mask = 1 << (lax.broadcasted_iota(jnp.int32, (1, columns), 1) & 7)
    return jnp.where((spread.astype(jnp.int32) & mask) != 0, 1.0, -1.0)


def spaced(lines, held):
    if held >= GROUP:
        return lines
    spare = jnp.zeros((GROUP - held, lines.shape[1]), F32)
    split = [lines[at : at + held] for at in range(0, lines.shape[0], held)]
    return jnp.concatenate([part for own in split for part in (own, spare)], axis=0)


def joined(chunks, start, stop):
    return jnp.concatenate([chunk[:, start:stop] for chunk in chunks], axis=0)


def flips(chunks, depth, cores, half):
    core = lax.axis_index("dp")
    words = depth // 16
    sent_words = cores * half // 16
    sent_start = depth + 2 * words

    def in_byte(column):
        return (column >> 4) + words * ((column >> 3) & 1)

    def out_byte(column):
        return core * (half // 16) + (column >> 4) + sent_words * ((column >> 3) & 1)

    flip_in = spread_signs(joined(chunks, depth, sent_start), in_byte, depth).astype(BF16)
    sent = joined(chunks, sent_start, sent_start + 2 * sent_words)
    return flip_in, spread_signs(sent, out_byte, half)


def products(chunks, flip_in, pieces, half):
    mean_part, noise_part = 0.0, 0.0
    for at, piece in enumerate(pieces):
        own = slice(at * piece.shape[0], (at + 1) * piece.shape[0])
        tokens = joined(chunks, own.start, own.stop)
        mean_part += jnp.dot(tokens, piece[:, :half], preferred_element_type=F32)
        noise_part += jnp.dot(tokens * flip_in[:, own], piece[:, half:], preferred_element_type=F32)
    return mean_part, noise_part


def project_kernel(near, cores, depth, *refs):
    mean_ref, noise_ref, flip_ref, flipped_ref, lags_ref = refs[-5:]
    count = near * cores - 1
    chunks, pieces = refs[:count][::-1], refs[count:-5]
    rows = chunks[0].shape[0]
    half = pieces[0].shape[1] // 2
    step = pieces[0].shape[0]
    flip_in, flip_out = flips(chunks, depth, cores, half)
    flip_ref[...] = flip_out.astype(BF16)
    flipped_ref[...] = joined(chunks, depth - step, depth) * flip_in[:, depth - step :]
    mean_ref[...], noise_ref[...] = products(chunks, flip_in, pieces, half)
    for turn in range(near):
        own_lags = chunks[turn][:, chunks[turn].shape[1] - lags_ref.shape[0] :].astype(F32).T
        at = pl.multiple_of((lax.axis_index("near") ^ turn) * rows, rows)
        lags_ref[:, pl.ds(at, rows)] = own_lags


def finish_kernel(near, far, cores, depth, mean_ref, noise_ref, flip_ref, flipped_ref, *refs):
    outs, whole_ref = refs[-1 - near : -1], refs[-1]
    chunks, pieces = refs[: near * cores][::-1], refs[near * cores : -1 - near]
    core, near_at = lax.axis_index("dp"), lax.axis_index("near")
    rows = chunks[0].shape[0]
    step, half = pieces[0].shape[0], pieces[0].shape[1] // 2
    last = pieces[-1]
    flip_in, flip_out = flips(chunks[-1:], depth, cores, half)
    mean_late, noise_late = products(chunks[-1:], flip_in, pieces, half)
    tokens = joined(chunks[:-1], depth - step, depth)
    mean_part = mean_ref[...] + jnp.dot(tokens, last[:, :half], preferred_element_type=F32)
    noise_part = noise_ref[...] + jnp.dot(flipped_ref[...], last[:, half:], preferred_element_type=F32)
    held = half // (near * far)
    stride = max(held, GROUP)
    value = jnp.concatenate(
        [mean_part + flip_ref[...].astype(F32) * noise_part, mean_late + flip_out * noise_late], axis=0
    )
    value = spaced(value.T, held)
    for part in range(cores):
        for turn in range(near):
            at = part * near + turn
            target = ((core ^ part) * near + (near_at ^ turn)) * rows
            whole_ref[:, pl.ds(pl.multiple_of(target, rows), rows)] = value[:, at * rows : (at + 1) * rows]
    for turn, out in enumerate(outs):
        for plane in range(far):
            at = pl.multiple_of((plane * near + (near_at ^ turn)) * stride, stride)
            out[plane * held : (plane + 1) * held, :] = whole_ref[pl.ds(at, held), :].astype(BF16)


def sum_kernel(near, far, lags_ref, *refs):
    parts, outs, whole_ref = refs[:near], refs[near : near + far], refs[-1]
    far_at = lax.axis_index("far")
    held = outs[0].shape[0]
    stride = max(held, GROUP)
    span = parts[0].shape[1]
    total = 0.0
    for part in parts:
        total += part[...].astype(F32)
    whole_ref[:, :span] = spaced(total, held)
    whole_ref[:, span:] = spaced(lags_ref[...], held)
    for turn, out in enumerate(outs):
        at = pl.multiple_of((far_at ^ turn) * stride, stride)
        out[...] = whole_ref[pl.ds(at, held), :].astype(BF16)


def shifted(values, steps):
    moved = pltpu.roll(values, steps, 1)
    at = lax.broadcasted_iota(jnp.int32, values.shape, 1)
    return jnp.where(at >= steps, moved, 0.0)


def lane_roll(values, steps):
    return pltpu.roll(values, steps % LANES, values.ndim - 1) if steps % LANES else values


def mix_kernel(near, far, cores, held, taps_ref, *refs):
    parts, (out_ref, left_ref, sums_ref, done_ref, table_ref, lines_ref) = refs[:-6][::-1], refs[-6:]
    tiles = out_ref.shape[0] // cores
    block_rows = cores * GROUP
    tile_rows = SLOTS * block_rows
    rows = tiles * tile_rows
    lane = lax.broadcasted_iota(jnp.int32, (1, LANES), 1)
    pair = 2 * LANES
    span = near * LANES

    def padded(lines):
        if held >= GROUP:
            return lines
        return jnp.concatenate([lines, jnp.zeros((GROUP - held, lines.shape[1]), F32)], axis=0)

    for turn, part in enumerate(parts):
        for plane in range(far // len(parts)):
            own = slice(plane * held, (plane + 1) * held)
            target = pl.multiple_of(((lax.axis_index("far") if len(parts) > 1 else plane) ^ turn) * span, span)
            for line in range(cores + 1):
                piece = part[own, line * span : (line + 1) * span]
                lines_ref[line, :, pl.ds(target, span)] = piece.astype(F32)
    half = held * near * far
    position = lax.axis_index("far") * near + lax.axis_index("near")
    first = lax.axis_index("dp") * half + position * held
    channel = lax.broadcasted_iota(jnp.int32, (held, cores * half), 1) - first
    chosen = channel == lax.broadcasted_iota(jnp.int32, (held, cores * half), 0)
    taps = [
        jnp.sum(jnp.where(chosen, taps_ref[lag : lag + 1, : cores * half], 0.0), axis=1, keepdims=True)
        for lag in range(3)
    ]
    signals = []
    for part in range(cores):
        value = lines_ref[part]
        signal = taps[0] * value
        for lag in range(1, 3):
            signal += taps[lag] * shifted(value, lag)
        signals.append(padded(signal))
    lags = padded(lines_ref[cores])

    for group in range(max(held, GROUP) // GROUP):
        own = slice(group * GROUP, (group + 1) * GROUP)
        for at in range(GROUP):
            row = lags[group * GROUP + at : group * GROUP + at + 1, :]
            repeated = jnp.broadcast_to(row, (BLOCK, row.shape[1]))
            turned = pltpu.roll(repeated, 0, 1, stride=1, stride_axis=0)
            column = lax.broadcasted_iota(jnp.int32, repeated.shape, 1)
            lag = lax.broadcasted_iota(jnp.int32, repeated.shape, 0)
            kept = jnp.where(column >= lag, turned, 0.0).astype(BF16)
            table_ref[at * BLOCK : (at + 1) * BLOCK, :] = kept

        stacked = jnp.concatenate(
            [
                signal[own, a * LANES : (a + 1) * LANES]
                for a in range(tiles)
                for signal in signals
            ],
            axis=0,
        )
        slot_of = lax.broadcasted_iota(jnp.int32, stacked.shape, 0) % SLOTS
        turned = stacked
        for slot in range(1, SLOTS):
            turned = jnp.where(slot_of == slot, lane_roll(stacked, BLOCK * slot), turned)
        spread = jnp.stack(
            [
                lane_roll(turned, -BLOCK * slot).reshape(tiles, block_rows, LANES)
                for slot in range(SLOTS)
            ],
            axis=1,
        ).reshape(rows, LANES)
        owner = lax.broadcasted_iota(jnp.int32, (rows, LANES), 0) % GROUP
        for half in range(GROUP // SLOTS):
            kept = jnp.where(owner == lane // BLOCK + half * SLOTS, spread, 0.0)
            left_ref[:, half * LANES : (half + 1) * LANES] = kept.astype(BF16)

        sums_ref[...] = jnp.zeros_like(sums_ref)
        if tiles <= 16:
            for at in range(tiles // 2):
                start = 2 * at * tile_rows
                partial = jnp.dot(
                    left_ref[: rows - start, :],
                    table_ref[:, at * pair : (at + 1) * pair],
                    preferred_element_type=F32,
                )
                sums_ref[start:rows, :] += partial[:, :LANES]
                sums_ref[start + tile_rows : rows, :] += partial[: rows - start - tile_rows, LANES:]
        else:

            def add(at, _):
                partial = jnp.dot(
                    left_ref[...],
                    table_ref[:, pl.ds(pl.multiple_of(at * pair, pair), pair)],
                    preferred_element_type=F32,
                )
                start = pl.multiple_of(2 * at * tile_rows, tile_rows)
                sums_ref[pl.ds(start, rows), :] += partial[:, :LANES]
                sums_ref[pl.ds(start + tile_rows, rows), :] += partial[:, LANES:]
                return 0

            lax.fori_loop(0, tiles // 2, add, 0)

        sums = sums_ref[:rows, :]
        landed = [0.0] * SLOTS
        for part in range(SLOTS):
            late = sums
            if part:
                ahead = jnp.zeros((part * block_rows, LANES), F32)
                late = jnp.concatenate([ahead, sums[: rows - part * block_rows]], axis=0)
            late = late.reshape(tiles, SLOTS, block_rows, LANES)
            for slot in range(SLOTS):
                moved = late[:, slot].reshape(tiles * block_rows, LANES)
                landed[slot] += lane_roll(moved, BLOCK * (slot - part))
        result = 0.0
        for slot in range(SLOTS):
            result += jnp.where(lane // BLOCK == slot, landed[slot], 0.0)
        result = result.reshape(tiles, cores, GROUP, LANES)
        for part in range(cores):
            done_ref[part * tiles : (part + 1) * tiles, own, :] = result[:, part]

    out_ref[...] = done_ref[:, :held, :].astype(BF16)


def gate_kernel(gate_ref, before_ref, taps_ref, out_ref):
    channels = gate_ref.shape[1]
    gate = gate_ref[...].astype(F32)
    extended = jnp.concatenate([before_ref[...].astype(F32), gate], axis=0)
    gate_short = taps_ref[0:1, channels:] * gate
    for lag in range(1, 3):
        gate_short += taps_ref[lag : lag + 1, channels:] * extended[2 - lag : 2 - lag + gate.shape[0]]
    out_ref[...] = gate_short


def out_kernel(gate_ref, mixed_ref, source_ref, target_ref, weight_ref, held_ref, read_sems, write_sems):
    chunks, _, step = weight_ref.shape
    reads = []
    for at in range(chunks):
        columns = source_ref.at[:, pl.ds(at * step, step)]
        reads.append(pltpu.make_async_copy(columns, weight_ref.at[at], read_sems.at[at]))
        reads[-1].start()
    gated = (gate_ref[...] * mixed_ref[...].astype(F32).T).astype(BF16)
    writes = []
    for at in range(chunks):
        reads[at].wait()
        held_ref[at] = jnp.dot(gated, weight_ref[at], preferred_element_type=F32).astype(BF16)
        columns = target_ref.at[:, pl.ds(at * step, step)]
        writes.append(pltpu.make_async_copy(held_ref.at[at], columns, write_sems.at[at]))
        writes[-1].start()
    for write in writes:
        write.wait()


def exchanged(value, axis, step):
    return lax.ppermute(value, axis, [(i, i ^ step) for i in range(lax.axis_size(axis))])


def all_exchanged(values, axis):
    result = list(values)
    for step in reversed(range(1, len(values))):
        result[step] = exchanged(values[step], axis, step)
    return result


def on_device(near, far, tokens, sign_in, sign_out, w_value, w_noise, w_gate, conv_taps, long_filter, w_out):
    rows, width = tokens.shape
    channels = w_gate.shape[1]
    cores = lax.axis_size("dp")
    count = near * far
    half = channels // cores
    held = half // count
    share = w_value.shape[0]
    depth = share * far
    length = count * rows
    near_at, core = lax.axis_index("near"), lax.axis_index("dp")

    lags_start = depth + depth // 8 + channels // 8
    packed_width = lags_start + far * held
    if share % LANES == 0 and far == 4:
        first = pl.pallas_call(
            weights_kernel,
            in_specs=[HBM] * 2,
            out_specs=VMEM,
            out_shape=jax.ShapeDtypeStruct((share, 2 * half), BF16),
            scratch_shapes=[pltpu.SemaphoreType.DMA((2,))],
            compiler_params=params(2),
            cost_estimate=cost(0, MIB // 2),
            name="weights",
        )(*in_hbm(w_value, w_noise))
        far_weights = exchanged(first, "far", 2)
        late_tokens, first = lax.optimization_barrier((tokens, first))
        weights, *chunks = pl.pallas_call(
            functools.partial(pack_kernel, near, far),
            in_specs=[HBM] * 6,
            out_specs=[VMEM] * (1 + near),
            out_shape=[jax.ShapeDtypeStruct((share, 2 * half), BF16)]
            + [jax.ShapeDtypeStruct((rows, packed_width), BF16)] * near,
            scratch_shapes=[
                pltpu.VMEM(sign_in.shape, jnp.int32),
                pltpu.VMEM(sign_out.shape[::-1], jnp.int32),
                pltpu.VMEM((rows, half), F32),
                pltpu.SemaphoreType.DMA((3,)),
                pltpu.SemaphoreType.DMA((2,)),
                pltpu.SemaphoreType.DMA((near * far,)),
            ],
            compiler_params=params(16),
            cost_estimate=cost(2 * rows * 512 * 512, 3 * MIB),
            name="pack",
        )(*in_hbm(late_tokens, sign_in, sign_out.T, long_filter, w_value, w_noise))
        pieces = [weights, exchanged(weights, "far", 1), far_weights, None]
    else:
        own = lax.dynamic_slice_in_dim(jnp.stack([w_value, w_noise]), core * half, half, axis=2)
        own = own.transpose(1, 0, 2).reshape(share, 2 * half)
        pieces = [lax.all_gather(own, "far", axis=0, tiled=True)]
        order = jnp.arange(near) ^ near_at

        def by_owner(array):
            parts = array.reshape(rows, far, near, -1).transpose(2, 0, 1, 3).reshape(near, rows, -1)
            return jnp.take(parts, order, axis=0)

        words = by_owner(sign_in)
        sent = jnp.broadcast_to(sign_out[None], (near, *sign_out.shape))
        own_lags = lax.dynamic_slice_in_dim(long_filter, core * half, half, axis=1)
        signs = [words & 255, words >> 8, sent & 255, sent >> 8, by_owner(own_lags)]
        packed = [by_owner(tokens)] + [part.astype(BF16) for part in signs]
        chunks = list(jnp.concatenate(packed, axis=2))
    chunks = all_exchanged(chunks, "near")

    late_tokens = tokens
    if len(pieces) > 1:
        late_tokens, pieces[2] = lax.optimization_barrier((tokens, pieces[2]))
        pieces[3] = exchanged(pieces[2], "far", 1)
    gate_rows = jnp.dot(late_tokens, w_gate, preferred_element_type=F32).astype(BF16)
    late = 1 % len(pieces)
    pieces[late], chunks[0], gate_rows = lax.optimization_barrier((pieces[late], chunks[0], gate_rows))
    for step in range(1, near):
        chunks[step], _ = lax.optimization_barrier((chunks[step], gate_rows))
    pieces[-1], chunks[-1] = lax.optimization_barrier((pieces[-1], chunks[-1]))
    chunks += [exchanged(chunk, "dp", 1) for chunk in chunks]

    if len(pieces) == 1:
        pieces = [pieces[0][: depth // 2], pieces[0][depth // 2 :]]
    step = depth // len(pieces)
    early = (cores * near - 1) * rows
    *kept, lags = pl.pallas_call(
        functools.partial(project_kernel, near, cores, depth),
        in_specs=[VMEM] * (len(chunks) + len(pieces) - 2),
        out_specs=[VMEM] * 5,
        out_shape=[
            jax.ShapeDtypeStruct((early, half), F32),
            jax.ShapeDtypeStruct((early, half), F32),
            jax.ShapeDtypeStruct((early, half), BF16),
            jax.ShapeDtypeStruct((early, step), BF16),
            jax.ShapeDtypeStruct((far * held, near * rows), F32),
        ],
        compiler_params=params(32),
        cost_estimate=cost(4 * early * (depth - step) * half, 5 * MIB),
        name="project",
    )(*chunks[-2::-1], *pieces[:-1])
    near_shape = jax.ShapeDtypeStruct((far * held, cores * near * rows), BF16)
    partial = pl.pallas_call(
        functools.partial(finish_kernel, near, far, cores, depth),
        in_specs=[VMEM] * (4 + len(chunks) + len(pieces)),
        out_specs=[VMEM] * near,
        out_shape=[near_shape] * near,
        scratch_shapes=[pltpu.VMEM((count * max(held, GROUP), near_shape.shape[1]), F32)],
        compiler_params=params(32),
        cost_estimate=cost(4 * (early * step + rows * depth) * half, 3 * MIB),
        name="finish",
    )(*kept, *chunks[::-1], *pieces)
    partial = list(partial)
    last_rows, partial[0] = lax.optimization_barrier((gate_rows[rows - 2 :], partial[0]))
    before = lax.ppermute(last_rows, ("far", "near"), [(i, i + 1) for i in range(count - 1)])
    partial = all_exchanged(partial, "near")
    *partial[::-1], before = lax.optimization_barrier((*partial[::-1], before))

    far_shape = (held, (cores + 1) * near * rows)
    parts = pl.pallas_call(
        functools.partial(sum_kernel, near, far),
        in_specs=[VMEM] * (1 + near),
        out_specs=[VMEM] * far,
        out_shape=[jax.ShapeDtypeStruct(far_shape, BF16)] * far,
        scratch_shapes=[pltpu.VMEM((far * max(held, GROUP), far_shape[1]), F32)],
        compiler_params=params(16),
        cost_estimate=cost(MIB, MIB),
        name="sum",
    )(lags, *partial[::-1])
    if far == 4:
        parts = all_exchanged(parts, "far")
    else:
        order = jnp.arange(far) ^ lax.axis_index("far")
        parts = lax.all_to_all(jnp.take(jnp.stack(parts), order, axis=0), "far", 0, 0, tiled=True)
        parts = [parts.reshape(far * held, far_shape[1])]

    gate_short = pl.pallas_call(
        gate_kernel,
        in_specs=[VMEM] * 3,
        out_specs=VMEM,
        out_shape=jax.ShapeDtypeStruct((rows, channels), F32),
        compiler_params=params(4),
        cost_estimate=cost(rows * channels * 6, MIB // 2),
        name="gate",
    )(gate_rows, before, conv_taps)
    parts[0], gate_short = lax.optimization_barrier((parts[0], gate_short))

    tiles = length // LANES
    all_rows = tiles * SLOTS * cores * GROUP
    held_rows = max(held, GROUP)
    mixed = pl.pallas_call(
        functools.partial(mix_kernel, near, far, cores, held),
        in_specs=[VMEM] * (1 + len(parts)),
        out_specs=VMEM,
        out_shape=jax.ShapeDtypeStruct((cores * tiles, held, LANES), BF16),
        scratch_shapes=[
            pltpu.VMEM((all_rows, GROUP * BLOCK), BF16),
            pltpu.VMEM((all_rows * (1 if tiles <= 16 else 2), LANES), F32),
            pltpu.VMEM((cores * tiles, held_rows, LANES), F32),
            pltpu.VMEM((GROUP * BLOCK, length), BF16),
            pltpu.VMEM((cores + 1, held, length), F32),
        ],
        compiler_params=params(48),
        cost_estimate=cost(cores * held_rows * BLOCK * length * 256, 2 * MIB),
        name="mix",
    )(conv_taps, *parts[::-1])

    landed = lax.all_to_all(mixed, ("dp", "far", "near"), 0, 0, tiled=True).reshape(channels, rows)
    chunks = 8
    return pl.pallas_call(
        out_kernel,
        in_specs=[VMEM] * 2 + [HBM],
        out_specs=HBM,
        out_shape=jax.ShapeDtypeStruct((rows, width), BF16),
        scratch_shapes=[
            pltpu.VMEM((chunks, channels, width // chunks), BF16),
            pltpu.VMEM((chunks, rows, width // chunks), BF16),
            pltpu.SemaphoreType.DMA((chunks,)),
            pltpu.SemaphoreType.DMA((chunks,)),
        ],
        compiler_params=params(16),
        cost_estimate=cost(2 * rows * width * channels, 5 * MIB),
        name="project_out",
    )(gate_short, landed, *in_hbm(w_out))


def solution(mesh):
    count = mesh.shape["seq"]
    near = 4 if count % 4 == 0 else 1
    far = count // near
    seq_at = mesh.axis_names.index("seq")
    shape = list(mesh.devices.shape)
    shape[seq_at : seq_at + 1] = [far, near]
    names = list(mesh.axis_names)
    names[seq_at : seq_at + 1] = ["far", "near"]
    inner = Mesh(mesh.devices.reshape(shape), tuple(names))
    by_token = P(("dp", "far", "near"), None)
    by_row = P(("far", "near"), None)
    placed = (by_token, by_token, by_token, by_row, by_row, P(), P(), by_row, P())
    return jax.shard_map(
        functools.partial(on_device, near, far),
        mesh=inner,
        in_specs=placed,
        out_specs=by_token,
        check_vma=False,
    )
```

```python
import functools

import jax
import jax.numpy as jnp
from jax import lax
from jax.experimental import pallas as pl
from jax.experimental.pallas import tpu as pltpu
from jax.sharding import Mesh, PartitionSpec as P

F32 = jnp.float32
BF16 = jnp.bfloat16
LANES = 128
GROUP = 8
BLOCK = 32
SLOTS = LANES // BLOCK
MIB = 1 << 20
VMEM = pl.BlockSpec(memory_space=pltpu.VMEM)
HBM = pl.BlockSpec(memory_space=pltpu.HBM)


def params(mib):
    return pltpu.CompilerParams(vmem_limit_bytes=mib * MIB)


def cost(flops, accessed):
    return pl.CostEstimate(flops=flops, bytes_accessed=accessed, transcendentals=0)


def in_hbm(*arrays):
    return [pltpu.with_memory_space_constraint(array, pltpu.HBM) for array in arrays]


def sign_bytes(packed):
    parts = jnp.concatenate([packed & 255, packed >> 8], axis=1)
    return parts.astype(F32).astype(BF16)


def one_hot(rows, columns, source_of):
    at = lax.broadcasted_iota(jnp.int32, (rows, columns), 0)
    column = lax.broadcasted_iota(jnp.int32, (1, columns), 1)
    return (at == source_of(column)).astype(F32).astype(BF16)


def weights_kernel(value_ref, noise_ref, weight_ref, sems):
    half = weight_ref.shape[1] // 2
    columns = pl.ds(pl.multiple_of(lax.axis_index("dp") * half, half), half)
    copies = []
    for at, source in enumerate((value_ref, noise_ref)):
        target = weight_ref.at[:, at * half : (at + 1) * half]
        copies.append(pltpu.make_async_copy(source.at[:, columns], target, sems.at[at]))
        copies[-1].start()
    for copy in copies:
        copy.wait()


def pack_kernel(
    near, far, tokens_ref, in_ref, sent_ref, lags_ref, value_ref, noise_ref, weight_ref, *refs
):
    outs, (in_held, sent_held, lags_held, read_sems, weight_sems, token_sems) = refs[:near], refs[near:]
    core, far_at, near_at = lax.axis_index("dp"), lax.axis_index("far"), lax.axis_index("near")
    half = weight_ref.shape[1] // 2
    share = weight_ref.shape[0]
    depth = share * far
    words = in_ref.shape[1]
    per_part = words // (near * far)
    own_words = per_part * far

    copies = []
    for at, source in enumerate((value_ref, noise_ref)):
        columns = pl.ds(pl.multiple_of(core * half, half), half)
        target = weight_ref.at[:, at * half : (at + 1) * half]
        copies.append(pltpu.make_async_copy(source.at[:, columns], target, weight_sems.at[at]))
    reads = [
        pltpu.make_async_copy(in_ref, in_held, read_sems.at[0]),
        pltpu.make_async_copy(sent_ref, sent_held, read_sems.at[1]),
        pltpu.make_async_copy(
            lags_ref.at[:, pl.ds(pl.multiple_of(core * half, half), half)], lags_held, read_sems.at[2]
        ),
    ]
    for step, out in enumerate(outs):
        for turn in range(far):
            start = ((far_at ^ turn) * near + (near_at ^ step)) * share
            columns = pl.ds(pl.multiple_of(start, share), share)
            target = out.at[:, turn * share : (turn + 1) * share]
            copies.append(
                pltpu.make_async_copy(tokens_ref.at[:, columns], target, token_sems.at[step * far + turn])
            )
    for copy in reads + copies:
        copy.start()

    def word_of(column):
        step, rest = column // (2 * own_words), column % (2 * own_words)
        part, word = rest // own_words, rest % own_words
        plane = (word // per_part) ^ far_at
        return part * words + (plane * near + (step ^ near_at)) * per_part + word % per_part

    by_word = one_hot(2 * words, 2 * words, word_of)
    reads[0].wait()
    moved = jnp.dot(sign_bytes(in_held[...]), by_word, preferred_element_type=F32).astype(BF16)
    reads[1].wait()
    sent = sign_bytes(sent_held[...].astype(F32).T.astype(jnp.int32))
    held = half // (near * far)

    def channel_of(column):
        step, rest = column // (far * held), column % (far * held)
        return (rest // held * near + (step ^ near_at)) * held + rest % held

    reads[2].wait()
    lags = jnp.dot(
        lags_held[...].astype(BF16), one_hot(half, half, channel_of), preferred_element_type=F32
    ).astype(BF16)
    width, own_lags = 2 * own_words, far * held
    for step, out in enumerate(outs):
        out[:, depth : depth + width] = moved[:, step * width : (step + 1) * width]
        out[:, depth + width :] = jnp.concatenate(
            [sent, lags[:, step * own_lags : (step + 1) * own_lags]], axis=1
        )
    for copy in copies:
        copy.wait()


def spread_signs(pair, byte_of, columns):
    spread = jnp.dot(pair, one_hot(pair.shape[1], columns, byte_of), preferred_element_type=F32)
    mask = 1 << (lax.broadcasted_iota(jnp.int32, (1, columns), 1) & 7)
    return jnp.where((spread.astype(jnp.int32) & mask) != 0, 1.0, -1.0)


def spaced(lines, held):
    if held >= GROUP:
        return lines
    spare = jnp.zeros((GROUP - held, lines.shape[1]), F32)
    split = [lines[at : at + held] for at in range(0, lines.shape[0], held)]
    return jnp.concatenate([part for own in split for part in (own, spare)], axis=0)


def joined(chunks, start, stop):
    return jnp.concatenate([chunk[:, start:stop] for chunk in chunks], axis=0)


def flips(chunks, depth, cores, half):
    core = lax.axis_index("dp")
    words = depth // 16
    sent_words = cores * half // 16
    sent_start = depth + 2 * words

    def in_byte(column):
        return (column >> 4) + words * ((column >> 3) & 1)

    def out_byte(column):
        return core * (half // 16) + (column >> 4) + sent_words * ((column >> 3) & 1)

    flip_in = spread_signs(joined(chunks, depth, sent_start), in_byte, depth).astype(BF16)
    sent = joined(chunks, sent_start, sent_start + 2 * sent_words)
    return flip_in, spread_signs(sent, out_byte, half)


def products(chunks, flip_in, pieces, half):
    mean_part, noise_part = 0.0, 0.0
    for at, piece in enumerate(pieces):
        own = slice(at * piece.shape[0], (at + 1) * piece.shape[0])
        tokens = joined(chunks, own.start, own.stop)
        mean_part += jnp.dot(tokens, piece[:, :half], preferred_element_type=F32)
        noise_part += jnp.dot(tokens * flip_in[:, own], piece[:, half:], preferred_element_type=F32)
    return mean_part, noise_part


def project_kernel(near, cores, depth, *refs):
    mean_ref, noise_ref, flip_ref, flipped_ref, lags_ref = refs[-5:]
    count = near * cores - 1
    chunks, pieces = refs[:count][::-1], refs[count:-5]
    rows = chunks[0].shape[0]
    half = pieces[0].shape[1] // 2
    step = pieces[0].shape[0]
    flip_in, flip_out = flips(chunks, depth, cores, half)
    flip_ref[...] = flip_out.astype(BF16)
    flipped_ref[...] = joined(chunks, depth - step, depth) * flip_in[:, depth - step :]
    mean_ref[...], noise_ref[...] = products(chunks, flip_in, pieces, half)
    for turn in range(near):
        own_lags = chunks[turn][:, chunks[turn].shape[1] - lags_ref.shape[0] :].astype(F32).T
        at = pl.multiple_of((lax.axis_index("near") ^ turn) * rows, rows)
        lags_ref[:, pl.ds(at, rows)] = own_lags


def finish_kernel(near, far, cores, depth, mean_ref, noise_ref, flip_ref, flipped_ref, *refs):
    outs, whole_ref = refs[-1 - near : -1], refs[-1]
    chunks, pieces = refs[: near * cores][::-1], refs[near * cores : -1 - near]
    core, near_at = lax.axis_index("dp"), lax.axis_index("near")
    rows = chunks[0].shape[0]
    step, half = pieces[0].shape[0], pieces[0].shape[1] // 2
    last = pieces[-1]
    flip_in, flip_out = flips(chunks[-1:], depth, cores, half)
    mean_late, noise_late = products(chunks[-1:], flip_in, pieces, half)
    tokens = joined(chunks[:-1], depth - step, depth)
    mean_part = mean_ref[...] + jnp.dot(tokens, last[:, :half], preferred_element_type=F32)
    noise_part = noise_ref[...] + jnp.dot(flipped_ref[...], last[:, half:], preferred_element_type=F32)
    held = half // (near * far)
    stride = max(held, GROUP)
    value = jnp.concatenate(
        [mean_part + flip_ref[...].astype(F32) * noise_part, mean_late + flip_out * noise_late], axis=0
    )
    value = spaced(value.T, held)
    for part in range(cores):
        for turn in range(near):
            at = part * near + turn
            target = ((core ^ part) * near + (near_at ^ turn)) * rows
            whole_ref[:, pl.ds(pl.multiple_of(target, rows), rows)] = value[:, at * rows : (at + 1) * rows]
    for turn, out in enumerate(outs):
        for plane in range(far):
            at = pl.multiple_of((plane * near + (near_at ^ turn)) * stride, stride)
            out[plane * held : (plane + 1) * held, :] = whole_ref[pl.ds(at, held), :].astype(BF16)


def sum_kernel(near, far, lags_ref, *refs):
    parts, outs, whole_ref = refs[:near], refs[near : near + far], refs[-1]
    far_at = lax.axis_index("far")
    held = outs[0].shape[0]
    stride = max(held, GROUP)
    span = parts[0].shape[1]
    total = 0.0
    for part in parts:
        total += part[...].astype(F32)
    whole_ref[:, :span] = spaced(total, held)
    whole_ref[:, span:] = spaced(lags_ref[...], held)
    for turn, out in enumerate(outs):
        at = pl.multiple_of((far_at ^ turn) * stride, stride)
        out[...] = whole_ref[pl.ds(at, held), :].astype(BF16)


def shifted(values, steps):
    moved = pltpu.roll(values, steps, 1)
    at = lax.broadcasted_iota(jnp.int32, values.shape, 1)
    return jnp.where(at >= steps, moved, 0.0)


def lane_roll(values, steps):
    return pltpu.roll(values, steps % LANES, values.ndim - 1) if steps % LANES else values


def mix_kernel(near, far, cores, held, taps_ref, *refs):
    parts, (out_ref, left_ref, sums_ref, done_ref, table_ref, lines_ref) = refs[:-6][::-1], refs[-6:]
    tiles = out_ref.shape[0] // cores
    block_rows = cores * GROUP
    tile_rows = SLOTS * block_rows
    rows = tiles * tile_rows
    lane = lax.broadcasted_iota(jnp.int32, (1, LANES), 1)
    pair = 2 * LANES
    span = near * LANES

    def padded(lines):
        if held >= GROUP:
            return lines
        return jnp.concatenate([lines, jnp.zeros((GROUP - held, lines.shape[1]), F32)], axis=0)

    for turn, part in enumerate(parts):
        for plane in range(far // len(parts)):
            own = slice(plane * held, (plane + 1) * held)
            target = pl.multiple_of(((lax.axis_index("far") if len(parts) > 1 else plane) ^ turn) * span, span)
            for line in range(cores + 1):
                piece = part[own, line * span : (line + 1) * span]
                lines_ref[line, :, pl.ds(target, span)] = piece.astype(F32)
    half = held * near * far
    position = lax.axis_index("far") * near + lax.axis_index("near")
    first = lax.axis_index("dp") * half + position * held
    channel = lax.broadcasted_iota(jnp.int32, (held, cores * half), 1) - first
    chosen = channel == lax.broadcasted_iota(jnp.int32, (held, cores * half), 0)
    taps = [
        jnp.sum(jnp.where(chosen, taps_ref[lag : lag + 1, : cores * half], 0.0), axis=1, keepdims=True)
        for lag in range(3)
    ]
    signals = []
    for part in range(cores):
        value = lines_ref[part]
        signal = taps[0] * value
        for lag in range(1, 3):
            signal += taps[lag] * shifted(value, lag)
        signals.append(padded(signal))
    lags = padded(lines_ref[cores])

    for group in range(max(held, GROUP) // GROUP):
        own = slice(group * GROUP, (group + 1) * GROUP)
        for at in range(GROUP):
            row = lags[group * GROUP + at : group * GROUP + at + 1, :]
            repeated = jnp.broadcast_to(row, (BLOCK, row.shape[1]))
            turned = pltpu.roll(repeated, 0, 1, stride=1, stride_axis=0)
            column = lax.broadcasted_iota(jnp.int32, repeated.shape, 1)
            lag = lax.broadcasted_iota(jnp.int32, repeated.shape, 0)
            kept = jnp.where(column >= lag, turned, 0.0).astype(BF16)
            table_ref[at * BLOCK : (at + 1) * BLOCK, :] = kept

        stacked = jnp.concatenate(
            [
                signal[own, a * LANES : (a + 1) * LANES]
                for a in range(tiles)
                for signal in signals
            ],
            axis=0,
        )
        slot_of = lax.broadcasted_iota(jnp.int32, stacked.shape, 0) % SLOTS
        turned = stacked
        for slot in range(1, SLOTS):
            turned = jnp.where(slot_of == slot, lane_roll(stacked, BLOCK * slot), turned)
        spread = jnp.stack(
            [
                lane_roll(turned, -BLOCK * slot).reshape(tiles, block_rows, LANES)
                for slot in range(SLOTS)
            ],
            axis=1,
        ).reshape(rows, LANES)
        owner = lax.broadcasted_iota(jnp.int32, (rows, LANES), 0) % GROUP
        for half in range(GROUP // SLOTS):
            kept = jnp.where(owner == lane // BLOCK + half * SLOTS, spread, 0.0)
            left_ref[:, half * LANES : (half + 1) * LANES] = kept.astype(BF16)

        if tiles <= 16:
            for at in range(tiles // 2):
                start = 2 * at * tile_rows
                partial = jnp.dot(
                    left_ref[: rows - start, :],
                    table_ref[:, at * pair : (at + 1) * pair],
                    preferred_element_type=F32,
                )
                if at == 0:
                    sums_ref[...] = partial[:, :LANES]
                else:
                    sums_ref[start:rows, :] += partial[:, :LANES]
                sums_ref[start + tile_rows : rows, :] += partial[: rows - start - tile_rows, LANES:]
        else:
            sums_ref[...] = jnp.zeros_like(sums_ref)

            def add(at, _):
                partial = jnp.dot(
                    left_ref[...],
                    table_ref[:, pl.ds(pl.multiple_of(at * pair, pair), pair)],
                    preferred_element_type=F32,
                )
                start = pl.multiple_of(2 * at * tile_rows, tile_rows)
                sums_ref[pl.ds(start, rows), :] += partial[:, :LANES]
                sums_ref[pl.ds(start + tile_rows, rows), :] += partial[:, LANES:]
                return 0

            lax.fori_loop(0, tiles // 2, add, 0)

        sums = sums_ref[:rows, :]
        landed = [0.0] * SLOTS
        for part in range(SLOTS):
            late = sums
            if part:
                ahead = jnp.zeros((part * block_rows, LANES), F32)
                late = jnp.concatenate([ahead, sums[: rows - part * block_rows]], axis=0)
            late = late.reshape(tiles, SLOTS, block_rows, LANES)
            for slot in range(SLOTS):
                moved = late[:, slot].reshape(tiles * block_rows, LANES)
                landed[slot] += lane_roll(moved, BLOCK * (slot - part))
        result = 0.0
        for slot in range(SLOTS):
            result += jnp.where(lane // BLOCK == slot, landed[slot], 0.0)
        result = result.reshape(tiles, cores, GROUP, LANES)
        for part in range(cores):
            done_ref[part * tiles : (part + 1) * tiles, own, :] = result[:, part]

    out_ref[...] = done_ref[:, :held, :].astype(BF16)


def gate_kernel(gate_ref, before_ref, taps_ref, out_ref):
    channels = gate_ref.shape[1]
    gate = gate_ref[...].astype(F32)
    extended = jnp.concatenate([before_ref[...].astype(F32), gate], axis=0)
    gate_short = taps_ref[0:1, channels:] * gate
    for lag in range(1, 3):
        gate_short += taps_ref[lag : lag + 1, channels:] * extended[2 - lag : 2 - lag + gate.shape[0]]
    out_ref[...] = gate_short


def out_kernel(gate_ref, mixed_ref, source_ref, target_ref, weight_ref, held_ref, read_sems, write_sems):
    chunks, _, step = weight_ref.shape
    reads = []
    for at in range(chunks):
        columns = source_ref.at[:, pl.ds(at * step, step)]
        reads.append(pltpu.make_async_copy(columns, weight_ref.at[at], read_sems.at[at]))
        reads[-1].start()
    gated = (gate_ref[...] * mixed_ref[...].astype(F32).T).astype(BF16)
    writes = []
    for at in range(chunks):
        reads[at].wait()
        held_ref[at] = jnp.dot(gated, weight_ref[at], preferred_element_type=F32).astype(BF16)
        columns = target_ref.at[:, pl.ds(at * step, step)]
        writes.append(pltpu.make_async_copy(held_ref.at[at], columns, write_sems.at[at]))
        writes[-1].start()
    for write in writes:
        write.wait()


def exchanged(value, axis, step):
    return lax.ppermute(value, axis, [(i, i ^ step) for i in range(lax.axis_size(axis))])


def all_exchanged(values, axis):
    result = list(values)
    for step in reversed(range(1, len(values))):
        result[step] = exchanged(values[step], axis, step)
    return result


def on_device(near, far, tokens, sign_in, sign_out, w_value, w_noise, w_gate, conv_taps, long_filter, w_out):
    rows, width = tokens.shape
    channels = w_gate.shape[1]
    cores = lax.axis_size("dp")
    count = near * far
    half = channels // cores
    held = half // count
    share = w_value.shape[0]
    depth = share * far
    length = count * rows
    near_at, core = lax.axis_index("near"), lax.axis_index("dp")

    lags_start = depth + depth // 8 + channels // 8
    packed_width = lags_start + far * held
    if share % LANES == 0 and far == 4:
        first = pl.pallas_call(
            weights_kernel,
            in_specs=[HBM] * 2,
            out_specs=VMEM,
            out_shape=jax.ShapeDtypeStruct((share, 2 * half), BF16),
            scratch_shapes=[pltpu.SemaphoreType.DMA((2,))],
            compiler_params=params(2),
            cost_estimate=cost(0, MIB // 2),
            name="weights",
        )(*in_hbm(w_value, w_noise))
        far_weights = exchanged(first, "far", 2)
        late_tokens, first = lax.optimization_barrier((tokens, first))
        weights, *chunks = pl.pallas_call(
            functools.partial(pack_kernel, near, far),
            in_specs=[HBM] * 6,
            out_specs=[VMEM] * (1 + near),
            out_shape=[jax.ShapeDtypeStruct((share, 2 * half), BF16)]
            + [jax.ShapeDtypeStruct((rows, packed_width), BF16)] * near,
            scratch_shapes=[
                pltpu.VMEM(sign_in.shape, jnp.int32),
                pltpu.VMEM(sign_out.shape[::-1], jnp.int32),
                pltpu.VMEM((rows, half), F32),
                pltpu.SemaphoreType.DMA((3,)),
                pltpu.SemaphoreType.DMA((2,)),
                pltpu.SemaphoreType.DMA((near * far,)),
            ],
            compiler_params=params(16),
            cost_estimate=cost(2 * rows * 512 * 512, 3 * MIB),
            name="pack",
        )(*in_hbm(late_tokens, sign_in, sign_out.T, long_filter, w_value, w_noise))
        pieces = [weights, exchanged(weights, "far", 1), far_weights, None]
    else:
        own = lax.dynamic_slice_in_dim(jnp.stack([w_value, w_noise]), core * half, half, axis=2)
        own = own.transpose(1, 0, 2).reshape(share, 2 * half)
        pieces = [lax.all_gather(own, "far", axis=0, tiled=True)]
        order = jnp.arange(near) ^ near_at

        def by_owner(array):
            parts = array.reshape(rows, far, near, -1).transpose(2, 0, 1, 3).reshape(near, rows, -1)
            return jnp.take(parts, order, axis=0)

        words = by_owner(sign_in)
        sent = jnp.broadcast_to(sign_out[None], (near, *sign_out.shape))
        own_lags = lax.dynamic_slice_in_dim(long_filter, core * half, half, axis=1)
        signs = [words & 255, words >> 8, sent & 255, sent >> 8, by_owner(own_lags)]
        packed = [by_owner(tokens)] + [part.astype(BF16) for part in signs]
        chunks = list(jnp.concatenate(packed, axis=2))
    chunks = all_exchanged(chunks, "near")

    late_tokens = tokens
    if len(pieces) > 1:
        late_tokens, pieces[2] = lax.optimization_barrier((tokens, pieces[2]))
        pieces[3] = exchanged(pieces[2], "far", 1)
    gate_rows = jnp.dot(late_tokens, w_gate, preferred_element_type=F32).astype(BF16)
    late = 1 % len(pieces)
    pieces[late], chunks[0], gate_rows = lax.optimization_barrier((pieces[late], chunks[0], gate_rows))
    for step in range(1, near):
        chunks[step], _ = lax.optimization_barrier((chunks[step], gate_rows))
    pieces[-1], chunks[-1] = lax.optimization_barrier((pieces[-1], chunks[-1]))
    chunks += [exchanged(chunk, "dp", 1) for chunk in chunks]

    if len(pieces) == 1:
        pieces = [pieces[0][: depth // 2], pieces[0][depth // 2 :]]
    step = depth // len(pieces)
    early = (cores * near - 1) * rows
    *kept, lags = pl.pallas_call(
        functools.partial(project_kernel, near, cores, depth),
        in_specs=[VMEM] * (len(chunks) + len(pieces) - 2),
        out_specs=[VMEM] * 5,
        out_shape=[
            jax.ShapeDtypeStruct((early, half), F32),
            jax.ShapeDtypeStruct((early, half), F32),
            jax.ShapeDtypeStruct((early, half), BF16),
            jax.ShapeDtypeStruct((early, step), BF16),
            jax.ShapeDtypeStruct((far * held, near * rows), F32),
        ],
        compiler_params=params(32),
        cost_estimate=cost(4 * early * (depth - step) * half, 5 * MIB),
        name="project",
    )(*chunks[-2::-1], *pieces[:-1])
    near_shape = jax.ShapeDtypeStruct((far * held, cores * near * rows), BF16)
    partial = pl.pallas_call(
        functools.partial(finish_kernel, near, far, cores, depth),
        in_specs=[VMEM] * (4 + len(chunks) + len(pieces)),
        out_specs=[VMEM] * near,
        out_shape=[near_shape] * near,
        scratch_shapes=[pltpu.VMEM((count * max(held, GROUP), near_shape.shape[1]), F32)],
        compiler_params=params(32),
        cost_estimate=cost(4 * (early * step + rows * depth) * half, 3 * MIB),
        name="finish",
    )(*kept, *chunks[::-1], *pieces)
    partial = list(partial)
    last_rows, partial[0] = lax.optimization_barrier((gate_rows[rows - 2 :], partial[0]))
    before = lax.ppermute(last_rows, ("far", "near"), [(i, i + 1) for i in range(count - 1)])
    partial = all_exchanged(partial, "near")
    *partial[::-1], before = lax.optimization_barrier((*partial[::-1], before))

    far_shape = (held, (cores + 1) * near * rows)
    parts = pl.pallas_call(
        functools.partial(sum_kernel, near, far),
        in_specs=[VMEM] * (1 + near),
        out_specs=[VMEM] * far,
        out_shape=[jax.ShapeDtypeStruct(far_shape, BF16)] * far,
        scratch_shapes=[pltpu.VMEM((far * max(held, GROUP), far_shape[1]), F32)],
        compiler_params=params(16),
        cost_estimate=cost(MIB, MIB),
        name="sum",
    )(lags, *partial[::-1])
    if far == 4:
        parts = all_exchanged(parts, "far")
    else:
        order = jnp.arange(far) ^ lax.axis_index("far")
        parts = lax.all_to_all(jnp.take(jnp.stack(parts), order, axis=0), "far", 0, 0, tiled=True)
        parts = [parts.reshape(far * held, far_shape[1])]

    gate_short = pl.pallas_call(
        gate_kernel,
        in_specs=[VMEM] * 3,
        out_specs=VMEM,
        out_shape=jax.ShapeDtypeStruct((rows, channels), F32),
        compiler_params=params(4),
        cost_estimate=cost(rows * channels * 6, MIB // 2),
        name="gate",
    )(gate_rows, before, conv_taps)
    parts[0], gate_short = lax.optimization_barrier((parts[0], gate_short))

    tiles = length // LANES
    all_rows = tiles * SLOTS * cores * GROUP
    held_rows = max(held, GROUP)
    mixed = pl.pallas_call(
        functools.partial(mix_kernel, near, far, cores, held),
        in_specs=[VMEM] * (1 + len(parts)),
        out_specs=VMEM,
        out_shape=jax.ShapeDtypeStruct((cores * tiles, held, LANES), BF16),
        scratch_shapes=[
            pltpu.VMEM((all_rows, GROUP * BLOCK), BF16),
            pltpu.VMEM((all_rows * (1 if tiles <= 16 else 2), LANES), F32),
            pltpu.VMEM((cores * tiles, held_rows, LANES), F32),
            pltpu.VMEM((GROUP * BLOCK, length), BF16),
            pltpu.VMEM((cores + 1, held, length), F32),
        ],
        compiler_params=params(48),
        cost_estimate=cost(cores * held_rows * BLOCK * length * 256, 2 * MIB),
        name="mix",
    )(conv_taps, *parts[::-1])

    landed = lax.all_to_all(mixed, ("dp", "far", "near"), 0, 0, tiled=True).reshape(channels, rows)
    chunks = 8
    return pl.pallas_call(
        out_kernel,
        in_specs=[VMEM] * 2 + [HBM],
        out_specs=HBM,
        out_shape=jax.ShapeDtypeStruct((rows, width), BF16),
        scratch_shapes=[
            pltpu.VMEM((chunks, channels, width // chunks), BF16),
            pltpu.VMEM((chunks, rows, width // chunks), BF16),
            pltpu.SemaphoreType.DMA((chunks,)),
            pltpu.SemaphoreType.DMA((chunks,)),
        ],
        compiler_params=params(16),
        cost_estimate=cost(2 * rows * width * channels, 5 * MIB),
        name="project_out",
    )(gate_short, landed, *in_hbm(w_out))


def solution(mesh):
    count = mesh.shape["seq"]
    near = 4 if count % 4 == 0 else 1
    far = count // near
    seq_at = mesh.axis_names.index("seq")
    shape = list(mesh.devices.shape)
    shape[seq_at : seq_at + 1] = [far, near]
    names = list(mesh.axis_names)
    names[seq_at : seq_at + 1] = ["far", "near"]
    inner = Mesh(mesh.devices.reshape(shape), tuple(names))
    by_token = P(("dp", "far", "near"), None)
    by_row = P(("far", "near"), None)
    placed = (by_token, by_token, by_token, by_row, by_row, P(), P(), by_row, P())
    return jax.shard_map(
        functools.partial(on_device, near, far),
        mesh=inner,
        in_specs=placed,
        out_specs=by_token,
        check_vma=False,
    )
```

```python
import functools

import jax
import jax.numpy as jnp
from jax import lax
from jax.experimental import pallas as pl
from jax.experimental.pallas import tpu as pltpu
from jax.sharding import Mesh, PartitionSpec as P

F32 = jnp.float32
BF16 = jnp.bfloat16
LANES = 128
GROUP = 8
BLOCK = 32
SLOTS = LANES // BLOCK
MIB = 1 << 20
VMEM = pl.BlockSpec(memory_space=pltpu.VMEM)
HBM = pl.BlockSpec(memory_space=pltpu.HBM)


def params(mib):
    return pltpu.CompilerParams(vmem_limit_bytes=mib * MIB)


def cost(flops, accessed):
    return pl.CostEstimate(flops=flops, bytes_accessed=accessed, transcendentals=0)


def in_hbm(*arrays):
    return [pltpu.with_memory_space_constraint(array, pltpu.HBM) for array in arrays]


def sign_bytes(packed):
    parts = jnp.concatenate([packed & 255, packed >> 8], axis=1)
    return parts.astype(F32).astype(BF16)


def one_hot(rows, columns, source_of):
    at = lax.broadcasted_iota(jnp.int32, (rows, columns), 0)
    column = lax.broadcasted_iota(jnp.int32, (1, columns), 1)
    return (at == source_of(column)).astype(F32).astype(BF16)


def weights_kernel(value_ref, noise_ref, weight_ref, sems):
    half = weight_ref.shape[1] // 2
    columns = pl.ds(pl.multiple_of(lax.axis_index("dp") * half, half), half)
    copies = []
    for at, source in enumerate((value_ref, noise_ref)):
        target = weight_ref.at[:, at * half : (at + 1) * half]
        copies.append(pltpu.make_async_copy(source.at[:, columns], target, sems.at[at]))
        copies[-1].start()
    for copy in copies:
        copy.wait()


def pack_kernel(
    near, far, tokens_ref, in_ref, sent_ref, lags_ref, value_ref, noise_ref, weight_ref, *refs
):
    outs, (in_held, sent_held, lags_held, read_sems, weight_sems, token_sems) = refs[:near], refs[near:]
    core, far_at, near_at = lax.axis_index("dp"), lax.axis_index("far"), lax.axis_index("near")
    half = weight_ref.shape[1] // 2
    share = weight_ref.shape[0]
    depth = share * far
    words = in_ref.shape[1]
    per_part = words // (near * far)
    own_words = per_part * far

    copies = []
    for at, source in enumerate((value_ref, noise_ref)):
        columns = pl.ds(pl.multiple_of(core * half, half), half)
        target = weight_ref.at[:, at * half : (at + 1) * half]
        copies.append(pltpu.make_async_copy(source.at[:, columns], target, weight_sems.at[at]))
    reads = [
        pltpu.make_async_copy(in_ref, in_held, read_sems.at[0]),
        pltpu.make_async_copy(sent_ref, sent_held, read_sems.at[1]),
        pltpu.make_async_copy(
            lags_ref.at[:, pl.ds(pl.multiple_of(core * half, half), half)], lags_held, read_sems.at[2]
        ),
    ]
    for step, out in enumerate(outs):
        for turn in range(far):
            start = ((far_at ^ turn) * near + (near_at ^ step)) * share
            columns = pl.ds(pl.multiple_of(start, share), share)
            target = out.at[:, turn * share : (turn + 1) * share]
            copies.append(
                pltpu.make_async_copy(tokens_ref.at[:, columns], target, token_sems.at[step * far + turn])
            )
    for copy in reads + copies:
        copy.start()

    def word_of(column):
        step, rest = column // (2 * own_words), column % (2 * own_words)
        part, word = rest // own_words, rest % own_words
        plane = (word // per_part) ^ far_at
        return part * words + (plane * near + (step ^ near_at)) * per_part + word % per_part

    by_word = one_hot(2 * words, 2 * words, word_of)
    reads[0].wait()
    moved = jnp.dot(sign_bytes(in_held[...]), by_word, preferred_element_type=F32).astype(BF16)
    reads[1].wait()
    sent = sign_bytes(sent_held[...].astype(F32).T.astype(jnp.int32))
    held = half // (near * far)

    def channel_of(column):
        step, rest = column // (far * held), column % (far * held)
        return (rest // held * near + (step ^ near_at)) * held + rest % held

    reads[2].wait()
    lags = jnp.dot(
        lags_held[...].astype(BF16), one_hot(half, half, channel_of), preferred_element_type=F32
    ).astype(BF16)
    width, own_lags = 2 * own_words, far * held
    for step, out in enumerate(outs):
        out[:, depth : depth + width] = moved[:, step * width : (step + 1) * width]
        out[:, depth + width :] = jnp.concatenate(
            [sent, lags[:, step * own_lags : (step + 1) * own_lags]], axis=1
        )
    for copy in copies:
        copy.wait()


def spread_signs(pair, byte_of, columns):
    spread = jnp.dot(pair, one_hot(pair.shape[1], columns, byte_of), preferred_element_type=F32)
    mask = 1 << (lax.broadcasted_iota(jnp.int32, (1, columns), 1) & 7)
    return jnp.where((spread.astype(jnp.int32) & mask) != 0, 1.0, -1.0)


def spaced(lines, held):
    if held >= GROUP:
        return lines
    spare = jnp.zeros((GROUP - held, lines.shape[1]), F32)
    split = [lines[at : at + held] for at in range(0, lines.shape[0], held)]
    return jnp.concatenate([part for own in split for part in (own, spare)], axis=0)


def joined(chunks, start, stop):
    return jnp.concatenate([chunk[:, start:stop] for chunk in chunks], axis=0)


def flips(chunks, depth, cores, half):
    core = lax.axis_index("dp")
    words = depth // 16
    sent_words = cores * half // 16
    sent_start = depth + 2 * words

    def in_byte(column):
        return (column >> 4) + words * ((column >> 3) & 1)

    def out_byte(column):
        return core * (half // 16) + (column >> 4) + sent_words * ((column >> 3) & 1)

    flip_in = spread_signs(joined(chunks, depth, sent_start), in_byte, depth).astype(BF16)
    sent = joined(chunks, sent_start, sent_start + 2 * sent_words)
    return flip_in, spread_signs(sent, out_byte, half)


def products(chunks, flip_in, pieces, half):
    mean_part, noise_part = 0.0, 0.0
    for at, piece in enumerate(pieces):
        own = slice(at * piece.shape[0], (at + 1) * piece.shape[0])
        tokens = joined(chunks, own.start, own.stop)
        mean_part += jnp.dot(tokens, piece[:, :half], preferred_element_type=F32)
        noise_part += jnp.dot(tokens * flip_in[:, own], piece[:, half:], preferred_element_type=F32)
    return mean_part, noise_part


def project_kernel(near, cores, depth, *refs):
    mean_ref, noise_ref, flip_ref, flipped_ref, lags_ref = refs[-5:]
    count = near * cores - 1
    chunks, pieces = refs[:count][::-1], refs[count:-5]
    rows = chunks[0].shape[0]
    half = pieces[0].shape[1] // 2
    step = pieces[0].shape[0]
    flip_in, flip_out = flips(chunks, depth, cores, half)
    flip_ref[...] = flip_out.astype(BF16)
    flipped_ref[...] = joined(chunks, depth - step, depth) * flip_in[:, depth - step :]
    mean_ref[...], noise_ref[...] = products(chunks, flip_in, pieces, half)
    for turn in range(near):
        own_lags = chunks[turn][:, chunks[turn].shape[1] - lags_ref.shape[0] :].astype(F32).T
        at = pl.multiple_of((lax.axis_index("near") ^ turn) * rows, rows)
        lags_ref[:, pl.ds(at, rows)] = own_lags


def finish_kernel(near, far, cores, depth, mean_ref, noise_ref, flip_ref, flipped_ref, *refs):
    outs, whole_ref = refs[-1 - near : -1], refs[-1]
    chunks, pieces = refs[: near * cores][::-1], refs[near * cores : -1 - near]
    core, near_at = lax.axis_index("dp"), lax.axis_index("near")
    rows = chunks[0].shape[0]
    step, half = pieces[0].shape[0], pieces[0].shape[1] // 2
    last = pieces[-1]
    flip_in, flip_out = flips(chunks[-1:], depth, cores, half)
    mean_late, noise_late = products(chunks[-1:], flip_in, pieces, half)
    tokens = joined(chunks[:-1], depth - step, depth)
    mean_part = mean_ref[...] + jnp.dot(tokens, last[:, :half], preferred_element_type=F32)
    noise_part = noise_ref[...] + jnp.dot(flipped_ref[...], last[:, half:], preferred_element_type=F32)
    held = half // (near * far)
    stride = max(held, GROUP)
    value = jnp.concatenate(
        [mean_part + flip_ref[...].astype(F32) * noise_part, mean_late + flip_out * noise_late], axis=0
    )
    value = spaced(value.T, held)
    for part in range(cores):
        for turn in range(near):
            at = part * near + turn
            target = ((core ^ part) * near + (near_at ^ turn)) * rows
            whole_ref[:, pl.ds(pl.multiple_of(target, rows), rows)] = value[:, at * rows : (at + 1) * rows]
    for turn, out in enumerate(outs):
        for plane in range(far):
            at = pl.multiple_of((plane * near + (near_at ^ turn)) * stride, stride)
            out[plane * held : (plane + 1) * held, :] = whole_ref[pl.ds(at, held), :].astype(BF16)


def sum_kernel(near, far, lags_ref, *refs):
    parts, outs, whole_ref = refs[:near], refs[near : near + far], refs[-1]
    far_at = lax.axis_index("far")
    held = outs[0].shape[0]
    stride = max(held, GROUP)
    span = parts[0].shape[1]
    total = 0.0
    for part in parts:
        total += part[...].astype(F32)
    whole_ref[:, :span] = spaced(total, held)
    whole_ref[:, span:] = spaced(lags_ref[...], held)
    for turn, out in enumerate(outs):
        at = pl.multiple_of((far_at ^ turn) * stride, stride)
        out[...] = whole_ref[pl.ds(at, held), :].astype(BF16)


def shifted(values, steps):
    moved = pltpu.roll(values, steps, 1)
    at = lax.broadcasted_iota(jnp.int32, values.shape, 1)
    return jnp.where(at >= steps, moved, 0.0)


def lane_roll(values, steps):
    return pltpu.roll(values, steps % LANES, values.ndim - 1) if steps % LANES else values


def mix_kernel(near, far, cores, held, taps_ref, *refs):
    parts, (out_ref, left_ref, sums_ref, done_ref, table_ref, lines_ref) = refs[:-6][::-1], refs[-6:]
    tiles = out_ref.shape[0] // cores
    block_rows = cores * GROUP
    tile_rows = SLOTS * block_rows
    rows = tiles * tile_rows
    lane = lax.broadcasted_iota(jnp.int32, (1, LANES), 1)
    pair = 2 * LANES
    span = near * LANES

    def padded(lines):
        if held >= GROUP:
            return lines
        return jnp.concatenate([lines, jnp.zeros((GROUP - held, lines.shape[1]), F32)], axis=0)

    for turn, part in enumerate(parts):
        for plane in range(far // len(parts)):
            own = slice(plane * held, (plane + 1) * held)
            target = pl.multiple_of(((lax.axis_index("far") if len(parts) > 1 else plane) ^ turn) * span, span)
            for line in range(cores + 1):
                piece = part[own, line * span : (line + 1) * span]
                lines_ref[line, :, pl.ds(target, span)] = piece.astype(F32)
    half = held * near * far
    position = lax.axis_index("far") * near + lax.axis_index("near")
    first = lax.axis_index("dp") * half + position * held
    channel = lax.broadcasted_iota(jnp.int32, (held, cores * half), 1) - first
    chosen = channel == lax.broadcasted_iota(jnp.int32, (held, cores * half), 0)
    taps = [
        jnp.sum(jnp.where(chosen, taps_ref[lag : lag + 1, : cores * half], 0.0), axis=1, keepdims=True)
        for lag in range(3)
    ]
    signals = []
    for part in range(cores):
        value = lines_ref[part]
        signal = taps[0] * value
        for lag in range(1, 3):
            signal += taps[lag] * shifted(value, lag)
        signals.append(padded(signal))
    lags = padded(lines_ref[cores])

    for group in range(max(held, GROUP) // GROUP):
        own = slice(group * GROUP, (group + 1) * GROUP)
        for at in range(GROUP):
            row = lags[group * GROUP + at : group * GROUP + at + 1, :]
            repeated = jnp.broadcast_to(row, (BLOCK, row.shape[1]))
            turned = pltpu.roll(repeated, 0, 1, stride=1, stride_axis=0)
            column = lax.broadcasted_iota(jnp.int32, repeated.shape, 1)
            lag = lax.broadcasted_iota(jnp.int32, repeated.shape, 0)
            kept = jnp.where(column >= lag, turned, 0.0).astype(BF16)
            table_ref[at * BLOCK : (at + 1) * BLOCK, :] = kept

        stacked = jnp.concatenate(
            [
                signal[own, a * LANES : (a + 1) * LANES]
                for a in range(tiles)
                for signal in signals
            ],
            axis=0,
        )
        slot_of = lax.broadcasted_iota(jnp.int32, stacked.shape, 0) % SLOTS
        turned = stacked
        for slot in range(1, SLOTS):
            turned = jnp.where(slot_of == slot, lane_roll(stacked, BLOCK * slot), turned)
        spread = jnp.stack(
            [
                lane_roll(turned, -BLOCK * slot).reshape(tiles, block_rows, LANES)
                for slot in range(SLOTS)
            ],
            axis=1,
        ).reshape(rows, LANES)
        owner = lax.broadcasted_iota(jnp.int32, (rows, LANES), 0) % GROUP
        for half in range(GROUP // SLOTS):
            kept = jnp.where(owner == lane // BLOCK + half * SLOTS, spread, 0.0)
            left_ref[:, half * LANES : (half + 1) * LANES] = kept.astype(BF16)

        if tiles <= 16:
            for at in range(tiles // 2):
                start = 2 * at * tile_rows
                partial = jnp.dot(
                    left_ref[: rows - start, :],
                    table_ref[:, at * pair : (at + 1) * pair],
                    preferred_element_type=F32,
                )
                if at == 0:
                    sums_ref[...] = partial[:, :LANES]
                else:
                    sums_ref[start:rows, :] += partial[:, :LANES]
                sums_ref[start + tile_rows : rows, :] += partial[: rows - start - tile_rows, LANES:]
        else:
            sums_ref[...] = jnp.zeros_like(sums_ref)

            def add(at, _):
                partial = jnp.dot(
                    left_ref[...],
                    table_ref[:, pl.ds(pl.multiple_of(at * pair, pair), pair)],
                    preferred_element_type=F32,
                )
                start = pl.multiple_of(2 * at * tile_rows, tile_rows)
                sums_ref[pl.ds(start, rows), :] += partial[:, :LANES]
                sums_ref[pl.ds(start + tile_rows, rows), :] += partial[:, LANES:]
                return 0

            lax.fori_loop(0, tiles // 2, add, 0)

        sums = sums_ref[:rows, :]
        landed = [0.0] * SLOTS
        for part in range(SLOTS):
            late = sums
            if part:
                ahead = jnp.zeros((part * block_rows, LANES), F32)
                late = jnp.concatenate([ahead, sums[: rows - part * block_rows]], axis=0)
            late = late.reshape(tiles, SLOTS, block_rows, LANES)
            for slot in range(SLOTS):
                moved = late[:, slot].reshape(tiles * block_rows, LANES)
                landed[slot] += lane_roll(moved, BLOCK * (slot - part))
        result = 0.0
        for slot in range(SLOTS):
            result += jnp.where(lane // BLOCK == slot, landed[slot], 0.0)
        result = result.reshape(tiles, cores, GROUP, LANES)
        for part in range(cores):
            done_ref[part * tiles : (part + 1) * tiles, own, :] = result[:, part]

    out_ref[...] = done_ref[:, :held, :].astype(BF16)


def gate_kernel(gate_ref, before_ref, taps_ref, out_ref):
    channels = gate_ref.shape[1]
    gate = gate_ref[...].astype(F32)
    extended = jnp.concatenate([before_ref[...].astype(F32), gate], axis=0)
    gate_short = taps_ref[0:1, channels:] * gate
    for lag in range(1, 3):
        gate_short += taps_ref[lag : lag + 1, channels:] * extended[2 - lag : 2 - lag + gate.shape[0]]
    out_ref[...] = gate_short


def out_kernel(gate_ref, mixed_ref, source_ref, target_ref, weight_ref, held_ref, read_sems, write_sems):
    chunks, _, step = weight_ref.shape
    reads = []
    for at in range(chunks):
        columns = source_ref.at[:, pl.ds(at * step, step)]
        reads.append(pltpu.make_async_copy(columns, weight_ref.at[at], read_sems.at[at]))
        reads[-1].start()
    gated = (gate_ref[...] * mixed_ref[...].astype(F32).T).astype(BF16)
    writes = []
    for at in range(chunks):
        reads[at].wait()
        held_ref[at] = jnp.dot(gated, weight_ref[at], preferred_element_type=F32).astype(BF16)
        columns = target_ref.at[:, pl.ds(at * step, step)]
        writes.append(pltpu.make_async_copy(held_ref.at[at], columns, write_sems.at[at]))
        writes[-1].start()
    for write in writes:
        write.wait()


def exchanged(value, axis, step):
    return lax.ppermute(value, axis, [(i, i ^ step) for i in range(lax.axis_size(axis))])


def all_exchanged(values, axis):
    result = list(values)
    for step in reversed(range(1, len(values))):
        result[step] = exchanged(values[step], axis, step)
    return result


def on_device(near, far, tokens, sign_in, sign_out, w_value, w_noise, w_gate, conv_taps, long_filter, w_out):
    rows, width = tokens.shape
    channels = w_gate.shape[1]
    cores = lax.axis_size("dp")
    count = near * far
    half = channels // cores
    held = half // count
    share = w_value.shape[0]
    depth = share * far
    length = count * rows
    near_at, core = lax.axis_index("near"), lax.axis_index("dp")

    lags_start = depth + depth // 8 + channels // 8
    packed_width = lags_start + far * held
    if share % LANES == 0 and far == 4:
        first = pl.pallas_call(
            weights_kernel,
            in_specs=[HBM] * 2,
            out_specs=VMEM,
            out_shape=jax.ShapeDtypeStruct((share, 2 * half), BF16),
            scratch_shapes=[pltpu.SemaphoreType.DMA((2,))],
            compiler_params=params(2),
            cost_estimate=cost(0, MIB // 2),
            name="weights",
        )(*in_hbm(w_value, w_noise))
        far_weights = exchanged(first, "far", 2)
        late_tokens, first = lax.optimization_barrier((tokens, first))
        weights, *chunks = pl.pallas_call(
            functools.partial(pack_kernel, near, far),
            in_specs=[HBM] * 6,
            out_specs=[VMEM] * (1 + near),
            out_shape=[jax.ShapeDtypeStruct((share, 2 * half), BF16)]
            + [jax.ShapeDtypeStruct((rows, packed_width), BF16)] * near,
            scratch_shapes=[
                pltpu.VMEM(sign_in.shape, jnp.int32),
                pltpu.VMEM(sign_out.shape[::-1], jnp.int32),
                pltpu.VMEM((rows, half), F32),
                pltpu.SemaphoreType.DMA((3,)),
                pltpu.SemaphoreType.DMA((2,)),
                pltpu.SemaphoreType.DMA((near * far,)),
            ],
            compiler_params=params(16),
            cost_estimate=cost(2 * rows * 512 * 512, 3 * MIB),
            name="pack",
        )(*in_hbm(late_tokens, sign_in, sign_out.T, long_filter, w_value, w_noise))
        pieces = [weights, exchanged(weights, "far", 1), far_weights, None]
    else:
        own = lax.dynamic_slice_in_dim(jnp.stack([w_value, w_noise]), core * half, half, axis=2)
        own = own.transpose(1, 0, 2).reshape(share, 2 * half)
        pieces = [lax.all_gather(own, "far", axis=0, tiled=True)]
        order = jnp.arange(near) ^ near_at

        def by_owner(array):
            parts = array.reshape(rows, far, near, -1).transpose(2, 0, 1, 3).reshape(near, rows, -1)
            return jnp.take(parts, order, axis=0)

        words = by_owner(sign_in)
        sent = jnp.broadcast_to(sign_out[None], (near, *sign_out.shape))
        own_lags = lax.dynamic_slice_in_dim(long_filter, core * half, half, axis=1)
        signs = [words & 255, words >> 8, sent & 255, sent >> 8, by_owner(own_lags)]
        packed = [by_owner(tokens)] + [part.astype(BF16) for part in signs]
        chunks = list(jnp.concatenate(packed, axis=2))
    chunks = all_exchanged(chunks, "near")

    late_tokens = tokens
    if len(pieces) > 1:
        late_tokens, pieces[2] = lax.optimization_barrier((tokens, pieces[2]))
        pieces[3] = exchanged(pieces[2], "far", 1)
    gate_rows = jnp.dot(late_tokens, w_gate, preferred_element_type=F32).astype(BF16)
    late = 1 % len(pieces)
    pieces[late], chunks[0], gate_rows = lax.optimization_barrier((pieces[late], chunks[0], gate_rows))
    for step in range(1, near):
        chunks[step], _ = lax.optimization_barrier((chunks[step], gate_rows))
    pieces[-1], chunks[-1] = lax.optimization_barrier((pieces[-1], chunks[-1]))
    chunks += [exchanged(chunk, "dp", 1) for chunk in chunks]

    if len(pieces) == 1:
        pieces = [pieces[0][: depth // 2], pieces[0][depth // 2 :]]
    step = depth // len(pieces)
    early = (cores * near - 1) * rows
    *kept, lags = pl.pallas_call(
        functools.partial(project_kernel, near, cores, depth),
        in_specs=[VMEM] * (len(chunks) + len(pieces) - 2),
        out_specs=[VMEM] * 5,
        out_shape=[
            jax.ShapeDtypeStruct((early, half), F32),
            jax.ShapeDtypeStruct((early, half), F32),
            jax.ShapeDtypeStruct((early, half), BF16),
            jax.ShapeDtypeStruct((early, step), BF16),
            jax.ShapeDtypeStruct((far * held, near * rows), F32),
        ],
        compiler_params=params(32),
        cost_estimate=cost(4 * early * (depth - step) * half, 5 * MIB),
        name="project",
    )(*chunks[-2::-1], *pieces[:-1])
    near_shape = jax.ShapeDtypeStruct((far * held, cores * near * rows), BF16)
    partial = pl.pallas_call(
        functools.partial(finish_kernel, near, far, cores, depth),
        in_specs=[VMEM] * (4 + len(chunks) + len(pieces)),
        out_specs=[VMEM] * near,
        out_shape=[near_shape] * near,
        scratch_shapes=[pltpu.VMEM((count * max(held, GROUP), near_shape.shape[1]), F32)],
        compiler_params=params(32),
        cost_estimate=cost(4 * (early * step + rows * depth) * half, 3 * MIB),
        name="finish",
    )(*kept, *chunks[::-1], *pieces)
    partial = list(partial)
    last_rows, partial[0] = lax.optimization_barrier((gate_rows[rows - 2 :], partial[0]))
    before = lax.ppermute(last_rows, ("far", "near"), [(i, i + 1) for i in range(count - 1)])
    partial = all_exchanged(partial, "near")
    *partial[::-1], before = lax.optimization_barrier((*partial[::-1], before))

    far_shape = (held, (cores + 1) * near * rows)
    parts = pl.pallas_call(
        functools.partial(sum_kernel, near, far),
        in_specs=[VMEM] * (1 + near),
        out_specs=[VMEM] * far,
        out_shape=[jax.ShapeDtypeStruct(far_shape, BF16)] * far,
        scratch_shapes=[pltpu.VMEM((far * max(held, GROUP), far_shape[1]), F32)],
        compiler_params=params(16),
        cost_estimate=cost(MIB, MIB),
        name="sum",
    )(lags, *partial[::-1])
    if far == 4:
        parts = all_exchanged(parts, "far")
    else:
        order = jnp.arange(far) ^ lax.axis_index("far")
        parts = lax.all_to_all(jnp.take(jnp.stack(parts), order, axis=0), "far", 0, 0, tiled=True)
        parts = [parts.reshape(far * held, far_shape[1])]

    gate_short = pl.pallas_call(
        gate_kernel,
        in_specs=[VMEM] * 3,
        out_specs=VMEM,
        out_shape=jax.ShapeDtypeStruct((rows, channels), F32),
        compiler_params=params(4),
        cost_estimate=cost(rows * channels * 6, MIB // 2),
        name="gate",
    )(gate_rows, before, conv_taps)
    parts[0], gate_short = lax.optimization_barrier((parts[0], gate_short))

    tiles = length // LANES
    all_rows = tiles * SLOTS * cores * GROUP
    held_rows = max(held, GROUP)
    mixed = pl.pallas_call(
        functools.partial(mix_kernel, near, far, cores, held),
        in_specs=[VMEM] * (1 + len(parts)),
        out_specs=VMEM,
        out_shape=jax.ShapeDtypeStruct((cores * tiles, held, LANES), BF16),
        scratch_shapes=[
            pltpu.VMEM((all_rows, GROUP * BLOCK), BF16),
            pltpu.VMEM((all_rows * (1 if tiles <= 16 else 2), LANES), F32),
            pltpu.VMEM((cores * tiles, held_rows, LANES), F32),
            pltpu.VMEM((GROUP * BLOCK, length), BF16),
            pltpu.VMEM((cores + 1, held, length), F32),
        ],
        compiler_params=params(48),
        cost_estimate=cost(cores * held_rows * BLOCK * length * 256, 2 * MIB),
        name="mix",
    )(conv_taps, *parts[::-1])

    landed = lax.all_to_all(mixed, ("dp", "far", "near"), 0, 0, tiled=True).reshape(channels, rows)
    chunks = 16
    return pl.pallas_call(
        out_kernel,
        in_specs=[VMEM] * 2 + [HBM],
        out_specs=HBM,
        out_shape=jax.ShapeDtypeStruct((rows, width), BF16),
        scratch_shapes=[
            pltpu.VMEM((chunks, channels, width // chunks), BF16),
            pltpu.VMEM((chunks, rows, width // chunks), BF16),
            pltpu.SemaphoreType.DMA((chunks,)),
            pltpu.SemaphoreType.DMA((chunks,)),
        ],
        compiler_params=params(16),
        cost_estimate=cost(2 * rows * width * channels, 5 * MIB),
        name="project_out",
    )(gate_short, landed, *in_hbm(w_out))


def solution(mesh):
    count = mesh.shape["seq"]
    near = 4 if count % 4 == 0 else 1
    far = count // near
    seq_at = mesh.axis_names.index("seq")
    shape = list(mesh.devices.shape)
    shape[seq_at : seq_at + 1] = [far, near]
    names = list(mesh.axis_names)
    names[seq_at : seq_at + 1] = ["far", "near"]
    inner = Mesh(mesh.devices.reshape(shape), tuple(names))
    by_token = P(("dp", "far", "near"), None)
    by_row = P(("far", "near"), None)
    placed = (by_token, by_token, by_token, by_row, by_row, P(), P(), by_row, P())
    return jax.shard_map(
        functools.partial(on_device, near, far),
        mesh=inner,
        in_specs=placed,
        out_specs=by_token,
        check_vma=False,
    )
```
